32 devices in a mesh: head: 2 (over x), blk: 16 (over z, y, core).
Axes of the slice: x: 2, y: 2, z: 4, core: 2. Of those that a mesh axis runs over, the one named last changes fastest.
Arguments:
- tokens: bfloat16 [4096, 768], P(('blk', 'head')), may hold values from -6 to 6
- cotangent: bfloat16 [4096, 768], P(('blk', 'head')), may hold values from -6 to 6
- prev_logits: float32 [4096, 12], P(('blk', 'head')), may hold values from -6 to 6
- routes: int32 [4096, 2], P(('blk', 'head')), may hold values from 0 to 11, all different within a row; in each aligned block of 128 rows (0 to 127, 128 to 255, ...) at most 24 rows name the same one
- lengths: int32 [2], replicated, may hold values from 512 to 2048, as said below
- w_qkv: bfloat16 [768, 2304], P(('head', 'blk')), may hold values from -0.21875 to 0.21875
- w_out: bfloat16 [768, 768], P(('head', 'blk')), may hold values from -3.5 to 3.5
- w_router: bfloat16 [768, 12], P(('head', 'blk')), may hold values from -0.109375 to 0.109375
- w_const: bfloat16 [768, 4], P(('head', 'blk')), may hold values from -0.21875 to 0.21875
- const_vec: bfloat16 [768, 2], P(('head', 'blk')), may hold values from -5 to 5
- norm_gains: bfloat16 [768, 2], P(('head', 'blk')), may hold values from 0.5 to 1.5
- gate_mix: float32 [12, 12], replicated, may hold values from -0.875 to 0.875
- expert_weights: bfloat16 [2048, 8, 3, 768], P('blk', 'head')
Outputs:
- output: bfloat16 [4096, 768], P(('blk', 'head'))
- aux_loss: float32 [], replicated
- d_tokens: bfloat16 [4096, 768], P(('blk', 'head'))
- g_qkv: float32 [768, 2304], P(('head', 'blk'))
- g_out: float32 [768, 768], P(('head', 'blk'))
- g_router: float32 [768, 12], P(('head', 'blk'))
- g_const: float32 [768, 4], P(('head', 'blk'))
- g_vector: float32 [768, 2], P(('head', 'blk'))
- g_gains: float32 [768, 2], P(('head', 'blk'))
- g_mix: float32 [12, 12], replicated
- g_experts: float32 [2048, 8, 3, 768], P('blk', 'head')
The draws below stay inside these ranges and needn't reach their ends.
Inputs may be any that keep to these rules, and one draw needn't show every extreme that they name: `routes`: in each aligned block of 128 rows (the rows of one device), no expert is named by more than 24 rows; the two experts of a row differ. `lengths`: some slot's length is exactly 2048 in every draw.
All inputs are finite; a program needn't handle non-finite values.
Results may differ from the reference program's by a relative error of at most 0.015.
Values may be sent and summed in bfloat16 or wider, within the bound.
A program may use at most 256 MiB of HBM per device.

```python
import math
import jax
import jax.numpy as jnp
import numpy as np
from jax import lax

D = 768
HEADS = 12
HD = 64
FF = 2048
NEXP = 8
NCONST = 2
TOK_DEV = 128
NE = 12
SEQ = 2048
NSEQ = 2
TOKENS = 4096
CAP = 24


def draw_lengths(key, part):
    key = jax.random.fold_in(key, 11)
    first_key, second_key = jax.random.split(key)
    drawn = jax.random.randint(first_key, (NSEQ,), SEQ // 4, SEQ + 1)
    longest = jax.random.randint(second_key, (), 0, NSEQ)
    return jnp.where(jnp.arange(NSEQ) == longest, SEQ, drawn).astype(jnp.int32)


def draw_expert_weights(key, part):
    key = jax.random.fold_in(key, 7)
    base = jax.random.normal(key, (FF, NEXP, 3, D), jnp.float32)
    which = jnp.arange(3)[None, None, :, None]
    scale = jnp.where(which == 2, 1.0 / math.sqrt(FF / 128.0), 1.0 / math.sqrt(D))
    return (jnp.clip(base, -5.0, 5.0) * scale).astype(jnp.bfloat16)


def steps_of(own_key, dims, pieces, least, top_value):
    loudness = 1.0
    for position, blocks in pieces:
        draws = jax.random.uniform(jax.random.fold_in(jax.random.fold_in(own_key, 6), position), (blocks,), jnp.float32, least / len(pieces), top_value / len(pieces))
        loudness = loudness * jnp.repeat(jnp.exp(draws), dims[position] // blocks).reshape((-1,) + (1,) * (len(dims) - 1 - position))
    return loudness


def shared_out(stream_key, own, number, rows, count, top, bound, slope):
    order = jax.random.permutation(stream_key, count)
    crowded, usual = portions_of(count, rows * top, bound, slope, True), portions_of(count, rows * top, bound, slope, False)
    places = jnp.arange(count)

    def named(sizes, turn):
        used = int((sizes > 0).sum())
        fixed = max(1, used // 4)
        moved = fixed + (places - fixed + turn * (used - fixed)) % max(1, count - fixed)
        return jnp.zeros((count,), jnp.int32).at[order[jnp.where(places < fixed, places, moved)]].set(jnp.asarray(sizes, jnp.int32))

    sizes = jnp.where(number % 4 == 0, named(crowded, number // 4), named(usual, number - number // 4 - 1))
    mixed = jax.random.permutation(jax.random.fold_in(own, 3), count)
    source_of, taker = mixed[0:count // 2 * 2:2], mixed[1:count // 2 * 2:2]
    room = jnp.minimum(sizes[source_of] - 1, bound - sizes[taker]) // 2
    room = jnp.where((source_of == order[0]) | (taker == order[0]) | (sizes[taker] == 0), 0, jnp.maximum(room, 0))
    moved = jax.random.randint(jax.random.fold_in(own, 4), (count // 2,), 0, 1 << 20) % (room + 1)
    sizes = sizes.at[source_of].add(-moved).at[taker].add(moved)
    labels = jnp.searchsorted(jnp.cumsum(sizes), jnp.arange(rows * top), side="right").astype(jnp.int32)
    listing = labels.reshape(top, rows).T
    listing = listing[jax.random.permutation(jax.random.fold_in(own, 1), rows)]
    turn = jax.random.randint(jax.random.fold_in(own, 2), (rows, 1), 0, top)
    return jnp.take_along_axis(listing, (jnp.arange(top)[None, :] + turn) % top, axis=1)


def portions_of(amount, total, limit, slope, full):
    loads = [(1 << 20) // math.isqrt(rank ** slope) + 1 for rank in range(1, amount + 1)]
    largest = limit if full else min(limit, max(-(-total // amount), total * loads[0] // sum(loads)))
    least = 1 if total - largest >= amount - 1 else 0
    holding, spare = [largest] + [least] * (amount - 1), total - largest - least * (amount - 1)
    while spare > 0:
        movable = [i for i in range(1, amount) if holding[i] < largest] or [i for i in range(1, amount) if holding[i] < limit]
        pool, left = sum([loads[i] for i in movable]), spare
        for i in movable:
            more = min(limit - holding[i], max(1, left * loads[i] // pool), spare)
            holding[i] = holding[i] + more
            spare = spare - more
    return np.array(holding)


def gaussian(stream_key, extent, deviation, bound, shards=(), kind=jnp.bfloat16):
    gain = steps_of(stream_key, extent, shards, -0.22, 0.18) if shards else 1.0
    entries = jax.random.normal(stream_key, extent, jnp.float32) * deviation * gain
    return jnp.minimum(jnp.maximum(entries, -bound), bound).astype(kind)


def setup_inputs(seed: int = 0) -> dict:
    streams_of = jax.random.split(jax.random.key(seed), 14)
    tokens = gaussian(streams_of[0], (TOKENS, D), 1.0, 6.0, ((0, 32),))
    cotangent = gaussian(streams_of[1], (TOKENS, D), 1.0, 6.0, ((0, 32),))
    prev_logits = gaussian(streams_of[2], (TOKENS, NE), 1.0, 6.0, ((0, 32),), jnp.float32)
    routes_keys = jax.random.split(jax.random.fold_in(streams_of[3], 1), TOKENS // TOK_DEV)
    routes_turns = jax.random.permutation(jax.random.fold_in(streams_of[3], 3), TOKENS // TOK_DEV)
    routes = jax.vmap(lambda own, number: shared_out(jax.random.fold_in(streams_of[3], 2), own, number, TOK_DEV, NE, 2, CAP, 1))(routes_keys, routes_turns).reshape((TOKENS, 2))
    lengths = draw_lengths(jax.random.fold_in(streams_of[13], 71), 0)
    w_qkv = gaussian(streams_of[5], (D, 3 * D), D ** -0.5, 0.21875, ((0, 32),))
    w_out = gaussian(streams_of[6], (D, D), (D // 256) ** -0.5, 3.5, ((0, 32),))
    w_router = gaussian(streams_of[7], (D, NE), (4 * D) ** -0.5, 0.109375, ((0, 32),))
    w_const = gaussian(streams_of[8], (D, 2 * NCONST), D ** -0.5, 0.21875, ((0, 32),))
    const_vec = gaussian(streams_of[9], (D, NCONST), 1.0, 5.0, ((0, 32),))
    norm_gains = jnp.clip(1.0 + 0.1 * jax.random.normal(streams_of[10], (D, 2), jnp.float32), 0.5, 1.5).astype(jnp.bfloat16)
    gate_mix = gaussian(streams_of[11], (NE, NE), (4 * NE) ** -0.5, 0.875, (), jnp.float32)
    expert_weights = draw_expert_weights(jax.random.fold_in(streams_of[13], 71), 0)
    return dict(tokens=tokens, cotangent=cotangent, prev_logits=prev_logits, routes=routes, lengths=lengths, w_qkv=w_qkv, w_out=w_out, w_router=w_router, w_const=w_const, const_vec=const_vec, norm_gains=norm_gains, gate_mix=gate_mix, expert_weights=expert_weights)


eps = 1e-06
aux_weight = 0.01
highest = lax.Precision.HIGHEST
masked_score = -1e+30

@jax.custom_vjp
def low(v):
    return lax.optimization_barrier(v.astype(jnp.bfloat16)).astype(jnp.float32)

@jax.custom_vjp
def low_back(v):
    return v

def low_keep(v):
    return (low(v), None)

def low_pass(kept, grad):
    return (grad,)

def back_keep(v):
    return (v, None)

def back_low(kept, grad):
    return (low(grad),)
low.defvjp(low_keep, low_pass)
low_back.defvjp(back_keep, back_low)

def rms_norm(values, gain_vector):
    return values * lax.rsqrt(lax.optimization_barrier(jnp.mean(values * values, axis=-1, keepdims=True)) + eps) * gain_vector

def rotary(values, positions, turn_sign):
    half_width = values.shape[-1] // 2
    frequency = jnp.exp(jnp.arange(half_width, dtype=jnp.float32) * (-2.0 * math.log(10000.0) / values.shape[-1]))
    angles = positions.astype(jnp.float32)[:, None] * frequency[None, :]
    cosine = jnp.cos(angles)[:, None, :]
    sine_part = turn_sign * jnp.sin(angles)[:, None, :]
    first_half = values[..., :half_width]
    second_half = values[..., half_width:]
    return jnp.concatenate([first_half * cosine - second_half * sine_part, second_half * cosine + first_half * sine_part], axis=-1)

def head_attention(query_head, key_head, value_head, allowed):
    scores = low_back(jnp.dot(query_head, key_head.T, precision=highest) * query_head.shape[-1] ** (-0.5))
    scores = jnp.where(allowed, scores, masked_score)
    weights = jax.nn.softmax(scores, axis=-1)
    return jnp.dot(low(weights), value_head, precision=highest)

def expert_apply(expert_in, weights):
    gate_part = low_back(jnp.dot(expert_in, weights[:, 0, :].T, precision=highest))
    up_part = low_back(jnp.dot(expert_in, weights[:, 1, :].T, precision=highest))
    hidden = low(jax.nn.silu(gate_part) * up_part)
    return jnp.dot(hidden, weights[:, 2, :], precision=highest)

def reference(tokens, cotangent, prev_logits, routes, lengths, w_qkv, w_out, w_router, w_const, const_vec, norm_gains, gate_mix, expert_weights):
    row_ids = jnp.arange(TOKENS, dtype=jnp.int32)
    slot_ids = row_ids // SEQ
    positions = row_ids - slot_ids * SEQ
    live_rows = (positions < lengths[slot_ids]).astype(jnp.float32)
    live_total = jnp.sum(lengths).astype(jnp.float32)
    choose = (routes[:, :, None] == jnp.arange(NE, dtype=jnp.int32)[None, None, :]).astype(jnp.float32)
    counts = lax.optimization_barrier(jnp.sum(lax.optimization_barrier(jnp.sum(choose, axis=1)) * live_rows[:, None], axis=0))
    fraction = counts / (2.0 * live_total)
    slot_pos = jnp.arange(SEQ, dtype=jnp.int32)
    prev_scores = prev_logits.astype(jnp.float32)

    def slot_attention(operands):
        queries, key_rows, value_rows, length = operands
        allowed = (slot_pos[None, :] <= slot_pos[:, None]) & (slot_pos[None, :] < length)

        def one_head(head_operands):
            return jax.checkpoint(head_attention)(head_operands[0], head_operands[1], head_operands[2], allowed)
        result = lax.map(one_head, (queries.transpose(1, 0, 2), key_rows.transpose(1, 0, 2), value_rows.transpose(1, 0, 2)))
        return result.transpose(1, 0, 2)

    def forward(inputs, qkv_w, out_w, router_w, const_w, vector_w, gains, mixing, experts):
        normed_one = low(rms_norm(inputs, gains[:, 0]))
        projected = low_back(jnp.dot(normed_one, qkv_w, precision=highest)).reshape(TOKENS, 3, HEADS, HD)
        queries = low(rotary(projected[:, 0], positions, 1.0)).reshape(NSEQ, SEQ, HEADS, HD)
        key_rows = low(rotary(projected[:, 1], positions, 1.0)).reshape(NSEQ, SEQ, HEADS, HD)
        value_rows = low(projected[:, 2]).reshape(NSEQ, SEQ, HEADS, HD)
        attended = lax.map(slot_attention, (queries, key_rows, value_rows, lengths))
        attended = low_back(low(attended.reshape(TOKENS, D)))
        residual = inputs + jnp.dot(attended, out_w, precision=highest)
        normed_two = low(rms_norm(residual, gains[:, 1]))
        logits = jnp.dot(normed_two, router_w, precision=highest) + jnp.dot(prev_scores, mixing, precision=highest)
        router_prob = jax.nn.softmax(logits, axis=-1)
        gate_values = lax.optimization_barrier(jnp.sum(choose * router_prob[:, None, :], axis=-1))
        expert_share = lax.optimization_barrier(jnp.sum(choose * gate_values[:, :, None], axis=1)) * live_rows[:, None]
        mean_prob = lax.optimization_barrier(jnp.sum(router_prob * live_rows[:, None], axis=0)) / live_total
        aux_loss = NE * jnp.sum(fraction * mean_prob)

        def expert_step(running, packed):
            weights, share_column = packed
            expert_in = low_back(normed_two)
            result = low_back(low(jax.checkpoint(expert_apply)(expert_in, weights)))
            return (running + share_column[:, None] * result, None)
        routed = lax.scan(expert_step, jnp.zeros((TOKENS, D), jnp.float32), (jnp.moveaxis(experts, 1, 0), expert_share[:, :NEXP].T))[0]
        routed = routed + expert_share[:, NEXP + 1:NEXP + 2] * normed_two
        const_mix = jax.nn.softmax(jnp.dot(normed_two, const_w, precision=highest).reshape(TOKENS, NCONST, 2), axis=-1)
        for const_index in range(NCONST):
            const_out = const_mix[:, const_index, 0:1] * normed_two + const_mix[:, const_index, 1:2] * vector_w[:, const_index][None, :]
            routed = routed + expert_share[:, NEXP + 2 + const_index:NEXP + 3 + const_index] * const_out
        return ((residual + routed) * live_rows[:, None], aux_loss)
    operands = (tokens.astype(jnp.float32), w_qkv.astype(jnp.float32), w_out.astype(jnp.float32), w_router.astype(jnp.float32), w_const.astype(jnp.float32), const_vec.astype(jnp.float32), norm_gains.astype(jnp.float32), gate_mix.astype(jnp.float32), expert_weights.astype(jnp.float32))
    (mixed, aux_loss), pullback = jax.vjp(forward, *operands)
    grads = pullback((cotangent.astype(jnp.float32), jnp.asarray(aux_weight, jnp.float32)))
    return (mixed.astype(jnp.bfloat16), aux_loss, grads[0].astype(jnp.bfloat16), grads[1], grads[2], grads[3], grads[4], grads[5], grads[6], grads[7], grads[8])
```

```python
from functools import partial
import functools
import math

import jax
import jax.numpy as jnp
import numpy as np
from jax import lax
from jax.experimental import pallas as pl
from jax.experimental.pallas import tpu as pltpu
from jax.sharding import PartitionSpec as P

HEADS = 12
MESH = pl.DeviceIdType.MESH
f32, bf16 = jnp.float32, jnp.bfloat16
NEG = -1e30
HD = 64
X, C, Y, Z = 1, 2, 4, 8


def place(mask, h, b):
    hb = 1 - h if mask & X else h
    cb = b % 2
    yb = (b // 2) % 2
    zb = (b // 4) % 2
    cb = 1 - cb if mask & C else cb
    yb = 1 - yb if mask & Y else yb
    zb = 1 - zb if mask & Z else zb
    low = zb * 4 + yb * 2 + cb
    return hb, (b // 8) * 8 + low, low * 2 + hb


def head_of(h, b):
    quad = b % 4
    return h * 6 + ((b % 8) // 4) * 3 + quad - quad // 3


def home_of(head):
    h, i = head // 6, head % 6
    return ((i // 3) * 4 + i % 3) * 2 + h


def greet(masks_or_all, h, b, n_blk):
    barrier = pltpu.get_barrier_semaphore()
    if masks_or_all == "all":
        me = b * 2 + h
        total = 2 * n_blk

        def say(k, carry):
            other = (me + k) % total
            pl.semaphore_signal(barrier, inc=1, device_id=(other % 2, other // 2), device_id_type=MESH)
            return carry

        lax.fori_loop(1, total, say, 0)
        pl.semaphore_wait(barrier, total - 1)
    else:
        for m in masks_or_all:
            ph, pb, _ = place(m, h, b)
            pl.semaphore_signal(barrier, inc=1, device_id=(ph, pb), device_id_type=MESH)
        pl.semaphore_wait(barrier, len(masks_or_all))


def turned(qk, cos, sin):
    lane = lax.broadcasted_iota(jnp.int32, qk.shape, 1)
    swapped = jnp.where(lane % 64 < 32, pltpu.roll(qk, 96, 1), pltpu.roll(qk, 32, 1))
    return qk * cos + swapped * sin


def rotary_tables(rows):
    freq = np.exp(np.arange(32, dtype=np.float32) * np.float32(-2.0 * math.log(10000.0) / 64)).astype(np.float32)
    ang = (np.arange(rows, dtype=np.float32)[:, None] * freq[None, :]).astype(np.float32).astype(np.float64)
    cos, sin = np.cos(ang), np.sin(ang)
    return (
        np.concatenate([cos, cos, cos, cos], 1).astype(np.float32),
        np.concatenate([-sin, sin, -sin, sin], 1).astype(np.float32),
    )


def forward_kernel(
    n_blk, lengths, tok, w_in, small_in, cos_hbm, sin_hbm,
    norm_hbm, q_hbm, k_hbm, v_hbm, o_hbm, att_out, sm_out, smt_out,
    xg, pieces, got, w_f, w_b, cos, sin, norm, q, k, v, o, sendbuf, att_in,
    ag_send, ag_recv, pc_send, pc_recv, at_send, at_recv, loc,
):
    h, b = lax.axis_index("head"), lax.axis_index("blk")
    me = b * 2 + h
    total = 2 * n_blk
    _, _, rank = place(0, h, b)
    cos_in = pltpu.make_async_copy(cos_hbm, cos, loc.at[0])
    sin_in = pltpu.make_async_copy(sin_hbm, sin, loc.at[1])
    cos_in.start()
    sin_in.start()
    for p in range(3):
        xg[p, rank] = tok[:, 256 * p : 256 * p + 256]
    greet("all", h, b, n_blk)

    def block_copy(p, m, d, slot):
        _, _, r = place(m, h, b)
        ph, pb, _ = place(d, h, b)
        return pltpu.make_async_remote_copy(
            src_ref=xg.at[p, r], dst_ref=xg.at[p, r],
            send_sem=ag_send.at[p, slot], recv_sem=ag_recv.at[p, m ^ d],
            device_id=(ph, pb), device_id_type=MESH,
        )

    def arrival(p, m):
        _, _, r = place(m, h, b)
        return pltpu.make_async_remote_copy(
            src_ref=xg.at[p, r], dst_ref=xg.at[p, r],
            send_sem=ag_send.at[p, 0], recv_sem=ag_recv.at[p, m],
            device_id=(h, b), device_id_type=MESH,
        )

    sends = []
    counts = [0, 0, 0]

    def send(p, m, d):
        copy = block_copy(p, m, d, counts[p])
        counts[p] += 1
        copy.start()
        sends.append(copy)

    dims = [X, Y, Z]
    orders = [dims[p:] + dims[:p] for p in range(3)]
    for t in range(3):
        for p in range(3):
            send(p, 0, orders[p][t])
    for p in range(3):
        send(p, 0, C)

    w24 = w_in[...].astype(f32)
    small = small_in[...]
    for j in range(12):
        cat = jnp.concatenate(
            [w24[:, 64 * j : 64 * j + 64], w24[:, 768 + 64 * j : 832 + 64 * j],
             w24[:, 1536 + 64 * j : 1600 + 64 * j], small], axis=1)
        pieces[j, :, 0:256] = cat[0:16].astype(bf16)
        pieces[j, :, 256:384] = jnp.concatenate([cat[16:24, 0:128], cat[16:24, 128:256]], axis=0).astype(bf16)

    def piece_copy(kk):
        other = (me + kk) % total
        oh, ob = other % 2, other // 2
        return pltpu.make_async_remote_copy(
            src_ref=pieces.at[head_of(oh, ob)], dst_ref=got.at[me],
            send_sem=pc_send.at[kk], recv_sem=pc_recv.at[me],
            device_id=(oh, ob), device_id_type=MESH,
        )

    def send_piece(kk, carry):
        piece_copy(kk).start()
        return carry

    lax.fori_loop(1, total, send_piece, 0)
    got[me] = pieces[head_of(h, b)]

    for p in range(3):
        d0, d1, d2 = orders[p]
        arrival(p, d0).wait_recv()
        for d in (d1, d2, C):
            send(p, d0, d)
    for p in range(3):
        d0, d1, d2 = orders[p]
        for m in (d1, d0 ^ d1):
            arrival(p, m).wait_recv()
            for d in (d2, C):
                send(p, m, d)
    for p in range(3):
        d0, d1, d2 = orders[p]
        for m in (d2, d0 ^ d2, d1 ^ d2, d0 ^ d1 ^ d2):
            arrival(p, m).wait_recv()
            send(p, m, C)

    def take_piece(kk, carry):
        src = (me + kk) % total
        pltpu.make_async_remote_copy(
            src_ref=pieces.at[0], dst_ref=got.at[src],
            send_sem=pc_send.at[0], recv_sem=pc_recv.at[src],
            device_id=(h, b), device_id_type=MESH,
        ).wait_recv()
        return carry

    lax.fori_loop(1, total, take_piece, 0)

    for src in range(2 * n_blk):
        row = 24 * ((src % 2) * n_blk + src // 2)
        w_f[row : row + 16, :] = got[src, :, 0:256].astype(f32)
        low = got[src, :, 256:384].astype(f32)
        w_f[row + 16 : row + 24, 0:128] = low[0:8]
        w_f[row + 16 : row + 24, 128:256] = low[8:16]
    w_b[...] = w_f[...].astype(bf16)
    sm_out[...] = w_f[:, 128:256]
    smt = jnp.transpose(w_f[:, 128:256])
    smt_out[...] = smt
    gain = smt[64:65, :]

    for p in range(3):
        for m in (C, C ^ X, C ^ Y, C ^ Z, C ^ X ^ Y, C ^ X ^ Z, C ^ Y ^ Z, C ^ X ^ Y ^ Z):
            arrival(p, m).wait_recv()
    cos_in.wait()
    sin_in.wait()

    def one_block(r, carry):
        x = [xg[p, r].astype(f32) for p in range(3)]
        mean = sum(jnp.sum(t * t, axis=1, keepdims=True) for t in x) * (1.0 / 768)
        scale = lax.rsqrt(mean + 1e-6)
        rows = pl.ds(pl.multiple_of(r * 128, 128), 128)
        acc = jnp.zeros((128, 256), f32)
        for p in range(3):
            n = (x[p] * scale * gain[:, 256 * p : 256 * p + 256]).astype(bf16)
            norm[rows, 256 * p : 256 * p + 256] = n
            acc = acc + jnp.dot(n, w_b[256 * p : 256 * p + 256, :], preferred_element_type=f32)
        qk = turned(acc[:, 0:128], cos[rows, :], sin[rows, :])
        q[rows, :] = (qk[:, 0:64] * 0.125).astype(bf16)
        k[rows, :] = qk[:, 64:128].astype(bf16)
        lane = lax.broadcasted_iota(jnp.int32, (128, 128), 1)
        v[rows, :] = jnp.where(lane < 64, acc[:, 128:256], jnp.where(lane == 64, 1.0, 0.0)).astype(bf16)
        return carry

    lax.fori_loop(0, 16, one_block, 0)
    stores = [
        pltpu.make_async_copy(norm, norm_hbm, loc.at[2]),
        pltpu.make_async_copy(q, q_hbm, loc.at[3]),
        pltpu.make_async_copy(k, k_hbm, loc.at[4]),
        pltpu.make_async_copy(v, v_hbm, loc.at[5]),
    ]
    for s in stores:
        s.start()

    length = lengths[b // 8]
    head = head_of(h, b)
    working = (b % 4) != 3
    base = (b // 8) * 8

    def out_copy(r):
        return pltpu.make_async_remote_copy(
            src_ref=sendbuf.at[r], dst_ref=att_in.at[head],
            send_sem=at_send.at[r], recv_sem=at_recv.at[head],
            device_id=(r % 2, base + r // 2), device_id_type=MESH,
        )

    for i in range(8):
        width = 256 * (i + 1)
        s = lax.dot_general(q[256 * i : width, :], k[0:width, :], (((1,), (1,)), ((), ())), preferred_element_type=f32)
        key = lax.broadcasted_iota(jnp.int32, (1, width), 1)
        s = s + jnp.where(key < length, 0.0, NEG)
        rowi = lax.broadcasted_iota(jnp.int32, (256, 256), 0)
        coli = lax.broadcasted_iota(jnp.int32, (256, 256), 1)
        last = jnp.where(coli <= rowi, s[:, width - 256 :], NEG)
        s = last if i == 0 else jnp.concatenate([s[:, : width - 256], last], axis=1)
        m = jnp.max(s, axis=1, keepdims=True)
        e = jnp.exp(s - m).astype(bf16)
        ov = jnp.dot(e, v[0:width, :], preferred_element_type=f32)
        l = ov[:, 64:65]
        lane = lax.broadcasted_iota(jnp.int32, (256, 128), 1)
        ov = jnp.where(lane < 64, ov / l, m + jnp.log(l))
        o[256 * i : width, :] = ov
        oh = ov[:, 0:64]
        for half in range(2):
            r = 2 * i + half
            packed = jnp.concatenate([oh[128 * half : 128 * half + 64], oh[128 * half + 64 : 128 * half + 128]], axis=1)
            sendbuf[r] = packed.astype(bf16)

            @pl.when(working & (r != rank))
            def _(r=r):
                out_copy(r).start()

    o_store = pltpu.make_async_copy(o, o_hbm, loc.at[6])
    o_store.start()

    @pl.when(working)
    def _():
        att_in[head] = sendbuf[rank]

    for j in range(12):
        @pl.when(rank != home_of(j))
        def _(j=j):
            pltpu.make_async_remote_copy(
                src_ref=sendbuf.at[0], dst_ref=att_in.at[j],
                send_sem=at_send.at[0], recv_sem=at_recv.at[j],
                device_id=(h, b), device_id_type=MESH,
            ).wait_recv()

    for j in range(0, 12, 2):
        one, two = att_in[j].astype(f32), att_in[j + 1].astype(f32)
        att_out[0:64, 64 * j : 64 * j + 128] = jnp.concatenate([one[:, 0:64], two[:, 0:64]], axis=1).astype(bf16)
        att_out[64:128, 64 * j : 64 * j + 128] = jnp.concatenate([one[:, 64:128], two[:, 64:128]], axis=1).astype(bf16)

    for copy in sends:
        copy.wait_send()

    def sent_piece(kk, carry):
        piece_copy(kk).wait_send()
        return carry

    lax.fori_loop(1, total, sent_piece, 0)
    for r in range(16):
        @pl.when(working & (r != rank))
        def _(r=r):
            out_copy(r).wait_send()
    for s in stores:
        s.wait()
    o_store.wait()


def attend_and_send(tokens, w_qkv, small, lengths, n_blk):
    cos, sin = rotary_tables(2048)
    vm = pl.BlockSpec(memory_space=pltpu.VMEM)
    hbm = pl.BlockSpec(memory_space=pl.ANY)
    sds = jax.ShapeDtypeStruct
    DMA = pltpu.SemaphoreType.DMA
    return pl.pallas_call(
        functools.partial(forward_kernel, n_blk),
        out_shape=(
            sds((2048, 768), bf16), sds((2048, 64), bf16), sds((2048, 64), bf16), sds((2048, 128), bf16),
            sds((2048, 128), f32), sds((128, 768), bf16), sds((768, 128), f32), sds((128, 768), f32),
        ),
        in_specs=[pl.BlockSpec(memory_space=pltpu.SMEM), vm, vm, vm, hbm, hbm],
        out_specs=(hbm, hbm, hbm, hbm, hbm, vm, vm, vm),
        scratch_shapes=[
            pltpu.VMEM((3, 16, 128, 256), bf16), pltpu.VMEM((12, 16, 384), bf16), pltpu.VMEM((2 * n_blk, 16, 384), bf16),
            pltpu.VMEM((768, 256), f32), pltpu.VMEM((768, 256), bf16),
            pltpu.VMEM((2048, 128), f32), pltpu.VMEM((2048, 128), f32),
            pltpu.VMEM((2048, 768), bf16), pltpu.VMEM((2048, 64), bf16), pltpu.VMEM((2048, 64), bf16), pltpu.VMEM((2048, 128), bf16),
            pltpu.VMEM((2048, 128), f32), pltpu.VMEM((16, 64, 128), bf16), pltpu.VMEM((12, 64, 128), bf16),
            DMA((3, 16)), DMA((3, 16)), DMA((2 * n_blk,)), DMA((2 * n_blk,)), DMA((16,)), DMA((12,)), DMA((8,)),
        ],
        compiler_params=pltpu.CompilerParams(collective_id=0, has_side_effects=True, vmem_limit_bytes=56 * 2**20),
        cost_estimate=pl.CostEstimate(flops=10**9, bytes_accessed=2 * 10**7, transcendentals=0),
        name="attend",
    )(lengths, tokens, w_qkv, small, jnp.asarray(cos), jnp.asarray(sin))


def backward_kernel(
    n_blk, lengths, ag, tok, res_grad, smt, norm_hbm, q_hbm, k_hbm, v_hbm, o_hbm, cos_hbm, sin_hbm, w_hbm,
    dtok_out, gq_out, gain_out,
    norm, q, k, v, o, cos, sin, w_all, agbuf, do_in, do, dk, dv, dqkv, obuf, got, dpq, dpv, g_f, gbuf, g_in,
    a_send, a_recv, b_send, b_recv, g_send, g_recv, loc,
):
    h, b = lax.axis_index("head"), lax.axis_index("blk")
    me = b * 2 + h
    total = 2 * n_blk
    _, _, rank = place(0, h, b)
    base = (b // 8) * 8
    head = head_of(h, b)
    working = (b % 4) != 3
    loads = [
        pltpu.make_async_copy(src, dst, loc.at[i])
        for i, (src, dst) in enumerate([
            (q_hbm, q), (k_hbm, k), (v_hbm, v), (o_hbm, o), (cos_hbm, cos), (sin_hbm, sin), (norm_hbm, norm),
            (w_hbm, w_all)])
    ]
    for c in loads:
        c.start()
    a = ag[...].astype(f32)
    for j in range(12):
        agbuf[j] = jnp.concatenate([a[0:64, 64 * j : 64 * j + 64], a[64:128, 64 * j : 64 * j + 64]], axis=1).astype(bf16)
    greet("all", h, b, n_blk)

    def to_head(j):
        r = home_of(j)
        return pltpu.make_async_remote_copy(
            src_ref=agbuf.at[j], dst_ref=do_in.at[rank], send_sem=a_send.at[j], recv_sem=a_recv.at[rank],
            device_id=(r % 2, base + r // 2), device_id_type=MESH,
        )

    for j in range(12):
        @pl.when(rank != home_of(j))
        def _(j=j):
            to_head(j).start()

    def to_tokens(r):
        return pltpu.make_async_remote_copy(
            src_ref=obuf.at[r], dst_ref=got.at[head], send_sem=b_send.at[r], recv_sem=b_recv.at[head],
            device_id=(r % 2, base + r // 2), device_id_type=MESH,
        )

    def to_owner(kk):
        other = (me + kk) % total
        oh, ob = other % 2, other // 2
        return pltpu.make_async_remote_copy(
            src_ref=gbuf.at[oh * n_blk + ob], dst_ref=g_in.at[me], send_sem=g_send.at[kk], recv_sem=g_recv.at[me],
            device_id=(oh, ob), device_id_type=MESH,
        )

    length = lengths[b // 8]

    @pl.when(working)
    def _():
        do_in[rank] = agbuf[head]
        for c in loads[:6]:
            c.wait()

        def unpack(r, carry):
            @pl.when(r != rank)
            def _():
                pltpu.make_async_remote_copy(
                    src_ref=agbuf.at[0], dst_ref=do_in.at[r], send_sem=a_send.at[0], recv_sem=a_recv.at[r],
                    device_id=(h, b), device_id_type=MESH,
                ).wait_recv()

            t = do_in[r].astype(f32)
            rows = pl.multiple_of(r * 128, 128)
            do[pl.ds(rows, 64), :] = t[:, 0:64].astype(bf16)
            do[pl.ds(rows + 64, 64), :] = t[:, 64:128].astype(bf16)
            return carry

        lax.fori_loop(0, 16, unpack, 0)
        for i in range(7, -1, -1):
            width = 256 * (i + 1)
            lo = 256 * i
            qi, doi = q[lo:width, :], do[lo:width, :]
            s = lax.dot_general(qi, k[0:width, :], (((1,), (1,)), ((), ())), preferred_element_type=f32)
            key = lax.broadcasted_iota(jnp.int32, (1, width), 1)
            ov = o[lo:width, :]
            lse = ov[:, 64:65]
            s = (s - lse) + jnp.where(key < length, 0.0, NEG)
            rowi = lax.broadcasted_iota(jnp.int32, (256, 256), 0)
            coli = lax.broadcasted_iota(jnp.int32, (256, 256), 1)
            last = jnp.where(coli <= rowi, s[:, lo:], NEG)
            s = last if i == 0 else jnp.concatenate([s[:, :lo], last], axis=1)
            p = jnp.exp(s)
            dp = lax.dot_general(doi, v[0:width, 0:64], (((1,), (1,)), ((), ())), preferred_element_type=f32)
            inner = jnp.sum(doi.astype(f32) * ov[:, 0:64], axis=1, keepdims=True)
            ds = (p * (dp - inner)).astype(bf16)
            p = p.astype(bf16)
            dq = jnp.dot(ds, k[0:width, :], preferred_element_type=f32) * 0.125
            dki = lax.dot_general(ds, qi, (((0,), (0,)), ((), ())), preferred_element_type=f32)
            dvi = lax.dot_general(p, doi, (((0,), (0,)), ((), ())), preferred_element_type=f32)
            if i == 7:
                dk[...] = dki
                dv[...] = dvi
            else:
                dk[0:width, :] += dki
                dv[0:width, :] += dvi
            both = jnp.concatenate([dq, dk[lo:width, :]], axis=1)
            both = turned(both, cos[lo:width, :], -sin[lo:width, :]).astype(bf16)
            dvl = dv[lo:width, :]
            dqkv[lo:width, 0:128] = both
            dqkv[lo:width, 128:256] = jnp.concatenate([dvl, jnp.zeros_like(dvl)], axis=1).astype(bf16)
            for half in range(2):
                r = 2 * i + half
                obuf[r, 0:128, :] = both[128 * half : 128 * half + 128]
                obuf[r, 128:192, :] = jnp.concatenate(
                    [dvl[128 * half : 128 * half + 64], dvl[128 * half + 64 : 128 * half + 128]], axis=1).astype(bf16)

                @pl.when(r != rank)
                def _(r=r):
                    to_tokens(r).start()

        got[head] = obuf[rank]
        loads[6].wait()
        for c in range(3):
            g_f[256 * c : 256 * c + 256, :] = lax.dot_general(
                norm[:, 256 * c : 256 * c + 256], dqkv[...], (((0,), (0,)), ((), ())), preferred_element_type=f32)
        for w in range(total):
            t = g_f[24 * w : 24 * w + 24, :]
            gbuf[w, :, 0:256] = t[0:16].astype(bf16)
            gbuf[w, :, 256:384] = jnp.concatenate([t[16:24, 0:128], t[16:24, 128:256]], axis=0).astype(bf16)

        def send_g(kk, carry):
            to_owner(kk).start()
            return carry

        lax.fori_loop(1, total, send_g, 0)
        g_in[me] = gbuf[h * n_blk + b]

    @pl.when(jnp.logical_not(working))
    def _():
        for c in loads[:7]:
            c.wait()

    for j in range(12):
        @pl.when(rank != home_of(j))
        def _(j=j):
            pltpu.make_async_remote_copy(
                src_ref=obuf.at[0], dst_ref=got.at[j], send_sem=b_send.at[0], recv_sem=b_recv.at[j],
                device_id=(h, b), device_id_type=MESH,
            ).wait_recv()
    for j in range(0, 12, 2):
        dpq[:, 128 * j : 128 * j + 128] = got[j, 0:128, :]
        dpq[:, 128 * j + 128 : 128 * j + 256] = got[j + 1, 0:128, :]
        one, two = got[j, 128:192, :].astype(f32), got[j + 1, 128:192, :].astype(f32)
        dpv[0:64, 64 * j : 64 * j + 128] = jnp.concatenate([one[:, 0:64], two[:, 0:64]], axis=1).astype(bf16)
        dpv[64:128, 64 * j : 64 * j + 128] = jnp.concatenate([one[:, 64:128], two[:, 64:128]], axis=1).astype(bf16)
    loads[7].wait()
    dn = lax.dot_general(dpq[...], w_all[:, 0:1536], (((1,), (1,)), ((), ())), preferred_element_type=f32)
    dn = dn + lax.dot_general(dpv[...], w_all[:, 1536:2304], (((1,), (1,)), ((), ())), preferred_element_type=f32)
    x = tok[...].astype(f32)
    scale = lax.rsqrt(jnp.sum(x * x, axis=1, keepdims=True) * (1.0 / 768) + 1e-6)
    xh = x * scale
    gain_out[...] = jnp.broadcast_to(jnp.sum(dn * xh, axis=0, keepdims=True), (8, 768))
    t = dn * smt[64:65, :]
    dx = scale * (t - xh * (jnp.sum(t * xh, axis=1, keepdims=True) * (1.0 / 768)))
    dtok_out[...] = (res_grad[...] + dx).astype(bf16)

    for src in range(total):
        if (src // 2) % 4 == 3:
            continue

        @pl.when(me != src)
        def _(src=src):
            pltpu.make_async_remote_copy(
                src_ref=gbuf.at[0], dst_ref=g_in.at[src], send_sem=g_send.at[0], recv_sem=g_recv.at[src],
                device_id=(h, b), device_id_type=MESH,
            ).wait_recv()
    for j in range(0, 12, 2):
        pair = []
        for jj in (j, j + 1):
            t = sum(g_in[16 * s + home_of(jj)].astype(f32) for s in range(total // 16))
            pair.append(jnp.concatenate(
                [t[:, 0:256], jnp.concatenate([t[0:8, 256:384], t[8:16, 256:384]], axis=1)], axis=0))
        one, two = pair
        for part in range(3):
            gq_out[:, 768 * part + 64 * j : 768 * part + 64 * j + 128] = jnp.concatenate(
                [one[:, 64 * part : 64 * part + 64], two[:, 64 * part : 64 * part + 64]], axis=1)

    for j in range(12):
        @pl.when(rank != home_of(j))
        def _(j=j):
            to_head(j).wait_send()

    @pl.when(working)
    def _():
        for r in range(16):
            @pl.when(r != rank)
            def _(r=r):
                to_tokens(r).wait_send()

        def sent(kk, carry):
            to_owner(kk).wait_send()
            return carry

        lax.fori_loop(1, total, sent, 0)


def attend_back(lengths, ag, tok, res_grad, smt, norm, q, k, v, o, w_all, n_blk):
    cos, sin = rotary_tables(2048)
    vm = pl.BlockSpec(memory_space=pltpu.VMEM)
    hbm = pl.BlockSpec(memory_space=pl.ANY)
    sds = jax.ShapeDtypeStruct
    DMA = pltpu.SemaphoreType.DMA
    V = pltpu.VMEM
    total = 2 * n_blk
    return pl.pallas_call(
        functools.partial(backward_kernel, n_blk),
        out_shape=(sds((128, 768), bf16), sds((24, 2304), f32), sds((8, 768), f32)),
        in_specs=[pl.BlockSpec(memory_space=pltpu.SMEM), vm, vm, vm, vm] + [hbm] * 8,
        out_specs=(vm, vm, vm),
        scratch_shapes=[
            V((2048, 768), bf16), V((2048, 64), bf16), V((2048, 64), bf16), V((2048, 128), bf16), V((2048, 128), f32),
            V((2048, 128), f32), V((2048, 128), f32), V((768, 2304), bf16),
            V((12, 64, 128), bf16), V((16, 64, 128), bf16), V((2048, 64), bf16), V((2048, 64), f32), V((2048, 64), f32),
            V((2048, 256), bf16), V((16, 192, 128), bf16), V((12, 192, 128), bf16), V((128, 1536), bf16), V((128, 768), bf16),
            V((768, 256), f32), V((total, 16, 384), bf16), V((total, 16, 384), bf16),
            DMA((12,)), DMA((16,)), DMA((16,)), DMA((12,)), DMA((total,)), DMA((total,)), DMA((8,)),
        ],
        compiler_params=pltpu.CompilerParams(collective_id=1, has_side_effects=True, vmem_limit_bytes=56 * 2**20),
        cost_estimate=pl.CostEstimate(flops=2 * 10**9, bytes_accessed=2 * 10**7, transcendentals=0),
        name="attend_back",
    )(lengths, ag, tok, res_grad, smt, norm, q, k, v, o, jnp.asarray(cos), jnp.asarray(sin), w_all)


CAP = 24


eps = 1e-06
aux_weight = 0.01
highest = lax.Precision.HIGHEST
masked_score = -1e30


def shifted(block, axis, distance):
    devices = range(lax.axis_size(axis))
    route = [(i - distance, i) for i in devices if i - distance in devices]
    return lax.ppermute(block, axis, route)


def for_sending(x):
    return jax.tree.map(lambda a: a.astype(jnp.bfloat16) if a.dtype == jnp.float32 else a, x)


def rms_norm(values, gain_vector):
    return values * lax.rsqrt(jnp.mean(values * values, axis=-1, keepdims=True) + eps) * gain_vector


def rotary(values, positions, turn_sign):
    half_width = values.shape[-1] // 2
    frequency = jnp.exp(
        jnp.arange(half_width, dtype=jnp.float32) * (-2.0 * math.log(10000.0) / values.shape[-1])
    )
    angles = positions.astype(jnp.float32)[:, None] * frequency[None, :]
    cosine = jnp.cos(angles)[:, None, :]
    sine_part = turn_sign * jnp.sin(angles)[:, None, :]
    first_half = values[..., :half_width]
    second_half = values[..., half_width:]
    return jnp.concatenate(
        [
            first_half * cosine - second_half * sine_part,
            second_half * cosine + first_half * sine_part,
        ],
        axis=-1,
    )


def slot_lengths(slot_ids, lengths):
    slot_table = jnp.arange(lengths.shape[0], dtype=jnp.int32)
    return jnp.sum(jnp.where(slot_ids[:, None] == slot_table[None, :], lengths[None, :], 0), axis=1)


def allowed_mask(query_ids, key_ids, slot_size, lengths):
    query_slot = query_ids // slot_size
    key_slot = key_ids // slot_size
    query_pos = query_ids - query_slot * slot_size
    key_pos = key_ids - key_slot * slot_size
    key_live = (key_pos < slot_lengths(key_slot, lengths)) & (key_ids >= 0)
    return (
        (query_slot[:, None] == key_slot[None, :])
        & (key_pos[None, :] <= query_pos[:, None])
        & key_live[None, :]
    )


def masked_scores(query_block, key_head, query_ids, key_ids, slot_size, lengths):
    scores = lax.dot_general(
        query_block, key_head, (((1,), (1,)), ((), ())), preferred_element_type=jnp.float32
    ) * HD ** (-0.5)
    return jnp.where(allowed_mask(query_ids, key_ids, slot_size, lengths), scores, masked_score)


def attend_forward(queries, key_all, value_all, query_ids, key_ids, slot_size, lengths):
    head_total = queries.shape[1] // HD

    def one_head(head_index):
        query_head = lax.dynamic_slice_in_dim(queries, head_index * HD, HD, 1)
        key_head = lax.dynamic_slice_in_dim(key_all, head_index * HD, HD, 1)
        value_head = lax.dynamic_slice_in_dim(value_all, head_index * HD, HD, 1)
        scores = masked_scores(query_head, key_head, query_ids, key_ids, slot_size, lengths)
        row_max = jnp.max(scores, axis=1, keepdims=True)
        weights = jnp.exp(scores - row_max)
        row_total = jnp.sum(weights, axis=1, keepdims=True)
        probs_low = (weights / row_total).astype(jnp.bfloat16)
        head_outputs = [jnp.dot(probs_low, value_head, preferred_element_type=jnp.float32)]
        log_parts = [row_max[:, 0] + jnp.log(row_total[:, 0])]
        return (jnp.concatenate(head_outputs, axis=0), jnp.concatenate(log_parts, axis=0))

    head_outputs, log_sums = lax.map(one_head, jnp.arange(head_total, dtype=jnp.int32))
    return (head_outputs.transpose(1, 0, 2).reshape(queries.shape[0], queries.shape[1]), log_sums)


def attend_backward(
    queries, key_all, value_all, out_grads, log_sums, query_ids, key_ids, slot_size, lengths
):
    head_total = queries.shape[1] // HD
    block_rows = min(512, queries.shape[0])

    def one_head(head_index):
        query_head = lax.dynamic_slice_in_dim(queries, head_index * HD, HD, 1)
        key_head = lax.dynamic_slice_in_dim(key_all, head_index * HD, HD, 1)
        value_head = lax.dynamic_slice_in_dim(value_all, head_index * HD, HD, 1)
        grad_head = lax.dynamic_slice_in_dim(out_grads, head_index * HD, HD, 1)
        log_head = lax.dynamic_index_in_dim(log_sums, head_index, 0, keepdims=False)
        key_grad = jnp.zeros(key_head.shape, jnp.float32)
        value_grad = jnp.zeros(value_head.shape, jnp.float32)
        grad_block = grad_head[0:block_rows]
        scores = masked_scores(query_head, key_head, query_ids, key_ids, slot_size, lengths)
        probs = jnp.exp(scores - log_head[0:block_rows][:, None])
        probs_low = probs.astype(jnp.bfloat16)
        prob_grads = lax.dot_general(
            grad_block, value_head, (((1,), (1,)), ((), ())), preferred_element_type=jnp.float32
        )
        row_inner = jnp.sum(probs * prob_grads, axis=1, keepdims=True)
        score_grads = (probs * (prob_grads - row_inner)).astype(jnp.bfloat16)
        query_parts = [
            jnp.dot(score_grads, key_head, preferred_element_type=jnp.float32) * HD ** (-0.5)
        ]
        key_grad = key_grad + lax.dot_general(
            score_grads, query_head, (((0,), (0,)), ((), ())), preferred_element_type=jnp.float32
        ) * HD ** (-0.5)
        value_grad = value_grad + lax.dot_general(
            probs_low, grad_block, (((0,), (0,)), ((), ())), preferred_element_type=jnp.float32
        )
        return (jnp.concatenate(query_parts, axis=0), key_grad, value_grad)

    query_grad, key_grad, value_grad = lax.map(one_head, jnp.arange(head_total, dtype=jnp.int32))
    return (
        query_grad.transpose(1, 0, 2).reshape(queries.shape[0], queries.shape[1]),
        key_grad.transpose(1, 0, 2).reshape(key_all.shape[0], key_all.shape[1]),
        value_grad.transpose(1, 0, 2).reshape(value_all.shape[0], value_all.shape[1]),
    )


def fetch_prev(key_heads, value_heads, span_count):
    key_parts = [key_heads]
    value_parts = [value_heads]
    for offset in range(1, span_count):
        arrived = shifted((key_heads, value_heads), "blk", offset)
        key_parts.append(arrived[0])
        value_parts.append(arrived[1])
    return (jnp.concatenate(key_parts, axis=0), jnp.concatenate(value_parts, axis=0))


def router_probs(normed, router_w, mixing, prev_scores):
    logits = jnp.dot(normed, router_w, precision=highest) + jnp.dot(
        prev_scores, mixing, precision=highest
    )
    return jax.nn.softmax(logits, axis=-1)


def branch_sum(router_prob, normed, const_w, vector_w, outputs_pair, choose, live_rows, real_count):
    gate_values = jnp.sum(choose * router_prob[:, None, :], axis=-1)
    expert_share = jnp.sum(choose * gate_values[:, :, None], axis=1) * live_rows[:, None]
    routed = jnp.sum(gate_values[:, :, None] * outputs_pair, axis=1)
    routed = routed + expert_share[:, real_count + 1 : real_count + 2] * normed
    const_count = vector_w.shape[1]
    const_mix = jax.nn.softmax(
        jnp.dot(normed, const_w, precision=highest).reshape(normed.shape[0], const_count, 2),
        axis=-1,
    )
    for const_index in range(const_count):
        const_out = (
            const_mix[:, const_index, 0:1] * normed
            + const_mix[:, const_index, 1:2] * vector_w[:, const_index][None, :]
        )
        routed = (
            routed
            + expert_share[:, real_count + 2 + const_index : real_count + 3 + const_index]
            * const_out
        )
    return routed


def on_device(
    tokens,
    cotangent,
    prev_logits,
    routes,
    lengths,
    w_qkv,
    w_out,
    w_router,
    w_const,
    const_vec,
    norm_gains,
    gate_mix,
    expert_weights,
):
    tok_dev = tokens.shape[0]
    model_width = tokens.shape[1]
    head_count = lax.axis_size("head")
    blk_count = lax.axis_size("blk")
    span_count = max(8, min(blk_count // 4, 8192 // (head_count * tok_dev)) * min(1, tok_dev // 64))
    head_index = lax.axis_index("head")
    blk_index = lax.axis_index("blk")
    slot_size = span_count * head_count * tok_dev
    tok_blk = head_count * tok_dev
    qkv_w, out_w, router_w, const_w, vector_w, gain_pair = (
        lax.all_gather(w_qkv, ("head", "blk"), axis=0, tiled=True),
        lax.all_gather(w_out, ("head", "blk"), axis=0, tiled=True),
        lax.all_gather(w_router, ("head", "blk"), axis=0, tiled=True),
        lax.all_gather(w_const, ("head", "blk"), axis=0, tiled=True),
        lax.all_gather(const_vec, ("head", "blk"), axis=0, tiled=True),
        lax.all_gather(norm_gains, ("head", "blk"), axis=0, tiled=True),
    )
    gain_pair = gain_pair.astype(jnp.float32)
    row_ids = (blk_index * head_count + head_index) * tok_dev + jnp.arange(tok_dev, dtype=jnp.int32)
    slot_ids = row_ids // slot_size
    positions = row_ids - slot_ids * slot_size
    live_rows = (positions < slot_lengths(slot_ids, lengths)).astype(jnp.float32)
    inputs = tokens.astype(jnp.float32)
    normed_one, norm_one_back = jax.vjp(rms_norm, inputs, gain_pair[:, 0])
    normed_one_low = normed_one.astype(jnp.bfloat16)
    projected = jnp.dot(normed_one_low, qkv_w, preferred_element_type=jnp.float32).reshape(
        tok_dev, 3, HEADS, HD
    )
    query_send = (
        rotary(projected[:, 0], positions, 1.0).astype(jnp.bfloat16).reshape(tok_dev, model_width)
    )
    key_send = (
        rotary(projected[:, 1], positions, 1.0).astype(jnp.bfloat16).reshape(tok_dev, model_width)
    )
    value_send = projected[:, 2].astype(jnp.bfloat16).reshape(tok_dev, model_width)
    query_heads, key_heads, value_heads = (
        lax.all_to_all(query_send, "head", split_axis=1, concat_axis=0, tiled=True),
        lax.all_to_all(key_send, "head", split_axis=1, concat_axis=0, tiled=True),
        lax.all_to_all(value_send, "head", split_axis=1, concat_axis=0, tiled=True),
    )
    blk_rows = blk_index * tok_blk + jnp.arange(tok_blk, dtype=jnp.int32)
    blk_pos = blk_rows - blk_rows // slot_size * slot_size
    key_ids = jnp.concatenate([blk_rows - offset * tok_blk for offset in range(span_count)], axis=0)
    key_all, value_all = fetch_prev(key_heads, value_heads, span_count)
    attended, log_sums = attend_forward(
        query_heads, key_all, value_all, blk_rows, key_ids, slot_size, lengths
    )
    attended_tok = lax.all_to_all(
        attended.astype(jnp.bfloat16), "head", split_axis=0, concat_axis=1, tiled=True
    )
    residual = inputs + jnp.dot(attended_tok, out_w, preferred_element_type=jnp.float32)
    normed_two, norm_two_back = jax.vjp(rms_norm, residual, gain_pair[:, 1])
    normed_two_low = normed_two.astype(jnp.bfloat16)
    normed_two_f = normed_two_low.astype(jnp.float32)
    router_prob, router_back = jax.vjp(
        partial(router_probs, prev_scores=prev_logits),
        normed_two_f,
        router_w.astype(jnp.float32),
        gate_mix,
    )
    expert_count = router_w.shape[1]
    real_count = expert_weights.shape[1] * head_count
    choose = (
        routes[:, :, None] == jnp.arange(expert_count, dtype=jnp.int32)[None, None, :]
    ).astype(jnp.float32)
    count_local = jnp.sum(jnp.sum(choose, axis=1) * live_rows[:, None], axis=0)
    prob_local = jnp.sum(router_prob * live_rows[:, None], axis=0)
    count_all, prob_all = lax.psum((count_local, prob_local), ("head", "blk"))
    live_total = jnp.sum(lengths).astype(jnp.float32)
    fraction = count_all / (2.0 * live_total)
    aux_loss = expert_count * jnp.sum(fraction * (prob_all / live_total))
    gate_values = jnp.sum(choose * router_prob[:, None, :], axis=-1)
    out_grad = live_rows[:, None] * cotangent.astype(jnp.float32)
    assigned = routes.reshape(-1)
    live_pairs = jnp.repeat(live_rows, 2)
    is_real = (assigned < real_count) & (live_pairs > 0)
    onehot = (
        (assigned[:, None] == jnp.arange(real_count, dtype=jnp.int32)[None, :]) & is_real[:, None]
    ).astype(jnp.int32)
    slot_rank = jnp.sum((jnp.cumsum(onehot, axis=0) - onehot) * onehot, axis=1)
    target = jnp.where(is_real, assigned * CAP + slot_rank, real_count * CAP)
    source = (
        jnp.full((real_count * CAP + 1,), 2 * tok_dev, jnp.int32)
        .at[target]
        .set(jnp.arange(2 * tok_dev, dtype=jnp.int32))[: real_count * CAP]
    )
    zero_row = jnp.zeros((1, model_width), jnp.bfloat16)
    send_rows = jnp.concatenate([normed_two_low, zero_row], axis=0)[source // 2].reshape(
        real_count, CAP, model_width
    )
    pair_grads = (gate_values.reshape(-1, 1) * jnp.repeat(out_grad, 2, axis=0)).astype(jnp.bfloat16)
    send_grads = jnp.concatenate([pair_grads, zero_row], axis=0)[source].reshape(
        real_count, CAP, model_width
    )
    expert_in, expert_cot = (
        lax.all_to_all(send_rows, "head", split_axis=0, concat_axis=1, tiled=True),
        lax.all_to_all(send_grads, "head", split_axis=0, concat_axis=1, tiled=True),
    )
    weight_piece = lax.all_gather(expert_weights, "blk", axis=0, tiled=True)
    gate_w = weight_piece[:, :, 0, :]
    up_w = weight_piece[:, :, 1, :]
    down_w = weight_piece[:, :, 2, :]
    gate_part = jnp.einsum("esd,ned->esn", expert_in, gate_w, preferred_element_type=jnp.float32)
    up_part = jnp.einsum("esd,ned->esn", expert_in, up_w, preferred_element_type=jnp.float32)
    sigmoid_part = jax.nn.sigmoid(gate_part)
    silu_part = gate_part * sigmoid_part
    hidden = (silu_part * up_part).astype(jnp.bfloat16)
    out_sum = jnp.einsum("esn,ned->esd", hidden, down_w, preferred_element_type=jnp.float32)
    hidden_grad = jnp.einsum("esd,ned->esn", expert_cot, down_w, preferred_element_type=jnp.float32)
    gate_grad = (
        hidden_grad * up_part * (sigmoid_part * (1.0 + gate_part * (1.0 - sigmoid_part)))
    ).astype(jnp.bfloat16)
    up_grad = (hidden_grad * silu_part).astype(jnp.bfloat16)
    in_grad = jnp.einsum("esn,ned->esd", gate_grad, gate_w, preferred_element_type=jnp.float32)
    in_grad = in_grad + jnp.einsum(
        "esn,ned->esd", up_grad, up_w, preferred_element_type=jnp.float32
    )
    hidden_all = hidden
    gate_all = gate_grad
    up_all = up_grad
    out_sum, in_grad, hidden_all, gate_all, up_all = (
        out_sum,
        in_grad,
        hidden_all,
        gate_all,
        up_all,
    )
    hidden_own, gate_own, up_own = (
        lax.all_to_all(hidden_all, "blk", split_axis=2, concat_axis=1, tiled=True),
        lax.all_to_all(gate_all, "blk", split_axis=2, concat_axis=1, tiled=True),
        lax.all_to_all(up_all, "blk", split_axis=2, concat_axis=1, tiled=True),
    )
    rows_in = lax.all_gather(expert_in, "blk", axis=1, tiled=True)
    rows_cot = lax.all_gather(expert_cot, "blk", axis=1, tiled=True)
    gate_w_grad = jnp.einsum("esn,esd->ned", gate_own, rows_in, preferred_element_type=jnp.float32)
    up_w_grad = jnp.einsum("esn,esd->ned", up_own, rows_in, preferred_element_type=jnp.float32)
    down_w_grad = jnp.einsum(
        "esn,esd->ned", hidden_own, rows_cot, preferred_element_type=jnp.float32
    )
    expert_grads = jnp.stack([gate_w_grad, up_w_grad, down_w_grad], axis=2)
    returned, returned_grad = (
        lax.all_to_all(
            out_sum.astype(jnp.bfloat16), "head", split_axis=1, concat_axis=0, tiled=True
        ),
        lax.all_to_all(
            in_grad.astype(jnp.bfloat16), "head", split_axis=1, concat_axis=0, tiled=True
        ),
    )
    outputs_pair = (
        jnp.concatenate([returned.reshape(-1, model_width), zero_row], axis=0)[target]
        .astype(jnp.float32)
        .reshape(tok_dev, 2, model_width)
    )
    input_pair = (
        jnp.concatenate([returned_grad.reshape(-1, model_width), zero_row], axis=0)[target]
        .astype(jnp.float32)
        .reshape(tok_dev, 2, model_width)
    )
    expert_input_grad = input_pair[:, 0] + input_pair[:, 1]
    branch, branch_back = jax.vjp(
        partial(branch_sum, choose=choose, live_rows=live_rows, real_count=real_count),
        router_prob,
        normed_two_f,
        const_w.astype(jnp.float32),
        vector_w.astype(jnp.float32),
        outputs_pair,
    )
    output = ((residual + branch) * live_rows[:, None]).astype(jnp.bfloat16)
    prob_grad, normed_grad_branch, const_grad, vector_grad, unused_grad = branch_back(out_grad)
    aux_grad = aux_weight * expert_count / live_total * fraction[None, :] * live_rows[:, None]
    normed_grad_router, router_grad, mixing_grad = router_back(prob_grad + aux_grad)
    normed_grad = normed_grad_router + normed_grad_branch + expert_input_grad
    residual_grad_norm, gain_two_grad = norm_two_back(normed_grad)
    residual_grad = out_grad + residual_grad_norm
    out_w_grad = jnp.dot(attended_tok.astype(jnp.float32).T, residual_grad, precision=highest)
    attended_grad = jnp.dot(residual_grad, out_w.astype(jnp.float32).T, precision=highest).astype(
        jnp.bfloat16
    )
    attended_grad_heads = lax.all_to_all(
        attended_grad, "head", split_axis=1, concat_axis=0, tiled=True
    )
    key_again, value_again = fetch_prev(key_heads, value_heads, span_count)
    query_grad, key_grad, value_grad = attend_backward(
        query_heads,
        key_again,
        value_again,
        attended_grad_heads,
        log_sums,
        blk_rows,
        key_ids,
        slot_size,
        lengths,
    )
    own_key = key_grad[:tok_blk]
    own_value = value_grad[:tok_blk]
    for offset in range(1, span_count):
        back_key, back_value = shifted(
            (
                for_sending(key_grad[offset * tok_blk : (offset + 1) * tok_blk]),
                for_sending(value_grad[offset * tok_blk : (offset + 1) * tok_blk]),
            ),
            "blk",
            -offset,
        )
        own_key = own_key + back_key
        own_value = own_value + back_value
    local_heads = query_heads.shape[1] // HD
    query_back = (
        rotary(query_grad.reshape(tok_blk, local_heads, HD), blk_pos, -1.0)
        .astype(jnp.bfloat16)
        .reshape(tok_blk, local_heads * HD)
    )
    key_back = (
        rotary(own_key.reshape(tok_blk, local_heads, HD), blk_pos, -1.0)
        .astype(jnp.bfloat16)
        .reshape(tok_blk, local_heads * HD)
    )
    value_back = own_value.astype(jnp.bfloat16)
    query_tok, key_tok, value_tok = (
        lax.all_to_all(query_back, "head", split_axis=0, concat_axis=1, tiled=True),
        lax.all_to_all(key_back, "head", split_axis=0, concat_axis=1, tiled=True),
        lax.all_to_all(value_back, "head", split_axis=0, concat_axis=1, tiled=True),
    )
    projected_grad = jnp.concatenate([query_tok, key_tok, value_tok], axis=1)
    qkv_grad = jnp.dot(normed_one_low.T, projected_grad, preferred_element_type=jnp.float32)
    normed_one_grad = jnp.dot(projected_grad, qkv_w.T, preferred_element_type=jnp.float32)
    inputs_grad_norm, gain_one_grad = norm_one_back(normed_one_grad)
    token_grad = (residual_grad + inputs_grad_norm).astype(jnp.bfloat16)
    weight_grads = (
        lax.psum_scatter(qkv_grad, ("head", "blk"), scatter_dimension=0, tiled=True),
        lax.psum_scatter(out_w_grad, ("head", "blk"), scatter_dimension=0, tiled=True),
        lax.psum_scatter(router_grad, ("head", "blk"), scatter_dimension=0, tiled=True),
        lax.psum_scatter(const_grad, ("head", "blk"), scatter_dimension=0, tiled=True),
        lax.psum_scatter(vector_grad, ("head", "blk"), scatter_dimension=0, tiled=True),
        lax.psum_scatter(
            jnp.stack([gain_one_grad, gain_two_grad], axis=1),
            ("head", "blk"),
            scatter_dimension=0,
            tiled=True,
        ),
    )
    mixing_total = lax.psum(mixing_grad, ("head", "blk"))
    return (
        output,
        aux_loss,
        token_grad,
        weight_grads[0],
        weight_grads[1],
        weight_grads[2],
        weight_grads[3],
        weight_grads[4],
        weight_grads[5],
        mixing_total,
        expert_grads,
    )


def on_device_small(
    tokens, cotangent, prev_logits, routes, lengths, w_qkv, w_out, w_router, w_const, const_vec, norm_gains, gate_mix,
    expert_weights,
):
    tok_dev, model_width = tokens.shape
    head_count, blk_count = lax.axis_size("head"), lax.axis_size("blk")
    head_index, blk_index = lax.axis_index("head"), lax.axis_index("blk")
    slot_size = 8 * head_count * tok_dev
    both = ("head", "blk")
    small = jnp.concatenate(
        [norm_gains, w_router, w_const, const_vec, jnp.zeros((24, 44), bf16)], axis=1).astype(f32)
    out_w = lax.all_gather(w_out, both, axis=0, tiled=True)
    w_local = w_qkv.reshape(24, 3, 12, 64)
    w_local = jnp.concatenate(
        [w_local[:, :2].transpose(0, 2, 1, 3).reshape(24, 1536), w_qkv[:, 1536:]], axis=1)
    w_all = lax.all_gather(w_local, both, axis=0, tiled=True)
    norm, q, k, v, o, attended_tok, sm, smt = attend_and_send(tokens, w_qkv, small, lengths, blk_count)
    router_w, const_w, vector_w = sm[:, 66:78], sm[:, 78:82], sm[:, 82:84]
    gain_two = smt[65]
    row_ids = (blk_index * head_count + head_index) * tok_dev + jnp.arange(tok_dev, dtype=jnp.int32)
    slot_ids = row_ids // slot_size
    positions = row_ids - slot_ids * slot_size
    live_rows = (positions < slot_lengths(slot_ids, lengths)).astype(f32)
    inputs = tokens.astype(f32)
    residual = inputs + jnp.dot(attended_tok, out_w, preferred_element_type=f32)
    normed_two, norm_two_back = jax.vjp(rms_norm, residual, gain_two)
    normed_two_low = normed_two.astype(bf16)
    normed_two_f = normed_two_low.astype(f32)
    router_prob, router_back = jax.vjp(
        partial(router_probs, prev_scores=prev_logits), normed_two_f, router_w, gate_mix)
    expert_count = 12
    real_count = expert_weights.shape[1] * head_count
    choose = (routes[:, :, None] == jnp.arange(expert_count, dtype=jnp.int32)[None, None, :]).astype(f32)
    count_local = jnp.sum(jnp.sum(choose, axis=1) * live_rows[:, None], axis=0)
    prob_local = jnp.sum(router_prob * live_rows[:, None], axis=0)
    count_all, prob_all = lax.psum((count_local, prob_local), both)
    live_total = jnp.sum(lengths).astype(f32)
    fraction = count_all / (2.0 * live_total)
    aux_loss = expert_count * jnp.sum(fraction * (prob_all / live_total))
    gate_values = jnp.sum(choose * router_prob[:, None, :], axis=-1)
    out_grad = live_rows[:, None] * cotangent.astype(f32)
    assigned = routes.reshape(-1)
    live_pairs = jnp.repeat(live_rows, 2)
    is_real = (assigned < real_count) & (live_pairs > 0)
    onehot = (
        (assigned[:, None] == jnp.arange(real_count, dtype=jnp.int32)[None, :]) & is_real[:, None]
    ).astype(jnp.int32)
    slot_rank = jnp.sum((jnp.cumsum(onehot, axis=0) - onehot) * onehot, axis=1)
    target = jnp.where(is_real, assigned * CAP + slot_rank, real_count * CAP)
    source = (
        jnp.full((real_count * CAP + 1,), 2 * tok_dev, jnp.int32)
        .at[target]
        .set(jnp.arange(2 * tok_dev, dtype=jnp.int32))[: real_count * CAP]
    )
    zero_row = jnp.zeros((1, model_width), bf16)
    send_rows = jnp.concatenate([normed_two_low, zero_row], axis=0)[source // 2].reshape(real_count, CAP, model_width)
    pair_grads = (gate_values.reshape(-1, 1) * jnp.repeat(out_grad, 2, axis=0)).astype(bf16)
    send_grads = jnp.concatenate([pair_grads, zero_row], axis=0)[source].reshape(real_count, CAP, model_width)
    expert_in, expert_cot = (
        lax.all_to_all(send_rows, "head", split_axis=0, concat_axis=1, tiled=True),
        lax.all_to_all(send_grads, "head", split_axis=0, concat_axis=1, tiled=True),
    )
    rows_in = lax.all_gather(expert_in, "blk", axis=1, tiled=True)
    rows_cot = lax.all_gather(expert_cot, "blk", axis=1, tiled=True)
    gate_w = expert_weights[:, :, 0, :]
    up_w = expert_weights[:, :, 1, :]
    down_w = expert_weights[:, :, 2, :]
    gate_part = jnp.einsum("esd,ned->esn", rows_in, gate_w, preferred_element_type=f32)
    up_part = jnp.einsum("esd,ned->esn", rows_in, up_w, preferred_element_type=f32)
    sigmoid_part = jax.nn.sigmoid(gate_part)
    silu_part = gate_part * sigmoid_part
    hidden = (silu_part * up_part).astype(bf16)
    hidden_grad = jnp.einsum("esd,ned->esn", rows_cot, down_w, preferred_element_type=f32)
    gate_grad = (hidden_grad * up_part * (sigmoid_part * (1.0 + gate_part * (1.0 - sigmoid_part)))).astype(bf16)
    up_grad = (hidden_grad * silu_part).astype(bf16)
    in_grad = jnp.einsum("esn,ned->esd", gate_grad, gate_w, preferred_element_type=f32)
    in_grad = in_grad + jnp.einsum("esn,ned->esd", up_grad, up_w, preferred_element_type=f32)
    in_grad = lax.psum_scatter(in_grad.astype(bf16), "blk", scatter_dimension=1, tiled=True)
    out_sum = jnp.einsum("esn,ned->esd", hidden, down_w, preferred_element_type=f32)
    out_sum = lax.psum_scatter(out_sum.astype(bf16), "blk", scatter_dimension=1, tiled=True)
    gate_w_grad = jnp.einsum("esn,esd->ned", gate_grad, rows_in, preferred_element_type=f32)
    up_w_grad = jnp.einsum("esn,esd->ned", up_grad, rows_in, preferred_element_type=f32)
    down_w_grad = jnp.einsum("esn,esd->ned", hidden, rows_cot, preferred_element_type=f32)
    expert_grads = jnp.stack([gate_w_grad, up_w_grad, down_w_grad], axis=2)
    returned, returned_grad = (
        lax.all_to_all(out_sum, "head", split_axis=1, concat_axis=0, tiled=True),
        lax.all_to_all(in_grad, "head", split_axis=1, concat_axis=0, tiled=True),
    )
    outputs_pair = (
        jnp.concatenate([returned.reshape(-1, model_width), zero_row], axis=0)[target]
        .astype(f32).reshape(tok_dev, 2, model_width)
    )
    input_pair = (
        jnp.concatenate([returned_grad.reshape(-1, model_width), zero_row], axis=0)[target]
        .astype(f32).reshape(tok_dev, 2, model_width)
    )
    expert_input_grad = input_pair[:, 0] + input_pair[:, 1]
    branch, branch_back = jax.vjp(
        partial(branch_sum, choose=choose, live_rows=live_rows, real_count=real_count),
        router_prob, normed_two_f, const_w, vector_w, outputs_pair)
    output = ((residual + branch) * live_rows[:, None]).astype(bf16)
    prob_grad, normed_grad_branch, const_grad, vector_grad, unused_grad = branch_back(out_grad)
    aux_grad = aux_weight * expert_count / live_total * fraction[None, :] * live_rows[:, None]
    normed_grad_router, router_grad, mixing_grad = router_back(prob_grad + aux_grad)
    normed_grad = normed_grad_router + normed_grad_branch + expert_input_grad
    residual_grad_norm, gain_two_grad = norm_two_back(normed_grad)
    residual_grad = out_grad + residual_grad_norm
    residual_grad_low = residual_grad.astype(bf16)
    out_w_grad = jnp.dot(attended_tok.T, residual_grad_low, preferred_element_type=f32)
    attended_grad = jnp.dot(residual_grad_low, out_w.T, preferred_element_type=f32).astype(bf16)
    token_grad, qkv_grad, gain_one = attend_back(
        lengths, attended_grad, tokens, residual_grad, smt, norm, q, k, v, o, w_all, blk_count)
    weight_grads = (
        lax.psum_scatter(out_w_grad, both, scatter_dimension=0, tiled=True),
        lax.psum_scatter(
            jnp.concatenate([router_grad, const_grad, vector_grad, gain_one[0][:, None], gain_two_grad[:, None]], axis=1),
            both, scatter_dimension=0, tiled=True),
    )
    mixing_total = lax.psum(mixing_grad, both)
    tail = weight_grads[1]
    return (
        output, aux_loss, token_grad, qkv_grad, weight_grads[0], tail[:, 0:12], tail[:, 12:16], tail[:, 16:18],
        tail[:, 18:20], mixing_total, expert_grads,
    )


def solution(mesh):
    small = mesh.shape["blk"] == 16 and mesh.shape["head"] == 2
    return jax.shard_map(
        on_device_small if small else on_device,
        mesh=mesh,
        in_specs=(
            P(("blk", "head"), None),
            P(("blk", "head"), None),
            P(("blk", "head"), None),
            P(("blk", "head"), None),
            P(),
            P(("head", "blk"), None),
            P(("head", "blk"), None),
            P(("head", "blk"), None),
            P(("head", "blk"), None),
            P(("head", "blk"), None),
            P(("head", "blk"), None),
            P(),
            P("blk", "head", None, None),
        ),
        out_specs=(
            P(("blk", "head"), None),
            P(),
            P(("blk", "head"), None),
            P(("head", "blk"), None),
            P(("head", "blk"), None),
            P(("head", "blk"), None),
            P(("head", "blk"), None),
            P(("head", "blk"), None),
            P(("head", "blk"), None),
            P(),
            P("blk", "head", None, None),
        ),
        check_vma=False,
    )
```

```python
from functools import partial
import functools
import math

import jax
import jax.numpy as jnp
import numpy as np
from jax import lax
from jax.experimental import pallas as pl
from jax.experimental.pallas import tpu as pltpu
from jax.sharding import PartitionSpec as P

HEADS = 12
MESH = pl.DeviceIdType.MESH
f32, bf16 = jnp.float32, jnp.bfloat16
NEG = -1e30
HD = 64
X, C, Y, Z = 1, 2, 4, 8


def place(mask, h, b):
    hb = 1 - h if mask & X else h
    cb = b % 2
    yb = (b // 2) % 2
    zb = (b // 4) % 2
    cb = 1 - cb if mask & C else cb
    yb = 1 - yb if mask & Y else yb
    zb = 1 - zb if mask & Z else zb
    low = zb * 4 + yb * 2 + cb
    return hb, (b // 8) * 8 + low, low * 2 + hb


def head_of(h, b):
    quad = b % 4
    return h * 6 + ((b % 8) // 4) * 3 + quad - quad // 3


def home_of(head):
    h, i = head // 6, head % 6
    return ((i // 3) * 4 + i % 3) * 2 + h


def greet(masks_or_all, h, b, n_blk):
    barrier = pltpu.get_barrier_semaphore()
    if masks_or_all == "all":
        me = b * 2 + h
        total = 2 * n_blk

        def say(k, carry):
            other = (me + k) % total
            pl.semaphore_signal(barrier, inc=1, device_id=(other % 2, other // 2), device_id_type=MESH)
            return carry

        lax.fori_loop(1, total, say, 0)
        pl.semaphore_wait(barrier, total - 1)
    else:
        for m in masks_or_all:
            ph, pb, _ = place(m, h, b)
            pl.semaphore_signal(barrier, inc=1, device_id=(ph, pb), device_id_type=MESH)
        pl.semaphore_wait(barrier, len(masks_or_all))


def turned(qk, cos, sin):
    lane = lax.broadcasted_iota(jnp.int32, qk.shape, 1)
    swapped = jnp.where(lane % 64 < 32, pltpu.roll(qk, 96, 1), pltpu.roll(qk, 32, 1))
    return qk * cos + swapped * sin


def rotary_tables(rows):
    freq = np.exp(np.arange(32, dtype=np.float32) * np.float32(-2.0 * math.log(10000.0) / 64)).astype(np.float32)
    ang = (np.arange(rows, dtype=np.float32)[:, None] * freq[None, :]).astype(np.float32).astype(np.float64)
    cos, sin = np.cos(ang), np.sin(ang)
    return (
        np.concatenate([cos, cos, cos, cos], 1).astype(np.float32),
        np.concatenate([-sin, sin, -sin, sin], 1).astype(np.float32),
    )


class RowGather:
    def __init__(self, buf, sems, h, b, straight=False):
        self.buf, self.h, self.b, self.straight = buf, h, b, straight
        self.parts = range(buf.shape[1])
        self.zs, self.ys, self.cs, self.zr, self.yr, self.cr = sems
        self.z, self.y, self.c = b // 4, (b // 2) % 2, b % 2

    def nth(self, k):
        return nearest(self.z, k)

    def at(self, z, y, c, p):
        return self.buf.at[z * 4 + y * 2 + c, p]

    def copy(self, where, send, recv, device):
        return pltpu.make_async_remote_copy(
            src_ref=where, dst_ref=where, send_sem=send, recv_sem=recv, device_id=device, device_id_type=MESH)

    def along_z(self, k, step, p):
        zz = self.nth(k)
        return self.copy(self.at(zz, self.y, self.c, p), self.zs.at[(step + 1) // 2, k, p], self.zr.at[zz, p],
                         (self.h, self.b + 4 * step))

    def to_z(self, k, p):
        return self.copy(self.at(self.z, self.y, self.c, p), self.zs.at[0, k, p], self.zr.at[self.z, p],
                         (self.h, self.nth(k) * 4 + self.b % 4))

    def over_y(self, k, p):
        zz = self.nth(k)
        return self.copy(self.at(zz, self.y, self.c, p), self.ys.at[k, p], self.yr.at[zz, p],
                         (self.h, self.b + 2 - 4 * self.y))

    def over_core(self, k, far, p):
        zz = self.nth(k)
        yy = 1 - self.y if far else self.y
        return self.copy(self.at(zz, yy, self.c, p), self.cs.at[far, k, p], self.cr.at[far, zz, p],
                         (self.h, self.b + 1 - 2 * self.c))

    def own_z(self, act):
        for p in self.parts:
            if self.straight:
                for k in range(1, 4):
                    act(self.to_z(k, p))
            else:
                for step in (1, -1):
                    @pl.when((self.z + step >= 0) & (self.z + step <= 3))
                    def _(step=step, p=p):
                        act(self.along_z(0, step, p))

    def relay(self, k, p, act):
        if self.straight:
            return
        zz = self.nth(k)

        @pl.when((zz < self.z) & (self.z < 3))
        def _():
            act(self.along_z(k, 1, p))

        @pl.when((zz > self.z) & (self.z > 0))
        def _():
            act(self.along_z(k, -1, p))

    def start(self):
        self.own_z(lambda c: c.start())
        for p in self.parts:
            self.over_y(0, p).start()
        for p in self.parts:
            self.over_core(0, 0, p).start()

    def arrived(self, where, sem):
        self.copy(where, self.zs.at[0, 0, 0], sem, (self.h, self.b)).wait_recv()

    def got_z(self, k):
        zz = self.nth(k)
        for p in self.parts:
            self.arrived(self.at(zz, self.y, self.c, p), self.zr.at[zz, p])
            self.relay(k, p, lambda c: c.start())
            self.over_y(k, p).start()
            self.over_core(k, 0, p).start()

    def got_y(self, k):
        zz = self.nth(k)
        for p in self.parts:
            self.arrived(self.at(zz, 1 - self.y, self.c, p), self.yr.at[zz, p])
            self.over_core(k, 1, p).start()

    def got_core(self, k):
        zz = self.nth(k)
        for far in range(2):
            yy = 1 - self.y if far else self.y
            for p in self.parts:
                self.arrived(self.at(zz, yy, 1 - self.c, p), self.cr.at[far, zz, p])

    def finish(self):
        self.own_z(lambda c: c.wait_send())
        for p in self.parts:
            for k in range(4):
                if k:
                    self.relay(k, p, lambda c: c.wait_send())
                self.over_y(k, p).wait_send()
                self.over_core(k, 0, p).wait_send()
                self.over_core(k, 1, p).wait_send()


def nearest(z, k):
    near = z - (z // 2) * (2 * z - 3)
    low = k + (1 - 2 * k) * near if k < 2 else k
    return low + (z // 2) * (3 - 2 * low)


def gather_sems(parts):
    DMA = pltpu.SemaphoreType.DMA
    return [DMA((2, 4, parts)), DMA((4, parts)), DMA((2, 4, parts)), DMA((4, parts)), DMA((4, parts)), DMA((2, 4, parts))]


def fold(rows):
    half = rows.shape[1] // 2
    low = jnp.concatenate([rows[16:24, :half], rows[16:24, half:]], axis=0)
    return jnp.concatenate([rows[0:16], low], axis=1).astype(bf16)


def routing_table(routes, live):
    lane = lax.broadcasted_iota(jnp.int32, (128, 128), 1)
    row = lax.broadcasted_iota(jnp.int32, (128, 128), 0)
    named = jnp.where((routes[:, 0:1] == lane) | (routes[:, 1:2] == lane), live, 0.0)
    before = jnp.where(lane < row, 1.0, 0.0).astype(bf16)
    rank = jnp.dot(before, named.astype(bf16), preferred_element_type=f32)
    return named, named * (rank + 1.0)


def expert_lanes(h):
    e = lax.broadcasted_iota(jnp.int32, (128, 256), 0)
    s = lax.broadcasted_iota(jnp.int32, (128, 256), 1)
    return jnp.where((s < 192) & (e == 4 * h + s // 48), 1.0, 0.0)


def slot_table(ranks, h, source_h):
    spread = jnp.dot(ranks.astype(bf16), expert_lanes(h).astype(bf16), preferred_element_type=f32)
    s = lax.broadcasted_iota(jnp.int32, (128, 256), 1)
    place_in = s % 48 - 24 * source_h
    inside = (place_in >= 0) & (place_in < 24) & (s < 192)
    return jnp.where(inside & (spread == (place_in + 1).astype(f32)), 1.0, 0.0)


def live_column(h, b, length):
    row = lax.broadcasted_iota(jnp.int32, (128, 1), 0) + ((b % 8) * 2 + h) * 128
    return jnp.where(row < length, 1.0, 0.0)


def forward_kernel(
    n_blk, lengths, tok, cot, routes, w_in, small_in, wo_in, cos_hbm, sin_hbm,
    norm_hbm, q_hbm, k_hbm, v_hbm, o_hbm, cot_hbm, att_out, sm_out, smt_out, cnt_out, wo_out, pt_out,
    xg, pieces, got, w_f, w_b, cos, sin, norm, q, k, v, o, sendbuf, att_in,
    rank_own, rank_far, cot_far, cot_rows, wo_all, wo_f,
    ag_send, ag_recv, pc_send, pc_recv, at_send, at_recv, loc, x_send, x_recv, *gathers,
):
    h, b = lax.axis_index("head"), lax.axis_index("blk")
    me = b * 2 + h
    total = 2 * n_blk
    _, _, rank = place(0, h, b)
    cos_in = pltpu.make_async_copy(cos_hbm, cos, loc.at[9])
    sin_in = pltpu.make_async_copy(sin_hbm, sin, loc.at[10])
    cos_in.start()
    sin_in.start()
    for p in range(3):
        xg[p, rank] = tok[:, 256 * p : 256 * p + 256]
    greet("all", h, b, n_blk)

    def block_copy(p, m, d, slot):
        _, _, r = place(m, h, b)
        ph, pb, _ = place(d, h, b)
        return pltpu.make_async_remote_copy(
            src_ref=xg.at[p, r], dst_ref=xg.at[p, r],
            send_sem=ag_send.at[p, slot], recv_sem=ag_recv.at[p, m ^ d],
            device_id=(ph, pb), device_id_type=MESH,
        )

    def arrival(p, m):
        _, _, r = place(m, h, b)
        return pltpu.make_async_remote_copy(
            src_ref=xg.at[p, r], dst_ref=xg.at[p, r],
            send_sem=ag_send.at[p, 0], recv_sem=ag_recv.at[p, m],
            device_id=(h, b), device_id_type=MESH,
        )

    sends = []
    counts = [0, 0, 0]

    def send(p, m, d):
        copy = block_copy(p, m, d, counts[p])
        counts[p] += 1
        copy.start()
        sends.append(copy)

    dims = [X, Y, Z]
    orders = [dims[p:] + dims[:p] for p in range(3)]
    for t in range(3):
        for p in range(3):
            send(p, 0, orders[p][t])
    for p in range(3):
        send(p, 0, C)

    length = lengths[b // 8]
    named, ranks = routing_table(routes[...], live_column(h, b, length))
    rank_own[...] = ranks.astype(bf16)
    wo_all[b, 0, h] = fold(wo_in[...].astype(f32))

    w24 = w_in[...].astype(f32)
    count = pltpu.roll(jnp.sum(named, axis=0, keepdims=True), 20, 1)[:, 0:64]
    small = small_in[...]
    small = small + jnp.where(lax.broadcasted_iota(jnp.int32, (24, 64), 0) == 0, count, 0.0)
    for j in range(12):
        cat = jnp.concatenate(
            [w24[:, 64 * j : 64 * j + 64], w24[:, 768 + 64 * j : 832 + 64 * j],
             w24[:, 1536 + 64 * j : 1600 + 64 * j], small], axis=1)
        pieces[j] = fold(cat)

    def piece_copy(kk):
        other = (me + kk) % total
        oh, ob = other % 2, other // 2
        return pltpu.make_async_remote_copy(
            src_ref=pieces.at[head_of(oh, ob)], dst_ref=got.at[me],
            send_sem=pc_send.at[kk], recv_sem=pc_recv.at[me],
            device_id=(oh, ob), device_id_type=MESH,
        )

    def send_piece(kk, carry):
        piece_copy(kk).start()
        return carry

    lax.fori_loop(1, total, send_piece, 0)
    got[me] = pieces[head_of(h, b)]

    for p in range(3):
        d0, d1, d2 = orders[p]
        arrival(p, d0).wait_recv()
        for d in (d1, d2, C):
            send(p, d0, d)
    for p in range(3):
        d0, d1, d2 = orders[p]
        for m in (d1, d0 ^ d1):
            arrival(p, m).wait_recv()
            for d in (d2, C):
                send(p, m, d)
    swaps = [
        pltpu.make_async_remote_copy(
            src_ref=src, dst_ref=dst, send_sem=x_send.at[n], recv_sem=x_recv.at[n],
            device_id=(1 - h, b), device_id_type=MESH)
        for n, (src, dst) in enumerate([(wo_all.at[b, 0, h], wo_all.at[b, 0, h]), (rank_own, rank_far), (cot, cot_far)])
    ]
    for c in swaps:
        c.start()
    for p in range(3):
        d0, d1, d2 = orders[p]
        for m in (d2, d0 ^ d2, d1 ^ d2, d0 ^ d1 ^ d2):
            arrival(p, m).wait_recv()
            send(p, m, C)

    def take_piece(kk, carry):
        src = (me + kk) % total
        pltpu.make_async_remote_copy(
            src_ref=pieces.at[0], dst_ref=got.at[src],
            send_sem=pc_send.at[0], recv_sem=pc_recv.at[src],
            device_id=(h, b), device_id_type=MESH,
        ).wait_recv()
        return carry

    lax.fori_loop(1, total, take_piece, 0)

    for src in range(2 * n_blk):
        row = 24 * ((src % 2) * n_blk + src // 2)
        w_f[row : row + 16, :] = got[src, :, 0:256].astype(f32)
        low = got[src, :, 256:384].astype(f32)
        w_f[row + 16 : row + 24, 0:128] = low[0:8]
        w_f[row + 16 : row + 24, 128:256] = low[8:16]
    w_b[...] = w_f[...].astype(bf16)
    sm = pltpu.roll(w_f[:, 128:256], 64, 1)
    lane = lax.broadcasted_iota(jnp.int32, (768, 128), 1)
    cnt = jnp.sum(jnp.where((lane >= 20) & (lane < 32), sm, 0.0), axis=0, keepdims=True)
    cnt_out[...] = jnp.broadcast_to(pltpu.roll(cnt, 108, 1), (8, 128))
    sm = jnp.where(lane < 20, sm, 0.0)
    sm_out[...] = sm.astype(bf16)
    smt = jnp.transpose(sm)
    smt_out[...] = smt[0:32, :]
    gain = smt[16:17, :]

    pltpu.make_async_remote_copy(
        src_ref=wo_all.at[b, 0, h], dst_ref=wo_all.at[b, 0, 1 - h], send_sem=x_send.at[0], recv_sem=x_recv.at[0],
        device_id=(h, b), device_id_type=MESH).wait_recv()
    wo_gather = RowGather(wo_all, gathers[0:6], h, b, straight=True)
    wo_gather.start()
    swaps[1].wait_recv()
    swaps[2].wait_recv()
    pt = [slot_table(ranks, h, h).astype(bf16), slot_table(rank_far[...].astype(f32), h, 1 - h).astype(bf16)]
    pt_out[0] = pt[0]
    pt_out[1] = pt[1]
    picked = sum(
        lax.dot_general(t[:, 0:192], c[...], (((0,), (0,)), ((), ())), preferred_element_type=f32)
        for t, c in zip(pt, (cot, cot_far))).astype(bf16)
    cot_rows[b, 0] = picked[0:96]
    cot_rows[b, 1] = picked[96:192]
    cot_gather = RowGather(cot_rows, gathers[6:12], h, b, straight=True)
    cot_gather.start()

    for p in range(3):
        for m in (C, C ^ X, C ^ Y, C ^ Z, C ^ X ^ Y, C ^ X ^ Z, C ^ Y ^ Z, C ^ X ^ Y ^ Z):
            arrival(p, m).wait_recv()
    cos_in.wait()
    sin_in.wait()

    def one_block(r, carry):
        x = [xg[p, r].astype(f32) for p in range(3)]
        mean = sum(jnp.sum(t * t, axis=1, keepdims=True) for t in x) * (1.0 / 768)
        scale = lax.rsqrt(mean + 1e-6)
        rows = pl.ds(pl.multiple_of(r * 128, 128), 128)
        acc = jnp.zeros((128, 256), f32)
        for p in range(3):
            n = (x[p] * scale * gain[:, 256 * p : 256 * p + 256]).astype(bf16)
            norm[rows, 256 * p : 256 * p + 256] = n
            acc = acc + jnp.dot(n, w_b[256 * p : 256 * p + 256, :], preferred_element_type=f32)
        qk = turned(acc[:, 0:128], cos[rows, :], sin[rows, :])
        q[rows, :] = (qk[:, 0:64] * 0.125).astype(bf16)
        k[rows, :] = qk[:, 64:128].astype(bf16)
        lane = lax.broadcasted_iota(jnp.int32, (128, 128), 1)
        v[rows, :] = jnp.where(lane < 64, acc[:, 128:256], jnp.where(lane == 64, 1.0, 0.0)).astype(bf16)
        return carry

    lax.fori_loop(0, 16, one_block, 0)
    stores = [
        pltpu.make_async_copy(norm, norm_hbm, loc.at[4]),
        pltpu.make_async_copy(q, q_hbm, loc.at[5]),
        pltpu.make_async_copy(k, k_hbm, loc.at[6]),
        pltpu.make_async_copy(v, v_hbm, loc.at[7]),
    ]
    for s in stores:
        s.start()

    head = head_of(h, b)
    working = (b % 4) != 3
    base = (b // 8) * 8

    def cot_store(kk):
        zz = cot_gather.nth(kk)
        return pltpu.make_async_copy(cot_rows.at[pl.ds(4 * zz, 4)], cot_hbm.at[pl.ds(4 * zz, 4)], loc.at[kk])

    def cot_done(kk):
        cot_gather.got_core(kk)
        cot_store(kk).start()

    w, c = wo_gather, cot_gather
    between = {
        0: [lambda: w.got_z(1), lambda: w.got_y(0)],
        1: [lambda: w.got_z(2), lambda: w.got_z(3)],
        2: [lambda: w.got_y(1)],
        3: [lambda: w.got_y(2), lambda: w.got_y(3), lambda: c.got_z(1), lambda: c.got_y(0)],
        4: [lambda: w.got_core(0), lambda: w.got_core(1)],
        5: [lambda: c.got_z(2), lambda: c.got_y(1), lambda: w.got_core(2), lambda: w.got_core(3)],
        6: [lambda: c.got_z(3), lambda: c.got_y(2), lambda: cot_done(0)],
        7: [lambda: cot_done(1)],
    }

    def out_copy(r):
        return pltpu.make_async_remote_copy(
            src_ref=sendbuf.at[r], dst_ref=att_in.at[head],
            send_sem=at_send.at[r], recv_sem=at_recv.at[head],
            device_id=(r % 2, base + r // 2), device_id_type=MESH,
        )

    for i in range(8):
        width = 256 * (i + 1)
        s = lax.dot_general(q[256 * i : width, :], k[0:width, :], (((1,), (1,)), ((), ())), preferred_element_type=f32)
        key = lax.broadcasted_iota(jnp.int32, (1, width), 1)
        s = s + jnp.where(key < length, 0.0, NEG)
        rowi = lax.broadcasted_iota(jnp.int32, (256, 256), 0)
        coli = lax.broadcasted_iota(jnp.int32, (256, 256), 1)
        last = jnp.where(coli <= rowi, s[:, width - 256 :], NEG)
        s = last if i == 0 else jnp.concatenate([s[:, : width - 256], last], axis=1)
        m = jnp.max(s, axis=1, keepdims=True)
        e = jnp.exp(s - m).astype(bf16)
        ov = jnp.dot(e, v[0:width, :], preferred_element_type=f32)
        l = ov[:, 64:65]
        lane = lax.broadcasted_iota(jnp.int32, (256, 128), 1)
        ov = jnp.where(lane < 64, ov / l, m + jnp.log(l))
        o[256 * i : width, :] = ov
        oh = ov[:, 0:64]
        for half in range(2):
            r = 2 * i + half
            packed = jnp.concatenate([oh[128 * half : 128 * half + 64], oh[128 * half + 64 : 128 * half + 128]], axis=1)
            sendbuf[r] = packed.astype(bf16)

            @pl.when(working & (r != rank))
            def _(r=r):
                out_copy(r).start()
        for act in between[i]:
            act()

    o_store = pltpu.make_async_copy(o, o_hbm, loc.at[8])
    o_store.start()

    @pl.when(working)
    def _():
        att_in[head] = sendbuf[rank]

    for j in range(12):
        @pl.when(rank != home_of(j))
        def _(j=j):
            pltpu.make_async_remote_copy(
                src_ref=sendbuf.at[0], dst_ref=att_in.at[j],
                send_sem=at_send.at[0], recv_sem=at_recv.at[j],
                device_id=(h, b), device_id_type=MESH,
            ).wait_recv()

    for j in range(0, 12, 2):
        one, two = att_in[j].astype(f32), att_in[j + 1].astype(f32)
        att_out[0:64, 64 * j : 64 * j + 128] = jnp.concatenate([one[:, 0:64], two[:, 0:64]], axis=1).astype(bf16)
        att_out[64:128, 64 * j : 64 * j + 128] = jnp.concatenate([one[:, 64:128], two[:, 64:128]], axis=1).astype(bf16)

    for hh in range(2):
        for blk in range(16):
            t = wo_all[blk, 0, hh].astype(f32)
            row = 24 * (hh * 16 + blk)
            wo_f[row : row + 16, :] = t[:, 0:768]
            wo_f[row + 16 : row + 24, 0:384] = t[0:8, 768:1152]
            wo_f[row + 16 : row + 24, 384:768] = t[8:16, 768:1152]
    wo_out[...] = wo_f[...].astype(bf16)
    cot_gather.got_y(3)
    cot_done(2)
    cot_done(3)
    for copy in sends:
        copy.wait_send()
    for c in swaps:
        c.wait_send()
    wo_gather.finish()
    cot_gather.finish()

    def sent_piece(kk, carry):
        piece_copy(kk).wait_send()
        return carry

    lax.fori_loop(1, total, sent_piece, 0)
    for r in range(16):
        @pl.when(working & (r != rank))
        def _(r=r):
            out_copy(r).wait_send()
    for s in stores:
        s.wait()
    o_store.wait()
    for kk in range(4):
        cot_store(kk).wait()


def attend_and_send(tokens, cotangent, routes, w_qkv, small, w_out, lengths, n_blk):
    cos, sin = rotary_tables(2048)
    vm = pl.BlockSpec(memory_space=pltpu.VMEM)
    hbm = pl.BlockSpec(memory_space=pl.ANY)
    sds = jax.ShapeDtypeStruct
    DMA = pltpu.SemaphoreType.DMA
    return pl.pallas_call(
        functools.partial(forward_kernel, n_blk),
        out_shape=(
            sds((2048, 768), bf16), sds((2048, 64), bf16), sds((2048, 64), bf16), sds((2048, 128), bf16),
            sds((2048, 128), f32), sds((n_blk, 2, 96, 768), bf16), sds((128, 768), bf16), sds((768, 128), bf16), sds((32, 768), f32),
            sds((8, 128), f32), sds((768, 768), bf16), sds((2, 128, 256), bf16),
        ),
        in_specs=[pl.BlockSpec(memory_space=pltpu.SMEM)] + [vm] * 6 + [hbm, hbm],
        out_specs=(hbm,) * 6 + (vm,) * 6,
        scratch_shapes=[
            pltpu.VMEM((3, 16, 128, 256), bf16), pltpu.VMEM((12, 16, 384), bf16), pltpu.VMEM((2 * n_blk, 16, 384), bf16),
            pltpu.VMEM((768, 256), f32), pltpu.VMEM((768, 256), bf16),
            pltpu.VMEM((2048, 128), f32), pltpu.VMEM((2048, 128), f32),
            pltpu.VMEM((2048, 768), bf16), pltpu.VMEM((2048, 64), bf16), pltpu.VMEM((2048, 64), bf16), pltpu.VMEM((2048, 128), bf16),
            pltpu.VMEM((2048, 128), f32), pltpu.VMEM((16, 64, 128), bf16), pltpu.VMEM((12, 64, 128), bf16),
            pltpu.VMEM((128, 128), bf16), pltpu.VMEM((128, 128), bf16), pltpu.VMEM((128, 768), bf16),
            pltpu.VMEM((n_blk, 2, 96, 768), bf16), pltpu.VMEM((n_blk, 1, 2, 16, 1152), bf16), pltpu.VMEM((768, 768), f32),
            DMA((3, 16)), DMA((3, 16)), DMA((2 * n_blk,)), DMA((2 * n_blk,)), DMA((16,)), DMA((12,)), DMA((11,)), DMA((3,)), DMA((3,)), *gather_sems(1), *gather_sems(2),
        ],
        compiler_params=pltpu.CompilerParams(collective_id=0, has_side_effects=True, vmem_limit_bytes=56 * 2**20),
        cost_estimate=pl.CostEstimate(flops=10**9, bytes_accessed=2 * 10**7, transcendentals=0),
        name="attend",
    )(lengths, tokens, cotangent, routes, w_qkv, small, w_out, jnp.asarray(cos), jnp.asarray(sin))


def split(x):
    high = x.astype(bf16)
    return high, (x - high.astype(f32)).astype(bf16)


def exact_dot(x, y, dims):
    high, low = split(x)
    return lax.dot_general(high, y, (dims, ((), ())), preferred_element_type=f32) + lax.dot_general(
        low, y, (dims, ((), ())), preferred_element_type=f32)


def softmax_back(p, d):
    return p * (d - jnp.sum(p * d, axis=1, keepdims=True))


def lane_of(column, n):
    lane = lax.broadcasted_iota(jnp.int32, (128, 128), 1)
    return jnp.where(lane == n, column, 0.0)


class RowScatter:
    def __init__(self, part, from_core, from_y, from_z, sems, h, b):
        self.part, self.from_core, self.from_y, self.from_z = part, from_core, from_y, from_z
        self.h, self.b = h, b
        self.cs, self.cr, self.ys, self.yr, self.zs, self.zr = sems
        self.parts = range(part.shape[1])
        self.order = [(k, p) for k in (3, 2, 1, 0) for p in self.parts]
        self.z, self.y, self.c = b // 4, (b // 2) % 2, b % 2

    def nth(self, k):
        return nearest(self.z, k)

    def blk(self, k, far_y, far_c):
        y = 1 - self.y if far_y else self.y
        c = 1 - self.c if far_c else self.c
        return self.nth(k) * 4 + y * 2 + c

    def remote(self, src, dst, send, recv, device):
        return pltpu.make_async_remote_copy(
            src_ref=src, dst_ref=dst, send_sem=send, recv_sem=recv, device_id=device, device_id_type=MESH)

    def core(self, k, far, p):
        return self.remote(self.part.at[self.blk(k, far, 1), p], self.from_core.at[k, far, p], self.cs.at[k, far, p],
                           self.cr.at[k, far, p], (self.h, self.b + 1 - 2 * self.c))

    def over_y(self, k, p):
        return self.remote(self.part.at[self.blk(k, 1, 0), p], self.from_y.at[k, p], self.ys.at[k, p], self.yr.at[k, p],
                           (self.h, self.b + 2 - 4 * self.y))

    def along_z(self, k, step, p):
        zz = self.nth(k)
        side = (1 - step) // 2
        return self.remote(self.part.at[self.blk(k, 0, 0), p], self.from_z.at[side, zz, p], self.zs.at[side, zz, p],
                           self.zr.at[side, zz, p], (self.h, self.b + 4 * step))

    def add(self, blk, p, other):
        self.part[blk, p] = (self.part[blk, p].astype(f32) + other[...].astype(f32)).astype(bf16)

    def send_core(self, k, p):
        self.core(k, 1, p).start()
        self.core(k, 0, p).start()

    def send_y(self, k, p):
        self.core(k, 1, p).wait_recv()
        self.add(self.blk(k, 1, 0), p, self.from_core.at[k, 1, p])
        self.over_y(k, p).start()
        self.core(k, 0, p).wait_recv()
        self.add(self.blk(k, 0, 0), p, self.from_core.at[k, 0, p])

    def take_z(self, side, zz, k, p):
        here = self.from_z.at[side, zz, p]
        self.remote(here, here, self.zs.at[0, 0, 0], self.zr.at[side, zz, p], (self.h, self.b)).wait_recv()
        self.add(self.blk(k, 0, 0), p, here)

    def send_z(self, k, p):
        zz = self.nth(k)
        self.over_y(k, p).wait_recv()
        self.add(self.blk(k, 0, 0), p, self.from_y.at[k, p])
        self.sums(k, p)

    def sums(self, k, p):
        zz = self.nth(k)

        @pl.when((zz >= self.z) & (self.z > 0))
        def _():
            self.take_z(0, zz, k, p)

        @pl.when((zz <= self.z) & (self.z < 3))
        def _():
            self.take_z(1, zz, k, p)

        if k:
            self.z_send(k, p, lambda c: c.start())

    def z_send(self, k, p, act):
        zz = self.nth(k)

        @pl.when(zz > self.z)
        def _():
            act(self.along_z(k, 1, p))

        @pl.when(zz < self.z)
        def _():
            act(self.along_z(k, -1, p))

    def finish(self):
        for p in self.parts:
            for k in range(4):
                self.core(k, 0, p).wait_send()
                self.core(k, 1, p).wait_send()
                self.over_y(k, p).wait_send()
                if k:
                    self.z_send(k, p, lambda c: c.wait_send())


def scatter_scratch(parts, rows, cols):
    DMA = pltpu.SemaphoreType.DMA
    V = pltpu.VMEM
    return [
        V((4, 2, parts, rows, cols), bf16), V((4, parts, rows, cols), bf16), V((2, 4, parts, rows, cols), bf16),
        DMA((4, 2, parts)), DMA((4, 2, parts)), DMA((4, parts)), DMA((4, parts)), DMA((2, 4, parts)), DMA((2, 4, parts)),
    ]


def expert_kernel(
    n_blk, lengths, att, tok, cot, prev, mix, routes, wout, sm, smt, cnt, pt, w_hbm, cot_hbm,
    part_hbm, g_hbm, local_out, res_out, ag_out, gs_out, misc_out, pg_out,
    x_all, cot_all, w, cc, dgu, hid, hc, inp, outp, gbuf, gates_in, vs_out, vs_in, n_own, n_far, g_own, g_far,
    d_out, d_in, dv_out, dv_in, ga_send, ga_recv, vs_send, vs_recv, x_send, x_recv, loc, *rest,
):
    gsems, (from_core, from_y, from_z), ssems = rest[0:6], rest[6:9], rest[9:15]
    h, b = lax.axis_index("head"), lax.axis_index("blk")
    loads = [pltpu.make_async_copy(w_hbm, w, loc.at[0]), pltpu.make_async_copy(cot_hbm, cot_all, loc.at[1])]
    for c in loads:
        c.start()
    barrier = pltpu.get_barrier_semaphore()
    pl.semaphore_signal(barrier, inc=1, device_id=(1 - h, b), device_id_type=MESH)

    def say(k, carry):
        pl.semaphore_signal(barrier, inc=1, device_id=(h, (b + k) % n_blk), device_id_type=MESH)
        return carry

    lax.fori_loop(1, n_blk, say, 0)
    length = lengths[b // 8]
    live_total = (lengths[0] + lengths[1]).astype(f32)
    live = live_column(h, b, length)
    lane = lax.broadcasted_iota(jnp.int32, (128, 128), 1)

    res = tok[...].astype(f32) + jnp.dot(att[...], wout[...], preferred_element_type=f32)
    scale = lax.rsqrt(jnp.sum(res * res, axis=1, keepdims=True) * (1.0 / 768) + 1e-6)
    xh = res * scale
    n2 = (xh * smt[17:18, :]).astype(bf16)
    small = sm[...]
    logits = jnp.dot(n2, small, preferred_element_type=f32)
    router = logits + jnp.dot(prev[...], mix[...], preferred_element_type=f32, precision=lax.Precision.HIGHEST)
    router = jnp.where(lane < 12, router, NEG)
    prob = jnp.exp(router - jnp.max(router, axis=1, keepdims=True))
    prob = prob / jnp.sum(prob, axis=1, keepdims=True)
    named = jnp.where((routes[:, 0:1] == lane) | (routes[:, 1:2] == lane), 1.0, 0.0)
    gates = prob * named
    n_own[...] = n2
    g_own[...] = gates
    pl.semaphore_wait(barrier, n_blk)
    swaps = [
        pltpu.make_async_remote_copy(
            src_ref=src, dst_ref=dst, send_sem=x_send.at[n], recv_sem=x_recv.at[n],
            device_id=(1 - h, b), device_id_type=MESH)
        for n, (src, dst) in enumerate([(n_own, n_far), (g_own, g_far), (d_out, d_in), (dv_out, dv_in)])
    ]
    swaps[0].start()
    swaps[1].start()
    p_own, p_far = pt[0, :, 0:192], pt[1, :, 0:192]
    rows = ((0,), (0,))
    mine = lax.dot_general(p_own, n2, (rows, ((), ())), preferred_element_type=f32)
    spread = expert_lanes(h).astype(bf16)
    pg_own = pt[0].astype(f32) * exact_dot(gates, spread, ((1,), (0,)))
    pg_out[0] = pg_own
    swaps[0].wait_recv()
    picked = (mine + lax.dot_general(p_far, n_far[...], (rows, ((), ())), preferred_element_type=f32)).astype(bf16)
    x_all[b, 0] = picked[0:96]
    x_all[b, 1] = picked[96:192]
    g = RowGather(x_all, gsems, h, b)
    g.start()
    swaps[1].wait_recv()
    pg_far = pt[1].astype(f32) * exact_dot(g_far[...], spread, ((1,), (0,)))
    pg_out[1] = pg_far
    gates_in[b] = jnp.broadcast_to(jnp.sum(pg_own + pg_far, axis=0, keepdims=True), (8, 256))

    def gate_copy(k):
        return pltpu.make_async_remote_copy(
            src_ref=gates_in.at[b], dst_ref=gates_in.at[b], send_sem=ga_send.at[k], recv_sem=ga_recv.at[b],
            device_id=(h, (b + k) % n_blk), device_id_type=MESH)

    def vs_copy(k):
        to = (b + k) % n_blk
        return pltpu.make_async_remote_copy(
            src_ref=vs_out.at[to], dst_ref=vs_in.at[b], send_sem=vs_send.at[k], recv_sem=vs_recv.at[b],
            device_id=(h, to), device_id_type=MESH)

    def each(act):
        def body(k, carry):
            act(k)
            return carry

        lax.fori_loop(1, n_blk, body, 0)

    each(lambda k: gate_copy(k).start())

    def group(ref, k, p, ee):
        return ref[pl.ds(4 * g.nth(k), 4), p, 48 * ee : 48 * ee + 48, :]

    def put(ref, k, p, ee, value):
        ref[pl.ds(4 * g.nth(k), 4), p, 48 * ee : 48 * ee + 48, :] = value.reshape(4, 48, value.shape[1]).astype(ref.dtype)

    cols = ((1,), (1,))

    def cot_task(k):
        for e in range(4):
            rows_c = group(cot_all, k, e // 2, e % 2).reshape(192, 768)
            put(cc, k, e // 2, e % 2, lax.dot_general(rows_c, w[3 * e + 2], (cols, ((), ())), preferred_element_type=f32))

    def up_task(k):
        for e in range(4):
            p, ee = e // 2, e % 2
            x = group(x_all, k, p, ee).reshape(192, 768)
            both = lax.dot_general(x, w[3 * e : 3 * e + 2].reshape(256, 768), (cols, ((), ())), preferred_element_type=f32)
            gate, up = both[:, 0:128], both[:, 128:256]
            sig = 1.0 / (1.0 + jnp.exp(-gate))
            silu = gate * sig
            hidden = silu * up
            c = group(cc, k, p, ee).reshape(192, 128)
            put(hid, k, p, ee, hidden)
            put(hc, k, p, ee, hidden * c)
            dg = c * up * (sig * (1.0 + gate * (1.0 - sig)))
            put(dgu, k, p, ee, jnp.concatenate([dg, c * silu], axis=1))

    two = jnp.where(lane % 2 == 0, pltpu.roll(logits, 127, 1), pltpu.roll(logits, 1, 1))
    top = jnp.maximum(logits, two)
    c_mix = jnp.exp(logits - top) / (jnp.exp(logits - top) + jnp.exp(two - top))
    share = gates * live
    n2f = n2.astype(f32)
    alpha = share[:, 9:10] + share[:, 10:11] * c_mix[:, 12:13] + share[:, 11:12] * c_mix[:, 14:15]
    beta = [share[:, 10:11] * c_mix[:, 13:14], share[:, 11:12] * c_mix[:, 15:16]]
    local_out[...] = live * (res + alpha * n2f + beta[0] * smt[18:19, :] + beta[1] * smt[19:20, :])
    og = live * cot[...].astype(f32)
    og_low = og.astype(bf16)

    loads[1].wait()
    loads[0].wait()
    cot_task(0)
    g.got_z(1)
    cot_task(1)
    g.got_z(2)
    g.got_y(0)
    cot_task(2)
    g.got_z(3)
    g.got_y(1)
    cot_task(3)
    g.got_core(0)
    up_task(0)
    g.got_y(2)
    g.got_core(1)
    up_task(1)
    g.got_y(3)
    g.got_core(2)
    up_task(2)
    g.got_core(3)
    up_task(3)

    s = RowScatter(inp, from_core, from_y, from_z, ssems, h, b)
    order = s.order
    for n, (k, p) in enumerate(order):
        for ee in range(2):
            e = 2 * p + ee
            d = group(dgu, k, p, ee).reshape(192, 256)
            put(inp, k, p, ee, jnp.dot(d, w[3 * e : 3 * e + 2].reshape(256, 768), preferred_element_type=f32))
        s.send_core(k, p)
        if n:
            s.send_y(*order[n - 1])
    s.send_y(*order[7])

    ones = jnp.ones((8, 128), f32)

    def one_blk(j, carry):
        for p in range(2):
            vs_out[j, :, 128 * p : 128 * p + 96] = lax.dot_general(
                ones, hc[j, p], (cols, ((), ())), preferred_element_type=f32, precision=lax.Precision.HIGHEST)
        return carry

    lax.fori_loop(0, n_blk, one_blk, 0)
    each(lambda k: vs_copy(k).start())
    vs_in[b] = vs_out[b]
    each(lambda k: pltpu.make_async_remote_copy(
        src_ref=gates_in.at[b], dst_ref=gates_in.at[(b + k) % n_blk], send_sem=ga_send.at[0],
        recv_sem=ga_recv.at[(b + k) % n_blk], device_id=(h, b), device_id_type=MESH).wait_recv())
    gate_cols = jnp.transpose(gates_in[:, 0, :])

    def scaled(ref, p, ee):
        e = 2 * p + ee
        t = ref[:, p, 48 * ee : 48 * ee + 48, :].astype(f32)
        col = jnp.concatenate([gate_cols[48 * e : 48 * e + 48, j : j + 1] for j in range(n_blk)], axis=0)
        return (t.reshape(48 * n_blk, t.shape[2]) * col).astype(bf16)

    def weight_task(e):
        p, ee = e // 2, e % 2
        x = x_all[:, p, 48 * ee : 48 * ee + 48, :].reshape(48 * n_blk, 768)
        c = cot_all[:, p, 48 * ee : 48 * ee + 48, :].reshape(48 * n_blk, 768)
        gbuf[3 * e : 3 * e + 2] = lax.dot_general(
            scaled(dgu, p, ee), x, (rows, ((), ())), preferred_element_type=f32).reshape(2, 128, 768)
        gbuf[3 * e + 2] = lax.dot_general(scaled(hid, p, ee), c, (rows, ((), ())), preferred_element_type=f32)
        pltpu.make_async_copy(gbuf.at[pl.ds(3 * e, 3)], g_hbm.at[pl.ds(3 * e, 3)], loc.at[2 + e]).start()

    def out_task(k):
        for e in range(4):
            d = group(hid, k, e // 2, e % 2).reshape(192, 128)
            put(outp, k, e // 2, e % 2, jnp.dot(d, w[3 * e + 2], preferred_element_type=f32))

    tasks = [lambda: weight_task(0), lambda: out_task(0), lambda: weight_task(1), lambda: out_task(1),
             lambda: weight_task(2), lambda: out_task(2), lambda: weight_task(3), lambda: out_task(3)]
    for (k, p), task in zip(order, tasks):
        task()
        s.send_z(k, p)
    part_store = pltpu.make_async_copy(outp, part_hbm, loc.at[6])
    part_store.start()

    din = jnp.concatenate([inp[b, 0], inp[b, 1]], axis=0)
    into = ((1,), (0,))
    d_out[...] = exact_dot(pg_far[:, 0:192], din, into).astype(bf16)
    swaps[2].start()
    each(lambda k: pltpu.make_async_remote_copy(
        src_ref=vs_in.at[b], dst_ref=vs_in.at[(b + k) % n_blk], send_sem=vs_send.at[0],
        recv_sem=vs_recv.at[(b + k) % n_blk], device_id=(h, b), device_id_type=MESH).wait_recv())
    vsum = jnp.sum(vs_in[:, 0, :], axis=0, keepdims=True)
    vrow = jnp.concatenate([vsum[:, 0:96], vsum[:, 128:224]], axis=1)
    spread = spread[:, 0:192]
    dv_out[...] = exact_dot(p_far.astype(f32) * vrow, spread, cols)
    swaps[3].start()
    d_own = exact_dot(pg_own[:, 0:192], din, into)
    dv_own = exact_dot(p_own.astype(f32) * vrow, spread, cols)

    u = jnp.sum(og * n2f, axis=1, keepdims=True)
    wj = jnp.dot(og_low, small, preferred_element_type=f32)
    w0, w1 = wj[:, 18:19], wj[:, 19:20]
    c = [c_mix[:, n : n + 1] for n in (12, 13, 14, 15)]
    dgate = lane_of(u, 9) + lane_of(c[0] * u + c[1] * w0, 10) + lane_of(c[2] * u + c[3] * w1, 11)
    dmix = lane_of(u, 12) + lane_of(w0, 13) + lane_of(u, 14) + lane_of(w1, 15)
    dmix = dmix * jnp.where(lane < 14, gates[:, 10:11], gates[:, 11:12])
    both = c_mix * dmix
    dmix = c_mix * (dmix - both - jnp.where(lane % 2 == 0, pltpu.roll(both, 127, 1), pltpu.roll(both, 1, 1)))
    dmix = jnp.where((lane >= 12) & (lane < 16), dmix, 0.0)
    aux = (0.01 * 12.0 / live_total) * (cnt[0:1, :] / (2.0 * live_total)) * live
    swaps[2].wait_recv()
    swaps[3].wait_recv()
    dprob = named * (dgate + dv_own + dv_in[...]) + aux
    dlog = softmax_back(prob, dprob) + dmix
    dn = d_own + d_in[...].astype(f32) + og * alpha + exact_dot(dlog, jnp.where(
        lax.broadcasted_iota(jnp.int32, (768, 128), 1) < 16, small, 0).astype(bf16), cols)
    t = dn * smt[17:18, :]
    rg = og + scale * (t - xh * (jnp.sum(t * xh, axis=1, keepdims=True) * (1.0 / 768)))
    res_out[...] = rg
    ag_out[...] = lax.dot_general(rg.astype(bf16), wout[...], (cols, ((), ())), preferred_element_type=f32).astype(bf16)

    dl_high, dl_low = split(dlog)
    gs = lax.dot_general(n2, dl_high, (rows, ((), ())), preferred_element_type=f32)
    gs = gs + lax.dot_general(n2, dl_low, (rows, ((), ())), preferred_element_type=f32)
    b_high, b_low = split(lane_of(beta[0], 18) + lane_of(beta[1], 19))
    gs = gs + lax.dot_general(og_low, b_high, (rows, ((), ())), preferred_element_type=f32)
    gs = gs + lax.dot_general(og_low, b_low, (rows, ((), ())), preferred_element_type=f32)
    gain = jnp.broadcast_to(jnp.sum(dn * xh, axis=0, keepdims=True), (128, 768))
    gs_out[...] = gs + jnp.where(lax.broadcasted_iota(jnp.int32, (768, 128), 1) == 17, jnp.transpose(gain), 0.0)
    mixed = lax.dot_general(prev[...], jnp.where(lane < 12, dlog, 0.0), (rows, ((), ())), preferred_element_type=f32,
                            precision=lax.Precision.HIGHEST)
    misc_out[0:16, :] = mixed[0:16]
    misc_out[16:24, :] = jnp.broadcast_to(jnp.sum(prob * live, axis=0, keepdims=True), (8, 128))

    g.finish()
    s.finish()
    each(lambda k: gate_copy(k).wait_send())
    each(lambda k: vs_copy(k).wait_send())
    for c in swaps:
        c.wait_send()
    part_store.wait()
    for e in range(4):
        pltpu.make_async_copy(gbuf.at[pl.ds(3 * e, 3)], g_hbm.at[pl.ds(3 * e, 3)], loc.at[2 + e]).wait()


def run_experts(lengths, att, tok, cot, prev, mix, routes, wout, sm, smt, cnt, pt, w, cot_rows, n_blk):
    vm = pl.BlockSpec(memory_space=pltpu.VMEM)
    hbm = pl.BlockSpec(memory_space=pl.ANY)
    sds = jax.ShapeDtypeStruct
    DMA = pltpu.SemaphoreType.DMA
    V = pltpu.VMEM
    return pl.pallas_call(
        functools.partial(expert_kernel, n_blk),
        out_shape=(
            sds((n_blk, 2, 96, 768), bf16), sds((12, 128, 768), f32), sds((128, 768), f32), sds((128, 768), f32),
            sds((128, 768), bf16), sds((768, 128), f32), sds((24, 128), f32), sds((2, 128, 256), f32),
        ),
        in_specs=[pl.BlockSpec(memory_space=pltpu.SMEM)] + [vm] * 11 + [hbm] * 2,
        out_specs=(hbm, hbm) + (vm,) * 6,
        scratch_shapes=[
            V((n_blk, 2, 96, 768), bf16), V((n_blk, 2, 96, 768), bf16), V((12, 128, 768), bf16),
            V((n_blk, 2, 96, 128), f32), V((n_blk, 2, 96, 256), bf16), V((n_blk, 2, 96, 128), bf16), V((n_blk, 2, 96, 128), f32),
            V((n_blk, 2, 96, 768), bf16), V((n_blk, 2, 96, 768), bf16), V((12, 128, 768), f32),
            V((n_blk, 8, 256), f32), V((n_blk, 8, 256), f32), V((n_blk, 8, 256), f32),
            V((128, 768), bf16), V((128, 768), bf16), V((128, 128), f32), V((128, 128), f32),
            V((128, 768), bf16), V((128, 768), bf16), V((128, 128), f32), V((128, 128), f32),
            DMA((n_blk,)), DMA((n_blk,)), DMA((n_blk,)), DMA((n_blk,)), DMA((4,)), DMA((4,)), DMA((7,)),
            *gather_sems(2), *scatter_scratch(2, 96, 768),
        ],
        compiler_params=pltpu.CompilerParams(collective_id=2, has_side_effects=True, vmem_limit_bytes=60 * 2**20),
        cost_estimate=pl.CostEstimate(flops=6 * 10**9, bytes_accessed=3 * 10**7, transcendentals=0),
        name="experts",
    )(lengths, att, tok, cot, prev, mix, routes, wout, sm, smt, cnt, pt, w, cot_rows)


def backward_kernel(
    n_blk, lengths, ag, tok, res_grad, smt, att, local_out, pg, g_small, misc, w_own, small,
    norm_hbm, q_hbm, k_hbm, v_hbm, o_hbm, cos_hbm, sin_hbm, w_hbm, part_hbm,
    out, dtok_out, gq_out, go_out, gs_out, misc_out,
    norm, q, k, v, o, cos, sin, w_all, agbuf, do_in, do, dk, dv, dqkv, obuf, got, dpq, dpv, g_f, gbuf, g_in,
    part, gpart, far_out, far_in, half_in, misc_sum, misc_in,
    a_send, a_recv, b_send, b_recv, g_send, g_recv, loc, x_send, x_recv, m_send, m_recv, *rest,
):
    h, b = lax.axis_index("head"), lax.axis_index("blk")
    me = b * 2 + h
    total = 2 * n_blk
    _, _, rank = place(0, h, b)
    base = (b // 8) * 8
    head = head_of(h, b)
    working = (b % 4) != 3
    loads = [
        pltpu.make_async_copy(src, dst, loc.at[i])
        for i, (src, dst) in enumerate([
            (q_hbm, q), (k_hbm, k), (v_hbm, v), (o_hbm, o), (cos_hbm, cos), (sin_hbm, sin), (norm_hbm, norm),
            (w_hbm, w_all), (part_hbm, part)])
    ]
    for c in loads:
        c.start()
    a = ag[...].astype(f32)
    for j in range(12):
        agbuf[j] = jnp.concatenate([a[0:64, 64 * j : 64 * j + 64], a[64:128, 64 * j : 64 * j + 64]], axis=1).astype(bf16)
    greet("all", h, b, n_blk)

    def to_head(j):
        r = home_of(j)
        return pltpu.make_async_remote_copy(
            src_ref=agbuf.at[j], dst_ref=do_in.at[rank], send_sem=a_send.at[j], recv_sem=a_recv.at[rank],
            device_id=(r % 2, base + r // 2), device_id_type=MESH,
        )

    for j in range(12):
        @pl.when(rank != home_of(j))
        def _(j=j):
            to_head(j).start()

    def to_tokens(r):
        return pltpu.make_async_remote_copy(
            src_ref=obuf.at[r], dst_ref=got.at[head], send_sem=b_send.at[r], recv_sem=b_recv.at[head],
            device_id=(r % 2, base + r // 2), device_id_type=MESH,
        )

    def to_owner(kk):
        other = (me + kk) % total
        oh, ob = other % 2, other // 2
        return pltpu.make_async_remote_copy(
            src_ref=gbuf.at[oh * n_blk + ob], dst_ref=g_in.at[me], send_sem=g_send.at[kk], recv_sem=g_recv.at[me],
            device_id=(oh, ob), device_id_type=MESH,
        )

    length = lengths[b // 8]

    rs = RowScatter(part, *rest[0:3], rest[3:9], h, b)
    gs = RowScatter(gpart, *rest[9:12], rest[12:18], h, b)
    g_f2 = lax.dot_general(att[...], res_grad[...].astype(bf16), (((0,), (0,)), ((), ())), preferred_element_type=f32)
    for w in range(total):
        cat = jnp.concatenate([g_f2[24 * w : 24 * w + 24], g_small[24 * w : 24 * w + 24, :]], axis=1)
        gpart[w % n_blk, 0, 16 * (w // n_blk) : 16 * (w // n_blk) + 16, :] = fold(cat)
    for n in gs.order:
        gs.send_core(*n)
    loads[8].wait()
    for n in rs.order:
        rs.send_core(*n)
    for n in gs.order:
        gs.send_y(*n)
    for n in rs.order:
        rs.send_y(*n)

    misc_sum[0] = misc[...]
    z = b // 4
    partners = [(1 - h, b), (h, b + 1 - 2 * (b % 2)), (h, b + 2 - 4 * ((b // 2) % 2)),
                (h, b + 4 - 8 * (z % 2)), (h, b + 8 - 16 * (z // 2))]

    def pairwise(t):
        return pltpu.make_async_remote_copy(
            src_ref=misc_sum.at[t], dst_ref=misc_in.at[t], send_sem=m_send.at[t], recv_sem=m_recv.at[t],
            device_id=partners[t], device_id_type=MESH)

    def pairwise_done(t):
        pairwise(t).wait_recv()
        misc_sum[t + 1] = misc_sum[t] + misc_in[t]
        if t < 4:
            pairwise(t + 1).start()

    pairwise(0).start()
    zsteps = [lambda n=n: rs.send_z(*n) for n in rs.order]
    gsteps = [lambda n=n: gs.send_z(*n) for n in gs.order]
    between = {
        7: [lambda: pairwise_done(0)], 6: [lambda: pairwise_done(1), gsteps[0]], 5: [zsteps[0]],
        4: [lambda: pairwise_done(2), gsteps[1]], 3: [zsteps[1]], 2: [lambda: pairwise_done(3), gsteps[2]],
        1: [zsteps[2]], 0: [lambda: pairwise_done(4), gsteps[3]],
    }

    @pl.when(jnp.logical_not(working))
    def _():
        do_in[...] = jnp.zeros_like(do_in)

    @pl.when(working)
    def _():
        do_in[rank] = agbuf[head]

    for c in loads[:6]:
        c.wait()
    if True:
        def unpack(r, carry):
            @pl.when((r != rank) & working)
            def _():
                pltpu.make_async_remote_copy(
                    src_ref=agbuf.at[0], dst_ref=do_in.at[r], send_sem=a_send.at[0], recv_sem=a_recv.at[r],
                    device_id=(h, b), device_id_type=MESH,
                ).wait_recv()

            t = do_in[r].astype(f32)
            rows = pl.multiple_of(r * 128, 128)
            do[pl.ds(rows, 64), :] = t[:, 0:64].astype(bf16)
            do[pl.ds(rows + 64, 64), :] = t[:, 64:128].astype(bf16)
            return carry

        lax.fori_loop(0, 16, unpack, 0)
        for i in range(7, -1, -1):
            width = 256 * (i + 1)
            lo = 256 * i
            qi, doi = q[lo:width, :], do[lo:width, :]
            s = lax.dot_general(qi, k[0:width, :], (((1,), (1,)), ((), ())), preferred_element_type=f32)
            key = lax.broadcasted_iota(jnp.int32, (1, width), 1)
            ov = o[lo:width, :]
            lse = ov[:, 64:65]
            s = (s - lse) + jnp.where(key < length, 0.0, NEG)
            rowi = lax.broadcasted_iota(jnp.int32, (256, 256), 0)
            coli = lax.broadcasted_iota(jnp.int32, (256, 256), 1)
            last = jnp.where(coli <= rowi, s[:, lo:], NEG)
            s = last if i == 0 else jnp.concatenate([s[:, :lo], last], axis=1)
            p = jnp.exp(s)
            dp = lax.dot_general(doi, v[0:width, 0:64], (((1,), (1,)), ((), ())), preferred_element_type=f32)
            inner = jnp.sum(doi.astype(f32) * ov[:, 0:64], axis=1, keepdims=True)
            ds = (p * (dp - inner)).astype(bf16)
            p = p.astype(bf16)
            dq = jnp.dot(ds, k[0:width, :], preferred_element_type=f32) * 0.125
            dki = lax.dot_general(ds, qi, (((0,), (0,)), ((), ())), preferred_element_type=f32)
            dvi = lax.dot_general(p, doi, (((0,), (0,)), ((), ())), preferred_element_type=f32)
            if i == 7:
                dk[...] = dki
                dv[...] = dvi
            else:
                dk[0:width, :] += dki
                dv[0:width, :] += dvi
            both = jnp.concatenate([dq, dk[lo:width, :]], axis=1)
            both = turned(both, cos[lo:width, :], -sin[lo:width, :]).astype(bf16)
            dvl = dv[lo:width, :]
            dqkv[lo:width, 0:128] = both
            dqkv[lo:width, 128:256] = jnp.concatenate([dvl, jnp.zeros_like(dvl)], axis=1).astype(bf16)
            for half in range(2):
                r = 2 * i + half
                obuf[r, 0:128, :] = both[128 * half : 128 * half + 128]
                obuf[r, 128:192, :] = jnp.concatenate(
                    [dvl[128 * half : 128 * half + 64], dvl[128 * half + 64 : 128 * half + 128]], axis=1).astype(bf16)

                @pl.when((r != rank) & working)
                def _(r=r):
                    to_tokens(r).start()
            for act in between[i]:
                act()

        @pl.when(working)
        def _():
            got[head] = obuf[rank]

        loads[6].wait()
        for c in range(3):
            g_f[256 * c : 256 * c + 256, :] = lax.dot_general(
                norm[:, 256 * c : 256 * c + 256], dqkv[...], (((0,), (0,)), ((), ())), preferred_element_type=f32)
        for w in range(total):
            gbuf[w] = fold(g_f[24 * w : 24 * w + 24, :])

        def send_g(kk, carry):
            to_owner(kk).start()
            return carry

        @pl.when(working)
        def _():
            lax.fori_loop(1, total, send_g, 0)
            g_in[me] = gbuf[h * n_blk + b]

    swaps = [
        pltpu.make_async_remote_copy(
            src_ref=src, dst_ref=dst, send_sem=x_send.at[n], recv_sem=x_recv.at[n],
            device_id=(1 - h, b), device_id_type=MESH)
        for n, (src, dst) in enumerate([
            (gpart.at[b, 0, pl.ds(pl.multiple_of(16 * (1 - h), 16), 16)], half_in), (far_out, far_in)])
    ]
    swaps[0].start()
    zsteps[3]()
    zsteps[4]()

    for j in range(12):
        @pl.when(rank != home_of(j))
        def _(j=j):
            pltpu.make_async_remote_copy(
                src_ref=obuf.at[0], dst_ref=got.at[j], send_sem=b_send.at[0], recv_sem=b_recv.at[j],
                device_id=(h, b), device_id_type=MESH,
            ).wait_recv()
    for j in range(0, 12, 2):
        dpq[:, 128 * j : 128 * j + 128] = got[j, 0:128, :]
        dpq[:, 128 * j + 128 : 128 * j + 256] = got[j + 1, 0:128, :]
        one, two = got[j, 128:192, :].astype(f32), got[j + 1, 128:192, :].astype(f32)
        dpv[0:64, 64 * j : 64 * j + 128] = jnp.concatenate([one[:, 0:64], two[:, 0:64]], axis=1).astype(bf16)
        dpv[64:128, 64 * j : 64 * j + 128] = jnp.concatenate([one[:, 64:128], two[:, 64:128]], axis=1).astype(bf16)
    loads[7].wait()
    dn = lax.dot_general(dpq[...], w_all[:, 0:1536], (((1,), (1,)), ((), ())), preferred_element_type=f32)
    dn = dn + lax.dot_general(dpv[...], w_all[:, 1536:2304], (((1,), (1,)), ((), ())), preferred_element_type=f32)
    x = tok[...].astype(f32)
    scale = lax.rsqrt(jnp.sum(x * x, axis=1, keepdims=True) * (1.0 / 768) + 1e-6)
    xh = x * scale
    t = dn * smt[16:17, :]
    dx = scale * (t - xh * (jnp.sum(t * xh, axis=1, keepdims=True) * (1.0 / 768)))
    dtok_out[...] = (res_grad[...] + dx).astype(bf16)

    zsteps[5]()
    zsteps[6]()
    zsteps[7]()
    rows = jnp.concatenate([part[b, 0], part[b, 1]], axis=0)
    far_out[...] = exact_dot(pg[1, :, 0:192], rows, ((1,), (0,))).astype(bf16)
    swaps[1].start()
    own = exact_dot(pg[0, :, 0:192], rows, ((1,), (0,))) + local_out[...]

    for src in range(total):
        if (src // 2) % 4 == 3:
            continue

        @pl.when(me != src)
        def _(src=src):
            pltpu.make_async_remote_copy(
                src_ref=gbuf.at[0], dst_ref=g_in.at[src], send_sem=g_send.at[0], recv_sem=g_recv.at[src],
                device_id=(h, b), device_id_type=MESH,
            ).wait_recv()
    for j in range(0, 12, 2):
        pair = []
        for jj in (j, j + 1):
            t = sum(g_in[16 * s + home_of(jj)].astype(f32) for s in range(total // 16))
            pair.append(jnp.concatenate(
                [t[:, 0:256], jnp.concatenate([t[0:8, 256:384], t[8:16, 256:384]], axis=1)], axis=0))
        one, two = pair
        for part in range(3):
            gq_out[:, 768 * part + 64 * j : 768 * part + 64 * j + 128] = jnp.concatenate(
                [one[:, 64 * part : 64 * part + 64], two[:, 64 * part : 64 * part + 64]], axis=1)

    lane = lax.broadcasted_iota(jnp.int32, (24, 128), 1)
    gain_grad = jnp.sum(gq_out[...] * w_own[...].astype(f32), axis=1, keepdims=True) / small[:, 16:17]
    swaps[0].wait_recv()
    t = gpart[b, 0, pl.ds(pl.multiple_of(16 * h, 16), 16), :].astype(f32) + half_in[...].astype(f32)
    t = jnp.concatenate([t[:, 0:896], jnp.concatenate([t[0:8, 896:1344], t[8:16, 896:1344]], axis=1)], axis=0)
    go_out[...] = t[:, 0:768]
    gs_out[...] = jnp.where(lane == 16, gain_grad, t[:, 768:896])
    misc_out[...] = misc_sum[5]
    swaps[1].wait_recv()
    out[...] = (own + far_in[...].astype(f32)).astype(bf16)

    rs.finish()
    gs.finish()
    for t in range(5):
        pairwise(t).wait_send()
    for c in swaps:
        c.wait_send()
    for j in range(12):
        @pl.when(rank != home_of(j))
        def _(j=j):
            to_head(j).wait_send()

    @pl.when(working)
    def _():
        for r in range(16):
            @pl.when(r != rank)
            def _(r=r):
                to_tokens(r).wait_send()

        def sent(kk, carry):
            to_owner(kk).wait_send()
            return carry

        lax.fori_loop(1, total, sent, 0)


def attend_back(
    lengths, ag, tok, res_grad, smt, att, local_out, pg, g_small, misc, w_own, small, norm, q, k, v, o, w_all, parts, n_blk,
):
    cos, sin = rotary_tables(2048)
    vm = pl.BlockSpec(memory_space=pltpu.VMEM)
    hbm = pl.BlockSpec(memory_space=pl.ANY)
    sds = jax.ShapeDtypeStruct
    DMA = pltpu.SemaphoreType.DMA
    V = pltpu.VMEM
    total = 2 * n_blk
    return pl.pallas_call(
        functools.partial(backward_kernel, n_blk),
        out_shape=(
            sds((128, 768), bf16), sds((128, 768), bf16), sds((24, 2304), f32), sds((24, 768), f32), sds((24, 128), f32),
            sds((24, 128), f32),
        ),
        in_specs=[pl.BlockSpec(memory_space=pltpu.SMEM)] + [vm] * 11 + [hbm] * 9,
        out_specs=(vm,) * 6,
        scratch_shapes=[
            V((2048, 768), bf16), V((2048, 64), bf16), V((2048, 64), bf16), V((2048, 128), bf16), V((2048, 128), f32),
            V((2048, 128), f32), V((2048, 128), f32), V((768, 2304), bf16),
            V((12, 64, 128), bf16), V((16, 64, 128), bf16), V((2048, 64), bf16), V((2048, 64), f32), V((2048, 64), f32),
            V((2048, 256), bf16), V((16, 192, 128), bf16), V((12, 192, 128), bf16), V((128, 1536), bf16), V((128, 768), bf16),
            V((768, 256), f32), V((total, 16, 384), bf16), V((total, 16, 384), bf16),
            V((n_blk, 2, 96, 768), bf16), V((n_blk, 1, 32, 1344), bf16), V((128, 768), bf16), V((128, 768), bf16),
            V((16, 1344), bf16), V((6, 24, 128), f32), V((5, 24, 128), f32),
            DMA((12,)), DMA((16,)), DMA((16,)), DMA((12,)), DMA((total,)), DMA((total,)), DMA((9,)), DMA((2,)), DMA((2,)),
            DMA((5,)), DMA((5,)), *scatter_scratch(2, 96, 768), *scatter_scratch(1, 32, 1344),
        ],
        compiler_params=pltpu.CompilerParams(collective_id=1, has_side_effects=True, vmem_limit_bytes=60 * 2**20),
        cost_estimate=pl.CostEstimate(flops=2 * 10**9, bytes_accessed=2 * 10**7, transcendentals=0),
        name="attend_back",
    )(lengths, ag, tok, res_grad, smt, att, local_out, pg, g_small, misc, w_own, small, norm, q, k, v, o,
      jnp.asarray(cos), jnp.asarray(sin), w_all, parts)


CAP = 24


eps = 1e-06
aux_weight = 0.01
highest = lax.Precision.HIGHEST
masked_score = -1e30


def shifted(block, axis, distance):
    devices = range(lax.axis_size(axis))
    route = [(i - distance, i) for i in devices if i - distance in devices]
    return lax.ppermute(block, axis, route)


def for_sending(x):
    return jax.tree.map(lambda a: a.astype(jnp.bfloat16) if a.dtype == jnp.float32 else a, x)


def rms_norm(values, gain_vector):
    return values * lax.rsqrt(jnp.mean(values * values, axis=-1, keepdims=True) + eps) * gain_vector


def rotary(values, positions, turn_sign):
    half_width = values.shape[-1] // 2
    frequency = jnp.exp(
        jnp.arange(half_width, dtype=jnp.float32) * (-2.0 * math.log(10000.0) / values.shape[-1])
    )
    angles = positions.astype(jnp.float32)[:, None] * frequency[None, :]
    cosine = jnp.cos(angles)[:, None, :]
    sine_part = turn_sign * jnp.sin(angles)[:, None, :]
    first_half = values[..., :half_width]
    second_half = values[..., half_width:]
    return jnp.concatenate(
        [
            first_half * cosine - second_half * sine_part,
            second_half * cosine + first_half * sine_part,
        ],
        axis=-1,
    )


def slot_lengths(slot_ids, lengths):
    slot_table = jnp.arange(lengths.shape[0], dtype=jnp.int32)
    return jnp.sum(jnp.where(slot_ids[:, None] == slot_table[None, :], lengths[None, :], 0), axis=1)


def allowed_mask(query_ids, key_ids, slot_size, lengths):
    query_slot = query_ids // slot_size
    key_slot = key_ids // slot_size
    query_pos = query_ids - query_slot * slot_size
    key_pos = key_ids - key_slot * slot_size
    key_live = (key_pos < slot_lengths(key_slot, lengths)) & (key_ids >= 0)
    return (
        (query_slot[:, None] == key_slot[None, :])
        & (key_pos[None, :] <= query_pos[:, None])
        & key_live[None, :]
    )


def masked_scores(query_block, key_head, query_ids, key_ids, slot_size, lengths):
    scores = lax.dot_general(
        query_block, key_head, (((1,), (1,)), ((), ())), preferred_element_type=jnp.float32
    ) * HD ** (-0.5)
    return jnp.where(allowed_mask(query_ids, key_ids, slot_size, lengths), scores, masked_score)


def attend_forward(queries, key_all, value_all, query_ids, key_ids, slot_size, lengths):
    head_total = queries.shape[1] // HD

    def one_head(head_index):
        query_head = lax.dynamic_slice_in_dim(queries, head_index * HD, HD, 1)
        key_head = lax.dynamic_slice_in_dim(key_all, head_index * HD, HD, 1)
        value_head = lax.dynamic_slice_in_dim(value_all, head_index * HD, HD, 1)
        scores = masked_scores(query_head, key_head, query_ids, key_ids, slot_size, lengths)
        row_max = jnp.max(scores, axis=1, keepdims=True)
        weights = jnp.exp(scores - row_max)
        row_total = jnp.sum(weights, axis=1, keepdims=True)
        probs_low = (weights / row_total).astype(jnp.bfloat16)
        head_outputs = [jnp.dot(probs_low, value_head, preferred_element_type=jnp.float32)]
        log_parts = [row_max[:, 0] + jnp.log(row_total[:, 0])]
        return (jnp.concatenate(head_outputs, axis=0), jnp.concatenate(log_parts, axis=0))

    head_outputs, log_sums = lax.map(one_head, jnp.arange(head_total, dtype=jnp.int32))
    return (head_outputs.transpose(1, 0, 2).reshape(queries.shape[0], queries.shape[1]), log_sums)


def attend_backward(
    queries, key_all, value_all, out_grads, log_sums, query_ids, key_ids, slot_size, lengths
):
    head_total = queries.shape[1] // HD
    block_rows = min(512, queries.shape[0])

    def one_head(head_index):
        query_head = lax.dynamic_slice_in_dim(queries, head_index * HD, HD, 1)
        key_head = lax.dynamic_slice_in_dim(key_all, head_index * HD, HD, 1)
        value_head = lax.dynamic_slice_in_dim(value_all, head_index * HD, HD, 1)
        grad_head = lax.dynamic_slice_in_dim(out_grads, head_index * HD, HD, 1)
        log_head = lax.dynamic_index_in_dim(log_sums, head_index, 0, keepdims=False)
        key_grad = jnp.zeros(key_head.shape, jnp.float32)
        value_grad = jnp.zeros(value_head.shape, jnp.float32)
        grad_block = grad_head[0:block_rows]
        scores = masked_scores(query_head, key_head, query_ids, key_ids, slot_size, lengths)
        probs = jnp.exp(scores - log_head[0:block_rows][:, None])
        probs_low = probs.astype(jnp.bfloat16)
        prob_grads = lax.dot_general(
            grad_block, value_head, (((1,), (1,)), ((), ())), preferred_element_type=jnp.float32
        )
        row_inner = jnp.sum(probs * prob_grads, axis=1, keepdims=True)
        score_grads = (probs * (prob_grads - row_inner)).astype(jnp.bfloat16)
        query_parts = [
            jnp.dot(score_grads, key_head, preferred_element_type=jnp.float32) * HD ** (-0.5)
        ]
        key_grad = key_grad + lax.dot_general(
            score_grads, query_head, (((0,), (0,)), ((), ())), preferred_element_type=jnp.float32
        ) * HD ** (-0.5)
        value_grad = value_grad + lax.dot_general(
            probs_low, grad_block, (((0,), (0,)), ((), ())), preferred_element_type=jnp.float32
        )
        return (jnp.concatenate(query_parts, axis=0), key_grad, value_grad)

    query_grad, key_grad, value_grad = lax.map(one_head, jnp.arange(head_total, dtype=jnp.int32))
    return (
        query_grad.transpose(1, 0, 2).reshape(queries.shape[0], queries.shape[1]),
        key_grad.transpose(1, 0, 2).reshape(key_all.shape[0], key_all.shape[1]),
        value_grad.transpose(1, 0, 2).reshape(value_all.shape[0], value_all.shape[1]),
    )


def fetch_prev(key_heads, value_heads, span_count):
    key_parts = [key_heads]
    value_parts = [value_heads]
    for offset in range(1, span_count):
        arrived = shifted((key_heads, value_heads), "blk", offset)
        key_parts.append(arrived[0])
        value_parts.append(arrived[1])
    return (jnp.concatenate(key_parts, axis=0), jnp.concatenate(value_parts, axis=0))


def router_probs(normed, router_w, mixing, prev_scores):
    logits = jnp.dot(normed, router_w, precision=highest) + jnp.dot(
        prev_scores, mixing, precision=highest
    )
    return jax.nn.softmax(logits, axis=-1)


def branch_sum(router_prob, normed, const_w, vector_w, outputs_pair, choose, live_rows, real_count):
    gate_values = jnp.sum(choose * router_prob[:, None, :], axis=-1)
    expert_share = jnp.sum(choose * gate_values[:, :, None], axis=1) * live_rows[:, None]
    routed = jnp.sum(gate_values[:, :, None] * outputs_pair, axis=1)
    routed = routed + expert_share[:, real_count + 1 : real_count + 2] * normed
    const_count = vector_w.shape[1]
    const_mix = jax.nn.softmax(
        jnp.dot(normed, const_w, precision=highest).reshape(normed.shape[0], const_count, 2),
        axis=-1,
    )
    for const_index in range(const_count):
        const_out = (
            const_mix[:, const_index, 0:1] * normed
            + const_mix[:, const_index, 1:2] * vector_w[:, const_index][None, :]
        )
        routed = (
            routed
            + expert_share[:, real_count + 2 + const_index : real_count + 3 + const_index]
            * const_out
        )
    return routed


def on_device(
    tokens,
    cotangent,
    prev_logits,
    routes,
    lengths,
    w_qkv,
    w_out,
    w_router,
    w_const,
    const_vec,
    norm_gains,
    gate_mix,
    expert_weights,
):
    tok_dev = tokens.shape[0]
    model_width = tokens.shape[1]
    head_count = lax.axis_size("head")
    blk_count = lax.axis_size("blk")
    span_count = max(8, min(blk_count // 4, 8192 // (head_count * tok_dev)) * min(1, tok_dev // 64))
    head_index = lax.axis_index("head")
    blk_index = lax.axis_index("blk")
    slot_size = span_count * head_count * tok_dev
    tok_blk = head_count * tok_dev
    qkv_w, out_w, router_w, const_w, vector_w, gain_pair = (
        lax.all_gather(w_qkv, ("head", "blk"), axis=0, tiled=True),
        lax.all_gather(w_out, ("head", "blk"), axis=0, tiled=True),
        lax.all_gather(w_router, ("head", "blk"), axis=0, tiled=True),
        lax.all_gather(w_const, ("head", "blk"), axis=0, tiled=True),
        lax.all_gather(const_vec, ("head", "blk"), axis=0, tiled=True),
        lax.all_gather(norm_gains, ("head", "blk"), axis=0, tiled=True),
    )
    gain_pair = gain_pair.astype(jnp.float32)
    row_ids = (blk_index * head_count + head_index) * tok_dev + jnp.arange(tok_dev, dtype=jnp.int32)
    slot_ids = row_ids // slot_size
    positions = row_ids - slot_ids * slot_size
    live_rows = (positions < slot_lengths(slot_ids, lengths)).astype(jnp.float32)
    inputs = tokens.astype(jnp.float32)
    normed_one, norm_one_back = jax.vjp(rms_norm, inputs, gain_pair[:, 0])
    normed_one_low = normed_one.astype(jnp.bfloat16)
    projected = jnp.dot(normed_one_low, qkv_w, preferred_element_type=jnp.float32).reshape(
        tok_dev, 3, HEADS, HD
    )
    query_send = (
        rotary(projected[:, 0], positions, 1.0).astype(jnp.bfloat16).reshape(tok_dev, model_width)
    )
    key_send = (
        rotary(projected[:, 1], positions, 1.0).astype(jnp.bfloat16).reshape(tok_dev, model_width)
    )
    value_send = projected[:, 2].astype(jnp.bfloat16).reshape(tok_dev, model_width)
    query_heads, key_heads, value_heads = (
        lax.all_to_all(query_send, "head", split_axis=1, concat_axis=0, tiled=True),
        lax.all_to_all(key_send, "head", split_axis=1, concat_axis=0, tiled=True),
        lax.all_to_all(value_send, "head", split_axis=1, concat_axis=0, tiled=True),
    )
    blk_rows = blk_index * tok_blk + jnp.arange(tok_blk, dtype=jnp.int32)
    blk_pos = blk_rows - blk_rows // slot_size * slot_size
    key_ids = jnp.concatenate([blk_rows - offset * tok_blk for offset in range(span_count)], axis=0)
    key_all, value_all = fetch_prev(key_heads, value_heads, span_count)
    attended, log_sums = attend_forward(
        query_heads, key_all, value_all, blk_rows, key_ids, slot_size, lengths
    )
    attended_tok = lax.all_to_all(
        attended.astype(jnp.bfloat16), "head", split_axis=0, concat_axis=1, tiled=True
    )
    residual = inputs + jnp.dot(attended_tok, out_w, preferred_element_type=jnp.float32)
    normed_two, norm_two_back = jax.vjp(rms_norm, residual, gain_pair[:, 1])
    normed_two_low = normed_two.astype(jnp.bfloat16)
    normed_two_f = normed_two_low.astype(jnp.float32)
    router_prob, router_back = jax.vjp(
        partial(router_probs, prev_scores=prev_logits),
        normed_two_f,
        router_w.astype(jnp.float32),
        gate_mix,
    )
    expert_count = router_w.shape[1]
    real_count = expert_weights.shape[1] * head_count
    choose = (
        routes[:, :, None] == jnp.arange(expert_count, dtype=jnp.int32)[None, None, :]
    ).astype(jnp.float32)
    count_local = jnp.sum(jnp.sum(choose, axis=1) * live_rows[:, None], axis=0)
    prob_local = jnp.sum(router_prob * live_rows[:, None], axis=0)
    count_all, prob_all = lax.psum((count_local, prob_local), ("head", "blk"))
    live_total = jnp.sum(lengths).astype(jnp.float32)
    fraction = count_all / (2.0 * live_total)
    aux_loss = expert_count * jnp.sum(fraction * (prob_all / live_total))
    gate_values = jnp.sum(choose * router_prob[:, None, :], axis=-1)
    out_grad = live_rows[:, None] * cotangent.astype(jnp.float32)
    assigned = routes.reshape(-1)
    live_pairs = jnp.repeat(live_rows, 2)
    is_real = (assigned < real_count) & (live_pairs > 0)
    onehot = (
        (assigned[:, None] == jnp.arange(real_count, dtype=jnp.int32)[None, :]) & is_real[:, None]
    ).astype(jnp.int32)
    slot_rank = jnp.sum((jnp.cumsum(onehot, axis=0) - onehot) * onehot, axis=1)
    target = jnp.where(is_real, assigned * CAP + slot_rank, real_count * CAP)
    source = (
        jnp.full((real_count * CAP + 1,), 2 * tok_dev, jnp.int32)
        .at[target]
        .set(jnp.arange(2 * tok_dev, dtype=jnp.int32))[: real_count * CAP]
    )
    zero_row = jnp.zeros((1, model_width), jnp.bfloat16)
    send_rows = jnp.concatenate([normed_two_low, zero_row], axis=0)[source // 2].reshape(
        real_count, CAP, model_width
    )
    pair_grads = (gate_values.reshape(-1, 1) * jnp.repeat(out_grad, 2, axis=0)).astype(jnp.bfloat16)
    send_grads = jnp.concatenate([pair_grads, zero_row], axis=0)[source].reshape(
        real_count, CAP, model_width
    )
    expert_in, expert_cot = (
        lax.all_to_all(send_rows, "head", split_axis=0, concat_axis=1, tiled=True),
        lax.all_to_all(send_grads, "head", split_axis=0, concat_axis=1, tiled=True),
    )
    weight_piece = lax.all_gather(expert_weights, "blk", axis=0, tiled=True)
    gate_w = weight_piece[:, :, 0, :]
    up_w = weight_piece[:, :, 1, :]
    down_w = weight_piece[:, :, 2, :]
    gate_part = jnp.einsum("esd,ned->esn", expert_in, gate_w, preferred_element_type=jnp.float32)
    up_part = jnp.einsum("esd,ned->esn", expert_in, up_w, preferred_element_type=jnp.float32)
    sigmoid_part = jax.nn.sigmoid(gate_part)
    silu_part = gate_part * sigmoid_part
    hidden = (silu_part * up_part).astype(jnp.bfloat16)
    out_sum = jnp.einsum("esn,ned->esd", hidden, down_w, preferred_element_type=jnp.float32)
    hidden_grad = jnp.einsum("esd,ned->esn", expert_cot, down_w, preferred_element_type=jnp.float32)
    gate_grad = (
        hidden_grad * up_part * (sigmoid_part * (1.0 + gate_part * (1.0 - sigmoid_part)))
    ).astype(jnp.bfloat16)
    up_grad = (hidden_grad * silu_part).astype(jnp.bfloat16)
    in_grad = jnp.einsum("esn,ned->esd", gate_grad, gate_w, preferred_element_type=jnp.float32)
    in_grad = in_grad + jnp.einsum(
        "esn,ned->esd", up_grad, up_w, preferred_element_type=jnp.float32
    )
    hidden_all = hidden
    gate_all = gate_grad
    up_all = up_grad
    out_sum, in_grad, hidden_all, gate_all, up_all = (
        out_sum,
        in_grad,
        hidden_all,
        gate_all,
        up_all,
    )
    hidden_own, gate_own, up_own = (
        lax.all_to_all(hidden_all, "blk", split_axis=2, concat_axis=1, tiled=True),
        lax.all_to_all(gate_all, "blk", split_axis=2, concat_axis=1, tiled=True),
        lax.all_to_all(up_all, "blk", split_axis=2, concat_axis=1, tiled=True),
    )
    rows_in = lax.all_gather(expert_in, "blk", axis=1, tiled=True)
    rows_cot = lax.all_gather(expert_cot, "blk", axis=1, tiled=True)
    gate_w_grad = jnp.einsum("esn,esd->ned", gate_own, rows_in, preferred_element_type=jnp.float32)
    up_w_grad = jnp.einsum("esn,esd->ned", up_own, rows_in, preferred_element_type=jnp.float32)
    down_w_grad = jnp.einsum(
        "esn,esd->ned", hidden_own, rows_cot, preferred_element_type=jnp.float32
    )
    expert_grads = jnp.stack([gate_w_grad, up_w_grad, down_w_grad], axis=2)
    returned, returned_grad = (
        lax.all_to_all(
            out_sum.astype(jnp.bfloat16), "head", split_axis=1, concat_axis=0, tiled=True
        ),
        lax.all_to_all(
            in_grad.astype(jnp.bfloat16), "head", split_axis=1, concat_axis=0, tiled=True
        ),
    )
    outputs_pair = (
        jnp.concatenate([returned.reshape(-1, model_width), zero_row], axis=0)[target]
        .astype(jnp.float32)
        .reshape(tok_dev, 2, model_width)
    )
    input_pair = (
        jnp.concatenate([returned_grad.reshape(-1, model_width), zero_row], axis=0)[target]
        .astype(jnp.float32)
        .reshape(tok_dev, 2, model_width)
    )
    expert_input_grad = input_pair[:, 0] + input_pair[:, 1]
    branch, branch_back = jax.vjp(
        partial(branch_sum, choose=choose, live_rows=live_rows, real_count=real_count),
        router_prob,
        normed_two_f,
        const_w.astype(jnp.float32),
        vector_w.astype(jnp.float32),
        outputs_pair,
    )
    output = ((residual + branch) * live_rows[:, None]).astype(jnp.bfloat16)
    prob_grad, normed_grad_branch, const_grad, vector_grad, unused_grad = branch_back(out_grad)
    aux_grad = aux_weight * expert_count / live_total * fraction[None, :] * live_rows[:, None]
    normed_grad_router, router_grad, mixing_grad = router_back(prob_grad + aux_grad)
    normed_grad = normed_grad_router + normed_grad_branch + expert_input_grad
    residual_grad_norm, gain_two_grad = norm_two_back(normed_grad)
    residual_grad = out_grad + residual_grad_norm
    out_w_grad = jnp.dot(attended_tok.astype(jnp.float32).T, residual_grad, precision=highest)
    attended_grad = jnp.dot(residual_grad, out_w.astype(jnp.float32).T, precision=highest).astype(
        jnp.bfloat16
    )
    attended_grad_heads = lax.all_to_all(
        attended_grad, "head", split_axis=1, concat_axis=0, tiled=True
    )
    key_again, value_again = fetch_prev(key_heads, value_heads, span_count)
    query_grad, key_grad, value_grad = attend_backward(
        query_heads,
        key_again,
        value_again,
        attended_grad_heads,
        log_sums,
        blk_rows,
        key_ids,
        slot_size,
        lengths,
    )
    own_key = key_grad[:tok_blk]
    own_value = value_grad[:tok_blk]
    for offset in range(1, span_count):
        back_key, back_value = shifted(
            (
                for_sending(key_grad[offset * tok_blk : (offset + 1) * tok_blk]),
                for_sending(value_grad[offset * tok_blk : (offset + 1) * tok_blk]),
            ),
            "blk",
            -offset,
        )
        own_key = own_key + back_key
        own_value = own_value + back_value
    local_heads = query_heads.shape[1] // HD
    query_back = (
        rotary(query_grad.reshape(tok_blk, local_heads, HD), blk_pos, -1.0)
        .astype(jnp.bfloat16)
        .reshape(tok_blk, local_heads * HD)
    )
    key_back = (
        rotary(own_key.reshape(tok_blk, local_heads, HD), blk_pos, -1.0)
        .astype(jnp.bfloat16)
        .reshape(tok_blk, local_heads * HD)
    )
    value_back = own_value.astype(jnp.bfloat16)
    query_tok, key_tok, value_tok = (
        lax.all_to_all(query_back, "head", split_axis=0, concat_axis=1, tiled=True),
        lax.all_to_all(key_back, "head", split_axis=0, concat_axis=1, tiled=True),
        lax.all_to_all(value_back, "head", split_axis=0, concat_axis=1, tiled=True),
    )
    projected_grad = jnp.concatenate([query_tok, key_tok, value_tok], axis=1)
    qkv_grad = jnp.dot(normed_one_low.T, projected_grad, preferred_element_type=jnp.float32)
    normed_one_grad = jnp.dot(projected_grad, qkv_w.T, preferred_element_type=jnp.float32)
    inputs_grad_norm, gain_one_grad = norm_one_back(normed_one_grad)
    token_grad = (residual_grad + inputs_grad_norm).astype(jnp.bfloat16)
    weight_grads = (
        lax.psum_scatter(qkv_grad, ("head", "blk"), scatter_dimension=0, tiled=True),
        lax.psum_scatter(out_w_grad, ("head", "blk"), scatter_dimension=0, tiled=True),
        lax.psum_scatter(router_grad, ("head", "blk"), scatter_dimension=0, tiled=True),
        lax.psum_scatter(const_grad, ("head", "blk"), scatter_dimension=0, tiled=True),
        lax.psum_scatter(vector_grad, ("head", "blk"), scatter_dimension=0, tiled=True),
        lax.psum_scatter(
            jnp.stack([gain_one_grad, gain_two_grad], axis=1),
            ("head", "blk"),
            scatter_dimension=0,
            tiled=True,
        ),
    )
    mixing_total = lax.psum(mixing_grad, ("head", "blk"))
    return (
        output,
        aux_loss,
        token_grad,
        weight_grads[0],
        weight_grads[1],
        weight_grads[2],
        weight_grads[3],
        weight_grads[4],
        weight_grads[5],
        mixing_total,
        expert_grads,
    )


def on_device_small(
    tokens, cotangent, prev_logits, routes, lengths, w_qkv, w_out, w_router, w_const, const_vec, norm_gains, gate_mix,
    expert_weights,
):
    n_blk = lax.axis_size("blk")
    both = ("head", "blk")
    small = jnp.concatenate(
        [w_router, w_const, norm_gains, const_vec, jnp.zeros((24, 44), bf16)], axis=1).astype(f32)
    w_local = w_qkv.reshape(24, 3, 12, 64)
    w_local = jnp.concatenate(
        [w_local[:, :2].transpose(0, 2, 1, 3).reshape(24, 1536), w_qkv[:, 1536:]], axis=1)
    w_all = lax.all_gather(w_local, both, axis=0, tiled=True)
    prev = jnp.pad(prev_logits, ((0, 0), (0, 116)))
    mix = jnp.pad(gate_mix, ((0, 116), (0, 116)))
    w_exp = expert_weights.reshape(128, 12, 768).transpose(1, 0, 2)
    norm, q, k, v, o, cot_rows, att, sm, smt, cnt, wout, pt = attend_and_send(
        tokens, cotangent, routes, w_qkv, small, w_out, lengths, n_blk)
    parts, g_exp, local_out, res_grad, att_grad, g_small, misc, pg = run_experts(
        lengths, att, tokens, cotangent, prev, mix, routes, wout, sm, smt, cnt, pt, w_exp, cot_rows, n_blk)
    output, token_grad, qkv_grad, g_out, tail, misc = attend_back(
        lengths, att_grad, tokens, res_grad, smt, att, local_out, pg, g_small, misc, w_qkv, small, norm, q, k, v, o, w_all,
        parts, n_blk)
    live_total = jnp.sum(lengths).astype(f32)
    aux_loss = 12 * jnp.sum(cnt[0, :12] / (2.0 * live_total) * (misc[16, :12] / live_total))
    return (
        output, aux_loss, token_grad, qkv_grad, g_out, tail[:, 0:12], tail[:, 12:16], tail[:, 18:20], tail[:, 16:18],
        misc[0:12, 0:12], g_exp.reshape(4, 3, 128, 768).transpose(2, 0, 1, 3),
    )


def solution(mesh):
    small = mesh.shape["blk"] == 16 and mesh.shape["head"] == 2
    return jax.shard_map(
        on_device_small if small else on_device,
        mesh=mesh,
        in_specs=(
            P(("blk", "head"), None),
            P(("blk", "head"), None),
            P(("blk", "head"), None),
            P(("blk", "head"), None),
            P(),
            P(("head", "blk"), None),
            P(("head", "blk"), None),
            P(("head", "blk"), None),
            P(("head", "blk"), None),
            P(("head", "blk"), None),
            P(("head", "blk"), None),
            P(),
            P("blk", "head", None, None),
        ),
        out_specs=(
            P(("blk", "head"), None),
            P(),
            P(("blk", "head"), None),
            P(("head", "blk"), None),
            P(("head", "blk"), None),
            P(("head", "blk"), None),
            P(("head", "blk"), None),
            P(("head", "blk"), None),
            P(("head", "blk"), None),
            P(),
            P("blk", "head", None, None),
        ),
        check_vma=False,
    )
```

```python
from functools import partial
import functools
import math

import jax
import jax.numpy as jnp
import numpy as np
from jax import lax
from jax.experimental import pallas as pl
from jax.experimental.pallas import tpu as pltpu
from jax.sharding import PartitionSpec as P

HEADS = 12
MESH = pl.DeviceIdType.MESH
f32, bf16 = jnp.float32, jnp.bfloat16
NEG = -1e30
HD = 64
X, C, Y, Z = 1, 2, 4, 8


def place(mask, h, b):
    hb = 1 - h if mask & X else h
    cb = b % 2
    yb = (b // 2) % 2
    zb = (b // 4) % 2
    cb = 1 - cb if mask & C else cb
    yb = 1 - yb if mask & Y else yb
    zb = 1 - zb if mask & Z else zb
    low = zb * 4 + yb * 2 + cb
    return hb, (b // 8) * 8 + low, low * 2 + hb


def head_of(h, b):
    quad = b % 4
    return h * 6 + ((b % 8) // 4) * 3 + quad - quad // 3


def home_of(head):
    h, i = head // 6, head % 6
    return ((i // 3) * 4 + i % 3) * 2 + h


def greet(masks_or_all, h, b, n_blk):
    barrier = pltpu.get_barrier_semaphore()
    if masks_or_all == "all":
        me = b * 2 + h
        total = 2 * n_blk

        def say(k, carry):
            other = (me + k) % total
            pl.semaphore_signal(barrier, inc=1, device_id=(other % 2, other // 2), device_id_type=MESH)
            return carry

        lax.fori_loop(1, total, say, 0)
        pl.semaphore_wait(barrier, total - 1)
    else:
        for m in masks_or_all:
            ph, pb, _ = place(m, h, b)
            pl.semaphore_signal(barrier, inc=1, device_id=(ph, pb), device_id_type=MESH)
        pl.semaphore_wait(barrier, len(masks_or_all))


def turned(qk, cos, sin):
    lane = lax.broadcasted_iota(jnp.int32, qk.shape, 1)
    swapped = jnp.where(lane % 64 < 32, pltpu.roll(qk, 96, 1), pltpu.roll(qk, 32, 1))
    return qk * cos + swapped * sin


def rotary_tables(rows):
    freq = np.exp(np.arange(32, dtype=np.float32) * np.float32(-2.0 * math.log(10000.0) / 64)).astype(np.float32)
    ang = (np.arange(rows, dtype=np.float32)[:, None] * freq[None, :]).astype(np.float32).astype(np.float64)
    cos, sin = np.cos(ang), np.sin(ang)
    return (
        np.concatenate([cos, cos, cos, cos], 1).astype(np.float32),
        np.concatenate([-sin, sin, -sin, sin], 1).astype(np.float32),
    )


class RowGather:
    def __init__(self, buf, sems, h, b, straight=False):
        self.buf, self.h, self.b, self.straight = buf, h, b, straight
        self.parts = range(buf.shape[1])
        self.zs, self.ys, self.cs, self.zr, self.yr, self.cr = sems
        self.z, self.y, self.c = b // 4, (b // 2) % 2, b % 2

    def nth(self, k):
        return nearest(self.z, k)

    def at(self, z, y, c, p):
        return self.buf.at[z * 4 + y * 2 + c, p]

    def copy(self, where, send, recv, device):
        return pltpu.make_async_remote_copy(
            src_ref=where, dst_ref=where, send_sem=send, recv_sem=recv, device_id=device, device_id_type=MESH)

    def along_z(self, k, step, p):
        zz = self.nth(k)
        return self.copy(self.at(zz, self.y, self.c, p), self.zs.at[(step + 1) // 2, k, p], self.zr.at[zz, p],
                         (self.h, self.b + 4 * step))

    def to_z(self, k, p):
        return self.copy(self.at(self.z, self.y, self.c, p), self.zs.at[0, k, p], self.zr.at[self.z, p],
                         (self.h, self.nth(k) * 4 + self.b % 4))

    def over_y(self, k, p):
        zz = self.nth(k)
        return self.copy(self.at(zz, self.y, self.c, p), self.ys.at[k, p], self.yr.at[zz, p],
                         (self.h, self.b + 2 - 4 * self.y))

    def over_core(self, k, far, p):
        zz = self.nth(k)
        yy = 1 - self.y if far else self.y
        return self.copy(self.at(zz, yy, self.c, p), self.cs.at[far, k, p], self.cr.at[far, zz, p],
                         (self.h, self.b + 1 - 2 * self.c))

    def own_z(self, act):
        for p in self.parts:
            if self.straight:
                for k in range(1, 4):
                    act(self.to_z(k, p))
            else:
                for step in (1, -1):
                    @pl.when((self.z + step >= 0) & (self.z + step <= 3))
                    def _(step=step, p=p):
                        act(self.along_z(0, step, p))

    def relay(self, k, p, act):
        if self.straight:
            return
        zz = self.nth(k)

        @pl.when((zz < self.z) & (self.z < 3))
        def _():
            act(self.along_z(k, 1, p))

        @pl.when((zz > self.z) & (self.z > 0))
        def _():
            act(self.along_z(k, -1, p))

    def start(self):
        self.own_z(lambda c: c.start())
        for p in self.parts:
            self.over_y(0, p).start()
        for p in self.parts:
            self.over_core(0, 0, p).start()

    def arrived(self, where, sem):
        self.copy(where, self.zs.at[0, 0, 0], sem, (self.h, self.b)).wait_recv()

    def got_z(self, k):
        zz = self.nth(k)
        for p in self.parts:
            self.arrived(self.at(zz, self.y, self.c, p), self.zr.at[zz, p])
            self.relay(k, p, lambda c: c.start())
            self.over_y(k, p).start()
            self.over_core(k, 0, p).start()

    def got_y(self, k):
        zz = self.nth(k)
        for p in self.parts:
            self.arrived(self.at(zz, 1 - self.y, self.c, p), self.yr.at[zz, p])
            self.over_core(k, 1, p).start()

    def got_core(self, k):
        zz = self.nth(k)
        for far in range(2):
            yy = 1 - self.y if far else self.y
            for p in self.parts:
                self.arrived(self.at(zz, yy, 1 - self.c, p), self.cr.at[far, zz, p])

    def finish(self):
        self.own_z(lambda c: c.wait_send())
        for p in self.parts:
            for k in range(4):
                if k:
                    self.relay(k, p, lambda c: c.wait_send())
                self.over_y(k, p).wait_send()
                self.over_core(k, 0, p).wait_send()
                self.over_core(k, 1, p).wait_send()


def nearest(z, k):
    near = z - (z // 2) * (2 * z - 3)
    low = k + (1 - 2 * k) * near if k < 2 else k
    return low + (z // 2) * (3 - 2 * low)


def gather_sems(parts):
    DMA = pltpu.SemaphoreType.DMA
    return [DMA((2, 4, parts)), DMA((4, parts)), DMA((2, 4, parts)), DMA((4, parts)), DMA((4, parts)), DMA((2, 4, parts))]


def fold(rows):
    half = rows.shape[1] // 2
    low = jnp.concatenate([rows[16:24, :half], rows[16:24, half:]], axis=0)
    return jnp.concatenate([rows[0:16], low], axis=1).astype(bf16)


def routing_table(routes, live):
    lane = lax.broadcasted_iota(jnp.int32, (128, 128), 1)
    row = lax.broadcasted_iota(jnp.int32, (128, 128), 0)
    expert = lane.astype(f32)
    named = jnp.where((routes[:, 0:1] == expert) | (routes[:, 1:2] == expert), live, 0.0)
    before = jnp.where(lane < row, 1.0, 0.0).astype(bf16)
    rank = jnp.dot(before, named.astype(bf16), preferred_element_type=f32)
    return named, named * (rank + 1.0)


def expert_lanes(h):
    e = lax.broadcasted_iota(jnp.int32, (128, 256), 0)
    s = lax.broadcasted_iota(jnp.int32, (128, 256), 1)
    return jnp.where((s < 192) & (e == 4 * h + s // 48), 1.0, 0.0)


def slot_table(ranks, h, source_h):
    spread = jnp.dot(ranks.astype(bf16), expert_lanes(h).astype(bf16), preferred_element_type=f32)
    s = lax.broadcasted_iota(jnp.int32, (128, 256), 1)
    place_in = s % 48 - 24 * source_h
    inside = (place_in >= 0) & (place_in < 24) & (s < 192)
    return jnp.where(inside & (spread == (place_in + 1).astype(f32)), 1.0, 0.0)


def live_column(h, b, length):
    row = lax.broadcasted_iota(jnp.int32, (128, 1), 0) + ((b % 8) * 2 + h) * 128
    return jnp.where(row < length, 1.0, 0.0)


def forward_kernel(
    n_blk, lengths, tok, cot, routes, w_in, small, wo_in, cos_hbm, sin_hbm, relay_w,
    norm_hbm, q_hbm, k_hbm, v_hbm, o_hbm, att_out, smt_out, cnt_out, sm_out, wo_out, pt_out, cot_rows,
    xg, pieces, got, w_f, w_b, cos, sin, norm, q, k, v, o, sendbuf, att_in, rank_own, rank_far, cot_far, wo_all,
    ag_send, ag_recv, pc_send, pc_recv, at_send, at_recv, loc, x_send, x_recv, *gathers,
):
    h, b = lax.axis_index("head"), lax.axis_index("blk")
    me = b * 2 + h
    total = 2 * n_blk
    _, _, rank = place(0, h, b)
    cos_in = pltpu.make_async_copy(cos_hbm, cos, loc.at[9])
    sin_in = pltpu.make_async_copy(sin_hbm, sin, loc.at[10])
    cos_in.start()
    sin_in.start()
    for p in range(3):
        xg[p, rank] = tok[:, 256 * p : 256 * p + 256]
    greet("all", h, b, n_blk)

    def block_copy(p, m, d, slot):
        _, _, r = place(m, h, b)
        ph, pb, _ = place(d, h, b)
        return pltpu.make_async_remote_copy(
            src_ref=xg.at[p, r], dst_ref=xg.at[p, r],
            send_sem=ag_send.at[p, slot], recv_sem=ag_recv.at[p, m ^ d],
            device_id=(ph, pb), device_id_type=MESH,
        )

    def arrival(p, m):
        _, _, r = place(m, h, b)
        return pltpu.make_async_remote_copy(
            src_ref=xg.at[p, r], dst_ref=xg.at[p, r],
            send_sem=ag_send.at[p, 0], recv_sem=ag_recv.at[p, m],
            device_id=(h, b), device_id_type=MESH,
        )

    sends = []
    counts = [0, 0, 0]

    def send(p, m, d):
        copy = block_copy(p, m, d, counts[p])
        counts[p] += 1
        copy.start()
        sends.append(copy)

    dims = [X, Y, Z]
    orders = [dims[p:] + dims[:p] for p in range(3)]
    for t in range(3):
        for p in range(3):
            send(p, 0, orders[p][t])
    for p in range(3):
        send(p, 0, C)

    length = lengths[b // 8]
    named, ranks = routing_table(routes[...], live_column(h, b, length))
    rank_own[...] = ranks.astype(bf16)
    wo_all[b, 0, h] = fold(wo_in[...].astype(f32))

    w24 = w_in[...].astype(f32)
    count = pltpu.roll(jnp.sum(named, axis=0, keepdims=True), 20, 1)[:, 0:64]
    small = small[...] + jnp.where(lax.broadcasted_iota(jnp.int32, (24, 64), 0) == 0, count, 0.0)
    for j in range(12):
        cat = jnp.concatenate(
            [w24[:, 64 * j : 64 * j + 64], w24[:, 768 + 64 * j : 832 + 64 * j],
             w24[:, 1536 + 64 * j : 1600 + 64 * j], small], axis=1)
        pieces[j] = fold(cat)

    def piece_copy(kk):
        other = (me + kk) % total
        oh, ob = other % 2, other // 2
        return pltpu.make_async_remote_copy(
            src_ref=pieces.at[head_of(oh, ob)], dst_ref=got.at[me],
            send_sem=pc_send.at[kk], recv_sem=pc_recv.at[me],
            device_id=(oh, ob), device_id_type=MESH,
        )

    def send_piece(kk, carry):
        piece_copy(kk).start()
        return carry

    lax.fori_loop(1, total, send_piece, 0)
    got[me] = pieces[head_of(h, b)]

    relay_w(0)
    for p in range(3):
        d0, d1, d2 = orders[p]
        arrival(p, d0).wait_recv()
        for d in (d1, d2, C):
            send(p, d0, d)
    relay_w(1)
    for p in range(3):
        d0, d1, d2 = orders[p]
        for m in (d1, d0 ^ d1):
            arrival(p, m).wait_recv()
            for d in (d2, C):
                send(p, m, d)
    swaps = [
        pltpu.make_async_remote_copy(
            src_ref=src, dst_ref=dst, send_sem=x_send.at[n], recv_sem=x_recv.at[n],
            device_id=(1 - h, b), device_id_type=MESH)
        for n, (src, dst) in enumerate([(wo_all.at[b, 0, h], wo_all.at[b, 0, h]), (rank_own, rank_far), (cot, cot_far)])
    ]
    for c in swaps:
        c.start()
    relay_w(2)
    for p in range(3):
        d0, d1, d2 = orders[p]
        for m in (d2, d0 ^ d2, d1 ^ d2, d0 ^ d1 ^ d2):
            arrival(p, m).wait_recv()
            send(p, m, C)

    def take_piece(kk, carry):
        src = (me + kk) % total
        pltpu.make_async_remote_copy(
            src_ref=pieces.at[0], dst_ref=got.at[src],
            send_sem=pc_send.at[0], recv_sem=pc_recv.at[src],
            device_id=(h, b), device_id_type=MESH,
        ).wait_recv()
        return carry

    lax.fori_loop(1, total, take_piece, 0)

    for src in range(2 * n_blk):
        row = 24 * ((src % 2) * n_blk + src // 2)
        w_f[row : row + 16, :] = got[src, :, 0:256].astype(f32)
        low = got[src, :, 256:384].astype(f32)
        w_f[row + 16 : row + 24, 0:128] = low[0:8]
        w_f[row + 16 : row + 24, 128:256] = low[8:16]
    w_b[...] = w_f[...].astype(bf16)
    sm = pltpu.roll(w_f[:, 128:256], 64, 1)
    lane = lax.broadcasted_iota(jnp.int32, (768, 128), 1)
    cnt = jnp.sum(jnp.where((lane >= 20) & (lane < 32), sm, 0.0), axis=0, keepdims=True)
    cnt_out[...] = jnp.broadcast_to(pltpu.roll(cnt, 108, 1), (8, 128))
    sm = jnp.where(lane < 20, sm, 0.0)
    sm_out[...] = sm.astype(bf16)
    smt = jnp.transpose(sm)
    smt_out[...] = smt[0:32, :]
    gain = smt[16:17, :]

    pltpu.make_async_remote_copy(
        src_ref=wo_all.at[b, 0, h], dst_ref=wo_all.at[b, 0, 1 - h], send_sem=x_send.at[0], recv_sem=x_recv.at[0],
        device_id=(h, b), device_id_type=MESH).wait_recv()
    wo_gather = RowGather(wo_all, gathers[0:6], h, b, straight=True)
    wo_gather.start()
    swaps[1].wait_recv()
    swaps[2].wait_recv()
    pt = [slot_table(ranks, h, h).astype(bf16), slot_table(rank_far[...].astype(f32), h, 1 - h).astype(bf16)]
    pt_out[0] = pt[0]
    pt_out[1] = pt[1]
    picked = sum(
        lax.dot_general(t[:, 0:192], c[...], (((0,), (0,)), ((), ())), preferred_element_type=f32)
        for t, c in zip(pt, (cot, cot_far))).astype(bf16)
    cot_rows[b, 0] = picked[0:96]
    cot_rows[b, 1] = picked[96:192]
    cot_gather = RowGather(cot_rows, gathers[6:12], h, b, straight=True)
    cot_gather.start()

    for p in range(3):
        for m in (C, C ^ X, C ^ Y, C ^ Z, C ^ X ^ Y, C ^ X ^ Z, C ^ Y ^ Z, C ^ X ^ Y ^ Z):
            arrival(p, m).wait_recv()
    cos_in.wait()
    sin_in.wait()

    def one_block(r, carry):
        x = [xg[p, r].astype(f32) for p in range(3)]
        mean = sum(jnp.sum(t * t, axis=1, keepdims=True) for t in x) * (1.0 / 768)
        scale = lax.rsqrt(mean + 1e-6)
        rows = pl.ds(pl.multiple_of(r * 128, 128), 128)
        acc = jnp.zeros((128, 256), f32)
        for p in range(3):
            n = (x[p] * scale * gain[:, 256 * p : 256 * p + 256]).astype(bf16)
            norm[rows, 256 * p : 256 * p + 256] = n
            acc = acc + jnp.dot(n, w_b[256 * p : 256 * p + 256, :], preferred_element_type=f32)
        qk = turned(acc[:, 0:128], cos[rows, :], sin[rows, :])
        q[rows, :] = (qk[:, 0:64] * 0.125).astype(bf16)
        k[rows, :] = qk[:, 64:128].astype(bf16)
        lane = lax.broadcasted_iota(jnp.int32, (128, 128), 1)
        v[rows, :] = jnp.where(lane < 64, acc[:, 128:256], jnp.where(lane == 64, 1.0, 0.0)).astype(bf16)
        return carry

    lax.fori_loop(0, 16, one_block, 0)
    stores = [
        pltpu.make_async_copy(norm, norm_hbm, loc.at[4]),
        pltpu.make_async_copy(q, q_hbm, loc.at[5]),
        pltpu.make_async_copy(k, k_hbm, loc.at[6]),
        pltpu.make_async_copy(v, v_hbm, loc.at[7]),
    ]
    for s in stores:
        s.start()

    head = head_of(h, b)
    working = (b % 4) != 3
    base = (b // 8) * 8

    w, c = wo_gather, cot_gather
    between = {
        0: [lambda: w.got_z(1), lambda: w.got_y(0)],
        1: [lambda: w.got_z(2), lambda: w.got_z(3)],
        2: [lambda: w.got_y(1)],
        3: [lambda: w.got_y(2), lambda: c.got_z(1)],
        4: [lambda: w.got_y(3)],
        5: [lambda: w.got_core(0), lambda: w.got_core(1), lambda: c.got_y(0)],
        6: [lambda: w.got_core(2), lambda: w.got_core(3)],
        7: [],
    }

    def out_copy(r):
        return pltpu.make_async_remote_copy(
            src_ref=sendbuf.at[r], dst_ref=att_in.at[head],
            send_sem=at_send.at[r], recv_sem=at_recv.at[head],
            device_id=(r % 2, base + r // 2), device_id_type=MESH,
        )

    for i in range(8):
        width = 256 * (i + 1)
        s = lax.dot_general(q[256 * i : width, :], k[0:width, :], (((1,), (1,)), ((), ())), preferred_element_type=f32)
        key = lax.broadcasted_iota(jnp.int32, (1, width), 1)
        s = s + jnp.where(key < length, 0.0, NEG)
        rowi = lax.broadcasted_iota(jnp.int32, (256, 256), 0)
        coli = lax.broadcasted_iota(jnp.int32, (256, 256), 1)
        last = jnp.where(coli <= rowi, s[:, width - 256 :], NEG)
        s = last if i == 0 else jnp.concatenate([s[:, : width - 256], last], axis=1)
        m = jnp.max(s, axis=1, keepdims=True)
        e = jnp.exp(s - m).astype(bf16)
        ov = jnp.dot(e, v[0:width, :], preferred_element_type=f32)
        l = ov[:, 64:65]
        lane = lax.broadcasted_iota(jnp.int32, (256, 128), 1)
        ov = jnp.where(lane < 64, ov / l, m + jnp.log(l))
        o[256 * i : width, :] = ov
        oh = ov[:, 0:64]
        for half in range(2):
            r = 2 * i + half
            packed = jnp.concatenate([oh[128 * half : 128 * half + 64], oh[128 * half + 64 : 128 * half + 128]], axis=1)
            sendbuf[r] = packed.astype(bf16)

            @pl.when(working & (r != rank))
            def _(r=r):
                out_copy(r).start()
        for act in between[i]:
            act()

    o_store = pltpu.make_async_copy(o, o_hbm, loc.at[8])
    o_store.start()

    def unfolded(blk, hh):
        t = wo_all[blk, 0, hh].astype(f32)
        return jnp.concatenate(
            [t[:, 0:768], jnp.concatenate([t[0:8, 768:1152], t[8:16, 768:1152]], axis=1)], axis=0)

    for hh in range(2):
        for blk in range(0, 16, 2):
            row = 24 * (hh * 16 + blk)
            wo_out[row : row + 48, :] = jnp.concatenate([unfolded(blk, hh), unfolded(blk + 1, hh)], axis=0).astype(bf16)

    @pl.when(working)
    def _():
        att_in[head] = sendbuf[rank]

    for j in range(12):
        @pl.when(rank != home_of(j))
        def _(j=j):
            pltpu.make_async_remote_copy(
                src_ref=sendbuf.at[0], dst_ref=att_in.at[j],
                send_sem=at_send.at[0], recv_sem=at_recv.at[j],
                device_id=(h, b), device_id_type=MESH,
            ).wait_recv()

    for j in range(0, 12, 2):
        one, two = att_in[j].astype(f32), att_in[j + 1].astype(f32)
        att_out[0:64, 64 * j : 64 * j + 128] = jnp.concatenate([one[:, 0:64], two[:, 0:64]], axis=1).astype(bf16)
        att_out[64:128, 64 * j : 64 * j + 128] = jnp.concatenate([one[:, 64:128], two[:, 64:128]], axis=1).astype(bf16)

    def finish():
        for copy in sends:
            copy.wait_send()
        for c in swaps:
            c.wait_send()
        wo_gather.finish()
        cot_gather.finish()

        def sent_piece(kk, carry):
            piece_copy(kk).wait_send()
            return carry

        lax.fori_loop(1, total, sent_piece, 0)
        for r in range(16):
            @pl.when(working & (r != rank))
            def _(r=r):
                out_copy(r).wait_send()
        for s in stores:
            s.wait()
        o_store.wait()

    return cot_gather, finish


def split(x):
    high = x.astype(bf16)
    return high, (x - high.astype(f32)).astype(bf16)


def exact_dot(x, y, dims):
    high, low = split(x)
    return lax.dot_general(high, y, (dims, ((), ())), preferred_element_type=f32) + lax.dot_general(
        low, y, (dims, ((), ())), preferred_element_type=f32)


def softmax_back(p, d):
    return p * (d - jnp.sum(p * d, axis=1, keepdims=True))


def lane_of(column, n):
    lane = lax.broadcasted_iota(jnp.int32, (128, 128), 1)
    return jnp.where(lane == n, column, 0.0)


class RowScatter:
    def __init__(self, part, from_core, from_y, from_z, sems, h, b):
        self.part, self.from_core, self.from_y, self.from_z = part, from_core, from_y, from_z
        self.h, self.b = h, b
        self.cs, self.cr, self.ys, self.yr, self.zs, self.zr = sems
        self.parts = range(part.shape[1])
        self.order = [(k, p) for k in (3, 2, 1, 0) for p in self.parts]
        self.z, self.y, self.c = b // 4, (b // 2) % 2, b % 2

    def nth(self, k):
        return nearest(self.z, k)

    def blk(self, k, far_y, far_c):
        y = 1 - self.y if far_y else self.y
        c = 1 - self.c if far_c else self.c
        return self.nth(k) * 4 + y * 2 + c

    def remote(self, src, dst, send, recv, device):
        return pltpu.make_async_remote_copy(
            src_ref=src, dst_ref=dst, send_sem=send, recv_sem=recv, device_id=device, device_id_type=MESH)

    def core(self, k, far, p):
        return self.remote(self.part.at[self.blk(k, far, 1), p], self.from_core.at[k, far, p], self.cs.at[k, far, p],
                           self.cr.at[k, far, p], (self.h, self.b + 1 - 2 * self.c))

    def over_y(self, k, p):
        return self.remote(self.part.at[self.blk(k, 1, 0), p], self.from_y.at[k, p], self.ys.at[k, p], self.yr.at[k, p],
                           (self.h, self.b + 2 - 4 * self.y))

    def to_z(self, k, p):
        return self.remote(self.part.at[self.blk(k, 0, 0), p], self.from_z.at[self.z, p], self.zs.at[k, p],
                           self.zr.at[self.z, p], (self.h, self.nth(k) * 4 + self.b % 4))

    def add(self, blk, p, *others):
        total = self.part[blk, p].astype(f32)
        for other in others:
            total = total + other[...].astype(f32)
        self.part[blk, p] = total.astype(bf16)

    def send_core(self, k, p):
        self.core(k, 1, p).start()
        self.core(k, 0, p).start()

    def send_y(self, k, p):
        self.core(k, 1, p).wait_recv()
        self.add(self.blk(k, 1, 0), p, self.from_core.at[k, 1, p])
        self.over_y(k, p).start()

    def send_z(self, k, p):
        self.core(k, 0, p).wait_recv()
        self.over_y(k, p).wait_recv()
        self.add(self.blk(k, 0, 0), p, self.from_core.at[k, 0, p], self.from_y.at[k, p])
        if k:
            self.to_z(k, p).start()

    def total(self, p):
        total = self.part[self.b, p].astype(f32)
        for k in range(1, 4):
            here = self.from_z.at[self.nth(k), p]
            self.remote(here, here, self.zs.at[0, 0], self.zr.at[self.nth(k), p], (self.h, self.b)).wait_recv()
            total = total + here[...].astype(f32)
        return total

    def finish(self):
        for p in self.parts:
            for k in range(4):
                self.core(k, 0, p).wait_send()
                self.core(k, 1, p).wait_send()
                self.over_y(k, p).wait_send()
                if k:
                    self.to_z(k, p).wait_send()


def scatter_scratch(parts, rows, cols):
    DMA = pltpu.SemaphoreType.DMA
    V = pltpu.VMEM
    return [
        V((4, 2, parts, rows, cols), bf16), V((4, parts, rows, cols), bf16), V((4, parts, rows, cols), bf16),
        DMA((4, 2, parts)), DMA((4, 2, parts)), DMA((4, parts)), DMA((4, parts)), DMA((4, parts)), DMA((4, parts)),
    ]


def expert_kernel(
    n_blk, cg, lengths, att, tok, cot, prev, mix, routes, wout, sm, smt, cnt, pt, w, cot_all,
    part_hbm, g_hbm, local_out, res_out, ag_out, gs_out, misc_out, pg_out,
    x_all, cc, dgu, hid, inp, outp, gbuf, gates_in, vs_out, vs_in, n_own, n_far, g_own, g_far,
    d_out, d_in, dv_out, dv_in, ga_send, ga_recv, vs_send, vs_recv, x_send, x_recv, loc, *rest,
):
    gsems, (from_core, from_y, from_z), ssems = rest[0:6], rest[6:9], rest[9:15]
    h, b = lax.axis_index("head"), lax.axis_index("blk")
    length = lengths[b // 8]
    live_total = (lengths[0] + lengths[1]).astype(f32)
    live = live_column(h, b, length)
    lane = lax.broadcasted_iota(jnp.int32, (128, 128), 1)

    res = tok[...].astype(f32) + jnp.dot(att[...], wout[...], preferred_element_type=f32)
    scale = lax.rsqrt(jnp.sum(res * res, axis=1, keepdims=True) * (1.0 / 768) + 1e-6)
    xh = res * scale
    n2 = (xh * smt[17:18, :]).astype(bf16)
    small = sm[...]
    logits = jnp.dot(n2, small, preferred_element_type=f32)
    router = logits + jnp.dot(prev[...], mix[...], preferred_element_type=f32, precision=lax.Precision.HIGHEST)
    router = jnp.where(lane < 12, router, NEG)
    prob = jnp.exp(router - jnp.max(router, axis=1, keepdims=True))
    prob = prob / jnp.sum(prob, axis=1, keepdims=True)
    expert = lane.astype(f32)
    named = jnp.where((routes[:, 0:1] == expert) | (routes[:, 1:2] == expert), 1.0, 0.0)
    gates = prob * named
    n_own[...] = n2
    g_own[...] = gates
    swaps = [
        pltpu.make_async_remote_copy(
            src_ref=src, dst_ref=dst, send_sem=x_send.at[n], recv_sem=x_recv.at[n],
            device_id=(1 - h, b), device_id_type=MESH)
        for n, (src, dst) in enumerate([(n_own, n_far), (g_own, g_far), (d_out, d_in), (dv_out, dv_in)])
    ]
    swaps[0].start()
    swaps[1].start()
    cg.got_z(2)
    cg.got_y(1)
    p_own, p_far = pt[0, :, 0:192], pt[1, :, 0:192]
    rows = ((0,), (0,))
    mine = lax.dot_general(p_own, n2, (rows, ((), ())), preferred_element_type=f32)
    spread = expert_lanes(h).astype(bf16)
    pg_own = pt[0].astype(f32) * exact_dot(gates, spread, ((1,), (0,)))
    pg_out[0] = pg_own
    swaps[0].wait_recv()
    picked = (mine + lax.dot_general(p_far, n_far[...], (rows, ((), ())), preferred_element_type=f32)).astype(bf16)
    x_all[b, 0] = picked[0:96]
    x_all[b, 1] = picked[96:192]
    g = RowGather(x_all, gsems, h, b)
    g.start()
    cg.got_z(3)
    cg.got_y(2)
    cg.got_y(3)
    swaps[1].wait_recv()
    pg_far = pt[1].astype(f32) * exact_dot(g_far[...], spread, ((1,), (0,)))
    pg_out[1] = pg_far
    gates_in[b] = jnp.broadcast_to(jnp.sum(pg_own + pg_far, axis=0, keepdims=True), (8, 256))

    def gate_copy(k):
        return pltpu.make_async_remote_copy(
            src_ref=gates_in.at[b], dst_ref=gates_in.at[b], send_sem=ga_send.at[k], recv_sem=ga_recv.at[b],
            device_id=(h, (b + k) % n_blk), device_id_type=MESH)

    def vs_copy(k):
        to = (b + k) % n_blk
        return pltpu.make_async_remote_copy(
            src_ref=vs_out.at[to], dst_ref=vs_in.at[b], send_sem=vs_send.at[k], recv_sem=vs_recv.at[b],
            device_id=(h, to), device_id_type=MESH)

    def each(act):
        def body(k, carry):
            act(k)
            return carry

        lax.fori_loop(1, n_blk, body, 0)

    each(lambda k: gate_copy(k).start())

    def group(ref, k, p, ee):
        return ref[pl.ds(4 * g.nth(k), 4), p, 48 * ee : 48 * ee + 48, :]

    def put(ref, k, p, ee, value):
        ref[pl.ds(4 * g.nth(k), 4), p, 48 * ee : 48 * ee + 48, :] = value.reshape(4, 48, value.shape[1]).astype(ref.dtype)

    cols = ((1,), (1,))

    def cot_task(k):
        for e in range(4):
            rows_c = group(cot_all, k, e // 2, e % 2).reshape(192, 768)
            put(cc, k, e // 2, e % 2, lax.dot_general(rows_c, w[3 * e + 2], (cols, ((), ())), preferred_element_type=f32))

    def up_task(k):
        for e in range(4):
            p, ee = e // 2, e % 2
            x = group(x_all, k, p, ee).reshape(192, 768)
            both = lax.dot_general(x, w[3 * e : 3 * e + 2].reshape(256, 768), (cols, ((), ())), preferred_element_type=f32)
            gate, up = both[:, 0:128], both[:, 128:256]
            sig = 1.0 / (1.0 + jnp.exp(-gate))
            silu = gate * sig
            hidden = silu * up
            c = group(cc, k, p, ee).reshape(192, 128)
            put(hid, k, p, ee, hidden)
            put(cc, k, p, ee, hidden * c)
            dg = c * up * (sig * (1.0 + gate * (1.0 - sig)))
            put(dgu, k, p, ee, jnp.concatenate([dg, c * silu], axis=1))

    two = jnp.where(lane % 2 == 0, pltpu.roll(logits, 127, 1), pltpu.roll(logits, 1, 1))
    top = jnp.maximum(logits, two)
    c_mix = jnp.exp(logits - top) / (jnp.exp(logits - top) + jnp.exp(two - top))
    share = gates * live
    n2f = n2.astype(f32)
    alpha = share[:, 9:10] + share[:, 10:11] * c_mix[:, 12:13] + share[:, 11:12] * c_mix[:, 14:15]
    beta = [share[:, 10:11] * c_mix[:, 13:14], share[:, 11:12] * c_mix[:, 15:16]]
    local_out[...] = live * (res + alpha * n2f + beta[0] * smt[18:19, :] + beta[1] * smt[19:20, :])
    og = live * cot[...].astype(f32)
    og_low = og.astype(bf16)

    g.got_z(1)
    cg.got_core(0)
    cot_task(0)
    g.got_z(2)
    g.got_y(0)
    cg.got_core(1)
    cot_task(1)
    g.got_z(3)
    g.got_y(1)
    cg.got_core(2)
    cot_task(2)
    cg.got_core(3)
    cot_task(3)
    g.got_core(0)
    up_task(0)
    g.got_y(2)
    g.got_core(1)
    up_task(1)
    g.got_y(3)
    g.got_core(2)
    up_task(2)
    g.got_core(3)
    up_task(3)

    s = RowScatter(inp, from_core, from_y, from_z, ssems, h, b)
    order = s.order
    for n, (k, p) in enumerate(order):
        for ee in range(2):
            e = 2 * p + ee
            d = group(dgu, k, p, ee).reshape(192, 256)
            put(inp, k, p, ee, jnp.dot(d, w[3 * e : 3 * e + 2].reshape(256, 768), preferred_element_type=f32))
        s.send_core(k, p)
        if n:
            s.send_y(*order[n - 1])
    s.send_y(*order[7])

    ones = jnp.ones((8, 128), f32)

    def one_blk(j, carry):
        for p in range(2):
            vs_out[j, :, 128 * p : 128 * p + 96] = lax.dot_general(
                ones, cc[j, p], (cols, ((), ())), preferred_element_type=f32, precision=lax.Precision.HIGHEST)
        return carry

    lax.fori_loop(0, n_blk, one_blk, 0)
    each(lambda k: vs_copy(k).start())
    vs_in[b] = vs_out[b]
    each(lambda k: pltpu.make_async_remote_copy(
        src_ref=gates_in.at[b], dst_ref=gates_in.at[(b + k) % n_blk], send_sem=ga_send.at[0],
        recv_sem=ga_recv.at[(b + k) % n_blk], device_id=(h, b), device_id_type=MESH).wait_recv())
    gate_cols = jnp.transpose(gates_in[:, 0, :])

    def scaled(ref, p, ee):
        e = 2 * p + ee
        t = ref[:, p, 48 * ee : 48 * ee + 48, :].astype(f32)
        col = jnp.concatenate([gate_cols[48 * e : 48 * e + 48, j : j + 1] for j in range(n_blk)], axis=0)
        return (t.reshape(48 * n_blk, t.shape[2]) * col).astype(bf16)

    def store_g(e, act):
        for kind in range(3):
            act(pltpu.make_async_copy(gbuf.at[kind], g_hbm.at[:, kind, e, :], loc.at[kind]))

    def weight_task(e):
        p, ee = e // 2, e % 2
        x = x_all[:, p, 48 * ee : 48 * ee + 48, :].reshape(48 * n_blk, 768)
        c = cot_all[:, p, 48 * ee : 48 * ee + 48, :].reshape(48 * n_blk, 768)
        if e:
            store_g(e - 1, lambda c: c.wait())
        gbuf[0:2] = lax.dot_general(
            scaled(dgu, p, ee), x, (rows, ((), ())), preferred_element_type=f32).reshape(2, 128, 768)
        gbuf[2] = lax.dot_general(scaled(hid, p, ee), c, (rows, ((), ())), preferred_element_type=f32)
        store_g(e, lambda c: c.start())

    def out_task(k):
        for e in range(4):
            d = group(hid, k, e // 2, e % 2).reshape(192, 128)
            put(outp, k, e // 2, e % 2, jnp.dot(d, w[3 * e + 2], preferred_element_type=f32))

    tasks = [lambda: weight_task(0), lambda: out_task(0), lambda: weight_task(1), lambda: out_task(1),
             lambda: weight_task(2), lambda: out_task(2), lambda: weight_task(3), lambda: out_task(3)]
    for (k, p), task in zip(order, tasks):
        task()
        s.send_z(k, p)
    part_store = pltpu.make_async_copy(outp, part_hbm, loc.at[6])
    part_store.start()

    din = jnp.concatenate([s.total(0), s.total(1)], axis=0).astype(bf16)
    into = ((1,), (0,))
    d_out[...] = exact_dot(pg_far[:, 0:192], din, into).astype(bf16)
    swaps[2].start()
    each(lambda k: pltpu.make_async_remote_copy(
        src_ref=vs_in.at[b], dst_ref=vs_in.at[(b + k) % n_blk], send_sem=vs_send.at[0],
        recv_sem=vs_recv.at[(b + k) % n_blk], device_id=(h, b), device_id_type=MESH).wait_recv())
    vsum = jnp.sum(vs_in[:, 0, :], axis=0, keepdims=True)
    vrow = jnp.concatenate([vsum[:, 0:96], vsum[:, 128:224]], axis=1)
    spread = spread[:, 0:192]
    dv_out[...] = exact_dot(p_far.astype(f32) * vrow, spread, cols)
    swaps[3].start()
    d_own = exact_dot(pg_own[:, 0:192], din, into)
    dv_own = exact_dot(p_own.astype(f32) * vrow, spread, cols)

    u = jnp.sum(og * n2f, axis=1, keepdims=True)
    wj = jnp.dot(og_low, small, preferred_element_type=f32)
    w0, w1 = wj[:, 18:19], wj[:, 19:20]
    c = [c_mix[:, n : n + 1] for n in (12, 13, 14, 15)]
    dgate = lane_of(u, 9) + lane_of(c[0] * u + c[1] * w0, 10) + lane_of(c[2] * u + c[3] * w1, 11)
    dmix = lane_of(u, 12) + lane_of(w0, 13) + lane_of(u, 14) + lane_of(w1, 15)
    dmix = dmix * jnp.where(lane < 14, gates[:, 10:11], gates[:, 11:12])
    both = c_mix * dmix
    dmix = c_mix * (dmix - both - jnp.where(lane % 2 == 0, pltpu.roll(both, 127, 1), pltpu.roll(both, 1, 1)))
    dmix = jnp.where((lane >= 12) & (lane < 16), dmix, 0.0)
    aux = (0.01 * 12.0 / live_total) * (cnt[0:1, :] / (2.0 * live_total)) * live
    swaps[2].wait_recv()
    swaps[3].wait_recv()
    dprob = named * (dgate + dv_own + dv_in[...]) + aux
    dlog = softmax_back(prob, dprob) + dmix
    dn = d_own + d_in[...].astype(f32) + og * alpha + exact_dot(dlog, jnp.where(
        lax.broadcasted_iota(jnp.int32, (768, 128), 1) < 16, small, 0).astype(bf16), cols)
    t = dn * smt[17:18, :]
    rg = og + scale * (t - xh * (jnp.sum(t * xh, axis=1, keepdims=True) * (1.0 / 768)))
    res_out[...] = rg
    ag_out[...] = lax.dot_general(rg.astype(bf16), wout[...], (cols, ((), ())), preferred_element_type=f32).astype(bf16)

    dl_high, dl_low = split(dlog)
    gs = lax.dot_general(n2, dl_high, (rows, ((), ())), preferred_element_type=f32)
    gs = gs + lax.dot_general(n2, dl_low, (rows, ((), ())), preferred_element_type=f32)
    b_high, b_low = split(lane_of(beta[0], 18) + lane_of(beta[1], 19))
    gs = gs + lax.dot_general(og_low, b_high, (rows, ((), ())), preferred_element_type=f32)
    gs = gs + lax.dot_general(og_low, b_low, (rows, ((), ())), preferred_element_type=f32)
    gain = jnp.broadcast_to(jnp.sum(dn * xh, axis=0, keepdims=True), (128, 768))
    gs_out[...] = gs + jnp.where(lax.broadcasted_iota(jnp.int32, (768, 128), 1) == 17, jnp.transpose(gain), 0.0)
    mixed = lax.dot_general(prev[...], jnp.where(lane < 12, dlog, 0.0), (rows, ((), ())), preferred_element_type=f32,
                            precision=lax.Precision.HIGHEST)
    misc_out[0:16, :] = mixed[0:16]
    misc_out[16:24, :] = jnp.broadcast_to(jnp.sum(prob * live, axis=0, keepdims=True), (8, 128))

    g.finish()
    s.finish()
    each(lambda k: gate_copy(k).wait_send())
    each(lambda k: vs_copy(k).wait_send())
    for c in swaps:
        c.wait_send()
    part_store.wait()
    store_g(3, lambda c: c.wait())


def front_kernel(n_blk, *refs):
    (lengths, tok, cot, routes_t, w_in, router_t, const_t, gains_t, vec_t, wo_in, prev_t, mix_in, cos_hbm, sin_hbm, w_hbm,
     norm_hbm, q_hbm, k_hbm, v_hbm, o_hbm, part_hbm, g_hbm, att, smt, cnt, local_out, res_out, ag_out, gs_out, misc_out, pg_out,
     gain_out, sm, wout, pt, cot_rows, turn, w, w_part, wsem, *scratch) = refs
    w_loads = [pltpu.make_async_copy(w_hbm.at[:, kind], w_part.at[kind], wsem.at[kind]) for kind in range(3)]
    for c in w_loads:
        c.start()
    turn[...] = jnp.zeros_like(turn)
    turn[0, 0:12, 0:24] = router_t[...].astype(f32)
    turn[0, 12:16, 0:24] = const_t[...].astype(f32)
    turn[0, 16:18, 0:24] = gains_t[...].astype(f32)
    turn[0, 18:20, 0:24] = vec_t[...].astype(f32)
    turn[1, 0:2, :] = routes_t[...].astype(f32)
    turn[2, 0:12, :] = prev_t[...]
    turn[3, 0:12, 0:12] = mix_in[...]
    small = jnp.transpose(turn[0])[0:24, 0:64]
    gain_out[...] = small
    routes = jnp.transpose(turn[1])
    prev = jnp.transpose(turn[2])

    def relay_w(kind):
        w_loads[kind].wait()
        t = w_part[kind].astype(f32)
        for e in range(4):
            w[3 * e + kind] = t[:, e, :].astype(bf16)

    cot_gather, finish = forward_kernel(
        n_blk, lengths, tok, cot, routes, w_in, small, wo_in, cos_hbm, sin_hbm, relay_w, norm_hbm, q_hbm, k_hbm, v_hbm, o_hbm,
        att, smt, cnt, sm, wout, pt, cot_rows, *scratch[: len(forward_scratch(n_blk))])
    expert_kernel(
        n_blk, cot_gather, lengths, att, tok, cot, prev, turn.at[3], routes, wout, sm, smt, cnt, pt, w, cot_rows,
        part_hbm, g_hbm, local_out, res_out, ag_out, gs_out, misc_out, pg_out, *scratch[len(forward_scratch(n_blk)) :])
    finish()


def forward_scratch(n_blk):
    V, DMA = pltpu.VMEM, pltpu.SemaphoreType.DMA
    return [
        V((3, 16, 128, 256), bf16), V((12, 16, 384), bf16), V((2 * n_blk, 16, 384), bf16), V((768, 256), f32),
        V((768, 256), bf16), V((2048, 128), f32), V((2048, 128), f32), V((2048, 768), bf16), V((2048, 64), bf16),
        V((2048, 64), bf16), V((2048, 128), bf16), V((2048, 128), f32), V((16, 64, 128), bf16), V((12, 64, 128), bf16),
        V((128, 128), bf16), V((128, 128), bf16), V((128, 768), bf16), V((n_blk, 1, 2, 16, 1152), bf16),
        DMA((3, 16)), DMA((3, 16)), DMA((2 * n_blk,)), DMA((2 * n_blk,)), DMA((16,)), DMA((12,)), DMA((11,)), DMA((3,)), DMA((3,)),
        *gather_sems(1), *gather_sems(2),
    ]


def expert_scratch(n_blk):
    V, DMA = pltpu.VMEM, pltpu.SemaphoreType.DMA
    return [
        V((n_blk, 2, 96, 768), bf16),
        V((n_blk, 2, 96, 128), f32), V((n_blk, 2, 96, 256), bf16), V((n_blk, 2, 96, 128), bf16),
        V((n_blk, 2, 96, 768), bf16), V((n_blk, 2, 96, 768), bf16), V((3, 128, 768), f32),
        V((n_blk, 8, 256), f32), V((n_blk, 8, 256), f32), V((n_blk, 8, 256), f32),
        V((128, 768), bf16), V((128, 768), bf16), V((128, 128), f32), V((128, 128), f32),
        V((128, 768), bf16), V((128, 768), bf16), V((128, 128), f32), V((128, 128), f32),
        DMA((n_blk,)), DMA((n_blk,)), DMA((n_blk,)), DMA((n_blk,)), DMA((4,)), DMA((4,)), DMA((7,)),
        *gather_sems(2), *scatter_scratch(2, 96, 768),
    ]


def front(lengths, tokens, cotangent, routes, w_qkv, w_router, w_const, gains, vec, w_out, prev, mix, w, n_blk):
    cos, sin = rotary_tables(2048)
    vm = pl.BlockSpec(memory_space=pltpu.VMEM)
    hbm = pl.BlockSpec(memory_space=pl.ANY)
    sds = jax.ShapeDtypeStruct
    V = pltpu.VMEM
    return pl.pallas_call(
        functools.partial(front_kernel, n_blk),
        out_shape=(
            sds((2048, 768), bf16), sds((2048, 64), bf16), sds((2048, 64), bf16), sds((2048, 128), bf16),
            sds((2048, 128), f32), sds((n_blk, 2, 96, 768), bf16), sds((128, 3, 4, 768), f32),
            sds((128, 768), bf16), sds((32, 768), f32), sds((8, 128), f32), sds((128, 768), f32), sds((128, 768), f32),
            sds((128, 768), bf16), sds((768, 128), f32), sds((24, 128), f32), sds((2, 128, 256), f32),
            sds((24, 64), f32),
        ),
        in_specs=[pl.BlockSpec(memory_space=pltpu.SMEM)] + [vm] * 11 + [hbm] * 3,
        out_specs=(hbm,) * 7 + (vm,) * 10,
        scratch_shapes=[
            V((768, 128), bf16), V((768, 768), bf16), V((2, 128, 256), bf16), V((n_blk, 2, 96, 768), bf16),
            V((4, 128, 128), f32), V((12, 128, 768), bf16), V((3, 128, 4, 768), bf16), pltpu.SemaphoreType.DMA((3,)),
            *forward_scratch(n_blk), *expert_scratch(n_blk),
        ],
        compiler_params=pltpu.CompilerParams(collective_id=0, has_side_effects=True, vmem_limit_bytes=63 * 2**20),
        cost_estimate=pl.CostEstimate(flops=8 * 10**9, bytes_accessed=3 * 10**7, transcendentals=0),
        name="front",
    )(lengths, tokens, cotangent, routes.T, w_qkv, w_router.T, w_const.T, gains.T, vec.T, w_out, prev.T, mix,
      jnp.asarray(cos), jnp.asarray(sin), w)


def backward_kernel(
    n_blk, lengths, ag, tok, res_grad, smt, att, local_out, pg, g_small, misc, w_own, small, cnt,
    norm_hbm, q_hbm, k_hbm, v_hbm, o_hbm, cos_hbm, sin_hbm, w_hbm, part_hbm,
    out, dtok_out, gq_out, go_out, router_out, const_out, vec_out, gains_out, mix_out, aux_out,
    norm, q, k, v, o, cos, sin, w_all, agbuf, do_in, do, dk, dv, dqkv, obuf, got, dproj, turn, g_f, gbuf, g_in,
    part, gpart, far_out, far_in, half_out, half_in, half_sum, misc_sum, misc_in,
    a_send, a_recv, b_send, b_recv, g_send, g_recv, loc, x_send, x_recv, m_send, m_recv, *rest,
):
    h, b = lax.axis_index("head"), lax.axis_index("blk")
    me = b * 2 + h
    total = 2 * n_blk
    _, _, rank = place(0, h, b)
    base = (b // 8) * 8
    head = head_of(h, b)
    working = (b % 4) != 3
    loads = [
        pltpu.make_async_copy(src, dst, loc.at[i])
        for i, (src, dst) in enumerate([
            (q_hbm, q), (k_hbm, k), (v_hbm, v), (o_hbm, o), (cos_hbm, cos), (sin_hbm, sin), (norm_hbm, norm),
            (w_hbm, w_all), (part_hbm, part)])
    ]
    for c in loads:
        c.start()
    a = ag[...].astype(f32)
    for j in range(12):
        agbuf[j] = jnp.concatenate([a[0:64, 64 * j : 64 * j + 64], a[64:128, 64 * j : 64 * j + 64]], axis=1).astype(bf16)
    greet("all", h, b, n_blk)

    def to_head(j):
        r = home_of(j)
        return pltpu.make_async_remote_copy(
            src_ref=agbuf.at[j], dst_ref=do_in.at[rank], send_sem=a_send.at[j], recv_sem=a_recv.at[rank],
            device_id=(r % 2, base + r // 2), device_id_type=MESH,
        )

    for j in range(12):
        @pl.when(rank != home_of(j))
        def _(j=j):
            to_head(j).start()

    def to_tokens(r):
        return pltpu.make_async_remote_copy(
            src_ref=obuf.at[r], dst_ref=got.at[head], send_sem=b_send.at[r], recv_sem=b_recv.at[head],
            device_id=(r % 2, base + r // 2), device_id_type=MESH,
        )

    def to_owner(kk):
        other = (me + kk) % total
        oh, ob = other % 2, other // 2
        return pltpu.make_async_remote_copy(
            src_ref=gbuf.at[oh * n_blk + ob], dst_ref=g_in.at[me], send_sem=g_send.at[kk], recv_sem=g_recv.at[me],
            device_id=(oh, ob), device_id_type=MESH,
        )

    length = lengths[b // 8]

    rs = RowScatter(part, *rest[0:3], rest[3:9], h, b)
    gs = RowScatter(gpart, *rest[9:12], rest[12:18], h, b)
    g_f2 = lax.dot_general(att[...], res_grad[...].astype(bf16), (((0,), (0,)), ((), ())), preferred_element_type=f32)
    for w in range(total):
        cat = jnp.concatenate([g_f2[24 * w : 24 * w + 24], g_small[24 * w : 24 * w + 24, :]], axis=1)
        gpart[w % n_blk, 0, 16 * (w // n_blk) : 16 * (w // n_blk) + 16, :] = fold(cat)
    for n in gs.order:
        gs.send_core(*n)
    loads[8].wait()
    for n in rs.order:
        rs.send_core(*n)

    misc_sum[0] = misc[...]
    z = b // 4
    partners = [(1 - h, b), (h, b + 1 - 2 * (b % 2)), (h, b + 2 - 4 * ((b // 2) % 2)),
                (h, b + 4 - 8 * (z % 2)), (h, b + 8 - 16 * (z // 2))]

    def pairwise(t):
        return pltpu.make_async_remote_copy(
            src_ref=misc_sum.at[t], dst_ref=misc_in.at[t], send_sem=m_send.at[t], recv_sem=m_recv.at[t],
            device_id=partners[t], device_id_type=MESH)

    def pairwise_done(t):
        pairwise(t).wait_recv()
        misc_sum[t + 1] = misc_sum[t] + misc_in[t]
        if t < 4:
            pairwise(t + 1).start()

    pairwise(0).start()
    def step(scatter, stage, n):
        k, p = scatter.order[n]
        return lambda: getattr(scatter, stage)(k, p)

    def ry(n):
        return step(rs, "send_y", n)

    def rz(n):
        return step(rs, "send_z", n)

    def gy(n):
        return step(gs, "send_y", n)

    def gz(n):
        return step(gs, "send_z", n)

    def pd(t):
        return lambda: pairwise_done(t)

    between = {
        8: [gy(0), ry(0)], 7: [pd(0), gy(1)], 6: [ry(1)], 5: [pd(1), gy(2)], 4: [ry(2), gz(0)], 3: [pd(2), gy(3), rz(0)],
        2: [ry(3), gz(1)], 1: [pd(3), rz(1)], 0: [gz(2), pd(4)],
    }

    @pl.when(jnp.logical_not(working))
    def _():
        do_in[...] = jnp.zeros_like(do_in)

    @pl.when(working)
    def _():
        do_in[rank] = agbuf[head]

    for c in loads[:6]:
        c.wait()
    if True:
        def unpack(r, carry):
            @pl.when((r != rank) & working)
            def _():
                pltpu.make_async_remote_copy(
                    src_ref=agbuf.at[0], dst_ref=do_in.at[r], send_sem=a_send.at[0], recv_sem=a_recv.at[r],
                    device_id=(h, b), device_id_type=MESH,
                ).wait_recv()

            t = do_in[r].astype(f32)
            rows = pl.multiple_of(r * 128, 128)
            do[pl.ds(rows, 64), :] = t[:, 0:64].astype(bf16)
            do[pl.ds(rows + 64, 64), :] = t[:, 64:128].astype(bf16)
            return carry

        lax.fori_loop(0, 16, unpack, 0)
        for act in between[8]:
            act()
        for i in range(7, -1, -1):
            width = 256 * (i + 1)
            lo = 256 * i
            qi, doi = q[lo:width, :], do[lo:width, :]
            s = lax.dot_general(qi, k[0:width, :], (((1,), (1,)), ((), ())), preferred_element_type=f32)
            key = lax.broadcasted_iota(jnp.int32, (1, width), 1)
            ov = o[lo:width, :]
            lse = ov[:, 64:65]
            s = (s - lse) + jnp.where(key < length, 0.0, NEG)
            rowi = lax.broadcasted_iota(jnp.int32, (256, 256), 0)
            coli = lax.broadcasted_iota(jnp.int32, (256, 256), 1)
            last = jnp.where(coli <= rowi, s[:, lo:], NEG)
            s = last if i == 0 else jnp.concatenate([s[:, :lo], last], axis=1)
            p = jnp.exp(s)
            dp = lax.dot_general(doi, v[0:width, 0:64], (((1,), (1,)), ((), ())), preferred_element_type=f32)
            inner = jnp.sum(doi.astype(f32) * ov[:, 0:64], axis=1, keepdims=True)
            ds = (p * (dp - inner)).astype(bf16)
            p = p.astype(bf16)
            dq = jnp.dot(ds, k[0:width, :], preferred_element_type=f32) * 0.125
            dki = lax.dot_general(ds, qi, (((0,), (0,)), ((), ())), preferred_element_type=f32)
            dvi = lax.dot_general(p, doi, (((0,), (0,)), ((), ())), preferred_element_type=f32)
            if i == 7:
                dk[...] = dki
                dv[...] = dvi
            else:
                dk[0:width, :] += dki
                dv[0:width, :] += dvi
            both = jnp.concatenate([dq, dk[lo:width, :]], axis=1)
            both = turned(both, cos[lo:width, :], -sin[lo:width, :]).astype(bf16)
            dvl = dv[lo:width, :]
            dqkv[lo:width, 0:128] = both
            dqkv[lo:width, 128:256] = jnp.concatenate([dvl, jnp.zeros_like(dvl)], axis=1).astype(bf16)
            for half in range(2):
                r = 2 * i + half
                obuf[r, 0:128, :] = both[128 * half : 128 * half + 128]
                obuf[r, 128:192, :] = jnp.concatenate(
                    [dvl[128 * half : 128 * half + 64], dvl[128 * half + 64 : 128 * half + 128]], axis=1).astype(bf16)

                @pl.when((r != rank) & working)
                def _(r=r):
                    to_tokens(r).start()
            for act in between[i]:
                act()

        @pl.when(working)
        def _():
            got[head] = obuf[rank]

        loads[6].wait()
        for c in range(3):
            g_f[256 * c : 256 * c + 256, :] = lax.dot_general(
                norm[:, 256 * c : 256 * c + 256], dqkv[...], (((0,), (0,)), ((), ())), preferred_element_type=f32)
        for w in range(total):
            gbuf[w] = fold(g_f[24 * w : 24 * w + 24, :])

        def send_g(kk, carry):
            to_owner(kk).start()
            return carry

        @pl.when(working)
        def _():
            lax.fori_loop(1, total, send_g, 0)
            g_in[me] = gbuf[h * n_blk + b]

    def swap_half():
        half_sum[...] = gs.total(0)
        half_out[...] = half_sum[pl.ds(pl.multiple_of(16 * (1 - h), 16), 16), :].astype(bf16)
        swaps[0].start()

    swaps = [
        pltpu.make_async_remote_copy(
            src_ref=src, dst_ref=dst, send_sem=x_send.at[n], recv_sem=x_recv.at[n],
            device_id=(1 - h, b), device_id_type=MESH)
        for n, (src, dst) in enumerate([
            (half_out, half_in), (far_out, far_in)])
    ]
    for act in (ry(4), ry(5), gz(3), ry(6), ry(7)):
        act()
    swap_half()
    rz(2)()
    rz(3)()

    for j in range(12):
        @pl.when(rank != home_of(j))
        def _(j=j):
            pltpu.make_async_remote_copy(
                src_ref=obuf.at[0], dst_ref=got.at[j], send_sem=b_send.at[0], recv_sem=b_recv.at[j],
                device_id=(h, b), device_id_type=MESH,
            ).wait_recv()
    for j in range(0, 12, 2):
        one, two = got[j].astype(f32), got[j + 1].astype(f32)
        lo = 64 * j
        for part_i, at in enumerate((0, 64)):
            dproj[:, 768 * part_i + lo : 768 * part_i + lo + 128] = jnp.concatenate(
                [one[0:128, at : at + 64], two[0:128, at : at + 64]], axis=1).astype(bf16)
        dproj[0:64, 1536 + lo : 1664 + lo] = jnp.concatenate([one[128:192, 0:64], two[128:192, 0:64]], axis=1).astype(bf16)
        dproj[64:128, 1536 + lo : 1664 + lo] = jnp.concatenate([one[128:192, 64:128], two[128:192, 64:128]], axis=1).astype(bf16)
    loads[7].wait()
    dn = lax.dot_general(dproj[...], w_all[...], (((1,), (1,)), ((), ())), preferred_element_type=f32)
    x = tok[...].astype(f32)
    scale = lax.rsqrt(jnp.sum(x * x, axis=1, keepdims=True) * (1.0 / 768) + 1e-6)
    xh = x * scale
    t = dn * smt[16:17, :]
    dx = scale * (t - xh * (jnp.sum(t * xh, axis=1, keepdims=True) * (1.0 / 768)))
    dtok_out[...] = (res_grad[...] + dx).astype(bf16)

    for n in range(4, 8):
        rz(n)()
    rows = jnp.concatenate([rs.total(0), rs.total(1)], axis=0).astype(bf16)
    far_out[...] = exact_dot(pg[1, :, 0:192], rows, ((1,), (0,))).astype(bf16)
    swaps[1].start()
    own = exact_dot(pg[0, :, 0:192], rows, ((1,), (0,))) + local_out[...]

    for src in range(total):
        if (src // 2) % 4 == 3:
            continue

        @pl.when(me != src)
        def _(src=src):
            pltpu.make_async_remote_copy(
                src_ref=gbuf.at[0], dst_ref=g_in.at[src], send_sem=g_send.at[0], recv_sem=g_recv.at[src],
                device_id=(h, b), device_id_type=MESH,
            ).wait_recv()
    for j in range(0, 12, 2):
        pair = []
        for jj in (j, j + 1):
            t = sum(g_in[16 * s + home_of(jj)].astype(f32) for s in range(total // 16))
            pair.append(jnp.concatenate(
                [t[:, 0:256], jnp.concatenate([t[0:8, 256:384], t[8:16, 256:384]], axis=1)], axis=0))
        one, two = pair
        for part in range(3):
            gq_out[:, 768 * part + 64 * j : 768 * part + 64 * j + 128] = jnp.concatenate(
                [one[:, 64 * part : 64 * part + 64], two[:, 64 * part : 64 * part + 64]], axis=1)

    lane = lax.broadcasted_iota(jnp.int32, (24, 128), 1)
    gain_grad = jnp.sum(gq_out[...] * w_own[...].astype(f32), axis=1, keepdims=True) / small[:, 16:17]
    swaps[0].wait_recv()
    t = half_sum[pl.ds(pl.multiple_of(16 * h, 16), 16), :] + half_in[...].astype(f32)
    t = jnp.concatenate([t[:, 0:896], jnp.concatenate([t[0:8, 896:1344], t[8:16, 896:1344]], axis=1)], axis=0)
    go_out[...] = t[:, 0:768]
    turn[...] = jnp.zeros_like(turn)
    turn[0:24, :] = jnp.where(lane == 16, gain_grad, t[:, 768:896])
    t = jnp.transpose(turn[...])
    router_out[...] = t[0:12, 0:24]
    const_out[...] = t[12:16, 0:24]
    gains_out[...] = t[16:18, 0:24]
    vec_out[...] = t[18:20, 0:24]
    t = misc_sum[5]
    mix_out[...] = t[0:12, 0:12]
    live_total = (lengths[0] + lengths[1]).astype(f32)
    aux = cnt[0:1, :] / (2.0 * live_total) * (t[16:17, :] / live_total)
    aux_out[...] = jnp.broadcast_to(12.0 * jnp.sum(aux, axis=1, keepdims=True), (8, 128))
    swaps[1].wait_recv()
    out[...] = (own + far_in[...].astype(f32)).astype(bf16)

    rs.finish()
    gs.finish()
    for t in range(5):
        pairwise(t).wait_send()
    for c in swaps:
        c.wait_send()
    for j in range(12):
        @pl.when(rank != home_of(j))
        def _(j=j):
            to_head(j).wait_send()

    @pl.when(working)
    def _():
        for r in range(16):
            @pl.when(r != rank)
            def _(r=r):
                to_tokens(r).wait_send()

        def sent(kk, carry):
            to_owner(kk).wait_send()
            return carry

        lax.fori_loop(1, total, sent, 0)


def attend_back(
    lengths, ag, tok, res_grad, smt, att, local_out, pg, g_small, misc, w_own, small, cnt, norm, q, k, v, o, w_all, parts,
    n_blk,
):
    cos, sin = rotary_tables(2048)
    vm = pl.BlockSpec(memory_space=pltpu.VMEM)
    hbm = pl.BlockSpec(memory_space=pl.ANY)
    sds = jax.ShapeDtypeStruct
    DMA = pltpu.SemaphoreType.DMA
    V = pltpu.VMEM
    total = 2 * n_blk
    return pl.pallas_call(
        functools.partial(backward_kernel, n_blk),
        out_shape=(
            sds((128, 768), bf16), sds((128, 768), bf16), sds((24, 2304), f32), sds((24, 768), f32), sds((12, 24), f32),
            sds((4, 24), f32), sds((2, 24), f32), sds((2, 24), f32), sds((12, 12), f32), sds((8, 128), f32),
        ),
        in_specs=[pl.BlockSpec(memory_space=pltpu.SMEM)] + [vm] * 12 + [hbm] * 9,
        out_specs=(vm,) * 10,
        scratch_shapes=[
            V((2048, 768), bf16), V((2048, 64), bf16), V((2048, 64), bf16), V((2048, 128), bf16), V((2048, 128), f32),
            V((2048, 128), f32), V((2048, 128), f32), V((768, 2304), bf16),
            V((12, 64, 128), bf16), V((16, 64, 128), bf16), V((2048, 64), bf16), V((2048, 64), f32), V((2048, 64), f32),
            V((2048, 256), bf16), V((16, 192, 128), bf16), V((12, 192, 128), bf16), V((128, 2304), bf16), V((128, 128), f32),
            V((768, 256), f32), V((total, 16, 384), bf16), V((total, 16, 384), bf16),
            V((n_blk, 2, 96, 768), bf16), V((n_blk, 1, 32, 1344), bf16), V((128, 768), bf16), V((128, 768), bf16),
            V((16, 1344), bf16), V((16, 1344), bf16), V((32, 1344), f32), V((6, 24, 128), f32), V((5, 24, 128), f32),
            DMA((12,)), DMA((16,)), DMA((16,)), DMA((12,)), DMA((total,)), DMA((total,)), DMA((9,)), DMA((2,)), DMA((2,)),
            DMA((5,)), DMA((5,)), *scatter_scratch(2, 96, 768), *scatter_scratch(1, 32, 1344),
        ],
        compiler_params=pltpu.CompilerParams(collective_id=1, has_side_effects=True, vmem_limit_bytes=60 * 2**20),
        cost_estimate=pl.CostEstimate(flops=2 * 10**9, bytes_accessed=2 * 10**7, transcendentals=0),
        name="attend_back",
    )(lengths, ag, tok, res_grad, smt, att, local_out, pg, g_small, misc, w_own, small, cnt, norm, q, k, v, o,
      jnp.asarray(cos), jnp.asarray(sin), w_all, parts)


CAP = 24


eps = 1e-06
aux_weight = 0.01
highest = lax.Precision.HIGHEST
masked_score = -1e30


def shifted(block, axis, distance):
    devices = range(lax.axis_size(axis))
    route = [(i - distance, i) for i in devices if i - distance in devices]
    return lax.ppermute(block, axis, route)


def for_sending(x):
    return jax.tree.map(lambda a: a.astype(jnp.bfloat16) if a.dtype == jnp.float32 else a, x)


def rms_norm(values, gain_vector):
    return values * lax.rsqrt(jnp.mean(values * values, axis=-1, keepdims=True) + eps) * gain_vector


def rotary(values, positions, turn_sign):
    half_width = values.shape[-1] // 2
    frequency = jnp.exp(
        jnp.arange(half_width, dtype=jnp.float32) * (-2.0 * math.log(10000.0) / values.shape[-1])
    )
    angles = positions.astype(jnp.float32)[:, None] * frequency[None, :]
    cosine = jnp.cos(angles)[:, None, :]
    sine_part = turn_sign * jnp.sin(angles)[:, None, :]
    first_half = values[..., :half_width]
    second_half = values[..., half_width:]
    return jnp.concatenate(
        [
            first_half * cosine - second_half * sine_part,
            second_half * cosine + first_half * sine_part,
        ],
        axis=-1,
    )


def slot_lengths(slot_ids, lengths):
    slot_table = jnp.arange(lengths.shape[0], dtype=jnp.int32)
    return jnp.sum(jnp.where(slot_ids[:, None] == slot_table[None, :], lengths[None, :], 0), axis=1)


def allowed_mask(query_ids, key_ids, slot_size, lengths):
    query_slot = query_ids // slot_size
    key_slot = key_ids // slot_size
    query_pos = query_ids - query_slot * slot_size
    key_pos = key_ids - key_slot * slot_size
    key_live = (key_pos < slot_lengths(key_slot, lengths)) & (key_ids >= 0)
    return (
        (query_slot[:, None] == key_slot[None, :])
        & (key_pos[None, :] <= query_pos[:, None])
        & key_live[None, :]
    )


def masked_scores(query_block, key_head, query_ids, key_ids, slot_size, lengths):
    scores = lax.dot_general(
        query_block, key_head, (((1,), (1,)), ((), ())), preferred_element_type=jnp.float32
    ) * HD ** (-0.5)
    return jnp.where(allowed_mask(query_ids, key_ids, slot_size, lengths), scores, masked_score)


def attend_forward(queries, key_all, value_all, query_ids, key_ids, slot_size, lengths):
    head_total = queries.shape[1] // HD

    def one_head(head_index):
        query_head = lax.dynamic_slice_in_dim(queries, head_index * HD, HD, 1)
        key_head = lax.dynamic_slice_in_dim(key_all, head_index * HD, HD, 1)
        value_head = lax.dynamic_slice_in_dim(value_all, head_index * HD, HD, 1)
        scores = masked_scores(query_head, key_head, query_ids, key_ids, slot_size, lengths)
        row_max = jnp.max(scores, axis=1, keepdims=True)
        weights = jnp.exp(scores - row_max)
        row_total = jnp.sum(weights, axis=1, keepdims=True)
        probs_low = (weights / row_total).astype(jnp.bfloat16)
        head_outputs = [jnp.dot(probs_low, value_head, preferred_element_type=jnp.float32)]
        log_parts = [row_max[:, 0] + jnp.log(row_total[:, 0])]
        return (jnp.concatenate(head_outputs, axis=0), jnp.concatenate(log_parts, axis=0))

    head_outputs, log_sums = lax.map(one_head, jnp.arange(head_total, dtype=jnp.int32))
    return (head_outputs.transpose(1, 0, 2).reshape(queries.shape[0], queries.shape[1]), log_sums)


def attend_backward(
    queries, key_all, value_all, out_grads, log_sums, query_ids, key_ids, slot_size, lengths
):
    head_total = queries.shape[1] // HD
    block_rows = min(512, queries.shape[0])

    def one_head(head_index):
        query_head = lax.dynamic_slice_in_dim(queries, head_index * HD, HD, 1)
        key_head = lax.dynamic_slice_in_dim(key_all, head_index * HD, HD, 1)
        value_head = lax.dynamic_slice_in_dim(value_all, head_index * HD, HD, 1)
        grad_head = lax.dynamic_slice_in_dim(out_grads, head_index * HD, HD, 1)
        log_head = lax.dynamic_index_in_dim(log_sums, head_index, 0, keepdims=False)
        key_grad = jnp.zeros(key_head.shape, jnp.float32)
        value_grad = jnp.zeros(value_head.shape, jnp.float32)
        grad_block = grad_head[0:block_rows]
        scores = masked_scores(query_head, key_head, query_ids, key_ids, slot_size, lengths)
        probs = jnp.exp(scores - log_head[0:block_rows][:, None])
        probs_low = probs.astype(jnp.bfloat16)
        prob_grads = lax.dot_general(
            grad_block, value_head, (((1,), (1,)), ((), ())), preferred_element_type=jnp.float32
        )
        row_inner = jnp.sum(probs * prob_grads, axis=1, keepdims=True)
        score_grads = (probs * (prob_grads - row_inner)).astype(jnp.bfloat16)
        query_parts = [
            jnp.dot(score_grads, key_head, preferred_element_type=jnp.float32) * HD ** (-0.5)
        ]
        key_grad = key_grad + lax.dot_general(
            score_grads, query_head, (((0,), (0,)), ((), ())), preferred_element_type=jnp.float32
        ) * HD ** (-0.5)
        value_grad = value_grad + lax.dot_general(
            probs_low, grad_block, (((0,), (0,)), ((), ())), preferred_element_type=jnp.float32
        )
        return (jnp.concatenate(query_parts, axis=0), key_grad, value_grad)

    query_grad, key_grad, value_grad = lax.map(one_head, jnp.arange(head_total, dtype=jnp.int32))
    return (
        query_grad.transpose(1, 0, 2).reshape(queries.shape[0], queries.shape[1]),
        key_grad.transpose(1, 0, 2).reshape(key_all.shape[0], key_all.shape[1]),
        value_grad.transpose(1, 0, 2).reshape(value_all.shape[0], value_all.shape[1]),
    )


def fetch_prev(key_heads, value_heads, span_count):
    key_parts = [key_heads]
    value_parts = [value_heads]
    for offset in range(1, span_count):
        arrived = shifted((key_heads, value_heads), "blk", offset)
        key_parts.append(arrived[0])
        value_parts.append(arrived[1])
    return (jnp.concatenate(key_parts, axis=0), jnp.concatenate(value_parts, axis=0))


def router_probs(normed, router_w, mixing, prev_scores):
    logits = jnp.dot(normed, router_w, precision=highest) + jnp.dot(
        prev_scores, mixing, precision=highest
    )
    return jax.nn.softmax(logits, axis=-1)


def branch_sum(router_prob, normed, const_w, vector_w, outputs_pair, choose, live_rows, real_count):
    gate_values = jnp.sum(choose * router_prob[:, None, :], axis=-1)
    expert_share = jnp.sum(choose * gate_values[:, :, None], axis=1) * live_rows[:, None]
    routed = jnp.sum(gate_values[:, :, None] * outputs_pair, axis=1)
    routed = routed + expert_share[:, real_count + 1 : real_count + 2] * normed
    const_count = vector_w.shape[1]
    const_mix = jax.nn.softmax(
        jnp.dot(normed, const_w, precision=highest).reshape(normed.shape[0], const_count, 2),
        axis=-1,
    )
    for const_index in range(const_count):
        const_out = (
            const_mix[:, const_index, 0:1] * normed
            + const_mix[:, const_index, 1:2] * vector_w[:, const_index][None, :]
        )
        routed = (
            routed
            + expert_share[:, real_count + 2 + const_index : real_count + 3 + const_index]
            * const_out
        )
    return routed


def on_device(
    tokens,
    cotangent,
    prev_logits,
    routes,
    lengths,
    w_qkv,
    w_out,
    w_router,
    w_const,
    const_vec,
    norm_gains,
    gate_mix,
    expert_weights,
):
    tok_dev = tokens.shape[0]
    model_width = tokens.shape[1]
    head_count = lax.axis_size("head")
    blk_count = lax.axis_size("blk")
    span_count = max(8, min(blk_count // 4, 8192 // (head_count * tok_dev)) * min(1, tok_dev // 64))
    head_index = lax.axis_index("head")
    blk_index = lax.axis_index("blk")
    slot_size = span_count * head_count * tok_dev
    tok_blk = head_count * tok_dev
    qkv_w, out_w, router_w, const_w, vector_w, gain_pair = (
        lax.all_gather(w_qkv, ("head", "blk"), axis=0, tiled=True),
        lax.all_gather(w_out, ("head", "blk"), axis=0, tiled=True),
        lax.all_gather(w_router, ("head", "blk"), axis=0, tiled=True),
        lax.all_gather(w_const, ("head", "blk"), axis=0, tiled=True),
        lax.all_gather(const_vec, ("head", "blk"), axis=0, tiled=True),
        lax.all_gather(norm_gains, ("head", "blk"), axis=0, tiled=True),
    )
    gain_pair = gain_pair.astype(jnp.float32)
    row_ids = (blk_index * head_count + head_index) * tok_dev + jnp.arange(tok_dev, dtype=jnp.int32)
    slot_ids = row_ids // slot_size
    positions = row_ids - slot_ids * slot_size
    live_rows = (positions < slot_lengths(slot_ids, lengths)).astype(jnp.float32)
    inputs = tokens.astype(jnp.float32)
    normed_one, norm_one_back = jax.vjp(rms_norm, inputs, gain_pair[:, 0])
    normed_one_low = normed_one.astype(jnp.bfloat16)
    projected = jnp.dot(normed_one_low, qkv_w, preferred_element_type=jnp.float32).reshape(
        tok_dev, 3, HEADS, HD
    )
    query_send = (
        rotary(projected[:, 0], positions, 1.0).astype(jnp.bfloat16).reshape(tok_dev, model_width)
    )
    key_send = (
        rotary(projected[:, 1], positions, 1.0).astype(jnp.bfloat16).reshape(tok_dev, model_width)
    )
    value_send = projected[:, 2].astype(jnp.bfloat16).reshape(tok_dev, model_width)
    query_heads, key_heads, value_heads = (
        lax.all_to_all(query_send, "head", split_axis=1, concat_axis=0, tiled=True),
        lax.all_to_all(key_send, "head", split_axis=1, concat_axis=0, tiled=True),
        lax.all_to_all(value_send, "head", split_axis=1, concat_axis=0, tiled=True),
    )
    blk_rows = blk_index * tok_blk + jnp.arange(tok_blk, dtype=jnp.int32)
    blk_pos = blk_rows - blk_rows // slot_size * slot_size
    key_ids = jnp.concatenate([blk_rows - offset * tok_blk for offset in range(span_count)], axis=0)
    key_all, value_all = fetch_prev(key_heads, value_heads, span_count)
    attended, log_sums = attend_forward(
        query_heads, key_all, value_all, blk_rows, key_ids, slot_size, lengths
    )
    attended_tok = lax.all_to_all(
        attended.astype(jnp.bfloat16), "head", split_axis=0, concat_axis=1, tiled=True
    )
    residual = inputs + jnp.dot(attended_tok, out_w, preferred_element_type=jnp.float32)
    normed_two, norm_two_back = jax.vjp(rms_norm, residual, gain_pair[:, 1])
    normed_two_low = normed_two.astype(jnp.bfloat16)
    normed_two_f = normed_two_low.astype(jnp.float32)
    router_prob, router_back = jax.vjp(
        partial(router_probs, prev_scores=prev_logits),
        normed_two_f,
        router_w.astype(jnp.float32),
        gate_mix,
    )
    expert_count = router_w.shape[1]
    real_count = expert_weights.shape[1] * head_count
    choose = (
        routes[:, :, None] == jnp.arange(expert_count, dtype=jnp.int32)[None, None, :]
    ).astype(jnp.float32)
    count_local = jnp.sum(jnp.sum(choose, axis=1) * live_rows[:, None], axis=0)
    prob_local = jnp.sum(router_prob * live_rows[:, None], axis=0)
    count_all, prob_all = lax.psum((count_local, prob_local), ("head", "blk"))
    live_total = jnp.sum(lengths).astype(jnp.float32)
    fraction = count_all / (2.0 * live_total)
    aux_loss = expert_count * jnp.sum(fraction * (prob_all / live_total))
    gate_values = jnp.sum(choose * router_prob[:, None, :], axis=-1)
    out_grad = live_rows[:, None] * cotangent.astype(jnp.float32)
    assigned = routes.reshape(-1)
    live_pairs = jnp.repeat(live_rows, 2)
    is_real = (assigned < real_count) & (live_pairs > 0)
    onehot = (
        (assigned[:, None] == jnp.arange(real_count, dtype=jnp.int32)[None, :]) & is_real[:, None]
    ).astype(jnp.int32)
    slot_rank = jnp.sum((jnp.cumsum(onehot, axis=0) - onehot) * onehot, axis=1)
    target = jnp.where(is_real, assigned * CAP + slot_rank, real_count * CAP)
    source = (
        jnp.full((real_count * CAP + 1,), 2 * tok_dev, jnp.int32)
        .at[target]
        .set(jnp.arange(2 * tok_dev, dtype=jnp.int32))[: real_count * CAP]
    )
    zero_row = jnp.zeros((1, model_width), jnp.bfloat16)
    send_rows = jnp.concatenate([normed_two_low, zero_row], axis=0)[source // 2].reshape(
        real_count, CAP, model_width
    )
    pair_grads = (gate_values.reshape(-1, 1) * jnp.repeat(out_grad, 2, axis=0)).astype(jnp.bfloat16)
    send_grads = jnp.concatenate([pair_grads, zero_row], axis=0)[source].reshape(
        real_count, CAP, model_width
    )
    expert_in, expert_cot = (
        lax.all_to_all(send_rows, "head", split_axis=0, concat_axis=1, tiled=True),
        lax.all_to_all(send_grads, "head", split_axis=0, concat_axis=1, tiled=True),
    )
    weight_piece = lax.all_gather(expert_weights, "blk", axis=0, tiled=True)
    gate_w = weight_piece[:, :, 0, :]
    up_w = weight_piece[:, :, 1, :]
    down_w = weight_piece[:, :, 2, :]
    gate_part = jnp.einsum("esd,ned->esn", expert_in, gate_w, preferred_element_type=jnp.float32)
    up_part = jnp.einsum("esd,ned->esn", expert_in, up_w, preferred_element_type=jnp.float32)
    sigmoid_part = jax.nn.sigmoid(gate_part)
    silu_part = gate_part * sigmoid_part
    hidden = (silu_part * up_part).astype(jnp.bfloat16)
    out_sum = jnp.einsum("esn,ned->esd", hidden, down_w, preferred_element_type=jnp.float32)
    hidden_grad = jnp.einsum("esd,ned->esn", expert_cot, down_w, preferred_element_type=jnp.float32)
    gate_grad = (
        hidden_grad * up_part * (sigmoid_part * (1.0 + gate_part * (1.0 - sigmoid_part)))
    ).astype(jnp.bfloat16)
    up_grad = (hidden_grad * silu_part).astype(jnp.bfloat16)
    in_grad = jnp.einsum("esn,ned->esd", gate_grad, gate_w, preferred_element_type=jnp.float32)
    in_grad = in_grad + jnp.einsum(
        "esn,ned->esd", up_grad, up_w, preferred_element_type=jnp.float32
    )
    hidden_all = hidden
    gate_all = gate_grad
    up_all = up_grad
    out_sum, in_grad, hidden_all, gate_all, up_all = (
        out_sum,
        in_grad,
        hidden_all,
        gate_all,
        up_all,
    )
    hidden_own, gate_own, up_own = (
        lax.all_to_all(hidden_all, "blk", split_axis=2, concat_axis=1, tiled=True),
        lax.all_to_all(gate_all, "blk", split_axis=2, concat_axis=1, tiled=True),
        lax.all_to_all(up_all, "blk", split_axis=2, concat_axis=1, tiled=True),
    )
    rows_in = lax.all_gather(expert_in, "blk", axis=1, tiled=True)
    rows_cot = lax.all_gather(expert_cot, "blk", axis=1, tiled=True)
    gate_w_grad = jnp.einsum("esn,esd->ned", gate_own, rows_in, preferred_element_type=jnp.float32)
    up_w_grad = jnp.einsum("esn,esd->ned", up_own, rows_in, preferred_element_type=jnp.float32)
    down_w_grad = jnp.einsum(
        "esn,esd->ned", hidden_own, rows_cot, preferred_element_type=jnp.float32
    )
    expert_grads = jnp.stack([gate_w_grad, up_w_grad, down_w_grad], axis=2)
    returned, returned_grad = (
        lax.all_to_all(
            out_sum.astype(jnp.bfloat16), "head", split_axis=1, concat_axis=0, tiled=True
        ),
        lax.all_to_all(
            in_grad.astype(jnp.bfloat16), "head", split_axis=1, concat_axis=0, tiled=True
        ),
    )
    outputs_pair = (
        jnp.concatenate([returned.reshape(-1, model_width), zero_row], axis=0)[target]
        .astype(jnp.float32)
        .reshape(tok_dev, 2, model_width)
    )
    input_pair = (
        jnp.concatenate([returned_grad.reshape(-1, model_width), zero_row], axis=0)[target]
        .astype(jnp.float32)
        .reshape(tok_dev, 2, model_width)
    )
    expert_input_grad = input_pair[:, 0] + input_pair[:, 1]
    branch, branch_back = jax.vjp(
        partial(branch_sum, choose=choose, live_rows=live_rows, real_count=real_count),
        router_prob,
        normed_two_f,
        const_w.astype(jnp.float32),
        vector_w.astype(jnp.float32),
        outputs_pair,
    )
    output = ((residual + branch) * live_rows[:, None]).astype(jnp.bfloat16)
    prob_grad, normed_grad_branch, const_grad, vector_grad, unused_grad = branch_back(out_grad)
    aux_grad = aux_weight * expert_count / live_total * fraction[None, :] * live_rows[:, None]
    normed_grad_router, router_grad, mixing_grad = router_back(prob_grad + aux_grad)
    normed_grad = normed_grad_router + normed_grad_branch + expert_input_grad
    residual_grad_norm, gain_two_grad = norm_two_back(normed_grad)
    residual_grad = out_grad + residual_grad_norm
    out_w_grad = jnp.dot(attended_tok.astype(jnp.float32).T, residual_grad, precision=highest)
    attended_grad = jnp.dot(residual_grad, out_w.astype(jnp.float32).T, precision=highest).astype(
        jnp.bfloat16
    )
    attended_grad_heads = lax.all_to_all(
        attended_grad, "head", split_axis=1, concat_axis=0, tiled=True
    )
    key_again, value_again = fetch_prev(key_heads, value_heads, span_count)
    query_grad, key_grad, value_grad = attend_backward(
        query_heads,
        key_again,
        value_again,
        attended_grad_heads,
        log_sums,
        blk_rows,
        key_ids,
        slot_size,
        lengths,
    )
    own_key = key_grad[:tok_blk]
    own_value = value_grad[:tok_blk]
    for offset in range(1, span_count):
        back_key, back_value = shifted(
            (
                for_sending(key_grad[offset * tok_blk : (offset + 1) * tok_blk]),
                for_sending(value_grad[offset * tok_blk : (offset + 1) * tok_blk]),
            ),
            "blk",
            -offset,
        )
        own_key = own_key + back_key
        own_value = own_value + back_value
    local_heads = query_heads.shape[1] // HD
    query_back = (
        rotary(query_grad.reshape(tok_blk, local_heads, HD), blk_pos, -1.0)
        .astype(jnp.bfloat16)
        .reshape(tok_blk, local_heads * HD)
    )
    key_back = (
        rotary(own_key.reshape(tok_blk, local_heads, HD), blk_pos, -1.0)
        .astype(jnp.bfloat16)
        .reshape(tok_blk, local_heads * HD)
    )
    value_back = own_value.astype(jnp.bfloat16)
    query_tok, key_tok, value_tok = (
        lax.all_to_all(query_back, "head", split_axis=0, concat_axis=1, tiled=True),
        lax.all_to_all(key_back, "head", split_axis=0, concat_axis=1, tiled=True),
        lax.all_to_all(value_back, "head", split_axis=0, concat_axis=1, tiled=True),
    )
    projected_grad = jnp.concatenate([query_tok, key_tok, value_tok], axis=1)
    qkv_grad = jnp.dot(normed_one_low.T, projected_grad, preferred_element_type=jnp.float32)
    normed_one_grad = jnp.dot(projected_grad, qkv_w.T, preferred_element_type=jnp.float32)
    inputs_grad_norm, gain_one_grad = norm_one_back(normed_one_grad)
    token_grad = (residual_grad + inputs_grad_norm).astype(jnp.bfloat16)
    weight_grads = (
        lax.psum_scatter(qkv_grad, ("head", "blk"), scatter_dimension=0, tiled=True),
        lax.psum_scatter(out_w_grad, ("head", "blk"), scatter_dimension=0, tiled=True),
        lax.psum_scatter(router_grad, ("head", "blk"), scatter_dimension=0, tiled=True),
        lax.psum_scatter(const_grad, ("head", "blk"), scatter_dimension=0, tiled=True),
        lax.psum_scatter(vector_grad, ("head", "blk"), scatter_dimension=0, tiled=True),
        lax.psum_scatter(
            jnp.stack([gain_one_grad, gain_two_grad], axis=1),
            ("head", "blk"),
            scatter_dimension=0,
            tiled=True,
        ),
    )
    mixing_total = lax.psum(mixing_grad, ("head", "blk"))
    return (
        output,
        aux_loss,
        token_grad,
        weight_grads[0],
        weight_grads[1],
        weight_grads[2],
        weight_grads[3],
        weight_grads[4],
        weight_grads[5],
        mixing_total,
        expert_grads,
    )


def settle_kernel(n, *refs):
    sources, results, (sems, *rooms) = refs[:n], refs[n : 2 * n], refs[2 * n :]
    ins, outs = [], []
    for i in range(n):
        parts = [(sources[i], rooms[i], results[i])]
        if i == n - 1:
            parts = [tuple(r.at[pl.ds(32 * c, 32)] for r in parts[0]) for c in range(4)]
        for src, room, dst in parts:
            ins.append(pltpu.make_async_copy(src, room, sems.at[0, len(ins)]))
            outs.append(pltpu.make_async_copy(room, dst, sems.at[1, len(outs)]))
    for c in ins[::-1]:
        c.start()
    for c, d in zip(ins[::-1], outs[::-1]):
        c.wait()
        d.start()
    for d in outs:
        d.wait()


def settle(*arrays):
    hbm = pl.BlockSpec(memory_space=pl.ANY)
    n = len(arrays)
    return pl.pallas_call(
        functools.partial(settle_kernel, n),
        out_shape=tuple(jax.ShapeDtypeStruct(a.shape, a.dtype) for a in arrays),
        in_specs=[hbm] * n,
        out_specs=(hbm,) * n,
        scratch_shapes=[pltpu.SemaphoreType.DMA((2, n + 3))] + [pltpu.VMEM(a.shape, a.dtype) for a in arrays],
        compiler_params=pltpu.CompilerParams(vmem_limit_bytes=63 * 2**20),
        name="settle",
    )(*arrays)


def on_device_small(
    tokens, cotangent, prev_logits, routes, lengths, w_qkv, w_out, w_router, w_const, const_vec, norm_gains, gate_mix,
    expert_weights,
):
    n_blk = lax.axis_size("blk")
    w_all = lax.all_gather(w_qkv, ("head", "blk"), axis=0, tiled=True)
    norm, q, k, v, o, parts, g_exp, att, smt, cnt, local_out, res_grad, att_grad, g_small, misc, pg, small = front(
        lengths, tokens, cotangent, routes, w_qkv, w_router, w_const, norm_gains, const_vec, w_out, prev_logits, gate_mix,
        expert_weights.transpose(0, 2, 1, 3), n_blk)
    output, token_grad, qkv_grad, g_out, g_router, g_const, g_vec, g_gains, g_mix, aux = attend_back(
        lengths, att_grad, tokens, res_grad, smt, att, local_out, pg, g_small, misc, w_qkv, small, cnt, norm, q, k, v, o, w_all,
        parts, n_blk)
    results = settle(output, token_grad, qkv_grad, g_out, g_router, g_const, g_vec, g_gains, g_mix, aux, g_exp)
    output, token_grad, qkv_grad, g_out, g_router, g_const, g_vec, g_gains, g_mix, aux, g_exp = results
    return (
        output, aux[0, 0], token_grad, qkv_grad, g_out, g_router.T, g_const.T, g_vec.T, g_gains.T, g_mix,
        g_exp.transpose(0, 2, 1, 3),
    )


def solution(mesh):
    small = mesh.shape["blk"] == 16 and mesh.shape["head"] == 2
    return jax.shard_map(
        on_device_small if small else on_device,
        mesh=mesh,
        in_specs=(
            P(("blk", "head"), None),
            P(("blk", "head"), None),
            P(("blk", "head"), None),
            P(("blk", "head"), None),
            P(),
            P(("head", "blk"), None),
            P(("head", "blk"), None),
            P(("head", "blk"), None),
            P(("head", "blk"), None),
            P(("head", "blk"), None),
            P(("head", "blk"), None),
            P(),
            P("blk", "head", None, None),
        ),
        out_specs=(
            P(("blk", "head"), None),
            P(),
            P(("blk", "head"), None),
            P(("head", "blk"), None),
            P(("head", "blk"), None),
            P(("head", "blk"), None),
            P(("head", "blk"), None),
            P(("head", "blk"), None),
            P(("head", "blk"), None),
            P(),
            P("blk", "head", None, None),
        ),
        check_vma=False,
    )
```

```python
from functools import partial
import functools
import math

import jax
import jax.numpy as jnp
import numpy as np
from jax import lax
from jax.experimental import pallas as pl
from jax.experimental.pallas import tpu as pltpu
from jax.sharding import PartitionSpec as P

HEADS = 12
MESH = pl.DeviceIdType.MESH
f32, bf16 = jnp.float32, jnp.bfloat16
NEG = -1e30
HD = 64
X, C, Y, Z = 1, 2, 4, 8
EARLY = (3, 2, 1)
Z_FIRST = (3, 2, 1)


def place(mask, h, b):
    hb = 1 - h if mask & X else h
    cb = b % 2
    yb = (b // 2) % 2
    zb = (b // 4) % 2
    cb = 1 - cb if mask & C else cb
    yb = 1 - yb if mask & Y else yb
    zb = 1 - zb if mask & Z else zb
    low = zb * 4 + yb * 2 + cb
    return hb, (b // 8) * 8 + low, low * 2 + hb


def head_of(h, b):
    quad = b % 4
    return h * 6 + ((b % 8) // 4) * 3 + quad - quad // 3


def home_of(head):
    h, i = head // 6, head % 6
    return ((i // 3) * 4 + i % 3) * 2 + h


def greet_all(h, b, n_blk):
    barrier = pltpu.get_barrier_semaphore()
    me = b * 2 + h
    total = 2 * n_blk

    def say(k, carry):
        other = (me + k) % total
        pl.semaphore_signal(barrier, inc=1, device_id=(other % 2, other // 2), device_id_type=MESH)
        return carry

    lax.fori_loop(1, total, say, 0)
    return lambda: pl.semaphore_wait(barrier, total - 1)


def turned(qk, cos, sin):
    lane = lax.broadcasted_iota(jnp.int32, qk.shape, 1)
    swapped = jnp.where(lane % 64 < 32, pltpu.roll(qk, 96, 1), pltpu.roll(qk, 32, 1))
    return qk * cos + swapped * sin


def rotary_tables(rows):
    freq = np.exp(np.arange(32, dtype=np.float32) * np.float32(-2.0 * math.log(10000.0) / 64)).astype(np.float32)
    ang = (np.arange(rows, dtype=np.float32)[:, None] * freq[None, :]).astype(np.float32).astype(np.float64)
    cos, sin = np.cos(ang), np.sin(ang)
    return (
        np.concatenate([cos, cos, cos, cos], 1).astype(np.float32),
        np.concatenate([-sin, sin, -sin, sin], 1).astype(np.float32),
    )


class RowGather:
    def __init__(self, buf, sems, h, b, straight=False):
        self.buf, self.h, self.b, self.straight = buf, h, b, straight
        self.parts = range(buf.shape[1])
        self.zs, self.ys, self.cs, self.zr, self.yr, self.cr = sems
        self.z, self.y, self.c = b // 4, (b // 2) % 2, b % 2

    def nth(self, k):
        return nearest(self.z, k)

    def at(self, z, y, c, p):
        return self.buf.at[z * 4 + y * 2 + c, p]

    def copy(self, where, send, recv, device):
        return pltpu.make_async_remote_copy(
            src_ref=where, dst_ref=where, send_sem=send, recv_sem=recv, device_id=device, device_id_type=MESH)

    def along_z(self, k, step, p):
        zz = self.nth(k)
        return self.copy(self.at(zz, self.y, self.c, p), self.zs.at[(step + 1) // 2, k, p], self.zr.at[zz, p],
                         (self.h, self.b + 4 * step))

    def to_z(self, k, p):
        return self.copy(self.at(self.z, self.y, self.c, p), self.zs.at[0, k, p], self.zr.at[self.z, p],
                         (self.h, self.nth(k) * 4 + self.b % 4))

    def over_y(self, k, p):
        zz = self.nth(k)
        return self.copy(self.at(zz, self.y, self.c, p), self.ys.at[k, p], self.yr.at[zz, p],
                         (self.h, self.b + 2 - 4 * self.y))

    def over_core(self, k, far, p):
        zz = self.nth(k)
        yy = 1 - self.y if far else self.y
        return self.copy(self.at(zz, yy, self.c, p), self.cs.at[far, k, p], self.cr.at[far, zz, p],
                         (self.h, self.b + 1 - 2 * self.c))

    def own_z(self, act):
        for p in self.parts:
            if self.straight:
                for k in range(1, 4):
                    act(self.to_z(k, p))
            else:
                for step in (1, -1):
                    @pl.when((self.z + step >= 0) & (self.z + step <= 3))
                    def _(step=step, p=p):
                        act(self.along_z(0, step, p))

    def relay(self, k, p, act):
        if self.straight:
            return
        zz = self.nth(k)

        @pl.when((zz < self.z) & (self.z < 3))
        def _():
            act(self.along_z(k, 1, p))

        @pl.when((zz > self.z) & (self.z > 0))
        def _():
            act(self.along_z(k, -1, p))

    def start(self):
        self.own_z(lambda c: c.start())
        for p in self.parts:
            self.over_y(0, p).start()
        for p in self.parts:
            self.over_core(0, 0, p).start()

    def arrived(self, where, sem):
        self.copy(where, self.zs.at[0, 0, 0], sem, (self.h, self.b)).wait_recv()

    def got_z(self, k):
        zz = self.nth(k)
        for p in self.parts:
            self.arrived(self.at(zz, self.y, self.c, p), self.zr.at[zz, p])
            self.relay(k, p, lambda c: c.start())
            self.over_y(k, p).start()
            self.over_core(k, 0, p).start()

    def got_y(self, k):
        zz = self.nth(k)
        for p in self.parts:
            self.arrived(self.at(zz, 1 - self.y, self.c, p), self.yr.at[zz, p])
            self.over_core(k, 1, p).start()

    def got_core(self, k):
        zz = self.nth(k)
        for far in range(2):
            yy = 1 - self.y if far else self.y
            for p in self.parts:
                self.arrived(self.at(zz, yy, 1 - self.c, p), self.cr.at[far, zz, p])

    def finish(self):
        self.own_z(lambda c: c.wait_send())
        for p in self.parts:
            for k in range(4):
                if k:
                    self.relay(k, p, lambda c: c.wait_send())
                self.over_y(k, p).wait_send()
                self.over_core(k, 0, p).wait_send()
                self.over_core(k, 1, p).wait_send()


def nearest(z, k):
    near = z - (z // 2) * (2 * z - 3)
    low = k + (1 - 2 * k) * near if k < 2 else k
    return low + (z // 2) * (3 - 2 * low)


def gather_sems(parts):
    DMA = pltpu.SemaphoreType.DMA
    return [DMA((2, 4, parts)), DMA((4, parts)), DMA((2, 4, parts)), DMA((4, parts)), DMA((4, parts)), DMA((2, 4, parts))]


def fold(rows):
    half = rows.shape[1] // 2
    low = jnp.concatenate([rows[16:24, :half], rows[16:24, half:]], axis=0)
    return jnp.concatenate([rows[0:16], low], axis=1).astype(bf16)


def routing_table(routes, live):
    lane = lax.broadcasted_iota(jnp.int32, (128, 128), 1)
    row = lax.broadcasted_iota(jnp.int32, (128, 128), 0)
    expert = lane.astype(f32)
    named = jnp.where((routes[:, 0:1] == expert) | (routes[:, 1:2] == expert), live, 0.0)
    before = jnp.where(lane < row, 1.0, 0.0).astype(bf16)
    rank = jnp.dot(before, named.astype(bf16), preferred_element_type=f32)
    return named, named * (rank + 1.0)


def expert_lanes(h):
    e = lax.broadcasted_iota(jnp.int32, (128, 256), 0)
    s = lax.broadcasted_iota(jnp.int32, (128, 256), 1)
    return jnp.where((s < 192) & (e == 4 * h + s // 48), 1.0, 0.0)


def slot_table(ranks, h, source_h):
    spread = jnp.dot(ranks.astype(bf16), expert_lanes(h).astype(bf16), preferred_element_type=f32)
    s = lax.broadcasted_iota(jnp.int32, (128, 256), 1)
    place_in = s % 48 - 24 * source_h
    inside = (place_in >= 0) & (place_in < 24) & (s < 192)
    return jnp.where(inside & (spread == (place_in + 1).astype(f32)), 1.0, 0.0)


def live_column(h, b, length):
    row = lax.broadcasted_iota(jnp.int32, (128, 1), 0) + ((b % 8) * 2 + h) * 128
    return jnp.where(row < length, 1.0, 0.0)


def forward_kernel(
    n_blk, all_here, lengths, tok, cot, routes, w_in, small, wo_in, cos_hbm, sin_hbm, relay_w,
    norm_hbm, q_hbm, k_hbm, v_hbm, o_hbm, att_out, smt_out, cnt_out, sm_out, wo_out, pt_out, cot_rows,
    xg, pieces, got, w_f, w_b, cos, sin, norm, q, k, v, o, sendbuf, att_in, rank_own, rank_far, cot_far, wo_all,
    ag_send, ag_recv, pc_send, pc_recv, at_send, at_recv, loc, x_send, x_recv, *gathers,
):
    h, b = lax.axis_index("head"), lax.axis_index("blk")
    me = b * 2 + h
    total = 2 * n_blk
    _, _, rank = place(0, h, b)
    cos_in = pltpu.make_async_copy(cos_hbm, cos, loc.at[9])
    sin_in = pltpu.make_async_copy(sin_hbm, sin, loc.at[10])
    cos_in.start()
    sin_in.start()
    for p in range(3):
        xg[p, rank] = tok[:, 256 * p : 256 * p + 256]
    all_here()

    def block_copy(p, m, d, slot):
        _, _, r = place(m, h, b)
        ph, pb, _ = place(d, h, b)
        return pltpu.make_async_remote_copy(
            src_ref=xg.at[p, r], dst_ref=xg.at[p, r],
            send_sem=ag_send.at[p, slot], recv_sem=ag_recv.at[p, m ^ d],
            device_id=(ph, pb), device_id_type=MESH,
        )

    def arrival(p, m):
        _, _, r = place(m, h, b)
        return pltpu.make_async_remote_copy(
            src_ref=xg.at[p, r], dst_ref=xg.at[p, r],
            send_sem=ag_send.at[p, 0], recv_sem=ag_recv.at[p, m],
            device_id=(h, b), device_id_type=MESH,
        )

    sends = []
    counts = [0, 0, 0]

    def send(p, m, d):
        copy = block_copy(p, m, d, counts[p])
        counts[p] += 1
        copy.start()
        sends.append(copy)

    dims = [X, Y, Z]
    orders = [dims[p:] + dims[:p] for p in range(3)]
    for t in range(3):
        for p in range(3):
            send(p, 0, orders[p][t])
    for p in range(3):
        send(p, 0, C)

    length = lengths[b // 8]
    named, ranks = routing_table(routes[...], live_column(h, b, length))
    rank_own[...] = ranks.astype(bf16)
    wo_all[b, 0, h] = fold(wo_in[...].astype(f32))

    w24 = w_in[...].astype(f32)
    count = pltpu.roll(jnp.sum(named, axis=0, keepdims=True), 20, 1)[:, 0:64]
    small = small[...] + jnp.where(lax.broadcasted_iota(jnp.int32, (24, 64), 0) == 0, count, 0.0)
    for j in range(12):
        cat = jnp.concatenate(
            [w24[:, 64 * j : 64 * j + 64], w24[:, 768 + 64 * j : 832 + 64 * j],
             w24[:, 1536 + 64 * j : 1600 + 64 * j], small], axis=1)
        pieces[j] = fold(cat)

    def piece_copy(kk):
        other = (me + kk) % total
        oh, ob = other % 2, other // 2
        return pltpu.make_async_remote_copy(
            src_ref=pieces.at[head_of(oh, ob)], dst_ref=got.at[me],
            send_sem=pc_send.at[kk], recv_sem=pc_recv.at[me],
            device_id=(oh, ob), device_id_type=MESH,
        )

    def send_piece(kk, carry):
        piece_copy(kk).start()
        return carry

    lax.fori_loop(1, total, send_piece, 0)
    got[me] = pieces[head_of(h, b)]

    relay_w(0)
    for p in range(3):
        d0, d1, d2 = orders[p]
        arrival(p, d0).wait_recv()
        for d in (d1, d2, C):
            send(p, d0, d)
    relay_w(1)
    for p in range(3):
        d0, d1, d2 = orders[p]
        for m in (d1, d0 ^ d1):
            arrival(p, m).wait_recv()
            for d in (d2, C):
                send(p, m, d)
    swaps = [
        pltpu.make_async_remote_copy(
            src_ref=src, dst_ref=dst, send_sem=x_send.at[n], recv_sem=x_recv.at[n],
            device_id=(1 - h, b), device_id_type=MESH)
        for n, (src, dst) in enumerate([(wo_all.at[b, 0, h], wo_all.at[b, 0, h]), (rank_own, rank_far), (cot, cot_far)])
    ]
    for c in swaps:
        c.start()
    relay_w(2)
    for p in range(3):
        d0, d1, d2 = orders[p]
        for m in (d2, d0 ^ d2, d1 ^ d2, d0 ^ d1 ^ d2):
            arrival(p, m).wait_recv()
            send(p, m, C)

    def take_piece(kk, carry):
        src = (me + kk) % total
        pltpu.make_async_remote_copy(
            src_ref=pieces.at[0], dst_ref=got.at[src],
            send_sem=pc_send.at[0], recv_sem=pc_recv.at[src],
            device_id=(h, b), device_id_type=MESH,
        ).wait_recv()
        return carry

    lax.fori_loop(1, total, take_piece, 0)

    for src in range(2 * n_blk):
        row = 24 * ((src % 2) * n_blk + src // 2)
        w_f[row : row + 16, :] = got[src, :, 0:256].astype(f32)
        low = got[src, :, 256:384].astype(f32)
        w_f[row + 16 : row + 24, 0:128] = low[0:8]
        w_f[row + 16 : row + 24, 128:256] = low[8:16]
    w_b[...] = w_f[...].astype(bf16)
    sm = pltpu.roll(w_f[:, 128:256], 64, 1)
    lane = lax.broadcasted_iota(jnp.int32, (768, 128), 1)
    cnt = jnp.sum(jnp.where((lane >= 20) & (lane < 32), sm, 0.0), axis=0, keepdims=True)
    cnt_out[...] = jnp.broadcast_to(pltpu.roll(cnt, 108, 1), (8, 128))
    sm = jnp.where(lane < 20, sm, 0.0)
    sm_out[...] = sm.astype(bf16)
    smt = jnp.transpose(sm)
    smt_out[...] = smt[0:32, :]
    gain = smt[16:17, :]

    pltpu.make_async_remote_copy(
        src_ref=wo_all.at[b, 0, h], dst_ref=wo_all.at[b, 0, 1 - h], send_sem=x_send.at[0], recv_sem=x_recv.at[0],
        device_id=(h, b), device_id_type=MESH).wait_recv()
    wo_gather = RowGather(wo_all, gathers[0:6], h, b, straight=True)
    wo_gather.start()
    swaps[1].wait_recv()
    swaps[2].wait_recv()
    pt = [slot_table(ranks, h, h).astype(bf16), slot_table(rank_far[...].astype(f32), h, 1 - h).astype(bf16)]
    pt_out[0] = pt[0]
    pt_out[1] = pt[1]
    picked = sum(
        lax.dot_general(t[:, 0:192], c[...], (((0,), (0,)), ((), ())), preferred_element_type=f32)
        for t, c in zip(pt, (cot, cot_far))).astype(bf16)
    cot_rows[b, 0] = picked[0:96]
    cot_rows[b, 1] = picked[96:192]
    cot_gather = RowGather(cot_rows, gathers[6:12], h, b, straight=True)
    cot_gather.start()

    cos_in.wait()
    sin_in.wait()

    def one_block(r, carry):
        x = [xg[p, r].astype(f32) for p in range(3)]
        mean = sum(jnp.sum(t * t, axis=1, keepdims=True) for t in x) * (1.0 / 768)
        scale = lax.rsqrt(mean + 1e-6)
        rows = pl.ds(pl.multiple_of(r * 128, 128), 128)
        acc = jnp.zeros((128, 256), f32)
        for p in range(3):
            n = (x[p] * scale * gain[:, 256 * p : 256 * p + 256]).astype(bf16)
            norm[rows, 256 * p : 256 * p + 256] = n
            acc = acc + jnp.dot(n, w_b[256 * p : 256 * p + 256, :], preferred_element_type=f32)
        qk = turned(acc[:, 0:128], cos[rows, :], sin[rows, :])
        q[rows, :] = (qk[:, 0:64] * 0.125).astype(bf16)
        k[rows, :] = qk[:, 64:128].astype(bf16)
        lane = lax.broadcasted_iota(jnp.int32, (128, 128), 1)
        v[rows, :] = jnp.where(lane < 64, acc[:, 128:256], jnp.where(lane == 64, 1.0, 0.0)).astype(bf16)
        return carry

    def of_core(core):
        return lambda i, carry: one_block((i // 4) * 8 + ((i // 2) % 2) * 4 + core * 2 + i % 2, carry)

    lax.fori_loop(0, 8, of_core(b % 2), 0)
    for p in range(3):
        for m in (C, C ^ X, C ^ Y, C ^ Z, C ^ X ^ Y, C ^ X ^ Z, C ^ Y ^ Z, C ^ X ^ Y ^ Z):
            arrival(p, m).wait_recv()
    lax.fori_loop(0, 8, of_core(1 - b % 2), 0)
    stores = [
        pltpu.make_async_copy(norm, norm_hbm, loc.at[4]),
        pltpu.make_async_copy(q, q_hbm, loc.at[5]),
        pltpu.make_async_copy(k, k_hbm, loc.at[6]),
        pltpu.make_async_copy(v, v_hbm, loc.at[7]),
    ]
    for s in stores:
        s.start()

    head = head_of(h, b)
    working = (b % 4) != 3
    base = (b // 8) * 8

    w, c = wo_gather, cot_gather
    between = {
        0: [lambda: w.got_z(1), lambda: w.got_y(0)],
        1: [lambda: w.got_z(2), lambda: w.got_z(3)],
        2: [lambda: w.got_y(1)],
        3: [lambda: w.got_y(2), lambda: c.got_z(1)],
        4: [lambda: w.got_y(3)],
        5: [lambda: w.got_core(0), lambda: w.got_core(1), lambda: c.got_y(0)],
        6: [lambda: w.got_core(2), lambda: w.got_core(3)],
        7: [],
    }

    def out_copy(r):
        return pltpu.make_async_remote_copy(
            src_ref=sendbuf.at[r], dst_ref=att_in.at[head],
            send_sem=at_send.at[r], recv_sem=at_recv.at[head],
            device_id=(r % 2, base + r // 2), device_id_type=MESH,
        )

    for i in range(8):
        width = 256 * (i + 1)
        s = lax.dot_general(q[256 * i : width, :], k[0:width, :], (((1,), (1,)), ((), ())), preferred_element_type=f32)
        key = lax.broadcasted_iota(jnp.int32, (1, width), 1)
        s = s + jnp.where(key < length, 0.0, NEG)
        rowi = lax.broadcasted_iota(jnp.int32, (256, 256), 0)
        coli = lax.broadcasted_iota(jnp.int32, (256, 256), 1)
        last = jnp.where(coli <= rowi, s[:, width - 256 :], NEG)
        s = last if i == 0 else jnp.concatenate([s[:, : width - 256], last], axis=1)
        m = jnp.max(s, axis=1, keepdims=True)
        e = jnp.exp(s - m).astype(bf16)
        ov = jnp.dot(e, v[0:width, :], preferred_element_type=f32)
        l = ov[:, 64:65]
        lane = lax.broadcasted_iota(jnp.int32, (256, 128), 1)
        ov = jnp.where(lane < 64, ov / l, m + jnp.log(l))
        o[256 * i : width, :] = ov
        oh = ov[:, 0:64]
        for half in range(2):
            r = 2 * i + half
            packed = jnp.concatenate([oh[128 * half : 128 * half + 64], oh[128 * half + 64 : 128 * half + 128]], axis=1)
            sendbuf[r] = packed.astype(bf16)

            @pl.when(working & (r != rank))
            def _(r=r):
                out_copy(r).start()
        for act in between[i]:
            act()

    o_store = pltpu.make_async_copy(o, o_hbm, loc.at[8])
    o_store.start()

    def unfolded(blk, hh):
        t = wo_all[blk, 0, hh].astype(f32)
        return jnp.concatenate(
            [t[:, 0:768], jnp.concatenate([t[0:8, 768:1152], t[8:16, 768:1152]], axis=1)], axis=0)

    for hh in range(2):
        for blk in range(0, 16, 2):
            row = 24 * (hh * 16 + blk)
            wo_out[row : row + 48, :] = jnp.concatenate([unfolded(blk, hh), unfolded(blk + 1, hh)], axis=0).astype(bf16)

    @pl.when(working)
    def _():
        att_in[head] = sendbuf[rank]

    for j in range(12):
        @pl.when(rank != home_of(j))
        def _(j=j):
            pltpu.make_async_remote_copy(
                src_ref=sendbuf.at[0], dst_ref=att_in.at[j],
                send_sem=at_send.at[0], recv_sem=at_recv.at[j],
                device_id=(h, b), device_id_type=MESH,
            ).wait_recv()

    for j in range(0, 12, 2):
        one, two = att_in[j].astype(f32), att_in[j + 1].astype(f32)
        att_out[0:64, 64 * j : 64 * j + 128] = jnp.concatenate([one[:, 0:64], two[:, 0:64]], axis=1).astype(bf16)
        att_out[64:128, 64 * j : 64 * j + 128] = jnp.concatenate([one[:, 64:128], two[:, 64:128]], axis=1).astype(bf16)

    def finish():
        for copy in sends:
            copy.wait_send()
        for c in swaps:
            c.wait_send()
        wo_gather.finish()
        cot_gather.finish()

        def sent_piece(kk, carry):
            piece_copy(kk).wait_send()
            return carry

        lax.fori_loop(1, total, sent_piece, 0)
        for r in range(16):
            @pl.when(working & (r != rank))
            def _(r=r):
                out_copy(r).wait_send()
        for s in stores:
            s.wait()
        o_store.wait()

    return cot_gather, finish


def split(x):
    high = x.astype(bf16)
    return high, (x - high.astype(f32)).astype(bf16)


def exact_dot(x, y, dims):
    high, low = split(x)
    return lax.dot_general(high, y, (dims, ((), ())), preferred_element_type=f32) + lax.dot_general(
        low, y, (dims, ((), ())), preferred_element_type=f32)


def softmax_back(p, d):
    return p * (d - jnp.sum(p * d, axis=1, keepdims=True))


def lane_of(column, n):
    lane = lax.broadcasted_iota(jnp.int32, (128, 128), 1)
    return jnp.where(lane == n, column, 0.0)


class RowScatter:
    def __init__(self, part, from_core, from_y, from_z, sems, h, b):
        self.part, self.from_core, self.from_y, self.from_z = part, from_core, from_y, from_z
        self.h, self.b = h, b
        self.cs, self.cr, self.ys, self.yr, self.zs, self.zr = sems
        self.parts = range(part.shape[1])
        self.order = [(k, p) for k in (3, 2, 1, 0) for p in self.parts]
        self.z, self.y, self.c = b // 4, (b // 2) % 2, b % 2

    def nth(self, k):
        return nearest(self.z, k)

    def blk(self, k, far_y, far_c):
        y = 1 - self.y if far_y else self.y
        c = 1 - self.c if far_c else self.c
        return self.nth(k) * 4 + y * 2 + c

    def remote(self, src, dst, send, recv, device):
        return pltpu.make_async_remote_copy(
            src_ref=src, dst_ref=dst, send_sem=send, recv_sem=recv, device_id=device, device_id_type=MESH)

    def core(self, k, far, p):
        return self.remote(self.part.at[self.blk(k, far, 1), p], self.from_core.at[k, far, p], self.cs.at[k, far, p],
                           self.cr.at[k, far, p], (self.h, self.b + 1 - 2 * self.c))

    def over_y(self, k, p):
        return self.remote(self.part.at[self.blk(k, 1, 0), p], self.from_y.at[k, p], self.ys.at[k, p], self.yr.at[k, p],
                           (self.h, self.b + 2 - 4 * self.y))

    def to_z(self, k, p):
        return self.remote(self.part.at[self.blk(k, 0, 0), p], self.from_z.at[self.z, p], self.zs.at[k, p],
                           self.zr.at[self.z, p], (self.h, self.nth(k) * 4 + self.b % 4))

    def join_y(self, k, p):
        self.core(k, 0, p).wait_recv()
        self.over_y(k, p).wait_recv()
        self.add(self.blk(k, 0, 0), p, self.from_core.at[k, 0, p], self.from_y.at[k, p])

    def add(self, blk, p, *others):
        total = self.part[blk, p].astype(f32)
        for other in others:
            total = total + other[...].astype(f32)
        self.part[blk, p] = total.astype(bf16)

    def send_core(self, k, p):
        self.core(k, 1, p).start()
        self.core(k, 0, p).start()

    def send_y(self, k, p):
        self.core(k, 1, p).wait_recv()
        self.add(self.blk(k, 1, 0), p, self.from_core.at[k, 1, p])
        self.over_y(k, p).start()

    def send_z(self, k, p):
        self.join_y(k, p)
        if k:
            self.to_z(k, p).start()

    def total(self, p):
        total = self.part[self.b, p].astype(f32)
        for k in range(1, 4):
            here = self.from_z.at[self.nth(k), p]
            self.remote(here, here, self.zs.at[0, 0], self.zr.at[self.nth(k), p], (self.h, self.b)).wait_recv()
            total = total + here[...].astype(f32)
        return total

    def finish(self, near=range(4), far=range(1, 4)):
        for p in self.parts:
            for k in near:
                self.core(k, 0, p).wait_send()
                self.core(k, 1, p).wait_send()
                self.over_y(k, p).wait_send()
            for k in far:
                self.to_z(k, p).wait_send()


def scatter_scratch(parts, rows, cols):
    DMA = pltpu.SemaphoreType.DMA
    V = pltpu.VMEM
    return [
        V((4, 2, parts, rows, cols), bf16), V((4, parts, rows, cols), bf16), V((4, parts, rows, cols), bf16),
        DMA((4, 2, parts)), DMA((4, 2, parts)), DMA((4, parts)), DMA((4, parts)), DMA((4, parts)), DMA((4, parts)),
    ]


def expert_kernel(
    n_blk, cg, lengths, att, tok, cot, prev, mix, routes, wout, sm, smt, cnt, pt, w, cot_all,
    part_hbm, g_hbm, local_out, res_out, ag_out, gs_out, misc_out, pg_out,
    x_all, cc, dgu, hid, inp, outp, gbuf, gates_in, vs_out, vs_in, n_own, n_far, g_own, g_far,
    d_out, d_in, dv_out, dv_in, ga_send, ga_recv, vs_send, vs_recv, x_send, x_recv, loc, *rest,
):
    gsems, (from_core, from_y, from_z), ssems, (out_core, out_y), osems = rest[0:6], rest[6:9], rest[9:15], rest[15:17], rest[17:21]
    h, b = lax.axis_index("head"), lax.axis_index("blk")
    length = lengths[b // 8]
    live_total = (lengths[0] + lengths[1]).astype(f32)
    live = live_column(h, b, length)
    lane = lax.broadcasted_iota(jnp.int32, (128, 128), 1)

    res = tok[...].astype(f32) + jnp.dot(att[...], wout[...], preferred_element_type=f32)
    scale = lax.rsqrt(jnp.sum(res * res, axis=1, keepdims=True) * (1.0 / 768) + 1e-6)
    xh = res * scale
    n2 = (xh * smt[17:18, :]).astype(bf16)
    small = sm[...]
    logits = jnp.dot(n2, small, preferred_element_type=f32)
    router = logits + jnp.dot(prev[...], mix[...], preferred_element_type=f32, precision=lax.Precision.HIGHEST)
    router = jnp.where(lane < 12, router, NEG)
    prob = jnp.exp(router - jnp.max(router, axis=1, keepdims=True))
    prob = prob / jnp.sum(prob, axis=1, keepdims=True)
    expert = lane.astype(f32)
    named = jnp.where((routes[:, 0:1] == expert) | (routes[:, 1:2] == expert), 1.0, 0.0)
    gates = prob * named
    n_own[...] = n2
    g_own[...] = gates
    swaps = [
        pltpu.make_async_remote_copy(
            src_ref=src, dst_ref=dst, send_sem=x_send.at[n], recv_sem=x_recv.at[n],
            device_id=(1 - h, b), device_id_type=MESH)
        for n, (src, dst) in enumerate([(n_own, n_far), (g_own, g_far), (d_out, d_in), (dv_out, dv_in)])
    ]
    swaps[0].start()
    swaps[1].start()
    cg.got_z(2)
    cg.got_y(1)
    p_own, p_far = pt[0, :, 0:192], pt[1, :, 0:192]
    rows = ((0,), (0,))
    mine = lax.dot_general(p_own, n2, (rows, ((), ())), preferred_element_type=f32)
    spread = expert_lanes(h).astype(bf16)
    pg_own = pt[0].astype(f32) * exact_dot(gates, spread, ((1,), (0,)))
    pg_out[0] = pg_own
    swaps[0].wait_recv()
    picked = (mine + lax.dot_general(p_far, n_far[...], (rows, ((), ())), preferred_element_type=f32)).astype(bf16)
    x_all[b, 0] = picked[0:96]
    x_all[b, 1] = picked[96:192]
    g = RowGather(x_all, gsems, h, b)
    g.start()
    cg.got_z(3)
    cg.got_y(2)
    cg.got_y(3)
    swaps[1].wait_recv()
    pg_far = pt[1].astype(f32) * exact_dot(g_far[...], spread, ((1,), (0,)))
    pg_out[1] = pg_far
    gates_in[b] = jnp.broadcast_to(jnp.sum(pg_own + pg_far, axis=0, keepdims=True), (8, 256))

    def gate_copy(k):
        return pltpu.make_async_remote_copy(
            src_ref=gates_in.at[b], dst_ref=gates_in.at[b], send_sem=ga_send.at[k], recv_sem=ga_recv.at[b],
            device_id=(h, (b + k) % n_blk), device_id_type=MESH)

    def vs_copy(k):
        to = (b + k) % n_blk
        return pltpu.make_async_remote_copy(
            src_ref=vs_out.at[to], dst_ref=vs_in.at[b], send_sem=vs_send.at[k], recv_sem=vs_recv.at[b],
            device_id=(h, to), device_id_type=MESH)

    def each(act):
        def body(k, carry):
            act(k)
            return carry

        lax.fori_loop(1, n_blk, body, 0)

    each(lambda k: gate_copy(k).start())

    def group(ref, k, p, ee):
        return ref[pl.ds(4 * g.nth(k), 4), p, 48 * ee : 48 * ee + 48, :]

    def put(ref, k, p, ee, value):
        ref[pl.ds(4 * g.nth(k), 4), p, 48 * ee : 48 * ee + 48, :] = value.reshape(4, 48, value.shape[1]).astype(ref.dtype)

    cols = ((1,), (1,))

    def cot_task(k):
        for e in range(4):
            rows_c = group(cot_all, k, e // 2, e % 2).reshape(192, 768)
            put(cc, k, e // 2, e % 2, lax.dot_general(rows_c, w[3 * e + 2], (cols, ((), ())), preferred_element_type=f32))

    def up_task(k):
        for e in range(4):
            p, ee = e // 2, e % 2
            x = group(x_all, k, p, ee).reshape(192, 768)
            both = lax.dot_general(x, w[3 * e : 3 * e + 2].reshape(256, 768), (cols, ((), ())), preferred_element_type=f32)
            gate, up = both[:, 0:128], both[:, 128:256]
            sig = 1.0 / (1.0 + jnp.exp(-gate))
            silu = gate * sig
            hidden = silu * up
            c = group(cc, k, p, ee).reshape(192, 128)
            put(hid, k, p, ee, hidden)
            put(cc, k, p, ee, hidden * c)
            dg = c * up * (sig * (1.0 + gate * (1.0 - sig)))
            put(dgu, k, p, ee, jnp.concatenate([dg, c * silu], axis=1))

    two = jnp.where(lane % 2 == 0, pltpu.roll(logits, 127, 1), pltpu.roll(logits, 1, 1))
    top = jnp.maximum(logits, two)
    c_mix = jnp.exp(logits - top) / (jnp.exp(logits - top) + jnp.exp(two - top))
    share = gates * live
    n2f = n2.astype(f32)
    alpha = share[:, 9:10] + share[:, 10:11] * c_mix[:, 12:13] + share[:, 11:12] * c_mix[:, 14:15]
    beta = [share[:, 10:11] * c_mix[:, 13:14], share[:, 11:12] * c_mix[:, 15:16]]
    local_out[...] = live * (res + alpha * n2f + beta[0] * smt[18:19, :] + beta[1] * smt[19:20, :])
    og = live * cot[...].astype(f32)
    og_low = og.astype(bf16)

    g.got_z(1)
    cg.got_core(0)
    cot_task(0)
    g.got_z(2)
    g.got_y(0)
    cg.got_core(1)
    cot_task(1)
    g.got_z(3)
    g.got_y(1)
    cg.got_core(2)
    cot_task(2)
    cg.got_core(3)
    cot_task(3)
    g.got_core(0)
    up_task(0)
    g.got_y(2)
    g.got_core(1)
    up_task(1)
    g.got_y(3)
    g.got_core(2)
    up_task(2)
    g.got_core(3)
    up_task(3)

    s = RowScatter(inp, from_core, from_y, from_z, ssems, h, b)
    order = s.order
    for n, (k, p) in enumerate(order):
        for ee in range(2):
            e = 2 * p + ee
            d = group(dgu, k, p, ee).reshape(192, 256)
            put(inp, k, p, ee, jnp.dot(d, w[3 * e : 3 * e + 2].reshape(256, 768), preferred_element_type=f32))
        s.send_core(k, p)
        if n:
            s.send_y(*order[n - 1])
    s.send_y(*order[7])

    ones = jnp.ones((8, 128), f32)

    def one_blk(j, carry):
        for p in range(2):
            vs_out[j, :, 128 * p : 128 * p + 96] = lax.dot_general(
                ones, cc[j, p], (cols, ((), ())), preferred_element_type=f32, precision=lax.Precision.HIGHEST)
        return carry

    lax.fori_loop(0, n_blk, one_blk, 0)
    each(lambda k: vs_copy(k).start())
    vs_in[b] = vs_out[b]
    each(lambda k: pltpu.make_async_remote_copy(
        src_ref=gates_in.at[b], dst_ref=gates_in.at[(b + k) % n_blk], send_sem=ga_send.at[0],
        recv_sem=ga_recv.at[(b + k) % n_blk], device_id=(h, b), device_id_type=MESH).wait_recv())
    gate_cols = jnp.transpose(gates_in[:, 0, :])

    def scaled(ref, p, ee):
        e = 2 * p + ee
        t = ref[:, p, 48 * ee : 48 * ee + 48, :].astype(f32)
        col = jnp.concatenate([gate_cols[48 * e : 48 * e + 48, j : j + 1] for j in range(n_blk)], axis=0)
        return (t.reshape(48 * n_blk, t.shape[2]) * col).astype(bf16)

    def store_g(e, act):
        for kind in range(3):
            act(pltpu.make_async_copy(gbuf.at[kind], g_hbm.at[:, kind, e, :], loc.at[kind]))

    def weight_task(e):
        p, ee = e // 2, e % 2
        x = x_all[:, p, 48 * ee : 48 * ee + 48, :].reshape(48 * n_blk, 768)
        c = cot_all[:, p, 48 * ee : 48 * ee + 48, :].reshape(48 * n_blk, 768)
        if e:
            store_g(e - 1, lambda c: c.wait())
        gbuf[0:2] = lax.dot_general(
            scaled(dgu, p, ee), x, (rows, ((), ())), preferred_element_type=f32).reshape(2, 128, 768)
        gbuf[2] = lax.dot_general(scaled(hid, p, ee), c, (rows, ((), ())), preferred_element_type=f32)
        store_g(e, lambda c: c.start())

    def out_task(k):
        for e in range(4):
            d = group(hid, k, e // 2, e % 2).reshape(192, 128)
            put(outp, k, e // 2, e % 2, jnp.dot(d, w[3 * e + 2], preferred_element_type=f32))

    outs = RowScatter(outp, out_core, out_y, None, (*osems, None, None), h, b)
    early = [(k, p) for k in EARLY for p in range(2)]

    def send_early():
        for n in early:
            outs.send_core(*n)
        for n in early:
            outs.send_y(*n)

    tasks = [[lambda: out_task(3), lambda: out_task(2)], [lambda: out_task(1), lambda: out_task(0)], [send_early],
             [lambda: weight_task(0)], [lambda: weight_task(1)], [lambda: weight_task(2)], [lambda: weight_task(3)], []]
    for (k, p), task in zip(order, tasks):
        for act in task:
            act()
        s.send_z(k, p)

    def part_store(k, whole):
        zz = g.nth(k)
        at = pl.ds(4 * zz, 4) if whole else pl.ds(outs.blk(k, 0, 0), 1)
        return pltpu.make_async_copy(outp.at[at], part_hbm.at[at], loc.at[3 + k])

    for k in range(4):
        if k not in EARLY:
            part_store(k, True).start()

    din = jnp.concatenate([s.total(0), s.total(1)], axis=0).astype(bf16)
    into = ((1,), (0,))
    d_out[...] = exact_dot(pg_far[:, 0:192], din, into).astype(bf16)
    swaps[2].start()
    each(lambda k: pltpu.make_async_remote_copy(
        src_ref=vs_in.at[b], dst_ref=vs_in.at[(b + k) % n_blk], send_sem=vs_send.at[0],
        recv_sem=vs_recv.at[(b + k) % n_blk], device_id=(h, b), device_id_type=MESH).wait_recv())
    vsum = jnp.sum(vs_in[:, 0, :], axis=0, keepdims=True)
    vrow = jnp.concatenate([vsum[:, 0:96], vsum[:, 128:224]], axis=1)
    spread = spread[:, 0:192]
    dv_out[...] = exact_dot(p_far.astype(f32) * vrow, spread, cols)
    swaps[3].start()
    d_own = exact_dot(pg_own[:, 0:192], din, into)
    dv_own = exact_dot(p_own.astype(f32) * vrow, spread, cols)

    u = jnp.sum(og * n2f, axis=1, keepdims=True)
    wj = jnp.dot(og_low, small, preferred_element_type=f32)
    w0, w1 = wj[:, 18:19], wj[:, 19:20]
    c = [c_mix[:, n : n + 1] for n in (12, 13, 14, 15)]
    dgate = lane_of(u, 9) + lane_of(c[0] * u + c[1] * w0, 10) + lane_of(c[2] * u + c[3] * w1, 11)
    dmix = lane_of(u, 12) + lane_of(w0, 13) + lane_of(u, 14) + lane_of(w1, 15)
    dmix = dmix * jnp.where(lane < 14, gates[:, 10:11], gates[:, 11:12])
    both = c_mix * dmix
    dmix = c_mix * (dmix - both - jnp.where(lane % 2 == 0, pltpu.roll(both, 127, 1), pltpu.roll(both, 1, 1)))
    dmix = jnp.where((lane >= 12) & (lane < 16), dmix, 0.0)
    aux = (0.01 * 12.0 / live_total) * (cnt[0:1, :] / (2.0 * live_total)) * live
    swaps[2].wait_recv()
    swaps[3].wait_recv()
    dprob = named * (dgate + dv_own + dv_in[...]) + aux
    dlog = softmax_back(prob, dprob) + dmix
    dn = d_own + d_in[...].astype(f32) + og * alpha + exact_dot(dlog, jnp.where(
        lax.broadcasted_iota(jnp.int32, (768, 128), 1) < 16, small, 0).astype(bf16), cols)
    t = dn * smt[17:18, :]
    rg = og + scale * (t - xh * (jnp.sum(t * xh, axis=1, keepdims=True) * (1.0 / 768)))
    res_out[...] = rg
    ag_out[...] = lax.dot_general(rg.astype(bf16), wout[...], (cols, ((), ())), preferred_element_type=f32).astype(bf16)

    dl_high, dl_low = split(dlog)
    gs = lax.dot_general(n2, dl_high, (rows, ((), ())), preferred_element_type=f32)
    gs = gs + lax.dot_general(n2, dl_low, (rows, ((), ())), preferred_element_type=f32)
    b_high, b_low = split(lane_of(beta[0], 18) + lane_of(beta[1], 19))
    gs = gs + lax.dot_general(og_low, b_high, (rows, ((), ())), preferred_element_type=f32)
    gs = gs + lax.dot_general(og_low, b_low, (rows, ((), ())), preferred_element_type=f32)
    gain = jnp.broadcast_to(jnp.sum(dn * xh, axis=0, keepdims=True), (128, 768))
    gs_out[...] = gs + jnp.where(lax.broadcasted_iota(jnp.int32, (768, 128), 1) == 17, jnp.transpose(gain), 0.0)
    mixed = lax.dot_general(prev[...], jnp.where(lane < 12, dlog, 0.0), (rows, ((), ())), preferred_element_type=f32,
                            precision=lax.Precision.HIGHEST)
    misc_out[0:16, :] = mixed[0:16]
    misc_out[16:24, :] = jnp.broadcast_to(jnp.sum(prob * live, axis=0, keepdims=True), (8, 128))

    for n in early:
        outs.join_y(*n)
    for k in EARLY:
        part_store(k, False).start()
    g.finish()
    s.finish()
    outs.finish(EARLY, ())
    each(lambda k: gate_copy(k).wait_send())
    each(lambda k: vs_copy(k).wait_send())
    for c in swaps:
        c.wait_send()
    for k in range(4):
        part_store(k, k not in EARLY).wait()
    store_g(3, lambda c: c.wait())


def front_kernel(n_blk, *refs):
    (lengths, tok, cot, routes_t, w_in, router_t, const_t, gains_t, vec_t, wo_in, prev_t, mix_in, cos_hbm, sin_hbm, w_hbm,
     norm_hbm, q_hbm, k_hbm, v_hbm, o_hbm, part_hbm, g_hbm, att, smt, cnt, local_out, res_out, ag_out, gs_out, misc_out, pg_out,
     gain_out, sm, wout, pt, cot_rows, turn, w, w_part, wsem, *scratch) = refs
    all_here = greet_all(lax.axis_index("head"), lax.axis_index("blk"), n_blk)
    w_loads = [pltpu.make_async_copy(w_hbm.at[:, kind], w_part.at[kind], wsem.at[kind]) for kind in range(3)]
    for c in w_loads:
        c.start()
    turn[...] = jnp.zeros_like(turn)
    turn[0, 0:12, 0:24] = router_t[...].astype(f32)
    turn[0, 12:16, 0:24] = const_t[...].astype(f32)
    turn[0, 16:18, 0:24] = gains_t[...].astype(f32)
    turn[0, 18:20, 0:24] = vec_t[...].astype(f32)
    turn[1, 0:2, :] = routes_t[...].astype(f32)
    turn[2, 0:12, :] = prev_t[...]
    turn[3, 0:12, 0:12] = mix_in[...]
    small = jnp.transpose(turn[0])[0:24, 0:64]
    gain_out[...] = small
    routes = jnp.transpose(turn[1])
    prev = jnp.transpose(turn[2])

    def relay_w(kind):
        w_loads[kind].wait()
        t = w_part[kind].astype(f32)
        for e in range(4):
            w[3 * e + kind] = t[:, e, :].astype(bf16)

    cot_gather, finish = forward_kernel(
        n_blk, all_here, lengths, tok, cot, routes, w_in, small, wo_in, cos_hbm, sin_hbm, relay_w, norm_hbm, q_hbm, k_hbm, v_hbm, o_hbm,
        att, smt, cnt, sm, wout, pt, cot_rows, *scratch[: len(forward_scratch(n_blk))])
    expert_kernel(
        n_blk, cot_gather, lengths, att, tok, cot, prev, turn.at[3], routes, wout, sm, smt, cnt, pt, w, cot_rows,
        part_hbm, g_hbm, local_out, res_out, ag_out, gs_out, misc_out, pg_out, *scratch[len(forward_scratch(n_blk)) :])
    finish()


def forward_scratch(n_blk):
    V, DMA = pltpu.VMEM, pltpu.SemaphoreType.DMA
    return [
        V((3, 16, 128, 256), bf16), V((12, 16, 384), bf16), V((2 * n_blk, 16, 384), bf16), V((768, 256), f32),
        V((768, 256), bf16), V((2048, 128), f32), V((2048, 128), f32), V((2048, 768), bf16), V((2048, 64), bf16),
        V((2048, 64), bf16), V((2048, 128), bf16), V((2048, 128), f32), V((16, 64, 128), bf16), V((12, 64, 128), bf16),
        V((128, 128), bf16), V((128, 128), bf16), V((128, 768), bf16), V((n_blk, 1, 2, 16, 1152), bf16),
        DMA((3, 16)), DMA((3, 16)), DMA((2 * n_blk,)), DMA((2 * n_blk,)), DMA((16,)), DMA((12,)), DMA((11,)), DMA((3,)), DMA((3,)),
        *gather_sems(1), *gather_sems(2),
    ]


def expert_scratch(n_blk):
    V, DMA = pltpu.VMEM, pltpu.SemaphoreType.DMA
    return [
        V((n_blk, 2, 96, 768), bf16),
        V((n_blk, 2, 96, 128), f32), V((n_blk, 2, 96, 256), bf16), V((n_blk, 2, 96, 128), bf16),
        V((n_blk, 2, 96, 768), bf16), V((n_blk, 2, 96, 768), bf16), V((3, 128, 768), f32),
        V((n_blk, 8, 256), f32), V((n_blk, 8, 256), f32), V((n_blk, 8, 256), f32),
        V((128, 768), bf16), V((128, 768), bf16), V((128, 128), f32), V((128, 128), f32),
        V((128, 768), bf16), V((128, 768), bf16), V((128, 128), f32), V((128, 128), f32),
        DMA((n_blk,)), DMA((n_blk,)), DMA((n_blk,)), DMA((n_blk,)), DMA((4,)), DMA((4,)), DMA((7,)),
        *gather_sems(2), *scatter_scratch(2, 96, 768),
        V((4, 2, 2, 96, 768), bf16), V((4, 2, 96, 768), bf16), DMA((4, 2, 2)), DMA((4, 2, 2)), DMA((4, 2)), DMA((4, 2)),
    ]


def front(lengths, tokens, cotangent, routes, w_qkv, w_router, w_const, gains, vec, w_out, prev, mix, w, n_blk):
    cos, sin = rotary_tables(2048)
    vm = pl.BlockSpec(memory_space=pltpu.VMEM)
    hbm = pl.BlockSpec(memory_space=pl.ANY)
    sds = jax.ShapeDtypeStruct
    V = pltpu.VMEM
    return pl.pallas_call(
        functools.partial(front_kernel, n_blk),
        out_shape=(
            sds((2048, 768), bf16), sds((2048, 64), bf16), sds((2048, 64), bf16), sds((2048, 128), bf16),
            sds((2048, 128), f32), sds((n_blk, 2, 96, 768), bf16), sds((128, 3, 4, 768), f32),
            sds((128, 768), bf16), sds((32, 768), f32), sds((8, 128), f32), sds((128, 768), f32), sds((128, 768), f32),
            sds((128, 768), bf16), sds((768, 128), f32), sds((24, 128), f32), sds((2, 128, 256), f32),
            sds((24, 64), f32),
        ),
        in_specs=[pl.BlockSpec(memory_space=pltpu.SMEM)] + [vm] * 11 + [hbm] * 3,
        out_specs=(hbm,) * 7 + (vm,) * 10,
        scratch_shapes=[
            V((768, 128), bf16), V((768, 768), bf16), V((2, 128, 256), bf16), V((n_blk, 2, 96, 768), bf16),
            V((4, 128, 128), f32), V((12, 128, 768), bf16), V((3, 128, 4, 768), bf16), pltpu.SemaphoreType.DMA((3,)),
            *forward_scratch(n_blk), *expert_scratch(n_blk),
        ],
        compiler_params=pltpu.CompilerParams(collective_id=0, has_side_effects=True, vmem_limit_bytes=63 * 2**20),
        cost_estimate=pl.CostEstimate(flops=8 * 10**9, bytes_accessed=3 * 10**7, transcendentals=0),
        name="front",
    )(lengths, tokens, cotangent, routes.T, w_qkv, w_router.T, w_const.T, gains.T, vec.T, w_out, prev.T, mix,
      jnp.asarray(cos), jnp.asarray(sin), w)


def backward_kernel(
    n_blk, lengths, ag, tok, res_grad, smt, att, local_out, pg, g_small, misc, w_own, small, cnt,
    norm_hbm, q_hbm, k_hbm, v_hbm, o_hbm, cos_hbm, sin_hbm, w_hbm, part_hbm,
    out, dtok_out, gq_out, go_out, router_out, const_out, vec_out, gains_out, mix_out, aux_out,
    norm, q, k, v, o, cos, sin, w_all, agbuf, do_in, do, dk, dv, dqkv, obuf, got, dproj, turn, g_f, gbuf, g_in,
    part, gpart, far_out, far_in, half_out, half_in, half_sum, misc_sum, misc_in,
    a_send, a_recv, b_send, b_recv, g_send, g_recv, loc, x_send, x_recv, m_send, m_recv, *rest,
):
    h, b = lax.axis_index("head"), lax.axis_index("blk")
    me = b * 2 + h
    total = 2 * n_blk
    _, _, rank = place(0, h, b)
    base = (b // 8) * 8
    head = head_of(h, b)
    working = (b % 4) != 3
    all_here = greet_all(h, b, n_blk)
    loads = [
        pltpu.make_async_copy(src, dst, loc.at[i])
        for i, (src, dst) in enumerate([
            (q_hbm, q), (k_hbm, k), (v_hbm, v), (o_hbm, o), (cos_hbm, cos), (sin_hbm, sin), (norm_hbm, norm),
            (w_hbm, w_all), (part_hbm, part)])
    ]
    for c in loads:
        c.start()
    a = ag[...].astype(f32)
    for j in range(12):
        agbuf[j] = jnp.concatenate([a[0:64, 64 * j : 64 * j + 64], a[64:128, 64 * j : 64 * j + 64]], axis=1).astype(bf16)
    all_here()

    def to_head(j):
        r = home_of(j)
        return pltpu.make_async_remote_copy(
            src_ref=agbuf.at[j], dst_ref=do_in.at[rank], send_sem=a_send.at[j], recv_sem=a_recv.at[rank],
            device_id=(r % 2, base + r // 2), device_id_type=MESH,
        )

    for j in range(12):
        @pl.when(rank != home_of(j))
        def _(j=j):
            to_head(j).start()

    def to_tokens(r):
        return pltpu.make_async_remote_copy(
            src_ref=obuf.at[r], dst_ref=got.at[head], send_sem=b_send.at[r], recv_sem=b_recv.at[head],
            device_id=(r % 2, base + r // 2), device_id_type=MESH,
        )

    def to_owner(kk):
        other = (me + kk) % total
        oh, ob = other % 2, other // 2
        return pltpu.make_async_remote_copy(
            src_ref=gbuf.at[oh * n_blk + ob], dst_ref=g_in.at[me], send_sem=g_send.at[kk], recv_sem=g_recv.at[me],
            device_id=(oh, ob), device_id_type=MESH,
        )

    length = lengths[b // 8]

    rs = RowScatter(part, *rest[0:3], rest[3:9], h, b)
    gs = RowScatter(gpart, *rest[9:12], rest[12:18], h, b)
    g_f2 = lax.dot_general(att[...], res_grad[...].astype(bf16), (((0,), (0,)), ((), ())), preferred_element_type=f32)
    for w in range(total):
        cat = jnp.concatenate([g_f2[24 * w : 24 * w + 24], g_small[24 * w : 24 * w + 24, :]], axis=1)
        gpart[w % n_blk, 0, 16 * (w // n_blk) : 16 * (w // n_blk) + 16, :] = fold(cat)
    for n in gs.order:
        gs.send_core(*n)
    loads[8].wait()
    late = [(k, p) for k in (3, 2, 1, 0) if k not in EARLY for p in range(2)]
    def z_early(ks):
        for kk in ks:
            if kk in EARLY and kk:
                for p in range(2):
                    rs.to_z(kk, p).start()

    z_early(Z_FIRST)
    for n in late:
        rs.send_core(*n)

    misc_sum[0] = misc[...]
    z = b // 4
    partners = [(1 - h, b), (h, b + 1 - 2 * (b % 2)), (h, b + 2 - 4 * ((b // 2) % 2)),
                (h, b + 4 - 8 * (z % 2)), (h, b + 8 - 16 * (z // 2))]

    def pairwise(t):
        return pltpu.make_async_remote_copy(
            src_ref=misc_sum.at[t], dst_ref=misc_in.at[t], send_sem=m_send.at[t], recv_sem=m_recv.at[t],
            device_id=partners[t], device_id_type=MESH)

    def pairwise_done(t):
        pairwise(t).wait_recv()
        misc_sum[t + 1] = misc_sum[t] + misc_in[t]
        if t < 4:
            pairwise(t + 1).start()

    pairwise(0).start()
    def step(scatter, stage, n):
        k, p = scatter.order[n]
        return lambda: getattr(scatter, stage)(k, p)

    def ry(n):
        return lambda: rs.send_y(*late[n]) if n < len(late) else None

    def rz(n):
        return lambda: rs.send_z(*late[n]) if n < len(late) else None

    def gy(n):
        return step(gs, "send_y", n)

    def gz(n):
        return step(gs, "send_z", n)

    def pd(t):
        return lambda: pairwise_done(t)

    between = {
        8: [gy(0), ry(0), pd(0)], 7: [], 6: [gy(1)], 5: [], 4: [ry(1), pd(1)], 3: [gz(0)], 2: [gy(2)], 1: [],
        0: [gz(1), gy(3), pd(2)],
    }

    @pl.when(jnp.logical_not(working))
    def _():
        do_in[...] = jnp.zeros_like(do_in)

    @pl.when(working)
    def _():
        do_in[rank] = agbuf[head]

    for c in loads[:6]:
        c.wait()
    if True:
        def unpack(r, carry):
            @pl.when((r != rank) & working)
            def _():
                pltpu.make_async_remote_copy(
                    src_ref=agbuf.at[0], dst_ref=do_in.at[r], send_sem=a_send.at[0], recv_sem=a_recv.at[r],
                    device_id=(h, b), device_id_type=MESH,
                ).wait_recv()

            t = do_in[r].astype(f32)
            rows = pl.multiple_of(r * 128, 128)
            do[pl.ds(rows, 64), :] = t[:, 0:64].astype(bf16)
            do[pl.ds(rows + 64, 64), :] = t[:, 64:128].astype(bf16)
            return carry

        lax.fori_loop(0, 16, unpack, 0)
        for act in between[8]:
            act()
        for i in range(7, -1, -1):
            width = 256 * (i + 1)
            lo = 256 * i
            qi, doi = q[lo:width, :], do[lo:width, :]
            s = lax.dot_general(qi, k[0:width, :], (((1,), (1,)), ((), ())), preferred_element_type=f32)
            key = lax.broadcasted_iota(jnp.int32, (1, width), 1)
            ov = o[lo:width, :]
            lse = ov[:, 64:65]
            s = (s - lse) + jnp.where(key < length, 0.0, NEG)
            rowi = lax.broadcasted_iota(jnp.int32, (256, 256), 0)
            coli = lax.broadcasted_iota(jnp.int32, (256, 256), 1)
            last = jnp.where(coli <= rowi, s[:, lo:], NEG)
            s = last if i == 0 else jnp.concatenate([s[:, :lo], last], axis=1)
            p = jnp.exp(s)
            dp = lax.dot_general(doi, v[0:width, 0:64], (((1,), (1,)), ((), ())), preferred_element_type=f32)
            inner = jnp.sum(doi.astype(f32) * ov[:, 0:64], axis=1, keepdims=True)
            ds = (p * (dp - inner)).astype(bf16)
            p = p.astype(bf16)
            dq = jnp.dot(ds, k[0:width, :], preferred_element_type=f32) * 0.125
            dki = lax.dot_general(ds, qi, (((0,), (0,)), ((), ())), preferred_element_type=f32)
            dvi = lax.dot_general(p, doi, (((0,), (0,)), ((), ())), preferred_element_type=f32)
            if i == 7:
                dk[...] = dki
                dv[...] = dvi
            else:
                dk[0:width, :] += dki
                dv[0:width, :] += dvi
            both = jnp.concatenate([dq, dk[lo:width, :]], axis=1)
            both = turned(both, cos[lo:width, :], -sin[lo:width, :]).astype(bf16)
            dvl = dv[lo:width, :]
            dqkv[lo:width, 0:128] = both
            dqkv[lo:width, 128:256] = jnp.concatenate([dvl, jnp.zeros_like(dvl)], axis=1).astype(bf16)
            for half in range(2):
                r = 2 * i + half
                obuf[r, 0:128, :] = both[128 * half : 128 * half + 128]
                obuf[r, 128:192, :] = jnp.concatenate(
                    [dvl[128 * half : 128 * half + 64], dvl[128 * half + 64 : 128 * half + 128]], axis=1).astype(bf16)

                @pl.when((r != rank) & working)
                def _(r=r):
                    to_tokens(r).start()
            for act in between[i]:
                act()

        @pl.when(working)
        def _():
            got[head] = obuf[rank]

        loads[6].wait()
        for c in range(3):
            g_f[256 * c : 256 * c + 256, :] = lax.dot_general(
                norm[:, 256 * c : 256 * c + 256], dqkv[...], (((0,), (0,)), ((), ())), preferred_element_type=f32)
        for w in range(total):
            gbuf[w] = fold(g_f[24 * w : 24 * w + 24, :])

        def send_g(kk, carry):
            to_owner(kk).start()
            return carry

        @pl.when(working)
        def _():
            lax.fori_loop(1, total, send_g, 0)
            g_in[me] = gbuf[h * n_blk + b]

    def swap_half():
        half_sum[...] = gs.total(0)
        half_out[...] = half_sum[pl.ds(pl.multiple_of(16 * (1 - h), 16), 16), :].astype(bf16)
        swaps[0].start()

    swaps = [
        pltpu.make_async_remote_copy(
            src_ref=src, dst_ref=dst, send_sem=x_send.at[n], recv_sem=x_recv.at[n],
            device_id=(1 - h, b), device_id_type=MESH)
        for n, (src, dst) in enumerate([
            (half_out, half_in), (far_out, far_in)])
    ]
    z_early([kk for kk in (3, 2, 1) if kk not in Z_FIRST])
    for act in (*(ry(n) for n in range(3, len(late))), gz(2), gz(3), rz(0)):
        act()
    swap_half()
    rz(1)()
    pairwise_done(3)

    for j in range(12):
        @pl.when(rank != home_of(j))
        def _(j=j):
            pltpu.make_async_remote_copy(
                src_ref=obuf.at[0], dst_ref=got.at[j], send_sem=b_send.at[0], recv_sem=b_recv.at[j],
                device_id=(h, b), device_id_type=MESH,
            ).wait_recv()
    for j in range(0, 12, 2):
        one, two = got[j].astype(f32), got[j + 1].astype(f32)
        lo = 64 * j
        for part_i, at in enumerate((0, 64)):
            dproj[:, 768 * part_i + lo : 768 * part_i + lo + 128] = jnp.concatenate(
                [one[0:128, at : at + 64], two[0:128, at : at + 64]], axis=1).astype(bf16)
        dproj[0:64, 1536 + lo : 1664 + lo] = jnp.concatenate([one[128:192, 0:64], two[128:192, 0:64]], axis=1).astype(bf16)
        dproj[64:128, 1536 + lo : 1664 + lo] = jnp.concatenate([one[128:192, 64:128], two[128:192, 64:128]], axis=1).astype(bf16)
    loads[7].wait()
    dn = lax.dot_general(dproj[...], w_all[...], (((1,), (1,)), ((), ())), preferred_element_type=f32)
    pairwise_done(4)
    x = tok[...].astype(f32)
    scale = lax.rsqrt(jnp.sum(x * x, axis=1, keepdims=True) * (1.0 / 768) + 1e-6)
    xh = x * scale
    t = dn * smt[16:17, :]
    dx = scale * (t - xh * (jnp.sum(t * xh, axis=1, keepdims=True) * (1.0 / 768)))
    dtok_out[...] = (res_grad[...] + dx).astype(bf16)

    for n in range(2, len(late)):
        rz(n)()
    rows = jnp.concatenate([rs.total(0), rs.total(1)], axis=0).astype(bf16)
    far_out[...] = exact_dot(pg[1, :, 0:192], rows, ((1,), (0,))).astype(bf16)
    swaps[1].start()
    own = exact_dot(pg[0, :, 0:192], rows, ((1,), (0,))) + local_out[...]

    for src in range(total):
        if (src // 2) % 4 == 3:
            continue

        @pl.when(me != src)
        def _(src=src):
            pltpu.make_async_remote_copy(
                src_ref=gbuf.at[0], dst_ref=g_in.at[src], send_sem=g_send.at[0], recv_sem=g_recv.at[src],
                device_id=(h, b), device_id_type=MESH,
            ).wait_recv()
    for j in range(0, 12, 2):
        pair = []
        for jj in (j, j + 1):
            t = sum(g_in[16 * s + home_of(jj)].astype(f32) for s in range(total // 16))
            pair.append(jnp.concatenate(
                [t[:, 0:256], jnp.concatenate([t[0:8, 256:384], t[8:16, 256:384]], axis=1)], axis=0))
        one, two = pair
        for part in range(3):
            gq_out[:, 768 * part + 64 * j : 768 * part + 64 * j + 128] = jnp.concatenate(
                [one[:, 64 * part : 64 * part + 64], two[:, 64 * part : 64 * part + 64]], axis=1)

    lane = lax.broadcasted_iota(jnp.int32, (24, 128), 1)
    gain_grad = jnp.sum(gq_out[...] * w_own[...].astype(f32), axis=1, keepdims=True) / small[:, 16:17]
    swaps[0].wait_recv()
    t = half_sum[pl.ds(pl.multiple_of(16 * h, 16), 16), :] + half_in[...].astype(f32)
    t = jnp.concatenate([t[:, 0:896], jnp.concatenate([t[0:8, 896:1344], t[8:16, 896:1344]], axis=1)], axis=0)
    go_out[...] = t[:, 0:768]
    turn[...] = jnp.zeros_like(turn)
    turn[0:24, :] = jnp.where(lane == 16, gain_grad, t[:, 768:896])
    t = jnp.transpose(turn[...])
    router_out[...] = t[0:12, 0:24]
    const_out[...] = t[12:16, 0:24]
    gains_out[...] = t[16:18, 0:24]
    vec_out[...] = t[18:20, 0:24]
    t = misc_sum[5]
    mix_out[...] = t[0:12, 0:12]
    live_total = (lengths[0] + lengths[1]).astype(f32)
    aux = cnt[0:1, :] / (2.0 * live_total) * (t[16:17, :] / live_total)
    aux_out[...] = 12.0 * jnp.sum(aux, axis=1, keepdims=True)
    swaps[1].wait_recv()
    out[...] = (own + far_in[...].astype(f32)).astype(bf16)

    rs.finish([k for k in range(4) if k not in EARLY])
    gs.finish()
    for t in range(5):
        pairwise(t).wait_send()
    for c in swaps:
        c.wait_send()
    for j in range(12):
        @pl.when(rank != home_of(j))
        def _(j=j):
            to_head(j).wait_send()

    @pl.when(working)
    def _():
        for r in range(16):
            @pl.when(r != rank)
            def _(r=r):
                to_tokens(r).wait_send()

        def sent(kk, carry):
            to_owner(kk).wait_send()
            return carry

        lax.fori_loop(1, total, sent, 0)


def attend_back(
    lengths, ag, tok, res_grad, smt, att, local_out, pg, g_small, misc, w_own, small, cnt, norm, q, k, v, o, w_all, parts,
    n_blk,
):
    cos, sin = rotary_tables(2048)
    vm = pl.BlockSpec(memory_space=pltpu.VMEM)
    hbm = pl.BlockSpec(memory_space=pl.ANY)
    sds = jax.ShapeDtypeStruct
    DMA = pltpu.SemaphoreType.DMA
    V = pltpu.VMEM
    total = 2 * n_blk
    return pl.pallas_call(
        functools.partial(backward_kernel, n_blk),
        out_shape=(
            sds((128, 768), bf16), sds((128, 768), bf16), sds((24, 2304), f32), sds((24, 768), f32), sds((12, 24), f32),
            sds((4, 24), f32), sds((2, 24), f32), sds((2, 24), f32), sds((12, 12), f32), sds((1, 1), f32),
        ),
        in_specs=[pl.BlockSpec(memory_space=pltpu.SMEM)] + [vm] * 12 + [hbm] * 9,
        out_specs=(vm,) * 10,
        scratch_shapes=[
            V((2048, 768), bf16), V((2048, 64), bf16), V((2048, 64), bf16), V((2048, 128), bf16), V((2048, 128), f32),
            V((2048, 128), f32), V((2048, 128), f32), V((768, 2304), bf16),
            V((12, 64, 128), bf16), V((16, 64, 128), bf16), V((2048, 64), bf16), V((2048, 64), f32), V((2048, 64), f32),
            V((2048, 256), bf16), V((16, 192, 128), bf16), V((12, 192, 128), bf16), V((128, 2304), bf16), V((128, 128), f32),
            V((768, 256), f32), V((total, 16, 384), bf16), V((total, 16, 384), bf16),
            V((n_blk, 2, 96, 768), bf16), V((n_blk, 1, 32, 1344), bf16), V((128, 768), bf16), V((128, 768), bf16),
            V((16, 1344), bf16), V((16, 1344), bf16), V((32, 1344), f32), V((6, 24, 128), f32), V((5, 24, 128), f32),
            DMA((12,)), DMA((16,)), DMA((16,)), DMA((12,)), DMA((total,)), DMA((total,)), DMA((9,)), DMA((2,)), DMA((2,)),
            DMA((5,)), DMA((5,)), *scatter_scratch(2, 96, 768), *scatter_scratch(1, 32, 1344),
        ],
        compiler_params=pltpu.CompilerParams(collective_id=1, has_side_effects=True, vmem_limit_bytes=60 * 2**20),
        cost_estimate=pl.CostEstimate(flops=2 * 10**9, bytes_accessed=2 * 10**7, transcendentals=0),
        name="attend_back",
    )(lengths, ag, tok, res_grad, smt, att, local_out, pg, g_small, misc, w_own, small, cnt, norm, q, k, v, o,
      jnp.asarray(cos), jnp.asarray(sin), w_all, parts)


CAP = 24


eps = 1e-06
aux_weight = 0.01
highest = lax.Precision.HIGHEST
masked_score = -1e30


def shifted(block, axis, distance):
    devices = range(lax.axis_size(axis))
    route = [(i - distance, i) for i in devices if i - distance in devices]
    return lax.ppermute(block, axis, route)


def for_sending(x):
    return jax.tree.map(lambda a: a.astype(jnp.bfloat16) if a.dtype == jnp.float32 else a, x)


def rms_norm(values, gain_vector):
    return values * lax.rsqrt(jnp.mean(values * values, axis=-1, keepdims=True) + eps) * gain_vector


def rotary(values, positions, turn_sign):
    half_width = values.shape[-1] // 2
    frequency = jnp.exp(
        jnp.arange(half_width, dtype=jnp.float32) * (-2.0 * math.log(10000.0) / values.shape[-1])
    )
    angles = positions.astype(jnp.float32)[:, None] * frequency[None, :]
    cosine = jnp.cos(angles)[:, None, :]
    sine_part = turn_sign * jnp.sin(angles)[:, None, :]
    first_half = values[..., :half_width]
    second_half = values[..., half_width:]
    return jnp.concatenate(
        [
            first_half * cosine - second_half * sine_part,
            second_half * cosine + first_half * sine_part,
        ],
        axis=-1,
    )


def slot_lengths(slot_ids, lengths):
    slot_table = jnp.arange(lengths.shape[0], dtype=jnp.int32)
    return jnp.sum(jnp.where(slot_ids[:, None] == slot_table[None, :], lengths[None, :], 0), axis=1)


def allowed_mask(query_ids, key_ids, slot_size, lengths):
    query_slot = query_ids // slot_size
    key_slot = key_ids // slot_size
    query_pos = query_ids - query_slot * slot_size
    key_pos = key_ids - key_slot * slot_size
    key_live = (key_pos < slot_lengths(key_slot, lengths)) & (key_ids >= 0)
    return (
        (query_slot[:, None] == key_slot[None, :])
        & (key_pos[None, :] <= query_pos[:, None])
        & key_live[None, :]
    )


def masked_scores(query_block, key_head, query_ids, key_ids, slot_size, lengths):
    scores = lax.dot_general(
        query_block, key_head, (((1,), (1,)), ((), ())), preferred_element_type=jnp.float32
    ) * HD ** (-0.5)
    return jnp.where(allowed_mask(query_ids, key_ids, slot_size, lengths), scores, masked_score)


def attend_forward(queries, key_all, value_all, query_ids, key_ids, slot_size, lengths):
    head_total = queries.shape[1] // HD

    def one_head(head_index):
        query_head = lax.dynamic_slice_in_dim(queries, head_index * HD, HD, 1)
        key_head = lax.dynamic_slice_in_dim(key_all, head_index * HD, HD, 1)
        value_head = lax.dynamic_slice_in_dim(value_all, head_index * HD, HD, 1)
        scores = masked_scores(query_head, key_head, query_ids, key_ids, slot_size, lengths)
        row_max = jnp.max(scores, axis=1, keepdims=True)
        weights = jnp.exp(scores - row_max)
        row_total = jnp.sum(weights, axis=1, keepdims=True)
        probs_low = (weights / row_total).astype(jnp.bfloat16)
        head_outputs = [jnp.dot(probs_low, value_head, preferred_element_type=jnp.float32)]
        log_parts = [row_max[:, 0] + jnp.log(row_total[:, 0])]
        return (jnp.concatenate(head_outputs, axis=0), jnp.concatenate(log_parts, axis=0))

    head_outputs, log_sums = lax.map(one_head, jnp.arange(head_total, dtype=jnp.int32))
    return (head_outputs.transpose(1, 0, 2).reshape(queries.shape[0], queries.shape[1]), log_sums)


def attend_backward(
    queries, key_all, value_all, out_grads, log_sums, query_ids, key_ids, slot_size, lengths
):
    head_total = queries.shape[1] // HD
    block_rows = min(512, queries.shape[0])

    def one_head(head_index):
        query_head = lax.dynamic_slice_in_dim(queries, head_index * HD, HD, 1)
        key_head = lax.dynamic_slice_in_dim(key_all, head_index * HD, HD, 1)
        value_head = lax.dynamic_slice_in_dim(value_all, head_index * HD, HD, 1)
        grad_head = lax.dynamic_slice_in_dim(out_grads, head_index * HD, HD, 1)
        log_head = lax.dynamic_index_in_dim(log_sums, head_index, 0, keepdims=False)
        key_grad = jnp.zeros(key_head.shape, jnp.float32)
        value_grad = jnp.zeros(value_head.shape, jnp.float32)
        grad_block = grad_head[0:block_rows]
        scores = masked_scores(query_head, key_head, query_ids, key_ids, slot_size, lengths)
        probs = jnp.exp(scores - log_head[0:block_rows][:, None])
        probs_low = probs.astype(jnp.bfloat16)
        prob_grads = lax.dot_general(
            grad_block, value_head, (((1,), (1,)), ((), ())), preferred_element_type=jnp.float32
        )
        row_inner = jnp.sum(probs * prob_grads, axis=1, keepdims=True)
        score_grads = (probs * (prob_grads - row_inner)).astype(jnp.bfloat16)
        query_parts = [
            jnp.dot(score_grads, key_head, preferred_element_type=jnp.float32) * HD ** (-0.5)
        ]
        key_grad = key_grad + lax.dot_general(
            score_grads, query_head, (((0,), (0,)), ((), ())), preferred_element_type=jnp.float32
        ) * HD ** (-0.5)
        value_grad = value_grad + lax.dot_general(
            probs_low, grad_block, (((0,), (0,)), ((), ())), preferred_element_type=jnp.float32
        )
        return (jnp.concatenate(query_parts, axis=0), key_grad, value_grad)

    query_grad, key_grad, value_grad = lax.map(one_head, jnp.arange(head_total, dtype=jnp.int32))
    return (
        query_grad.transpose(1, 0, 2).reshape(queries.shape[0], queries.shape[1]),
        key_grad.transpose(1, 0, 2).reshape(key_all.shape[0], key_all.shape[1]),
        value_grad.transpose(1, 0, 2).reshape(value_all.shape[0], value_all.shape[1]),
    )


def fetch_prev(key_heads, value_heads, span_count):
    key_parts = [key_heads]
    value_parts = [value_heads]
    for offset in range(1, span_count):
        arrived = shifted((key_heads, value_heads), "blk", offset)
        key_parts.append(arrived[0])
        value_parts.append(arrived[1])
    return (jnp.concatenate(key_parts, axis=0), jnp.concatenate(value_parts, axis=0))


def router_probs(normed, router_w, mixing, prev_scores):
    logits = jnp.dot(normed, router_w, precision=highest) + jnp.dot(
        prev_scores, mixing, precision=highest
    )
    return jax.nn.softmax(logits, axis=-1)


def branch_sum(router_prob, normed, const_w, vector_w, outputs_pair, choose, live_rows, real_count):
    gate_values = jnp.sum(choose * router_prob[:, None, :], axis=-1)
    expert_share = jnp.sum(choose * gate_values[:, :, None], axis=1) * live_rows[:, None]
    routed = jnp.sum(gate_values[:, :, None] * outputs_pair, axis=1)
    routed = routed + expert_share[:, real_count + 1 : real_count + 2] * normed
    const_count = vector_w.shape[1]
    const_mix = jax.nn.softmax(
        jnp.dot(normed, const_w, precision=highest).reshape(normed.shape[0], const_count, 2),
        axis=-1,
    )
    for const_index in range(const_count):
        const_out = (
            const_mix[:, const_index, 0:1] * normed
            + const_mix[:, const_index, 1:2] * vector_w[:, const_index][None, :]
        )
        routed = (
            routed
            + expert_share[:, real_count + 2 + const_index : real_count + 3 + const_index]
            * const_out
        )
    return routed


def on_device(
    tokens,
    cotangent,
    prev_logits,
    routes,
    lengths,
    w_qkv,
    w_out,
    w_router,
    w_const,
    const_vec,
    norm_gains,
    gate_mix,
    expert_weights,
):
    tok_dev = tokens.shape[0]
    model_width = tokens.shape[1]
    head_count = lax.axis_size("head")
    blk_count = lax.axis_size("blk")
    span_count = max(8, min(blk_count // 4, 8192 // (head_count * tok_dev)) * min(1, tok_dev // 64))
    head_index = lax.axis_index("head")
    blk_index = lax.axis_index("blk")
    slot_size = span_count * head_count * tok_dev
    tok_blk = head_count * tok_dev
    qkv_w, out_w, router_w, const_w, vector_w, gain_pair = (
        lax.all_gather(w_qkv, ("head", "blk"), axis=0, tiled=True),
        lax.all_gather(w_out, ("head", "blk"), axis=0, tiled=True),
        lax.all_gather(w_router, ("head", "blk"), axis=0, tiled=True),
        lax.all_gather(w_const, ("head", "blk"), axis=0, tiled=True),
        lax.all_gather(const_vec, ("head", "blk"), axis=0, tiled=True),
        lax.all_gather(norm_gains, ("head", "blk"), axis=0, tiled=True),
    )
    gain_pair = gain_pair.astype(jnp.float32)
    row_ids = (blk_index * head_count + head_index) * tok_dev + jnp.arange(tok_dev, dtype=jnp.int32)
    slot_ids = row_ids // slot_size
    positions = row_ids - slot_ids * slot_size
    live_rows = (positions < slot_lengths(slot_ids, lengths)).astype(jnp.float32)
    inputs = tokens.astype(jnp.float32)
    normed_one, norm_one_back = jax.vjp(rms_norm, inputs, gain_pair[:, 0])
    normed_one_low = normed_one.astype(jnp.bfloat16)
    projected = jnp.dot(normed_one_low, qkv_w, preferred_element_type=jnp.float32).reshape(
        tok_dev, 3, HEADS, HD
    )
    query_send = (
        rotary(projected[:, 0], positions, 1.0).astype(jnp.bfloat16).reshape(tok_dev, model_width)
    )
    key_send = (
        rotary(projected[:, 1], positions, 1.0).astype(jnp.bfloat16).reshape(tok_dev, model_width)
    )
    value_send = projected[:, 2].astype(jnp.bfloat16).reshape(tok_dev, model_width)
    query_heads, key_heads, value_heads = (
        lax.all_to_all(query_send, "head", split_axis=1, concat_axis=0, tiled=True),
        lax.all_to_all(key_send, "head", split_axis=1, concat_axis=0, tiled=True),
        lax.all_to_all(value_send, "head", split_axis=1, concat_axis=0, tiled=True),
    )
    blk_rows = blk_index * tok_blk + jnp.arange(tok_blk, dtype=jnp.int32)
    blk_pos = blk_rows - blk_rows // slot_size * slot_size
    key_ids = jnp.concatenate([blk_rows - offset * tok_blk for offset in range(span_count)], axis=0)
    key_all, value_all = fetch_prev(key_heads, value_heads, span_count)
    attended, log_sums = attend_forward(
        query_heads, key_all, value_all, blk_rows, key_ids, slot_size, lengths
    )
    attended_tok = lax.all_to_all(
        attended.astype(jnp.bfloat16), "head", split_axis=0, concat_axis=1, tiled=True
    )
    residual = inputs + jnp.dot(attended_tok, out_w, preferred_element_type=jnp.float32)
    normed_two, norm_two_back = jax.vjp(rms_norm, residual, gain_pair[:, 1])
    normed_two_low = normed_two.astype(jnp.bfloat16)
    normed_two_f = normed_two_low.astype(jnp.float32)
    router_prob, router_back = jax.vjp(
        partial(router_probs, prev_scores=prev_logits),
        normed_two_f,
        router_w.astype(jnp.float32),
        gate_mix,
    )
    expert_count = router_w.shape[1]
    real_count = expert_weights.shape[1] * head_count
    choose = (
        routes[:, :, None] == jnp.arange(expert_count, dtype=jnp.int32)[None, None, :]
    ).astype(jnp.float32)
    count_local = jnp.sum(jnp.sum(choose, axis=1) * live_rows[:, None], axis=0)
    prob_local = jnp.sum(router_prob * live_rows[:, None], axis=0)
    count_all, prob_all = lax.psum((count_local, prob_local), ("head", "blk"))
    live_total = jnp.sum(lengths).astype(jnp.float32)
    fraction = count_all / (2.0 * live_total)
    aux_loss = expert_count * jnp.sum(fraction * (prob_all / live_total))
    gate_values = jnp.sum(choose * router_prob[:, None, :], axis=-1)
    out_grad = live_rows[:, None] * cotangent.astype(jnp.float32)
    assigned = routes.reshape(-1)
    live_pairs = jnp.repeat(live_rows, 2)
    is_real = (assigned < real_count) & (live_pairs > 0)
    onehot = (
        (assigned[:, None] == jnp.arange(real_count, dtype=jnp.int32)[None, :]) & is_real[:, None]
    ).astype(jnp.int32)
    slot_rank = jnp.sum((jnp.cumsum(onehot, axis=0) - onehot) * onehot, axis=1)
    target = jnp.where(is_real, assigned * CAP + slot_rank, real_count * CAP)
    source = (
        jnp.full((real_count * CAP + 1,), 2 * tok_dev, jnp.int32)
        .at[target]
        .set(jnp.arange(2 * tok_dev, dtype=jnp.int32))[: real_count * CAP]
    )
    zero_row = jnp.zeros((1, model_width), jnp.bfloat16)
    send_rows = jnp.concatenate([normed_two_low, zero_row], axis=0)[source // 2].reshape(
        real_count, CAP, model_width
    )
    pair_grads = (gate_values.reshape(-1, 1) * jnp.repeat(out_grad, 2, axis=0)).astype(jnp.bfloat16)
    send_grads = jnp.concatenate([pair_grads, zero_row], axis=0)[source].reshape(
        real_count, CAP, model_width
    )
    expert_in, expert_cot = (
        lax.all_to_all(send_rows, "head", split_axis=0, concat_axis=1, tiled=True),
        lax.all_to_all(send_grads, "head", split_axis=0, concat_axis=1, tiled=True),
    )
    weight_piece = lax.all_gather(expert_weights, "blk", axis=0, tiled=True)
    gate_w = weight_piece[:, :, 0, :]
    up_w = weight_piece[:, :, 1, :]
    down_w = weight_piece[:, :, 2, :]
    gate_part = jnp.einsum("esd,ned->esn", expert_in, gate_w, preferred_element_type=jnp.float32)
    up_part = jnp.einsum("esd,ned->esn", expert_in, up_w, preferred_element_type=jnp.float32)
    sigmoid_part = jax.nn.sigmoid(gate_part)
    silu_part = gate_part * sigmoid_part
    hidden = (silu_part * up_part).astype(jnp.bfloat16)
    out_sum = jnp.einsum("esn,ned->esd", hidden, down_w, preferred_element_type=jnp.float32)
    hidden_grad = jnp.einsum("esd,ned->esn", expert_cot, down_w, preferred_element_type=jnp.float32)
    gate_grad = (
        hidden_grad * up_part * (sigmoid_part * (1.0 + gate_part * (1.0 - sigmoid_part)))
    ).astype(jnp.bfloat16)
    up_grad = (hidden_grad * silu_part).astype(jnp.bfloat16)
    in_grad = jnp.einsum("esn,ned->esd", gate_grad, gate_w, preferred_element_type=jnp.float32)
    in_grad = in_grad + jnp.einsum(
        "esn,ned->esd", up_grad, up_w, preferred_element_type=jnp.float32
    )
    hidden_all = hidden
    gate_all = gate_grad
    up_all = up_grad
    out_sum, in_grad, hidden_all, gate_all, up_all = (
        out_sum,
        in_grad,
        hidden_all,
        gate_all,
        up_all,
    )
    hidden_own, gate_own, up_own = (
        lax.all_to_all(hidden_all, "blk", split_axis=2, concat_axis=1, tiled=True),
        lax.all_to_all(gate_all, "blk", split_axis=2, concat_axis=1, tiled=True),
        lax.all_to_all(up_all, "blk", split_axis=2, concat_axis=1, tiled=True),
    )
    rows_in = lax.all_gather(expert_in, "blk", axis=1, tiled=True)
    rows_cot = lax.all_gather(expert_cot, "blk", axis=1, tiled=True)
    gate_w_grad = jnp.einsum("esn,esd->ned", gate_own, rows_in, preferred_element_type=jnp.float32)
    up_w_grad = jnp.einsum("esn,esd->ned", up_own, rows_in, preferred_element_type=jnp.float32)
    down_w_grad = jnp.einsum(
        "esn,esd->ned", hidden_own, rows_cot, preferred_element_type=jnp.float32
    )
    expert_grads = jnp.stack([gate_w_grad, up_w_grad, down_w_grad], axis=2)
    returned, returned_grad = (
        lax.all_to_all(
            out_sum.astype(jnp.bfloat16), "head", split_axis=1, concat_axis=0, tiled=True
        ),
        lax.all_to_all(
            in_grad.astype(jnp.bfloat16), "head", split_axis=1, concat_axis=0, tiled=True
        ),
    )
    outputs_pair = (
        jnp.concatenate([returned.reshape(-1, model_width), zero_row], axis=0)[target]
        .astype(jnp.float32)
        .reshape(tok_dev, 2, model_width)
    )
    input_pair = (
        jnp.concatenate([returned_grad.reshape(-1, model_width), zero_row], axis=0)[target]
        .astype(jnp.float32)
        .reshape(tok_dev, 2, model_width)
    )
    expert_input_grad = input_pair[:, 0] + input_pair[:, 1]
    branch, branch_back = jax.vjp(
        partial(branch_sum, choose=choose, live_rows=live_rows, real_count=real_count),
        router_prob,
        normed_two_f,
        const_w.astype(jnp.float32),
        vector_w.astype(jnp.float32),
        outputs_pair,
    )
    output = ((residual + branch) * live_rows[:, None]).astype(jnp.bfloat16)
    prob_grad, normed_grad_branch, const_grad, vector_grad, unused_grad = branch_back(out_grad)
    aux_grad = aux_weight * expert_count / live_total * fraction[None, :] * live_rows[:, None]
    normed_grad_router, router_grad, mixing_grad = router_back(prob_grad + aux_grad)
    normed_grad = normed_grad_router + normed_grad_branch + expert_input_grad
    residual_grad_norm, gain_two_grad = norm_two_back(normed_grad)
    residual_grad = out_grad + residual_grad_norm
    out_w_grad = jnp.dot(attended_tok.astype(jnp.float32).T, residual_grad, precision=highest)
    attended_grad = jnp.dot(residual_grad, out_w.astype(jnp.float32).T, precision=highest).astype(
        jnp.bfloat16
    )
    attended_grad_heads = lax.all_to_all(
        attended_grad, "head", split_axis=1, concat_axis=0, tiled=True
    )
    key_again, value_again = fetch_prev(key_heads, value_heads, span_count)
    query_grad, key_grad, value_grad = attend_backward(
        query_heads,
        key_again,
        value_again,
        attended_grad_heads,
        log_sums,
        blk_rows,
        key_ids,
        slot_size,
        lengths,
    )
    own_key = key_grad[:tok_blk]
    own_value = value_grad[:tok_blk]
    for offset in range(1, span_count):
        back_key, back_value = shifted(
            (
                for_sending(key_grad[offset * tok_blk : (offset + 1) * tok_blk]),
                for_sending(value_grad[offset * tok_blk : (offset + 1) * tok_blk]),
            ),
            "blk",
            -offset,
        )
        own_key = own_key + back_key
        own_value = own_value + back_value
    local_heads = query_heads.shape[1] // HD
    query_back = (
        rotary(query_grad.reshape(tok_blk, local_heads, HD), blk_pos, -1.0)
        .astype(jnp.bfloat16)
        .reshape(tok_blk, local_heads * HD)
    )
    key_back = (
        rotary(own_key.reshape(tok_blk, local_heads, HD), blk_pos, -1.0)
        .astype(jnp.bfloat16)
        .reshape(tok_blk, local_heads * HD)
    )
    value_back = own_value.astype(jnp.bfloat16)
    query_tok, key_tok, value_tok = (
        lax.all_to_all(query_back, "head", split_axis=0, concat_axis=1, tiled=True),
        lax.all_to_all(key_back, "head", split_axis=0, concat_axis=1, tiled=True),
        lax.all_to_all(value_back, "head", split_axis=0, concat_axis=1, tiled=True),
    )
    projected_grad = jnp.concatenate([query_tok, key_tok, value_tok], axis=1)
    qkv_grad = jnp.dot(normed_one_low.T, projected_grad, preferred_element_type=jnp.float32)
    normed_one_grad = jnp.dot(projected_grad, qkv_w.T, preferred_element_type=jnp.float32)
    inputs_grad_norm, gain_one_grad = norm_one_back(normed_one_grad)
    token_grad = (residual_grad + inputs_grad_norm).astype(jnp.bfloat16)
    weight_grads = (
        lax.psum_scatter(qkv_grad, ("head", "blk"), scatter_dimension=0, tiled=True),
        lax.psum_scatter(out_w_grad, ("head", "blk"), scatter_dimension=0, tiled=True),
        lax.psum_scatter(router_grad, ("head", "blk"), scatter_dimension=0, tiled=True),
        lax.psum_scatter(const_grad, ("head", "blk"), scatter_dimension=0, tiled=True),
        lax.psum_scatter(vector_grad, ("head", "blk"), scatter_dimension=0, tiled=True),
        lax.psum_scatter(
            jnp.stack([gain_one_grad, gain_two_grad], axis=1),
            ("head", "blk"),
            scatter_dimension=0,
            tiled=True,
        ),
    )
    mixing_total = lax.psum(mixing_grad, ("head", "blk"))
    return (
        output,
        aux_loss,
        token_grad,
        weight_grads[0],
        weight_grads[1],
        weight_grads[2],
        weight_grads[3],
        weight_grads[4],
        weight_grads[5],
        mixing_total,
        expert_grads,
    )


def settle_kernel(n, *refs):
    sources, results, (sems, *rooms) = refs[:n], refs[n : 2 * n], refs[2 * n :]
    ins, outs = [], []
    for i in range(n):
        parts = [(sources[i], rooms[i], results[i])]
        if i == n - 1:
            parts = [tuple(r.at[pl.ds(32 * c, 32)] for r in parts[0]) for c in range(4)]
        for src, room, dst in parts:
            ins.append(pltpu.make_async_copy(src, room, sems.at[0, len(ins)]))
            outs.append(pltpu.make_async_copy(room, dst, sems.at[1, len(outs)]))
    for c in ins[::-1]:
        c.start()
    for c, d in zip(ins[::-1], outs[::-1]):
        c.wait()
        d.start()
    for d in outs:
        d.wait()


def settle(*arrays):
    hbm = pl.BlockSpec(memory_space=pl.ANY)
    n = len(arrays)
    return pl.pallas_call(
        functools.partial(settle_kernel, n),
        out_shape=tuple(jax.ShapeDtypeStruct(a.shape, a.dtype) for a in arrays),
        in_specs=[hbm] * n,
        out_specs=(hbm,) * n,
        scratch_shapes=[pltpu.SemaphoreType.DMA((2, n + 3))] + [pltpu.VMEM(a.shape, a.dtype) for a in arrays],
        compiler_params=pltpu.CompilerParams(vmem_limit_bytes=63 * 2**20),
        name="settle",
    )(*arrays)


def on_device_small(
    tokens, cotangent, prev_logits, routes, lengths, w_qkv, w_out, w_router, w_const, const_vec, norm_gains, gate_mix,
    expert_weights,
):
    n_blk = lax.axis_size("blk")
    w_all = lax.all_gather(w_qkv, ("head", "blk"), axis=0, tiled=True)
    norm, q, k, v, o, parts, g_exp, att, smt, cnt, local_out, res_grad, att_grad, g_small, misc, pg, small = front(
        lengths, tokens, cotangent, routes, w_qkv, w_router, w_const, norm_gains, const_vec, w_out, prev_logits, gate_mix,
        expert_weights.transpose(0, 2, 1, 3), n_blk)
    output, token_grad, qkv_grad, g_out, g_router, g_const, g_vec, g_gains, g_mix, aux = attend_back(
        lengths, att_grad, tokens, res_grad, smt, att, local_out, pg, g_small, misc, w_qkv, small, cnt, norm, q, k, v, o, w_all,
        parts, n_blk)
    results = settle(output, token_grad, qkv_grad, g_out, g_router, g_const, g_vec, g_gains, g_mix, aux, g_exp)
    output, token_grad, qkv_grad, g_out, g_router, g_const, g_vec, g_gains, g_mix, aux, g_exp = results
    return (
        output, aux.reshape(()), token_grad, qkv_grad, g_out, g_router.T, g_const.T, g_vec.T, g_gains.T, g_mix,
        g_exp.transpose(0, 2, 1, 3),
    )


def solution(mesh):
    small = mesh.shape["blk"] == 16 and mesh.shape["head"] == 2
    return jax.shard_map(
        on_device_small if small else on_device,
        mesh=mesh,
        in_specs=(
            P(("blk", "head"), None),
            P(("blk", "head"), None),
            P(("blk", "head"), None),
            P(("blk", "head"), None),
            P(),
            P(("head", "blk"), None),
            P(("head", "blk"), None),
            P(("head", "blk"), None),
            P(("head", "blk"), None),
            P(("head", "blk"), None),
            P(("head", "blk"), None),
            P(),
            P("blk", "head", None, None),
        ),
        out_specs=(
            P(("blk", "head"), None),
            P(),
            P(("blk", "head"), None),
            P(("head", "blk"), None),
            P(("head", "blk"), None),
            P(("head", "blk"), None),
            P(("head", "blk"), None),
            P(("head", "blk"), None),
            P(("head", "blk"), None),
            P(),
            P("blk", "head", None, None),
        ),
        check_vma=False,
    )
```

```python
from functools import partial
import functools
import math

import jax
import jax.numpy as jnp
import numpy as np
from jax import lax
from jax.experimental import pallas as pl
from jax.experimental.pallas import tpu as pltpu
from jax.sharding import PartitionSpec as P

HEADS = 12
MESH = pl.DeviceIdType.MESH
f32, bf16 = jnp.float32, jnp.bfloat16
NEG = -1e30
HD = 64
X, C, Y, Z = 1, 2, 4, 8
EARLY = (3, 2, 1)
Z_FIRST = (3, 2, 1)


def place(mask, h, b):
    hb = 1 - h if mask & X else h
    cb = b % 2
    yb = (b // 2) % 2
    zb = (b // 4) % 2
    cb = 1 - cb if mask & C else cb
    yb = 1 - yb if mask & Y else yb
    zb = 1 - zb if mask & Z else zb
    low = zb * 4 + yb * 2 + cb
    return hb, (b // 8) * 8 + low, low * 2 + hb


def head_of(h, b):
    quad = b % 4
    return h * 6 + ((b % 8) // 4) * 3 + quad - quad // 3


def home_of(head):
    h, i = head // 6, head % 6
    return ((i // 3) * 4 + i % 3) * 2 + h


def greet_all(h, b, n_blk):
    barrier = pltpu.get_barrier_semaphore()
    me = b * 2 + h
    total = 2 * n_blk

    def say(k, carry):
        other = (me + k) % total
        pl.semaphore_signal(barrier, inc=1, device_id=(other % 2, other // 2), device_id_type=MESH)
        return carry

    lax.fori_loop(1, total, say, 0)
    return lambda: pl.semaphore_wait(barrier, total - 1)


def turned(qk, cos, sin):
    lane = lax.broadcasted_iota(jnp.int32, qk.shape, 1)
    swapped = jnp.where(lane % 64 < 32, pltpu.roll(qk, 96, 1), pltpu.roll(qk, 32, 1))
    return qk * cos + swapped * sin


def rotary_tables(rows):
    freq = np.exp(np.arange(32, dtype=np.float32) * np.float32(-2.0 * math.log(10000.0) / 64)).astype(np.float32)
    ang = (np.arange(rows, dtype=np.float32)[:, None] * freq[None, :]).astype(np.float32).astype(np.float64)
    cos, sin = np.cos(ang), np.sin(ang)
    return (
        np.concatenate([cos, cos, cos, cos], 1).astype(np.float32),
        np.concatenate([-sin, sin, -sin, sin], 1).astype(np.float32),
    )


class RowGather:
    def __init__(self, buf, sems, h, b, straight=False):
        self.buf, self.h, self.b, self.straight = buf, h, b, straight
        self.parts = range(buf.shape[1])
        self.zs, self.ys, self.cs, self.zr, self.yr, self.cr = sems
        self.z, self.y, self.c = b // 4, (b // 2) % 2, b % 2

    def nth(self, k):
        return nearest(self.z, k)

    def at(self, z, y, c, p):
        return self.buf.at[z * 4 + y * 2 + c, p]

    def copy(self, where, send, recv, device):
        return pltpu.make_async_remote_copy(
            src_ref=where, dst_ref=where, send_sem=send, recv_sem=recv, device_id=device, device_id_type=MESH)

    def along_z(self, k, step, p):
        zz = self.nth(k)
        return self.copy(self.at(zz, self.y, self.c, p), self.zs.at[(step + 1) // 2, k, p], self.zr.at[zz, p],
                         (self.h, self.b + 4 * step))

    def to_z(self, k, p):
        return self.copy(self.at(self.z, self.y, self.c, p), self.zs.at[0, k, p], self.zr.at[self.z, p],
                         (self.h, self.nth(k) * 4 + self.b % 4))

    def over_y(self, k, p):
        zz = self.nth(k)
        return self.copy(self.at(zz, self.y, self.c, p), self.ys.at[k, p], self.yr.at[zz, p],
                         (self.h, self.b + 2 - 4 * self.y))

    def over_core(self, k, far, p):
        zz = self.nth(k)
        yy = 1 - self.y if far else self.y
        return self.copy(self.at(zz, yy, self.c, p), self.cs.at[far, k, p], self.cr.at[far, zz, p],
                         (self.h, self.b + 1 - 2 * self.c))

    def own_z(self, act):
        for p in self.parts:
            if self.straight:
                for k in range(1, 4):
                    act(self.to_z(k, p))
            else:
                for step in (1, -1):
                    @pl.when((self.z + step >= 0) & (self.z + step <= 3))
                    def _(step=step, p=p):
                        act(self.along_z(0, step, p))

    def relay(self, k, p, act):
        if self.straight:
            return
        zz = self.nth(k)

        @pl.when((zz < self.z) & (self.z < 3))
        def _():
            act(self.along_z(k, 1, p))

        @pl.when((zz > self.z) & (self.z > 0))
        def _():
            act(self.along_z(k, -1, p))

    def start(self):
        self.own_z(lambda c: c.start())
        for p in self.parts:
            self.over_y(0, p).start()
        for p in self.parts:
            self.over_core(0, 0, p).start()

    def arrived(self, where, sem):
        self.copy(where, self.zs.at[0, 0, 0], sem, (self.h, self.b)).wait_recv()

    def got_z(self, k):
        zz = self.nth(k)
        for p in self.parts:
            self.arrived(self.at(zz, self.y, self.c, p), self.zr.at[zz, p])
            self.relay(k, p, lambda c: c.start())
            self.over_y(k, p).start()
            self.over_core(k, 0, p).start()

    def got_y(self, k):
        zz = self.nth(k)
        for p in self.parts:
            self.arrived(self.at(zz, 1 - self.y, self.c, p), self.yr.at[zz, p])
            self.over_core(k, 1, p).start()

    def got_core(self, k):
        zz = self.nth(k)
        for far in range(2):
            yy = 1 - self.y if far else self.y
            for p in self.parts:
                self.arrived(self.at(zz, yy, 1 - self.c, p), self.cr.at[far, zz, p])

    def finish(self):
        self.own_z(lambda c: c.wait_send())
        for p in self.parts:
            for k in range(4):
                if k:
                    self.relay(k, p, lambda c: c.wait_send())
                self.over_y(k, p).wait_send()
                self.over_core(k, 0, p).wait_send()
                self.over_core(k, 1, p).wait_send()


def nearest(z, k):
    near = z - (z // 2) * (2 * z - 3)
    low = k + (1 - 2 * k) * near if k < 2 else k
    return low + (z // 2) * (3 - 2 * low)


def gather_sems(parts):
    DMA = pltpu.SemaphoreType.DMA
    return [DMA((2, 4, parts)), DMA((4, parts)), DMA((2, 4, parts)), DMA((4, parts)), DMA((4, parts)), DMA((2, 4, parts))]


def fold(rows):
    half = rows.shape[1] // 2
    low = jnp.concatenate([rows[16:24, :half], rows[16:24, half:]], axis=0)
    return jnp.concatenate([rows[0:16], low], axis=1).astype(bf16)


def routing_table(routes, live):
    lane = lax.broadcasted_iota(jnp.int32, (128, 128), 1)
    row = lax.broadcasted_iota(jnp.int32, (128, 128), 0)
    expert = lane.astype(f32)
    named = jnp.where((routes[:, 0:1] == expert) | (routes[:, 1:2] == expert), live, 0.0)
    before = jnp.where(lane < row, 1.0, 0.0).astype(bf16)
    rank = jnp.dot(before, named.astype(bf16), preferred_element_type=f32)
    return named, named * (rank + 1.0)


def expert_lanes(h):
    e = lax.broadcasted_iota(jnp.int32, (128, 256), 0)
    s = lax.broadcasted_iota(jnp.int32, (128, 256), 1)
    return jnp.where((s < 192) & (e == 4 * h + s // 48), 1.0, 0.0)


def slot_table(ranks, h, source_h):
    spread = jnp.dot(ranks.astype(bf16), expert_lanes(h).astype(bf16), preferred_element_type=f32)
    s = lax.broadcasted_iota(jnp.int32, (128, 256), 1)
    place_in = s % 48 - 24 * source_h
    inside = (place_in >= 0) & (place_in < 24) & (s < 192)
    return jnp.where(inside & (spread == (place_in + 1).astype(f32)), 1.0, 0.0)


def live_column(h, b, length):
    row = lax.broadcasted_iota(jnp.int32, (128, 1), 0) + ((b % 8) * 2 + h) * 128
    return jnp.where(row < length, 1.0, 0.0)


def forward_kernel(
    n_blk, all_here, lengths, tok, cot, routes, w_in, small, wo_in, cos_hbm, sin_hbm, relay_w,
    norm_hbm, q_hbm, k_hbm, v_hbm, o_hbm, att_out, smt_out, cnt_out, sm_out, wo_out, pt_out, cot_rows,
    xg, pieces, got, w_f, w_b, cos, sin, norm, q, k, v, o, sendbuf, att_in, rank_own, rank_far, cot_far, wo_all,
    ag_send, ag_recv, pc_send, pc_recv, at_send, at_recv, loc, x_send, x_recv, *gathers,
):
    h, b = lax.axis_index("head"), lax.axis_index("blk")
    me = b * 2 + h
    total = 2 * n_blk
    _, _, rank = place(0, h, b)
    cos_in = pltpu.make_async_copy(cos_hbm, cos, loc.at[9])
    sin_in = pltpu.make_async_copy(sin_hbm, sin, loc.at[10])
    cos_in.start()
    sin_in.start()
    for p in range(3):
        xg[p, rank] = tok[:, 256 * p : 256 * p + 256]
    all_here()

    def block_copy(p, m, d, slot):
        _, _, r = place(m, h, b)
        ph, pb, _ = place(d, h, b)
        return pltpu.make_async_remote_copy(
            src_ref=xg.at[p, r], dst_ref=xg.at[p, r],
            send_sem=ag_send.at[p, slot], recv_sem=ag_recv.at[p, m ^ d],
            device_id=(ph, pb), device_id_type=MESH,
        )

    def arrival(p, m):
        _, _, r = place(m, h, b)
        return pltpu.make_async_remote_copy(
            src_ref=xg.at[p, r], dst_ref=xg.at[p, r],
            send_sem=ag_send.at[p, 0], recv_sem=ag_recv.at[p, m],
            device_id=(h, b), device_id_type=MESH,
        )

    sends = []
    counts = [0, 0, 0]

    def send(p, m, d):
        copy = block_copy(p, m, d, counts[p])
        counts[p] += 1
        copy.start()
        sends.append(copy)

    dims = [X, Y, Z]
    orders = [dims[p:] + dims[:p] for p in range(3)]
    for t in range(3):
        for p in range(3):
            send(p, 0, orders[p][t])
    for p in range(3):
        send(p, 0, C)

    length = lengths[b // 8]
    named, ranks = routing_table(routes[...], live_column(h, b, length))
    rank_own[...] = ranks.astype(bf16)
    wo_all[b, 0, h] = fold(wo_in[...].astype(f32))

    w24 = w_in[...].astype(f32)
    count = pltpu.roll(jnp.sum(named, axis=0, keepdims=True), 20, 1)[:, 0:64]
    small = small[...] + jnp.where(lax.broadcasted_iota(jnp.int32, (24, 64), 0) == 0, count, 0.0)
    for j in range(12):
        cat = jnp.concatenate(
            [w24[:, 64 * j : 64 * j + 64], w24[:, 768 + 64 * j : 832 + 64 * j],
             w24[:, 1536 + 64 * j : 1600 + 64 * j], small], axis=1)
        pieces[j] = fold(cat)

    def piece_copy(kk):
        other = (me + kk) % total
        oh, ob = other % 2, other // 2
        return pltpu.make_async_remote_copy(
            src_ref=pieces.at[head_of(oh, ob)], dst_ref=got.at[me],
            send_sem=pc_send.at[kk], recv_sem=pc_recv.at[me],
            device_id=(oh, ob), device_id_type=MESH,
        )

    def send_piece(kk, carry):
        piece_copy(kk).start()
        return carry

    lax.fori_loop(1, total, send_piece, 0)
    got[me] = pieces[head_of(h, b)]

    relay_w(0)
    for p in range(3):
        d0, d1, d2 = orders[p]
        arrival(p, d0).wait_recv()
        for d in (d1, d2, C):
            send(p, d0, d)
    relay_w(1)
    for p in range(3):
        d0, d1, d2 = orders[p]
        for m in (d1, d0 ^ d1):
            arrival(p, m).wait_recv()
            for d in (d2, C):
                send(p, m, d)
    swaps = [
        pltpu.make_async_remote_copy(
            src_ref=src, dst_ref=dst, send_sem=x_send.at[n], recv_sem=x_recv.at[n],
            device_id=(1 - h, b), device_id_type=MESH)
        for n, (src, dst) in enumerate([(wo_all.at[b, 0, h], wo_all.at[b, 0, h]), (rank_own, rank_far), (cot, cot_far)])
    ]
    for c in swaps:
        c.start()
    relay_w(2)
    for p in range(3):
        d0, d1, d2 = orders[p]
        for m in (d2, d0 ^ d2, d1 ^ d2, d0 ^ d1 ^ d2):
            arrival(p, m).wait_recv()
            send(p, m, C)

    def take_piece(kk, carry):
        src = (me + kk) % total
        pltpu.make_async_remote_copy(
            src_ref=pieces.at[0], dst_ref=got.at[src],
            send_sem=pc_send.at[0], recv_sem=pc_recv.at[src],
            device_id=(h, b), device_id_type=MESH,
        ).wait_recv()
        return carry

    lax.fori_loop(1, total, take_piece, 0)

    for src in range(2 * n_blk):
        row = 24 * ((src % 2) * n_blk + src // 2)
        w_f[row : row + 16, :] = got[src, :, 0:256].astype(f32)
        low = got[src, :, 256:384].astype(f32)
        w_f[row + 16 : row + 24, 0:128] = low[0:8]
        w_f[row + 16 : row + 24, 128:256] = low[8:16]
    w_b[...] = w_f[...].astype(bf16)
    sm = pltpu.roll(w_f[:, 128:256], 64, 1)
    lane = lax.broadcasted_iota(jnp.int32, (768, 128), 1)
    cnt = jnp.sum(jnp.where((lane >= 20) & (lane < 32), sm, 0.0), axis=0, keepdims=True)
    cnt_out[...] = jnp.broadcast_to(pltpu.roll(cnt, 108, 1), (8, 128))
    sm = jnp.where(lane < 20, sm, 0.0)
    sm_out[...] = sm.astype(bf16)
    smt = jnp.transpose(sm)
    smt_out[...] = smt[0:32, :]
    gain = smt[16:17, :]

    pltpu.make_async_remote_copy(
        src_ref=wo_all.at[b, 0, h], dst_ref=wo_all.at[b, 0, 1 - h], send_sem=x_send.at[0], recv_sem=x_recv.at[0],
        device_id=(h, b), device_id_type=MESH).wait_recv()
    wo_gather = RowGather(wo_all, gathers[0:6], h, b, straight=True)
    wo_gather.start()
    swaps[1].wait_recv()
    swaps[2].wait_recv()
    pt = [slot_table(ranks, h, h).astype(bf16), slot_table(rank_far[...].astype(f32), h, 1 - h).astype(bf16)]
    pt_out[0] = pt[0]
    pt_out[1] = pt[1]
    picked = sum(
        lax.dot_general(t[:, 0:192], c[...], (((0,), (0,)), ((), ())), preferred_element_type=f32)
        for t, c in zip(pt, (cot, cot_far))).astype(bf16)
    cot_rows[b, 0] = picked[0:96]
    cot_rows[b, 1] = picked[96:192]
    cot_gather = RowGather(cot_rows, gathers[6:12], h, b, straight=True)
    cot_gather.start()

    cos_in.wait()
    sin_in.wait()

    def one_block(r, carry):
        x = [xg[p, r].astype(f32) for p in range(3)]
        mean = sum(jnp.sum(t * t, axis=1, keepdims=True) for t in x) * (1.0 / 768)
        scale = lax.rsqrt(mean + 1e-6)
        rows = pl.ds(pl.multiple_of(r * 128, 128), 128)
        acc = jnp.zeros((128, 256), f32)
        for p in range(3):
            n = (x[p] * scale * gain[:, 256 * p : 256 * p + 256]).astype(bf16)
            norm[rows, 256 * p : 256 * p + 256] = n
            acc = acc + jnp.dot(n, w_b[256 * p : 256 * p + 256, :], preferred_element_type=f32)
        qk = turned(acc[:, 0:128], cos[rows, :], sin[rows, :])
        q[rows, :] = (qk[:, 0:64] * 0.125).astype(bf16)
        k[rows, :] = qk[:, 64:128].astype(bf16)
        lane = lax.broadcasted_iota(jnp.int32, (128, 128), 1)
        v[rows, :] = jnp.where(lane < 64, acc[:, 128:256], jnp.where(lane == 64, 1.0, 0.0)).astype(bf16)
        return carry

    def of_core(core):
        return lambda i, carry: one_block((i // 4) * 8 + ((i // 2) % 2) * 4 + core * 2 + i % 2, carry)

    lax.fori_loop(0, 8, of_core(b % 2), 0)
    for p in range(3):
        for m in (C, C ^ X, C ^ Y, C ^ Z, C ^ X ^ Y, C ^ X ^ Z, C ^ Y ^ Z, C ^ X ^ Y ^ Z):
            arrival(p, m).wait_recv()
    lax.fori_loop(0, 8, of_core(1 - b % 2), 0)
    stores = [
        pltpu.make_async_copy(norm, norm_hbm, loc.at[4]),
        pltpu.make_async_copy(q, q_hbm, loc.at[5]),
        pltpu.make_async_copy(k, k_hbm, loc.at[6]),
        pltpu.make_async_copy(v, v_hbm, loc.at[7]),
    ]
    for s in stores:
        s.start()

    head = head_of(h, b)
    working = (b % 4) != 3
    base = (b // 8) * 8

    w, c = wo_gather, cot_gather
    between = {
        0: [lambda: w.got_z(1), lambda: w.got_y(0)],
        1: [lambda: w.got_z(2), lambda: w.got_z(3)],
        2: [lambda: w.got_y(1)],
        3: [lambda: w.got_y(2), lambda: c.got_z(1)],
        4: [lambda: w.got_y(3)],
        5: [lambda: w.got_core(0), lambda: w.got_core(1), lambda: c.got_y(0)],
        6: [lambda: w.got_core(2), lambda: w.got_core(3)],
        7: [],
    }

    def out_copy(r):
        return pltpu.make_async_remote_copy(
            src_ref=sendbuf.at[r], dst_ref=att_in.at[head],
            send_sem=at_send.at[r], recv_sem=at_recv.at[head],
            device_id=(r % 2, base + r // 2), device_id_type=MESH,
        )

    for i in range(8):
        width = 256 * (i + 1)
        s = lax.dot_general(q[256 * i : width, :], k[0:width, :], (((1,), (1,)), ((), ())), preferred_element_type=f32)
        key = lax.broadcasted_iota(jnp.int32, (1, width), 1)
        s = s + jnp.where(key < length, 0.0, NEG)
        rowi = lax.broadcasted_iota(jnp.int32, (256, 256), 0)
        coli = lax.broadcasted_iota(jnp.int32, (256, 256), 1)
        last = jnp.where(coli <= rowi, s[:, width - 256 :], NEG)
        s = last if i == 0 else jnp.concatenate([s[:, : width - 256], last], axis=1)
        m = jnp.max(s, axis=1, keepdims=True)
        e = jnp.exp(s - m).astype(bf16)
        ov = jnp.dot(e, v[0:width, :], preferred_element_type=f32)
        l = ov[:, 64:65]
        lane = lax.broadcasted_iota(jnp.int32, (256, 128), 1)
        ov = jnp.where(lane < 64, ov / l, m + jnp.log(l))
        o[256 * i : width, :] = ov
        oh = ov[:, 0:64]
        for half in range(2):
            r = 2 * i + half
            packed = jnp.concatenate([oh[128 * half : 128 * half + 64], oh[128 * half + 64 : 128 * half + 128]], axis=1)
            sendbuf[r] = packed.astype(bf16)

            @pl.when(working & (r != rank))
            def _(r=r):
                out_copy(r).start()
        for act in between[i]:
            act()

    o_store = pltpu.make_async_copy(o, o_hbm, loc.at[8])
    o_store.start()

    def unfolded(blk, hh):
        t = wo_all[blk, 0, hh].astype(f32)
        return jnp.concatenate(
            [t[:, 0:768], jnp.concatenate([t[0:8, 768:1152], t[8:16, 768:1152]], axis=1)], axis=0)

    for hh in range(2):
        for blk in range(0, 16, 2):
            row = 24 * (hh * 16 + blk)
            wo_out[row : row + 48, :] = jnp.concatenate([unfolded(blk, hh), unfolded(blk + 1, hh)], axis=0).astype(bf16)

    @pl.when(working)
    def _():
        att_in[head] = sendbuf[rank]

    for j in range(12):
        @pl.when(rank != home_of(j))
        def _(j=j):
            pltpu.make_async_remote_copy(
                src_ref=sendbuf.at[0], dst_ref=att_in.at[j],
                send_sem=at_send.at[0], recv_sem=at_recv.at[j],
                device_id=(h, b), device_id_type=MESH,
            ).wait_recv()

    for j in range(0, 12, 2):
        one, two = att_in[j].astype(f32), att_in[j + 1].astype(f32)
        att_out[0:64, 64 * j : 64 * j + 128] = jnp.concatenate([one[:, 0:64], two[:, 0:64]], axis=1).astype(bf16)
        att_out[64:128, 64 * j : 64 * j + 128] = jnp.concatenate([one[:, 64:128], two[:, 64:128]], axis=1).astype(bf16)

    def finish():
        for copy in sends:
            copy.wait_send()
        for c in swaps:
            c.wait_send()
        wo_gather.finish()
        cot_gather.finish()

        def sent_piece(kk, carry):
            piece_copy(kk).wait_send()
            return carry

        lax.fori_loop(1, total, sent_piece, 0)
        for r in range(16):
            @pl.when(working & (r != rank))
            def _(r=r):
                out_copy(r).wait_send()
        for s in stores:
            s.wait()
        o_store.wait()

    return cot_gather, finish


def split(x):
    high = x.astype(bf16)
    return high, (x - high.astype(f32)).astype(bf16)


def exact_dot(x, y, dims):
    high, low = split(x)
    return lax.dot_general(high, y, (dims, ((), ())), preferred_element_type=f32) + lax.dot_general(
        low, y, (dims, ((), ())), preferred_element_type=f32)


def softmax_back(p, d):
    return p * (d - jnp.sum(p * d, axis=1, keepdims=True))


def lane_of(column, n):
    lane = lax.broadcasted_iota(jnp.int32, (128, 128), 1)
    return jnp.where(lane == n, column, 0.0)


class RowScatter:
    def __init__(self, part, from_core, from_y, from_z, sems, h, b):
        self.part, self.from_core, self.from_y, self.from_z = part, from_core, from_y, from_z
        self.h, self.b = h, b
        self.cs, self.cr, self.ys, self.yr, self.zs, self.zr = sems
        self.parts = range(part.shape[1])
        self.order = [(k, p) for k in (3, 2, 1, 0) for p in self.parts]
        self.z, self.y, self.c = b // 4, (b // 2) % 2, b % 2

    def nth(self, k):
        return nearest(self.z, k)

    def blk(self, k, far_y, far_c):
        y = 1 - self.y if far_y else self.y
        c = 1 - self.c if far_c else self.c
        return self.nth(k) * 4 + y * 2 + c

    def remote(self, src, dst, send, recv, device):
        return pltpu.make_async_remote_copy(
            src_ref=src, dst_ref=dst, send_sem=send, recv_sem=recv, device_id=device, device_id_type=MESH)

    def core(self, k, far, p):
        return self.remote(self.part.at[self.blk(k, far, 1), p], self.from_core.at[k, far, p], self.cs.at[k, far, p],
                           self.cr.at[k, far, p], (self.h, self.b + 1 - 2 * self.c))

    def over_y(self, k, p):
        return self.remote(self.part.at[self.blk(k, 1, 0), p], self.from_y.at[k, p], self.ys.at[k, p], self.yr.at[k, p],
                           (self.h, self.b + 2 - 4 * self.y))

    def to_z(self, k, p):
        return self.remote(self.part.at[self.blk(k, 0, 0), p], self.from_z.at[self.z, p], self.zs.at[k, p],
                           self.zr.at[self.z, p], (self.h, self.nth(k) * 4 + self.b % 4))

    def join_y(self, k, p):
        self.core(k, 0, p).wait_recv()
        self.over_y(k, p).wait_recv()
        self.add(self.blk(k, 0, 0), p, self.from_core.at[k, 0, p], self.from_y.at[k, p])

    def add(self, blk, p, *others):
        total = self.part[blk, p].astype(f32)
        for other in others:
            total = total + other[...].astype(f32)
        self.part[blk, p] = total.astype(bf16)

    def send_core(self, k, p):
        self.core(k, 1, p).start()
        self.core(k, 0, p).start()

    def send_y(self, k, p):
        self.core(k, 1, p).wait_recv()
        self.add(self.blk(k, 1, 0), p, self.from_core.at[k, 1, p])
        self.over_y(k, p).start()

    def send_z(self, k, p):
        self.join_y(k, p)
        if k:
            self.to_z(k, p).start()

    def total(self, p):
        total = self.part[self.b, p].astype(f32)
        for k in range(1, 4):
            here = self.from_z.at[self.nth(k), p]
            self.remote(here, here, self.zs.at[0, 0], self.zr.at[self.nth(k), p], (self.h, self.b)).wait_recv()
            total = total + here[...].astype(f32)
        return total

    def finish(self, near=range(4), far=range(1, 4)):
        for p in self.parts:
            for k in near:
                self.core(k, 0, p).wait_send()
                self.core(k, 1, p).wait_send()
                self.over_y(k, p).wait_send()
            for k in far:
                self.to_z(k, p).wait_send()


def scatter_scratch(parts, rows, cols):
    DMA = pltpu.SemaphoreType.DMA
    V = pltpu.VMEM
    return [
        V((4, 2, parts, rows, cols), bf16), V((4, parts, rows, cols), bf16), V((4, parts, rows, cols), bf16),
        DMA((4, 2, parts)), DMA((4, 2, parts)), DMA((4, parts)), DMA((4, parts)), DMA((4, parts)), DMA((4, parts)),
    ]


def expert_kernel(
    n_blk, cg, lengths, att, tok, cot, prev, mix, routes, wout, sm, smt, cnt, pt, w, cot_all,
    part_hbm, g_hbm, local_out, res_out, ag_out, gs_out, misc_out, pg_out,
    x_all, cc, dgu, hid, inp, outp, gbuf, gates_in, vs_out, vs_in, n_own, n_far, g_own, g_far,
    d_out, d_in, dv_out, dv_in, ga_send, ga_recv, vs_send, vs_recv, x_send, x_recv, loc, *rest,
):
    gsems, (from_core, from_y, from_z), ssems, (out_core, out_y), osems = rest[0:6], rest[6:9], rest[9:15], rest[15:17], rest[17:21]
    h, b = lax.axis_index("head"), lax.axis_index("blk")
    length = lengths[b // 8]
    live_total = (lengths[0] + lengths[1]).astype(f32)
    live = live_column(h, b, length)
    lane = lax.broadcasted_iota(jnp.int32, (128, 128), 1)

    res = tok[...].astype(f32) + jnp.dot(att[...], wout[...], preferred_element_type=f32)
    scale = lax.rsqrt(jnp.sum(res * res, axis=1, keepdims=True) * (1.0 / 768) + 1e-6)
    xh = res * scale
    n2 = (xh * smt[17:18, :]).astype(bf16)
    small = sm[...]
    logits = jnp.dot(n2, small, preferred_element_type=f32)
    router = logits + jnp.dot(prev[...], mix[...], preferred_element_type=f32, precision=lax.Precision.HIGHEST)
    router = jnp.where(lane < 12, router, NEG)
    prob = jnp.exp(router - jnp.max(router, axis=1, keepdims=True))
    prob = prob / jnp.sum(prob, axis=1, keepdims=True)
    expert = lane.astype(f32)
    named = jnp.where((routes[:, 0:1] == expert) | (routes[:, 1:2] == expert), 1.0, 0.0)
    gates = prob * named
    n_own[...] = n2
    g_own[...] = gates
    swaps = [
        pltpu.make_async_remote_copy(
            src_ref=src, dst_ref=dst, send_sem=x_send.at[n], recv_sem=x_recv.at[n],
            device_id=(1 - h, b), device_id_type=MESH)
        for n, (src, dst) in enumerate([(n_own, n_far), (g_own, g_far), (d_out, d_in), (dv_out, dv_in)])
    ]
    swaps[0].start()
    swaps[1].start()
    cg.got_z(2)
    cg.got_y(1)
    p_own, p_far = pt[0, :, 0:192], pt[1, :, 0:192]
    rows = ((0,), (0,))
    mine = lax.dot_general(p_own, n2, (rows, ((), ())), preferred_element_type=f32)
    spread = expert_lanes(h).astype(bf16)
    pg_own = pt[0].astype(f32) * exact_dot(gates, spread, ((1,), (0,)))
    pg_out[0] = pg_own
    swaps[0].wait_recv()
    picked = (mine + lax.dot_general(p_far, n_far[...], (rows, ((), ())), preferred_element_type=f32)).astype(bf16)
    x_all[b, 0] = picked[0:96]
    x_all[b, 1] = picked[96:192]
    g = RowGather(x_all, gsems, h, b)
    g.start()
    cg.got_z(3)
    cg.got_y(2)
    cg.got_y(3)
    swaps[1].wait_recv()
    pg_far = pt[1].astype(f32) * exact_dot(g_far[...], spread, ((1,), (0,)))
    pg_out[1] = pg_far
    gates_in[b] = jnp.broadcast_to(jnp.sum(pg_own + pg_far, axis=0, keepdims=True), (8, 256))

    def gate_copy(k):
        return pltpu.make_async_remote_copy(
            src_ref=gates_in.at[b], dst_ref=gates_in.at[b], send_sem=ga_send.at[k], recv_sem=ga_recv.at[b],
            device_id=(h, (b + k) % n_blk), device_id_type=MESH)

    def vs_copy(k):
        to = (b + k) % n_blk
        return pltpu.make_async_remote_copy(
            src_ref=vs_out.at[to], dst_ref=vs_in.at[b], send_sem=vs_send.at[k], recv_sem=vs_recv.at[b],
            device_id=(h, to), device_id_type=MESH)

    def each(act):
        def body(k, carry):
            act(k)
            return carry

        lax.fori_loop(1, n_blk, body, 0)

    each(lambda k: gate_copy(k).start())

    def group(ref, k, p, ee):
        return ref[pl.ds(4 * g.nth(k), 4), p, 48 * ee : 48 * ee + 48, :]

    def put(ref, k, p, ee, value):
        ref[pl.ds(4 * g.nth(k), 4), p, 48 * ee : 48 * ee + 48, :] = value.reshape(4, 48, value.shape[1]).astype(ref.dtype)

    cols = ((1,), (1,))

    def cot_task(k):
        for e in range(4):
            rows_c = group(cot_all, k, e // 2, e % 2).reshape(192, 768)
            put(cc, k, e // 2, e % 2, lax.dot_general(rows_c, w[3 * e + 2], (cols, ((), ())), preferred_element_type=f32))

    def up_task(k):
        for e in range(4):
            p, ee = e // 2, e % 2
            x = group(x_all, k, p, ee).reshape(192, 768)
            both = lax.dot_general(x, w[3 * e : 3 * e + 2].reshape(256, 768), (cols, ((), ())), preferred_element_type=f32)
            gate, up = both[:, 0:128], both[:, 128:256]
            sig = 1.0 / (1.0 + jnp.exp(-gate))
            silu = gate * sig
            hidden = silu * up
            c = group(cc, k, p, ee).reshape(192, 128)
            put(hid, k, p, ee, hidden)
            put(cc, k, p, ee, hidden * c)
            dg = c * up * (sig * (1.0 + gate * (1.0 - sig)))
            put(dgu, k, p, ee, jnp.concatenate([dg, c * silu], axis=1))

    two = jnp.where(lane % 2 == 0, pltpu.roll(logits, 127, 1), pltpu.roll(logits, 1, 1))
    top = jnp.maximum(logits, two)
    c_mix = jnp.exp(logits - top) / (jnp.exp(logits - top) + jnp.exp(two - top))
    share = gates * live
    n2f = n2.astype(f32)
    alpha = share[:, 9:10] + share[:, 10:11] * c_mix[:, 12:13] + share[:, 11:12] * c_mix[:, 14:15]
    beta = [share[:, 10:11] * c_mix[:, 13:14], share[:, 11:12] * c_mix[:, 15:16]]
    local_out[...] = live * (res + alpha * n2f + beta[0] * smt[18:19, :] + beta[1] * smt[19:20, :])
    og = live * cot[...].astype(f32)
    og_low = og.astype(bf16)

    g.got_z(1)
    cg.got_core(0)
    cot_task(0)
    g.got_z(2)
    g.got_y(0)
    cg.got_core(1)
    cot_task(1)
    g.got_z(3)
    g.got_y(1)
    cg.got_core(2)
    cot_task(2)
    cg.got_core(3)
    cot_task(3)
    g.got_core(0)
    up_task(0)
    g.got_y(2)
    g.got_core(1)
    up_task(1)
    g.got_y(3)
    g.got_core(2)
    up_task(2)
    g.got_core(3)
    up_task(3)

    s = RowScatter(inp, from_core, from_y, from_z, ssems, h, b)
    order = s.order
    for n, (k, p) in enumerate(order):
        for ee in range(2):
            e = 2 * p + ee
            d = group(dgu, k, p, ee).reshape(192, 256)
            put(inp, k, p, ee, jnp.dot(d, w[3 * e : 3 * e + 2].reshape(256, 768), preferred_element_type=f32))
        s.send_core(k, p)
        if n:
            s.send_y(*order[n - 1])
    s.send_y(*order[7])

    ones = jnp.ones((8, 128), f32)

    def one_blk(j, carry):
        for p in range(2):
            vs_out[j, :, 128 * p : 128 * p + 96] = lax.dot_general(
                ones, cc[j, p], (cols, ((), ())), preferred_element_type=f32, precision=lax.Precision.HIGHEST)
        return carry

    lax.fori_loop(0, n_blk, one_blk, 0)
    each(lambda k: vs_copy(k).start())
    vs_in[b] = vs_out[b]
    each(lambda k: pltpu.make_async_remote_copy(
        src_ref=gates_in.at[b], dst_ref=gates_in.at[(b + k) % n_blk], send_sem=ga_send.at[0],
        recv_sem=ga_recv.at[(b + k) % n_blk], device_id=(h, b), device_id_type=MESH).wait_recv())
    gate_cols = jnp.transpose(gates_in[:, 0, :])

    def scaled(ref, p, ee):
        e = 2 * p + ee
        t = ref[:, p, 48 * ee : 48 * ee + 48, :].astype(f32)
        col = jnp.concatenate([gate_cols[48 * e : 48 * e + 48, j : j + 1] for j in range(n_blk)], axis=0)
        return (t.reshape(48 * n_blk, t.shape[2]) * col).astype(bf16)

    def store_g(e, act):
        for kind in range(3):
            act(pltpu.make_async_copy(gbuf.at[kind], g_hbm.at[:, kind, e, :], loc.at[kind]))

    def weight_task(e):
        p, ee = e // 2, e % 2
        x = x_all[:, p, 48 * ee : 48 * ee + 48, :].reshape(48 * n_blk, 768)
        c = cot_all[:, p, 48 * ee : 48 * ee + 48, :].reshape(48 * n_blk, 768)
        if e:
            store_g(e - 1, lambda c: c.wait())
        gbuf[0:2] = lax.dot_general(
            scaled(dgu, p, ee), x, (rows, ((), ())), preferred_element_type=f32).reshape(2, 128, 768)
        gbuf[2] = lax.dot_general(scaled(hid, p, ee), c, (rows, ((), ())), preferred_element_type=f32)
        store_g(e, lambda c: c.start())

    def out_task(k):
        for e in range(4):
            d = group(hid, k, e // 2, e % 2).reshape(192, 128)
            put(outp, k, e // 2, e % 2, jnp.dot(d, w[3 * e + 2], preferred_element_type=f32))

    outs = RowScatter(outp, out_core, out_y, None, (*osems, None, None), h, b)
    early = [(k, p) for k in EARLY for p in range(2)]

    def send_early():
        for n in early:
            outs.send_core(*n)
        for n in early:
            outs.send_y(*n)

    tasks = [[lambda: out_task(3), lambda: out_task(2)], [lambda: out_task(1), lambda: out_task(0)], [send_early],
             [lambda: weight_task(0)], [lambda: weight_task(1)], [lambda: weight_task(2)], [lambda: weight_task(3)], []]
    def sum_step(n):
        for act in tasks[n]:
            act()
        s.send_z(*order[n])

    def part_store(k, whole):
        zz = g.nth(k)
        at = pl.ds(4 * zz, 4) if whole else pl.ds(outs.blk(k, 0, 0), 1)
        return pltpu.make_async_copy(outp.at[at], part_hbm.at[at], loc.at[3 + k])

    for n in range(6):
        sum_step(n)
    for k in range(4):
        if k not in EARLY:
            part_store(k, True).start()

    each(lambda k: pltpu.make_async_remote_copy(
        src_ref=vs_in.at[b], dst_ref=vs_in.at[(b + k) % n_blk], send_sem=vs_send.at[0],
        recv_sem=vs_recv.at[(b + k) % n_blk], device_id=(h, b), device_id_type=MESH).wait_recv())
    vsum = jnp.sum(vs_in[:, 0, :], axis=0, keepdims=True)
    vrow = jnp.concatenate([vsum[:, 0:96], vsum[:, 128:224]], axis=1)
    spread = spread[:, 0:192]
    dv_out[...] = exact_dot(p_far.astype(f32) * vrow, spread, cols)
    swaps[3].start()
    dv_own = exact_dot(p_own.astype(f32) * vrow, spread, cols)
    u = jnp.sum(og * n2f, axis=1, keepdims=True)
    wj = jnp.dot(og_low, small, preferred_element_type=f32)
    w0, w1 = wj[:, 18:19], wj[:, 19:20]
    c = [c_mix[:, n : n + 1] for n in (12, 13, 14, 15)]
    dgate = lane_of(u, 9) + lane_of(c[0] * u + c[1] * w0, 10) + lane_of(c[2] * u + c[3] * w1, 11)
    dmix = lane_of(u, 12) + lane_of(w0, 13) + lane_of(u, 14) + lane_of(w1, 15)
    dmix = dmix * jnp.where(lane < 14, gates[:, 10:11], gates[:, 11:12])
    both = c_mix * dmix
    dmix = c_mix * (dmix - both - jnp.where(lane % 2 == 0, pltpu.roll(both, 127, 1), pltpu.roll(both, 1, 1)))
    dmix = jnp.where((lane >= 12) & (lane < 16), dmix, 0.0)
    aux = (0.01 * 12.0 / live_total) * (cnt[0:1, :] / (2.0 * live_total)) * live
    sum_step(6)
    swaps[3].wait_recv()
    dprob = named * (dgate + dv_own + dv_in[...]) + aux
    dlog = softmax_back(prob, dprob) + dmix
    dn_near = og * alpha + exact_dot(dlog, jnp.where(
        lax.broadcasted_iota(jnp.int32, (768, 128), 1) < 16, small, 0).astype(bf16), cols)
    dl_high, dl_low = split(dlog)
    gs = lax.dot_general(n2, dl_high, (rows, ((), ())), preferred_element_type=f32)
    gs = gs + lax.dot_general(n2, dl_low, (rows, ((), ())), preferred_element_type=f32)
    b_high, b_low = split(lane_of(beta[0], 18) + lane_of(beta[1], 19))
    gs = gs + lax.dot_general(og_low, b_high, (rows, ((), ())), preferred_element_type=f32)
    gs_out[...] = gs + lax.dot_general(og_low, b_low, (rows, ((), ())), preferred_element_type=f32)
    mixed = lax.dot_general(prev[...], jnp.where(lane < 12, dlog, 0.0), (rows, ((), ())), preferred_element_type=f32,
                            precision=lax.Precision.HIGHEST)
    misc_out[0:16, :] = mixed[0:16]
    misc_out[16:24, :] = jnp.broadcast_to(jnp.sum(prob * live, axis=0, keepdims=True), (8, 128))
    sum_step(7)

    din = jnp.concatenate([s.total(0), s.total(1)], axis=0).astype(bf16)
    into = ((1,), (0,))
    d_out[...] = exact_dot(pg_far[:, 0:192], din, into).astype(bf16)
    swaps[2].start()
    dn_near = dn_near + exact_dot(pg_own[:, 0:192], din, into)
    swaps[2].wait_recv()
    dn = dn_near + d_in[...].astype(f32)
    t = dn * smt[17:18, :]
    rg = og + scale * (t - xh * (jnp.sum(t * xh, axis=1, keepdims=True) * (1.0 / 768)))
    res_out[...] = rg
    ag_out[...] = lax.dot_general(rg.astype(bf16), wout[...], (cols, ((), ())), preferred_element_type=f32).astype(bf16)
    gain = jnp.broadcast_to(jnp.sum(dn * xh, axis=0, keepdims=True), (128, 768))
    gs_out[...] += jnp.where(lax.broadcasted_iota(jnp.int32, (768, 128), 1) == 17, jnp.transpose(gain), 0.0)

    for n in early:
        outs.join_y(*n)
    for k in EARLY:
        part_store(k, False).start()
    g.finish()
    s.finish()
    outs.finish(EARLY, ())
    each(lambda k: gate_copy(k).wait_send())
    each(lambda k: vs_copy(k).wait_send())
    for c in swaps:
        c.wait_send()
    for k in range(4):
        part_store(k, k not in EARLY).wait()
    store_g(3, lambda c: c.wait())


def front_kernel(n_blk, *refs):
    (lengths, tok, cot, routes_t, w_in, router_t, const_t, gains_t, vec_t, wo_in, prev_t, mix_in, cos_hbm, sin_hbm, w_hbm,
     norm_hbm, q_hbm, k_hbm, v_hbm, o_hbm, part_hbm, g_hbm, att, smt, cnt, local_out, res_out, ag_out, gs_out, misc_out, pg_out,
     gain_out, sm, wout, pt, cot_rows, turn, w, w_part, wsem, *scratch) = refs
    all_here = greet_all(lax.axis_index("head"), lax.axis_index("blk"), n_blk)
    w_loads = [pltpu.make_async_copy(w_hbm.at[:, kind], w_part.at[kind], wsem.at[kind]) for kind in range(3)]
    for c in w_loads:
        c.start()
    turn[...] = jnp.zeros_like(turn)
    turn[0, 0:12, 0:24] = router_t[...].astype(f32)
    turn[0, 12:16, 0:24] = const_t[...].astype(f32)
    turn[0, 16:18, 0:24] = gains_t[...].astype(f32)
    turn[0, 18:20, 0:24] = vec_t[...].astype(f32)
    turn[1, 0:2, :] = routes_t[...].astype(f32)
    turn[2, 0:12, :] = prev_t[...]
    turn[3, 0:12, 0:12] = mix_in[...]
    small = jnp.transpose(turn[0])[0:24, 0:64]
    gain_out[...] = small
    routes = jnp.transpose(turn[1])
    prev = jnp.transpose(turn[2])

    def relay_w(kind):
        w_loads[kind].wait()
        t = w_part[kind].astype(f32)
        for e in range(4):
            w[3 * e + kind] = t[:, e, :].astype(bf16)

    cot_gather, finish = forward_kernel(
        n_blk, all_here, lengths, tok, cot, routes, w_in, small, wo_in, cos_hbm, sin_hbm, relay_w, norm_hbm, q_hbm, k_hbm, v_hbm, o_hbm,
        att, smt, cnt, sm, wout, pt, cot_rows, *scratch[: len(forward_scratch(n_blk))])
    expert_kernel(
        n_blk, cot_gather, lengths, att, tok, cot, prev, turn.at[3], routes, wout, sm, smt, cnt, pt, w, cot_rows,
        part_hbm, g_hbm, local_out, res_out, ag_out, gs_out, misc_out, pg_out, *scratch[len(forward_scratch(n_blk)) :])
    finish()


def forward_scratch(n_blk):
    V, DMA = pltpu.VMEM, pltpu.SemaphoreType.DMA
    return [
        V((3, 16, 128, 256), bf16), V((12, 16, 384), bf16), V((2 * n_blk, 16, 384), bf16), V((768, 256), f32),
        V((768, 256), bf16), V((2048, 128), f32), V((2048, 128), f32), V((2048, 768), bf16), V((2048, 64), bf16),
        V((2048, 64), bf16), V((2048, 128), bf16), V((2048, 128), f32), V((16, 64, 128), bf16), V((12, 64, 128), bf16),
        V((128, 128), bf16), V((128, 128), bf16), V((128, 768), bf16), V((n_blk, 1, 2, 16, 1152), bf16),
        DMA((3, 16)), DMA((3, 16)), DMA((2 * n_blk,)), DMA((2 * n_blk,)), DMA((16,)), DMA((12,)), DMA((11,)), DMA((3,)), DMA((3,)),
        *gather_sems(1), *gather_sems(2),
    ]


def expert_scratch(n_blk):
    V, DMA = pltpu.VMEM, pltpu.SemaphoreType.DMA
    return [
        V((n_blk, 2, 96, 768), bf16),
        V((n_blk, 2, 96, 128), f32), V((n_blk, 2, 96, 256), bf16), V((n_blk, 2, 96, 128), bf16),
        V((n_blk, 2, 96, 768), bf16), V((n_blk, 2, 96, 768), bf16), V((3, 128, 768), f32),
        V((n_blk, 8, 256), f32), V((n_blk, 8, 256), f32), V((n_blk, 8, 256), f32),
        V((128, 768), bf16), V((128, 768), bf16), V((128, 128), f32), V((128, 128), f32),
        V((128, 768), bf16), V((128, 768), bf16), V((128, 128), f32), V((128, 128), f32),
        DMA((n_blk,)), DMA((n_blk,)), DMA((n_blk,)), DMA((n_blk,)), DMA((4,)), DMA((4,)), DMA((7,)),
        *gather_sems(2), *scatter_scratch(2, 96, 768),
        V((4, 2, 2, 96, 768), bf16), V((4, 2, 96, 768), bf16), DMA((4, 2, 2)), DMA((4, 2, 2)), DMA((4, 2)), DMA((4, 2)),
    ]


def front(lengths, tokens, cotangent, routes, w_qkv, w_router, w_const, gains, vec, w_out, prev, mix, w, n_blk):
    cos, sin = rotary_tables(2048)
    vm = pl.BlockSpec(memory_space=pltpu.VMEM)
    hbm = pl.BlockSpec(memory_space=pl.ANY)
    sds = jax.ShapeDtypeStruct
    V = pltpu.VMEM
    return pl.pallas_call(
        functools.partial(front_kernel, n_blk),
        out_shape=(
            sds((2048, 768), bf16), sds((2048, 64), bf16), sds((2048, 64), bf16), sds((2048, 128), bf16),
            sds((2048, 128), f32), sds((n_blk, 2, 96, 768), bf16), sds((128, 3, 4, 768), f32),
            sds((128, 768), bf16), sds((32, 768), f32), sds((8, 128), f32), sds((128, 768), f32), sds((128, 768), f32),
            sds((128, 768), bf16), sds((768, 128), f32), sds((24, 128), f32), sds((2, 128, 256), f32),
            sds((24, 64), f32),
        ),
        in_specs=[pl.BlockSpec(memory_space=pltpu.SMEM)] + [vm] * 11 + [hbm] * 3,
        out_specs=(hbm,) * 7 + (vm,) * 10,
        scratch_shapes=[
            V((768, 128), bf16), V((768, 768), bf16), V((2, 128, 256), bf16), V((n_blk, 2, 96, 768), bf16),
            V((4, 128, 128), f32), V((12, 128, 768), bf16), V((3, 128, 4, 768), bf16), pltpu.SemaphoreType.DMA((3,)),
            *forward_scratch(n_blk), *expert_scratch(n_blk),
        ],
        compiler_params=pltpu.CompilerParams(collective_id=0, has_side_effects=True, vmem_limit_bytes=63 * 2**20),
        cost_estimate=pl.CostEstimate(flops=8 * 10**9, bytes_accessed=3 * 10**7, transcendentals=0),
        name="front",
    )(lengths, tokens, cotangent, routes.T, w_qkv, w_router.T, w_const.T, gains.T, vec.T, w_out, prev.T, mix,
      jnp.asarray(cos), jnp.asarray(sin), w)


def backward_kernel(
    n_blk, lengths, ag, tok, res_grad, smt, att, local_out, pg, g_small, misc, w_own, small, cnt,
    norm_hbm, q_hbm, k_hbm, v_hbm, o_hbm, cos_hbm, sin_hbm, w_hbm, part_hbm,
    out, dtok_out, gq_out, go_out, router_out, const_out, vec_out, gains_out, mix_out, aux_out,
    norm, q, k, v, o, cos, sin, w_all, agbuf, do_in, do, dk, dv, dqkv, obuf, got, dproj, turn, g_f, gbuf, g_in,
    part, gpart, gfar, gsum, far_out, far_in, misc_sum, misc_in,
    a_send, a_recv, b_send, b_recv, g_send, g_recv, loc, x_send, x_recv, m_send, m_recv, *rest,
):
    h, b = lax.axis_index("head"), lax.axis_index("blk")
    me = b * 2 + h
    total = 2 * n_blk
    _, _, rank = place(0, h, b)
    base = (b // 8) * 8
    head = head_of(h, b)
    working = (b % 4) != 3
    all_here = greet_all(h, b, n_blk)
    loads = [
        pltpu.make_async_copy(src, dst, loc.at[i])
        for i, (src, dst) in enumerate([
            (q_hbm, q), (k_hbm, k), (v_hbm, v), (o_hbm, o), (cos_hbm, cos), (sin_hbm, sin), (norm_hbm, norm),
            (w_hbm, w_all), (part_hbm, part)])
    ]
    for c in loads:
        c.start()
    a = ag[...].astype(f32)
    for j in range(12):
        agbuf[j] = jnp.concatenate([a[0:64, 64 * j : 64 * j + 64], a[64:128, 64 * j : 64 * j + 64]], axis=1).astype(bf16)
    all_here()

    def to_head(j):
        r = home_of(j)
        return pltpu.make_async_remote_copy(
            src_ref=agbuf.at[j], dst_ref=do_in.at[rank], send_sem=a_send.at[j], recv_sem=a_recv.at[rank],
            device_id=(r % 2, base + r // 2), device_id_type=MESH,
        )

    for j in range(12):
        @pl.when(rank != home_of(j))
        def _(j=j):
            to_head(j).start()

    def to_tokens(r):
        return pltpu.make_async_remote_copy(
            src_ref=obuf.at[r], dst_ref=got.at[head], send_sem=b_send.at[r], recv_sem=b_recv.at[head],
            device_id=(r % 2, base + r // 2), device_id_type=MESH,
        )

    def to_owner(kk):
        other = (me + kk) % total
        oh, ob = other % 2, other // 2
        return pltpu.make_async_remote_copy(
            src_ref=gbuf.at[oh * n_blk + ob], dst_ref=g_in.at[me], send_sem=g_send.at[kk], recv_sem=g_recv.at[me],
            device_id=(oh, ob), device_id_type=MESH,
        )

    length = lengths[b // 8]

    rs = RowScatter(part, *rest[0:3], rest[3:9], h, b)
    gs = RowScatter(gsum, *rest[9:12], rest[12:18], h, b)
    g_f2 = lax.dot_general(att[...], res_grad[...].astype(bf16), (((0,), (0,)), ((), ())), preferred_element_type=f32)
    for w in range(total):
        cat = jnp.concatenate([g_f2[24 * w : 24 * w + 24], g_small[24 * w : 24 * w + 24, :]], axis=1)
        gpart[w // n_blk, w % n_blk, 0] = fold(cat)
    swaps = [
        pltpu.make_async_remote_copy(
            src_ref=src, dst_ref=dst, send_sem=x_send.at[n], recv_sem=x_recv.at[n],
            device_id=(1 - h, b), device_id_type=MESH)
        for n, (src, dst) in enumerate([(gpart.at[1 - h], gfar), (far_out, far_in)])
    ]
    swaps[0].start()

    def join_planes():
        swaps[0].wait_recv()
        gsum[...] = (gpart[h].astype(f32) + gfar[...].astype(f32)).astype(bf16)
        for n in gs.order:
            gs.send_core(*n)

    loads[8].wait()
    late = [(k, p) for k in (3, 2, 1, 0) if k not in EARLY for p in range(2)]
    def z_early(ks):
        for kk in ks:
            if kk in EARLY and kk:
                for p in range(2):
                    rs.to_z(kk, p).start()

    z_early(Z_FIRST)
    for n in late:
        rs.send_core(*n)

    misc_sum[0] = misc[...]
    z = b // 4
    partners = [(1 - h, b), (h, b + 1 - 2 * (b % 2)), (h, b + 2 - 4 * ((b // 2) % 2)),
                (h, b + 4 - 8 * (z % 2)), (h, b + 8 - 16 * (z // 2))]

    def pairwise(t):
        return pltpu.make_async_remote_copy(
            src_ref=misc_sum.at[t], dst_ref=misc_in.at[t], send_sem=m_send.at[t], recv_sem=m_recv.at[t],
            device_id=partners[t], device_id_type=MESH)

    def pairwise_done(t):
        pairwise(t).wait_recv()
        misc_sum[t + 1] = misc_sum[t] + misc_in[t]
        if t < 4:
            pairwise(t + 1).start()

    pairwise(0).start()
    def step(scatter, stage, n):
        k, p = scatter.order[n]
        return lambda: getattr(scatter, stage)(k, p)

    def ry(n):
        return lambda: rs.send_y(*late[n]) if n < len(late) else None

    def rz(n):
        return lambda: rs.send_z(*late[n]) if n < len(late) else None

    def gy(n):
        return step(gs, "send_y", n)

    def gz(n):
        return step(gs, "send_z", n)

    def pd(t):
        return lambda: pairwise_done(t)

    between = {
        8: [ry(0), pd(0)], 7: [], 6: [], 5: [], 4: [ry(1), pd(1)], 3: [], 2: [], 1: [],
        0: [join_planes, ry(2), pd(2)],
    }

    @pl.when(jnp.logical_not(working))
    def _():
        do_in[...] = jnp.zeros_like(do_in)

    @pl.when(working)
    def _():
        do_in[rank] = agbuf[head]

    for c in loads[:6]:
        c.wait()
    if True:
        def unpack(r, carry):
            @pl.when((r != rank) & working)
            def _():
                pltpu.make_async_remote_copy(
                    src_ref=agbuf.at[0], dst_ref=do_in.at[r], send_sem=a_send.at[0], recv_sem=a_recv.at[r],
                    device_id=(h, b), device_id_type=MESH,
                ).wait_recv()

            t = do_in[r].astype(f32)
            rows = pl.multiple_of(r * 128, 128)
            do[pl.ds(rows, 64), :] = t[:, 0:64].astype(bf16)
            do[pl.ds(rows + 64, 64), :] = t[:, 64:128].astype(bf16)
            return carry

        lax.fori_loop(0, 16, unpack, 0)
        for act in between[8]:
            act()
        for i in range(7, -1, -1):
            width = 256 * (i + 1)
            lo = 256 * i
            qi, doi = q[lo:width, :], do[lo:width, :]
            s = lax.dot_general(qi, k[0:width, :], (((1,), (1,)), ((), ())), preferred_element_type=f32)
            key = lax.broadcasted_iota(jnp.int32, (1, width), 1)
            ov = o[lo:width, :]
            lse = ov[:, 64:65]
            s = (s - lse) + jnp.where(key < length, 0.0, NEG)
            rowi = lax.broadcasted_iota(jnp.int32, (256, 256), 0)
            coli = lax.broadcasted_iota(jnp.int32, (256, 256), 1)
            last = jnp.where(coli <= rowi, s[:, lo:], NEG)
            s = last if i == 0 else jnp.concatenate([s[:, :lo], last], axis=1)
            p = jnp.exp(s)
            dp = lax.dot_general(doi, v[0:width, 0:64], (((1,), (1,)), ((), ())), preferred_element_type=f32)
            inner = jnp.sum(doi.astype(f32) * ov[:, 0:64], axis=1, keepdims=True)
            ds = (p * (dp - inner)).astype(bf16)
            p = p.astype(bf16)
            dq = jnp.dot(ds, k[0:width, :], preferred_element_type=f32) * 0.125
            dki = lax.dot_general(ds, qi, (((0,), (0,)), ((), ())), preferred_element_type=f32)
            dvi = lax.dot_general(p, doi, (((0,), (0,)), ((), ())), preferred_element_type=f32)
            if i == 7:
                dk[...] = dki
                dv[...] = dvi
            else:
                dk[0:width, :] += dki
                dv[0:width, :] += dvi
            both = jnp.concatenate([dq, dk[lo:width, :]], axis=1)
            both = turned(both, cos[lo:width, :], -sin[lo:width, :]).astype(bf16)
            dvl = dv[lo:width, :]
            dqkv[lo:width, 0:128] = both
            dqkv[lo:width, 128:256] = jnp.concatenate([dvl, jnp.zeros_like(dvl)], axis=1).astype(bf16)
            for half in range(2):
                r = 2 * i + half
                obuf[r, 0:128, :] = both[128 * half : 128 * half + 128]
                obuf[r, 128:192, :] = jnp.concatenate(
                    [dvl[128 * half : 128 * half + 64], dvl[128 * half + 64 : 128 * half + 128]], axis=1).astype(bf16)

                @pl.when((r != rank) & working)
                def _(r=r):
                    to_tokens(r).start()
            for act in between[i]:
                act()

        @pl.when(working)
        def _():
            got[head] = obuf[rank]

        loads[6].wait()
        for c in range(3):
            g_f[256 * c : 256 * c + 256, :] = lax.dot_general(
                norm[:, 256 * c : 256 * c + 256], dqkv[...], (((0,), (0,)), ((), ())), preferred_element_type=f32)
        for w in range(total):
            gbuf[w] = fold(g_f[24 * w : 24 * w + 24, :])

        def send_g(kk, carry):
            to_owner(kk).start()
            return carry

        @pl.when(working)
        def _():
            lax.fori_loop(1, total, send_g, 0)
            g_in[me] = gbuf[h * n_blk + b]

    z_early([kk for kk in (3, 2, 1) if kk not in Z_FIRST])
    for act in (*(ry(n) for n in range(3, len(late))), gy(0), gy(1), gy(2), gy(3), rz(0)):
        act()
    rz(1)()
    pairwise_done(3)

    for j in range(12):
        @pl.when(rank != home_of(j))
        def _(j=j):
            pltpu.make_async_remote_copy(
                src_ref=obuf.at[0], dst_ref=got.at[j], send_sem=b_send.at[0], recv_sem=b_recv.at[j],
                device_id=(h, b), device_id_type=MESH,
            ).wait_recv()
    for j in range(0, 12, 2):
        one, two = got[j].astype(f32), got[j + 1].astype(f32)
        lo = 64 * j
        for part_i, at in enumerate((0, 64)):
            dproj[:, 768 * part_i + lo : 768 * part_i + lo + 128] = jnp.concatenate(
                [one[0:128, at : at + 64], two[0:128, at : at + 64]], axis=1).astype(bf16)
        dproj[0:64, 1536 + lo : 1664 + lo] = jnp.concatenate([one[128:192, 0:64], two[128:192, 0:64]], axis=1).astype(bf16)
        dproj[64:128, 1536 + lo : 1664 + lo] = jnp.concatenate([one[128:192, 64:128], two[128:192, 64:128]], axis=1).astype(bf16)
    loads[7].wait()
    dn = lax.dot_general(dproj[...], w_all[...], (((1,), (1,)), ((), ())), preferred_element_type=f32)
    pairwise_done(4)
    x = tok[...].astype(f32)
    scale = lax.rsqrt(jnp.sum(x * x, axis=1, keepdims=True) * (1.0 / 768) + 1e-6)
    xh = x * scale
    t = dn * smt[16:17, :]
    dx = scale * (t - xh * (jnp.sum(t * xh, axis=1, keepdims=True) * (1.0 / 768)))
    dtok_out[...] = (res_grad[...] + dx).astype(bf16)

    for n in range(2, len(late)):
        rz(n)()
    rows = jnp.concatenate([rs.total(0), rs.total(1)], axis=0).astype(bf16)
    far_out[...] = exact_dot(pg[1, :, 0:192], rows, ((1,), (0,))).astype(bf16)
    swaps[1].start()
    for n in range(4):
        gz(n)()
    own = exact_dot(pg[0, :, 0:192], rows, ((1,), (0,))) + local_out[...]

    for src in range(total):
        if (src // 2) % 4 == 3:
            continue

        @pl.when(me != src)
        def _(src=src):
            pltpu.make_async_remote_copy(
                src_ref=gbuf.at[0], dst_ref=g_in.at[src], send_sem=g_send.at[0], recv_sem=g_recv.at[src],
                device_id=(h, b), device_id_type=MESH,
            ).wait_recv()
    for j in range(0, 12, 2):
        pair = []
        for jj in (j, j + 1):
            t = sum(g_in[16 * s + home_of(jj)].astype(f32) for s in range(total // 16))
            pair.append(jnp.concatenate(
                [t[:, 0:256], jnp.concatenate([t[0:8, 256:384], t[8:16, 256:384]], axis=1)], axis=0))
        one, two = pair
        for part in range(3):
            gq_out[:, 768 * part + 64 * j : 768 * part + 64 * j + 128] = jnp.concatenate(
                [one[:, 64 * part : 64 * part + 64], two[:, 64 * part : 64 * part + 64]], axis=1)

    lane = lax.broadcasted_iota(jnp.int32, (24, 128), 1)
    gain_grad = jnp.sum(gq_out[...] * w_own[...].astype(f32), axis=1, keepdims=True) / small[:, 16:17]
    t = gs.total(0)
    t = jnp.concatenate([t[:, 0:896], jnp.concatenate([t[0:8, 896:1344], t[8:16, 896:1344]], axis=1)], axis=0)
    go_out[...] = t[:, 0:768]
    turn[...] = jnp.zeros_like(turn)
    turn[0:24, :] = jnp.where(lane == 16, gain_grad, t[:, 768:896])
    t = jnp.transpose(turn[...])
    router_out[...] = t[0:12, 0:24]
    const_out[...] = t[12:16, 0:24]
    gains_out[...] = t[16:18, 0:24]
    vec_out[...] = t[18:20, 0:24]
    t = misc_sum[5]
    mix_out[...] = t[0:12, 0:12]
    live_total = (lengths[0] + lengths[1]).astype(f32)
    aux = cnt[0:1, :] / (2.0 * live_total) * (t[16:17, :] / live_total)
    aux_out[...] = 12.0 * jnp.sum(aux, axis=1, keepdims=True)
    swaps[1].wait_recv()
    out[...] = (own + far_in[...].astype(f32)).astype(bf16)

    rs.finish([k for k in range(4) if k not in EARLY])
    gs.finish()
    for t in range(5):
        pairwise(t).wait_send()
    for c in swaps:
        c.wait_send()
    for j in range(12):
        @pl.when(rank != home_of(j))
        def _(j=j):
            to_head(j).wait_send()

    @pl.when(working)
    def _():
        for r in range(16):
            @pl.when(r != rank)
            def _(r=r):
                to_tokens(r).wait_send()

        def sent(kk, carry):
            to_owner(kk).wait_send()
            return carry

        lax.fori_loop(1, total, sent, 0)


def attend_back(
    lengths, ag, tok, res_grad, smt, att, local_out, pg, g_small, misc, w_own, small, cnt, norm, q, k, v, o, w_all, parts,
    n_blk,
):
    cos, sin = rotary_tables(2048)
    vm = pl.BlockSpec(memory_space=pltpu.VMEM)
    hbm = pl.BlockSpec(memory_space=pl.ANY)
    sds = jax.ShapeDtypeStruct
    DMA = pltpu.SemaphoreType.DMA
    V = pltpu.VMEM
    total = 2 * n_blk
    return pl.pallas_call(
        functools.partial(backward_kernel, n_blk),
        out_shape=(
            sds((128, 768), bf16), sds((128, 768), bf16), sds((24, 2304), f32), sds((24, 768), f32), sds((12, 24), f32),
            sds((4, 24), f32), sds((2, 24), f32), sds((2, 24), f32), sds((12, 12), f32), sds((1, 1), f32),
        ),
        in_specs=[pl.BlockSpec(memory_space=pltpu.SMEM)] + [vm] * 12 + [hbm] * 9,
        out_specs=(vm,) * 10,
        scratch_shapes=[
            V((2048, 768), bf16), V((2048, 64), bf16), V((2048, 64), bf16), V((2048, 128), bf16), V((2048, 128), f32),
            V((2048, 128), f32), V((2048, 128), f32), V((768, 2304), bf16),
            V((12, 64, 128), bf16), V((16, 64, 128), bf16), V((2048, 64), bf16), V((2048, 64), f32), V((2048, 64), f32),
            V((2048, 256), bf16), V((16, 192, 128), bf16), V((12, 192, 128), bf16), V((128, 2304), bf16), V((128, 128), f32),
            V((768, 256), f32), V((total, 16, 384), bf16), V((total, 16, 384), bf16),
            V((n_blk, 2, 96, 768), bf16), V((2, n_blk, 1, 16, 1344), bf16), V((n_blk, 1, 16, 1344), bf16), V((n_blk, 1, 16, 1344), bf16),
            V((128, 768), bf16), V((128, 768), bf16),
            V((6, 24, 128), f32), V((5, 24, 128), f32),
            DMA((12,)), DMA((16,)), DMA((16,)), DMA((12,)), DMA((total,)), DMA((total,)), DMA((9,)), DMA((2,)), DMA((2,)),
            DMA((5,)), DMA((5,)), *scatter_scratch(2, 96, 768), *scatter_scratch(1, 16, 1344),
        ],
        compiler_params=pltpu.CompilerParams(collective_id=1, has_side_effects=True, vmem_limit_bytes=60 * 2**20),
        cost_estimate=pl.CostEstimate(flops=2 * 10**9, bytes_accessed=2 * 10**7, transcendentals=0),
        name="attend_back",
    )(lengths, ag, tok, res_grad, smt, att, local_out, pg, g_small, misc, w_own, small, cnt, norm, q, k, v, o,
      jnp.asarray(cos), jnp.asarray(sin), w_all, parts)


CAP = 24


eps = 1e-06
aux_weight = 0.01
highest = lax.Precision.HIGHEST
masked_score = -1e30


def shifted(block, axis, distance):
    devices = range(lax.axis_size(axis))
    route = [(i - distance, i) for i in devices if i - distance in devices]
    return lax.ppermute(block, axis, route)


def for_sending(x):
    return jax.tree.map(lambda a: a.astype(jnp.bfloat16) if a.dtype == jnp.float32 else a, x)


def rms_norm(values, gain_vector):
    return values * lax.rsqrt(jnp.mean(values * values, axis=-1, keepdims=True) + eps) * gain_vector


def rotary(values, positions, turn_sign):
    half_width = values.shape[-1] // 2
    frequency = jnp.exp(
        jnp.arange(half_width, dtype=jnp.float32) * (-2.0 * math.log(10000.0) / values.shape[-1])
    )
    angles = positions.astype(jnp.float32)[:, None] * frequency[None, :]
    cosine = jnp.cos(angles)[:, None, :]
    sine_part = turn_sign * jnp.sin(angles)[:, None, :]
    first_half = values[..., :half_width]
    second_half = values[..., half_width:]
    return jnp.concatenate(
        [
            first_half * cosine - second_half * sine_part,
            second_half * cosine + first_half * sine_part,
        ],
        axis=-1,
    )


def slot_lengths(slot_ids, lengths):
    slot_table = jnp.arange(lengths.shape[0], dtype=jnp.int32)
    return jnp.sum(jnp.where(slot_ids[:, None] == slot_table[None, :], lengths[None, :], 0), axis=1)


def allowed_mask(query_ids, key_ids, slot_size, lengths):
    query_slot = query_ids // slot_size
    key_slot = key_ids // slot_size
    query_pos = query_ids - query_slot * slot_size
    key_pos = key_ids - key_slot * slot_size
    key_live = (key_pos < slot_lengths(key_slot, lengths)) & (key_ids >= 0)
    return (
        (query_slot[:, None] == key_slot[None, :])
        & (key_pos[None, :] <= query_pos[:, None])
        & key_live[None, :]
    )


def masked_scores(query_block, key_head, query_ids, key_ids, slot_size, lengths):
    scores = lax.dot_general(
        query_block, key_head, (((1,), (1,)), ((), ())), preferred_element_type=jnp.float32
    ) * HD ** (-0.5)
    return jnp.where(allowed_mask(query_ids, key_ids, slot_size, lengths), scores, masked_score)


def attend_forward(queries, key_all, value_all, query_ids, key_ids, slot_size, lengths):
    head_total = queries.shape[1] // HD

    def one_head(head_index):
        query_head = lax.dynamic_slice_in_dim(queries, head_index * HD, HD, 1)
        key_head = lax.dynamic_slice_in_dim(key_all, head_index * HD, HD, 1)
        value_head = lax.dynamic_slice_in_dim(value_all, head_index * HD, HD, 1)
        scores = masked_scores(query_head, key_head, query_ids, key_ids, slot_size, lengths)
        row_max = jnp.max(scores, axis=1, keepdims=True)
        weights = jnp.exp(scores - row_max)
        row_total = jnp.sum(weights, axis=1, keepdims=True)
        probs_low = (weights / row_total).astype(jnp.bfloat16)
        head_outputs = [jnp.dot(probs_low, value_head, preferred_element_type=jnp.float32)]
        log_parts = [row_max[:, 0] + jnp.log(row_total[:, 0])]
        return (jnp.concatenate(head_outputs, axis=0), jnp.concatenate(log_parts, axis=0))

    head_outputs, log_sums = lax.map(one_head, jnp.arange(head_total, dtype=jnp.int32))
    return (head_outputs.transpose(1, 0, 2).reshape(queries.shape[0], queries.shape[1]), log_sums)


def attend_backward(
    queries, key_all, value_all, out_grads, log_sums, query_ids, key_ids, slot_size, lengths
):
    head_total = queries.shape[1] // HD
    block_rows = min(512, queries.shape[0])

    def one_head(head_index):
        query_head = lax.dynamic_slice_in_dim(queries, head_index * HD, HD, 1)
        key_head = lax.dynamic_slice_in_dim(key_all, head_index * HD, HD, 1)
        value_head = lax.dynamic_slice_in_dim(value_all, head_index * HD, HD, 1)
        grad_head = lax.dynamic_slice_in_dim(out_grads, head_index * HD, HD, 1)
        log_head = lax.dynamic_index_in_dim(log_sums, head_index, 0, keepdims=False)
        key_grad = jnp.zeros(key_head.shape, jnp.float32)
        value_grad = jnp.zeros(value_head.shape, jnp.float32)
        grad_block = grad_head[0:block_rows]
        scores = masked_scores(query_head, key_head, query_ids, key_ids, slot_size, lengths)
        probs = jnp.exp(scores - log_head[0:block_rows][:, None])
        probs_low = probs.astype(jnp.bfloat16)
        prob_grads = lax.dot_general(
            grad_block, value_head, (((1,), (1,)), ((), ())), preferred_element_type=jnp.float32
        )
        row_inner = jnp.sum(probs * prob_grads, axis=1, keepdims=True)
        score_grads = (probs * (prob_grads - row_inner)).astype(jnp.bfloat16)
        query_parts = [
            jnp.dot(score_grads, key_head, preferred_element_type=jnp.float32) * HD ** (-0.5)
        ]
        key_grad = key_grad + lax.dot_general(
            score_grads, query_head, (((0,), (0,)), ((), ())), preferred_element_type=jnp.float32
        ) * HD ** (-0.5)
        value_grad = value_grad + lax.dot_general(
            probs_low, grad_block, (((0,), (0,)), ((), ())), preferred_element_type=jnp.float32
        )
        return (jnp.concatenate(query_parts, axis=0), key_grad, value_grad)

    query_grad, key_grad, value_grad = lax.map(one_head, jnp.arange(head_total, dtype=jnp.int32))
    return (
        query_grad.transpose(1, 0, 2).reshape(queries.shape[0], queries.shape[1]),
        key_grad.transpose(1, 0, 2).reshape(key_all.shape[0], key_all.shape[1]),
        value_grad.transpose(1, 0, 2).reshape(value_all.shape[0], value_all.shape[1]),
    )


def fetch_prev(key_heads, value_heads, span_count):
    key_parts = [key_heads]
    value_parts = [value_heads]
    for offset in range(1, span_count):
        arrived = shifted((key_heads, value_heads), "blk", offset)
        key_parts.append(arrived[0])
        value_parts.append(arrived[1])
    return (jnp.concatenate(key_parts, axis=0), jnp.concatenate(value_parts, axis=0))


def router_probs(normed, router_w, mixing, prev_scores):
    logits = jnp.dot(normed, router_w, precision=highest) + jnp.dot(
        prev_scores, mixing, precision=highest
    )
    return jax.nn.softmax(logits, axis=-1)


def branch_sum(router_prob, normed, const_w, vector_w, outputs_pair, choose, live_rows, real_count):
    gate_values = jnp.sum(choose * router_prob[:, None, :], axis=-1)
    expert_share = jnp.sum(choose * gate_values[:, :, None], axis=1) * live_rows[:, None]
    routed = jnp.sum(gate_values[:, :, None] * outputs_pair, axis=1)
    routed = routed + expert_share[:, real_count + 1 : real_count + 2] * normed
    const_count = vector_w.shape[1]
    const_mix = jax.nn.softmax(
        jnp.dot(normed, const_w, precision=highest).reshape(normed.shape[0], const_count, 2),
        axis=-1,
    )
    for const_index in range(const_count):
        const_out = (
            const_mix[:, const_index, 0:1] * normed
            + const_mix[:, const_index, 1:2] * vector_w[:, const_index][None, :]
        )
        routed = (
            routed
            + expert_share[:, real_count + 2 + const_index : real_count + 3 + const_index]
            * const_out
        )
    return routed


def on_device(
    tokens,
    cotangent,
    prev_logits,
    routes,
    lengths,
    w_qkv,
    w_out,
    w_router,
    w_const,
    const_vec,
    norm_gains,
    gate_mix,
    expert_weights,
):
    tok_dev = tokens.shape[0]
    model_width = tokens.shape[1]
    head_count = lax.axis_size("head")
    blk_count = lax.axis_size("blk")
    span_count = max(8, min(blk_count // 4, 8192 // (head_count * tok_dev)) * min(1, tok_dev // 64))
    head_index = lax.axis_index("head")
    blk_index = lax.axis_index("blk")
    slot_size = span_count * head_count * tok_dev
    tok_blk = head_count * tok_dev
    qkv_w, out_w, router_w, const_w, vector_w, gain_pair = (
        lax.all_gather(w_qkv, ("head", "blk"), axis=0, tiled=True),
        lax.all_gather(w_out, ("head", "blk"), axis=0, tiled=True),
        lax.all_gather(w_router, ("head", "blk"), axis=0, tiled=True),
        lax.all_gather(w_const, ("head", "blk"), axis=0, tiled=True),
        lax.all_gather(const_vec, ("head", "blk"), axis=0, tiled=True),
        lax.all_gather(norm_gains, ("head", "blk"), axis=0, tiled=True),
    )
    gain_pair = gain_pair.astype(jnp.float32)
    row_ids = (blk_index * head_count + head_index) * tok_dev + jnp.arange(tok_dev, dtype=jnp.int32)
    slot_ids = row_ids // slot_size
    positions = row_ids - slot_ids * slot_size
    live_rows = (positions < slot_lengths(slot_ids, lengths)).astype(jnp.float32)
    inputs = tokens.astype(jnp.float32)
    normed_one, norm_one_back = jax.vjp(rms_norm, inputs, gain_pair[:, 0])
    normed_one_low = normed_one.astype(jnp.bfloat16)
    projected = jnp.dot(normed_one_low, qkv_w, preferred_element_type=jnp.float32).reshape(
        tok_dev, 3, HEADS, HD
    )
    query_send = (
        rotary(projected[:, 0], positions, 1.0).astype(jnp.bfloat16).reshape(tok_dev, model_width)
    )
    key_send = (
        rotary(projected[:, 1], positions, 1.0).astype(jnp.bfloat16).reshape(tok_dev, model_width)
    )
    value_send = projected[:, 2].astype(jnp.bfloat16).reshape(tok_dev, model_width)
    query_heads, key_heads, value_heads = (
        lax.all_to_all(query_send, "head", split_axis=1, concat_axis=0, tiled=True),
        lax.all_to_all(key_send, "head", split_axis=1, concat_axis=0, tiled=True),
        lax.all_to_all(value_send, "head", split_axis=1, concat_axis=0, tiled=True),
    )
    blk_rows = blk_index * tok_blk + jnp.arange(tok_blk, dtype=jnp.int32)
    blk_pos = blk_rows - blk_rows // slot_size * slot_size
    key_ids = jnp.concatenate([blk_rows - offset * tok_blk for offset in range(span_count)], axis=0)
    key_all, value_all = fetch_prev(key_heads, value_heads, span_count)
    attended, log_sums = attend_forward(
        query_heads, key_all, value_all, blk_rows, key_ids, slot_size, lengths
    )
    attended_tok = lax.all_to_all(
        attended.astype(jnp.bfloat16), "head", split_axis=0, concat_axis=1, tiled=True
    )
    residual = inputs + jnp.dot(attended_tok, out_w, preferred_element_type=jnp.float32)
    normed_two, norm_two_back = jax.vjp(rms_norm, residual, gain_pair[:, 1])
    normed_two_low = normed_two.astype(jnp.bfloat16)
    normed_two_f = normed_two_low.astype(jnp.float32)
    router_prob, router_back = jax.vjp(
        partial(router_probs, prev_scores=prev_logits),
        normed_two_f,
        router_w.astype(jnp.float32),
        gate_mix,
    )
    expert_count = router_w.shape[1]
    real_count = expert_weights.shape[1] * head_count
    choose = (
        routes[:, :, None] == jnp.arange(expert_count, dtype=jnp.int32)[None, None, :]
    ).astype(jnp.float32)
    count_local = jnp.sum(jnp.sum(choose, axis=1) * live_rows[:, None], axis=0)
    prob_local = jnp.sum(router_prob * live_rows[:, None], axis=0)
    count_all, prob_all = lax.psum((count_local, prob_local), ("head", "blk"))
    live_total = jnp.sum(lengths).astype(jnp.float32)
    fraction = count_all / (2.0 * live_total)
    aux_loss = expert_count * jnp.sum(fraction * (prob_all / live_total))
    gate_values = jnp.sum(choose * router_prob[:, None, :], axis=-1)
    out_grad = live_rows[:, None] * cotangent.astype(jnp.float32)
    assigned = routes.reshape(-1)
    live_pairs = jnp.repeat(live_rows, 2)
    is_real = (assigned < real_count) & (live_pairs > 0)
    onehot = (
        (assigned[:, None] == jnp.arange(real_count, dtype=jnp.int32)[None, :]) & is_real[:, None]
    ).astype(jnp.int32)
    slot_rank = jnp.sum((jnp.cumsum(onehot, axis=0) - onehot) * onehot, axis=1)
    target = jnp.where(is_real, assigned * CAP + slot_rank, real_count * CAP)
    source = (
        jnp.full((real_count * CAP + 1,), 2 * tok_dev, jnp.int32)
        .at[target]
        .set(jnp.arange(2 * tok_dev, dtype=jnp.int32))[: real_count * CAP]
    )
    zero_row = jnp.zeros((1, model_width), jnp.bfloat16)
    send_rows = jnp.concatenate([normed_two_low, zero_row], axis=0)[source // 2].reshape(
        real_count, CAP, model_width
    )
    pair_grads = (gate_values.reshape(-1, 1) * jnp.repeat(out_grad, 2, axis=0)).astype(jnp.bfloat16)
    send_grads = jnp.concatenate([pair_grads, zero_row], axis=0)[source].reshape(
        real_count, CAP, model_width
    )
    expert_in, expert_cot = (
        lax.all_to_all(send_rows, "head", split_axis=0, concat_axis=1, tiled=True),
        lax.all_to_all(send_grads, "head", split_axis=0, concat_axis=1, tiled=True),
    )
    weight_piece = lax.all_gather(expert_weights, "blk", axis=0, tiled=True)
    gate_w = weight_piece[:, :, 0, :]
    up_w = weight_piece[:, :, 1, :]
    down_w = weight_piece[:, :, 2, :]
    gate_part = jnp.einsum("esd,ned->esn", expert_in, gate_w, preferred_element_type=jnp.float32)
    up_part = jnp.einsum("esd,ned->esn", expert_in, up_w, preferred_element_type=jnp.float32)
    sigmoid_part = jax.nn.sigmoid(gate_part)
    silu_part = gate_part * sigmoid_part
    hidden = (silu_part * up_part).astype(jnp.bfloat16)
    out_sum = jnp.einsum("esn,ned->esd", hidden, down_w, preferred_element_type=jnp.float32)
    hidden_grad = jnp.einsum("esd,ned->esn", expert_cot, down_w, preferred_element_type=jnp.float32)
    gate_grad = (
        hidden_grad * up_part * (sigmoid_part * (1.0 + gate_part * (1.0 - sigmoid_part)))
    ).astype(jnp.bfloat16)
    up_grad = (hidden_grad * silu_part).astype(jnp.bfloat16)
    in_grad = jnp.einsum("esn,ned->esd", gate_grad, gate_w, preferred_element_type=jnp.float32)
    in_grad = in_grad + jnp.einsum(
        "esn,ned->esd", up_grad, up_w, preferred_element_type=jnp.float32
    )
    hidden_all = hidden
    gate_all = gate_grad
    up_all = up_grad
    out_sum, in_grad, hidden_all, gate_all, up_all = (
        out_sum,
        in_grad,
        hidden_all,
        gate_all,
        up_all,
    )
    hidden_own, gate_own, up_own = (
        lax.all_to_all(hidden_all, "blk", split_axis=2, concat_axis=1, tiled=True),
        lax.all_to_all(gate_all, "blk", split_axis=2, concat_axis=1, tiled=True),
        lax.all_to_all(up_all, "blk", split_axis=2, concat_axis=1, tiled=True),
    )
    rows_in = lax.all_gather(expert_in, "blk", axis=1, tiled=True)
    rows_cot = lax.all_gather(expert_cot, "blk", axis=1, tiled=True)
    gate_w_grad = jnp.einsum("esn,esd->ned", gate_own, rows_in, preferred_element_type=jnp.float32)
    up_w_grad = jnp.einsum("esn,esd->ned", up_own, rows_in, preferred_element_type=jnp.float32)
    down_w_grad = jnp.einsum(
        "esn,esd->ned", hidden_own, rows_cot, preferred_element_type=jnp.float32
    )
    expert_grads = jnp.stack([gate_w_grad, up_w_grad, down_w_grad], axis=2)
    returned, returned_grad = (
        lax.all_to_all(
            out_sum.astype(jnp.bfloat16), "head", split_axis=1, concat_axis=0, tiled=True
        ),
        lax.all_to_all(
            in_grad.astype(jnp.bfloat16), "head", split_axis=1, concat_axis=0, tiled=True
        ),
    )
    outputs_pair = (
        jnp.concatenate([returned.reshape(-1, model_width), zero_row], axis=0)[target]
        .astype(jnp.float32)
        .reshape(tok_dev, 2, model_width)
    )
    input_pair = (
        jnp.concatenate([returned_grad.reshape(-1, model_width), zero_row], axis=0)[target]
        .astype(jnp.float32)
        .reshape(tok_dev, 2, model_width)
    )
    expert_input_grad = input_pair[:, 0] + input_pair[:, 1]
    branch, branch_back = jax.vjp(
        partial(branch_sum, choose=choose, live_rows=live_rows, real_count=real_count),
        router_prob,
        normed_two_f,
        const_w.astype(jnp.float32),
        vector_w.astype(jnp.float32),
        outputs_pair,
    )
    output = ((residual + branch) * live_rows[:, None]).astype(jnp.bfloat16)
    prob_grad, normed_grad_branch, const_grad, vector_grad, unused_grad = branch_back(out_grad)
    aux_grad = aux_weight * expert_count / live_total * fraction[None, :] * live_rows[:, None]
    normed_grad_router, router_grad, mixing_grad = router_back(prob_grad + aux_grad)
    normed_grad = normed_grad_router + normed_grad_branch + expert_input_grad
    residual_grad_norm, gain_two_grad = norm_two_back(normed_grad)
    residual_grad = out_grad + residual_grad_norm
    out_w_grad = jnp.dot(attended_tok.astype(jnp.float32).T, residual_grad, precision=highest)
    attended_grad = jnp.dot(residual_grad, out_w.astype(jnp.float32).T, precision=highest).astype(
        jnp.bfloat16
    )
    attended_grad_heads = lax.all_to_all(
        attended_grad, "head", split_axis=1, concat_axis=0, tiled=True
    )
    key_again, value_again = fetch_prev(key_heads, value_heads, span_count)
    query_grad, key_grad, value_grad = attend_backward(
        query_heads,
        key_again,
        value_again,
        attended_grad_heads,
        log_sums,
        blk_rows,
        key_ids,
        slot_size,
        lengths,
    )
    own_key = key_grad[:tok_blk]
    own_value = value_grad[:tok_blk]
    for offset in range(1, span_count):
        back_key, back_value = shifted(
            (
                for_sending(key_grad[offset * tok_blk : (offset + 1) * tok_blk]),
                for_sending(value_grad[offset * tok_blk : (offset + 1) * tok_blk]),
            ),
            "blk",
            -offset,
        )
        own_key = own_key + back_key
        own_value = own_value + back_value
    local_heads = query_heads.shape[1] // HD
    query_back = (
        rotary(query_grad.reshape(tok_blk, local_heads, HD), blk_pos, -1.0)
        .astype(jnp.bfloat16)
        .reshape(tok_blk, local_heads * HD)
    )
    key_back = (
        rotary(own_key.reshape(tok_blk, local_heads, HD), blk_pos, -1.0)
        .astype(jnp.bfloat16)
        .reshape(tok_blk, local_heads * HD)
    )
    value_back = own_value.astype(jnp.bfloat16)
    query_tok, key_tok, value_tok = (
        lax.all_to_all(query_back, "head", split_axis=0, concat_axis=1, tiled=True),
        lax.all_to_all(key_back, "head", split_axis=0, concat_axis=1, tiled=True),
        lax.all_to_all(value_back, "head", split_axis=0, concat_axis=1, tiled=True),
    )
    projected_grad = jnp.concatenate([query_tok, key_tok, value_tok], axis=1)
    qkv_grad = jnp.dot(normed_one_low.T, projected_grad, preferred_element_type=jnp.float32)
    normed_one_grad = jnp.dot(projected_grad, qkv_w.T, preferred_element_type=jnp.float32)
    inputs_grad_norm, gain_one_grad = norm_one_back(normed_one_grad)
    token_grad = (residual_grad + inputs_grad_norm).astype(jnp.bfloat16)
    weight_grads = (
        lax.psum_scatter(qkv_grad, ("head", "blk"), scatter_dimension=0, tiled=True),
        lax.psum_scatter(out_w_grad, ("head", "blk"), scatter_dimension=0, tiled=True),
        lax.psum_scatter(router_grad, ("head", "blk"), scatter_dimension=0, tiled=True),
        lax.psum_scatter(const_grad, ("head", "blk"), scatter_dimension=0, tiled=True),
        lax.psum_scatter(vector_grad, ("head", "blk"), scatter_dimension=0, tiled=True),
        lax.psum_scatter(
            jnp.stack([gain_one_grad, gain_two_grad], axis=1),
            ("head", "blk"),
            scatter_dimension=0,
            tiled=True,
        ),
    )
    mixing_total = lax.psum(mixing_grad, ("head", "blk"))
    return (
        output,
        aux_loss,
        token_grad,
        weight_grads[0],
        weight_grads[1],
        weight_grads[2],
        weight_grads[3],
        weight_grads[4],
        weight_grads[5],
        mixing_total,
        expert_grads,
    )


def settle_kernel(n, *refs):
    sources, results, (sems, *rooms) = refs[:n], refs[n : 2 * n], refs[2 * n :]
    ins, outs = [], []
    for i in range(n):
        parts = [(sources[i], rooms[i], results[i])]
        if i == n - 1:
            parts = [tuple(r.at[pl.ds(32 * c, 32)] for r in parts[0]) for c in range(4)]
        for src, room, dst in parts:
            ins.append(pltpu.make_async_copy(src, room, sems.at[0, len(ins)]))
            outs.append(pltpu.make_async_copy(room, dst, sems.at[1, len(outs)]))
    for c in ins[::-1]:
        c.start()
    for c, d in zip(ins[::-1], outs[::-1]):
        c.wait()
        d.start()
    for d in outs:
        d.wait()


def settle(*arrays):
    hbm = pl.BlockSpec(memory_space=pl.ANY)
    n = len(arrays)
    return pl.pallas_call(
        functools.partial(settle_kernel, n),
        out_shape=tuple(jax.ShapeDtypeStruct(a.shape, a.dtype) for a in arrays),
        in_specs=[hbm] * n,
        out_specs=(hbm,) * n,
        scratch_shapes=[pltpu.SemaphoreType.DMA((2, n + 3))] + [pltpu.VMEM(a.shape, a.dtype) for a in arrays],
        compiler_params=pltpu.CompilerParams(vmem_limit_bytes=63 * 2**20),
        name="settle",
    )(*arrays)


def on_device_small(
    tokens, cotangent, prev_logits, routes, lengths, w_qkv, w_out, w_router, w_const, const_vec, norm_gains, gate_mix,
    expert_weights,
):
    n_blk = lax.axis_size("blk")
    w_all = lax.all_gather(w_qkv, ("head", "blk"), axis=0, tiled=True)
    norm, q, k, v, o, parts, g_exp, att, smt, cnt, local_out, res_grad, att_grad, g_small, misc, pg, small = front(
        lengths, tokens, cotangent, routes, w_qkv, w_router, w_const, norm_gains, const_vec, w_out, prev_logits, gate_mix,
        expert_weights.transpose(0, 2, 1, 3), n_blk)
    output, token_grad, qkv_grad, g_out, g_router, g_const, g_vec, g_gains, g_mix, aux = attend_back(
        lengths, att_grad, tokens, res_grad, smt, att, local_out, pg, g_small, misc, w_qkv, small, cnt, norm, q, k, v, o, w_all,
        parts, n_blk)
    results = settle(output, token_grad, qkv_grad, g_out, g_router, g_const, g_vec, g_gains, g_mix, aux, g_exp)
    output, token_grad, qkv_grad, g_out, g_router, g_const, g_vec, g_gains, g_mix, aux, g_exp = results
    return (
        output, aux.reshape(()), token_grad, qkv_grad, g_out, g_router.T, g_const.T, g_vec.T, g_gains.T, g_mix,
        g_exp.transpose(0, 2, 1, 3),
    )


def solution(mesh):
    small = mesh.shape["blk"] == 16 and mesh.shape["head"] == 2
    return jax.shard_map(
        on_device_small if small else on_device,
        mesh=mesh,
        in_specs=(
            P(("blk", "head"), None),
            P(("blk", "head"), None),
            P(("blk", "head"), None),
            P(("blk", "head"), None),
            P(),
            P(("head", "blk"), None),
            P(("head", "blk"), None),
            P(("head", "blk"), None),
            P(("head", "blk"), None),
            P(("head", "blk"), None),
            P(("head", "blk"), None),
            P(),
            P("blk", "head", None, None),
        ),
        out_specs=(
            P(("blk", "head"), None),
            P(),
            P(("blk", "head"), None),
            P(("head", "blk"), None),
            P(("head", "blk"), None),
            P(("head", "blk"), None),
            P(("head", "blk"), None),
            P(("head", "blk"), None),
            P(("head", "blk"), None),
            P(),
            P("blk", "head", None, None),
        ),
        check_vma=False,
    )
```

```python
from functools import partial
import functools
import math

import jax
import jax.numpy as jnp
import numpy as np
from jax import lax
from jax.experimental import pallas as pl
from jax.experimental.pallas import tpu as pltpu
from jax.sharding import PartitionSpec as P

HEADS = 12
MESH = pl.DeviceIdType.MESH
f32, bf16 = jnp.float32, jnp.bfloat16
NEG = -1e30
HD = 64
X, C, Y, Z = 1, 2, 4, 8
EARLY = (3, 2, 1)
Z_FIRST = (3, 2, 1)


def place(mask, h, b):
    hb = 1 - h if mask & X else h
    cb = b % 2
    yb = (b // 2) % 2
    zb = (b // 4) % 2
    cb = 1 - cb if mask & C else cb
    yb = 1 - yb if mask & Y else yb
    zb = 1 - zb if mask & Z else zb
    low = zb * 4 + yb * 2 + cb
    return hb, (b // 8) * 8 + low, low * 2 + hb


def head_of(h, b):
    quad = b % 4
    return h * 6 + ((b % 8) // 4) * 3 + quad - quad // 3


def home_of(head):
    h, i = head // 6, head % 6
    return ((i // 3) * 4 + i % 3) * 2 + h


def greet_all(h, b, n_blk):
    barrier = pltpu.get_barrier_semaphore()
    me = b * 2 + h
    total = 2 * n_blk

    def say(k, carry):
        other = (me + k) % total
        pl.semaphore_signal(barrier, inc=1, device_id=(other % 2, other // 2), device_id_type=MESH)
        return carry

    lax.fori_loop(1, total, say, 0)
    return lambda: pl.semaphore_wait(barrier, total - 1)


def turned(qk, cos, sin):
    lane = lax.broadcasted_iota(jnp.int32, qk.shape, 1)
    swapped = jnp.where(lane % 64 < 32, pltpu.roll(qk, 96, 1), pltpu.roll(qk, 32, 1))
    return qk * cos + swapped * sin


def rotary_tables(rows):
    freq = np.exp(np.arange(32, dtype=np.float32) * np.float32(-2.0 * math.log(10000.0) / 64)).astype(np.float32)
    ang = (np.arange(rows, dtype=np.float32)[:, None] * freq[None, :]).astype(np.float32).astype(np.float64)
    cos, sin = np.cos(ang), np.sin(ang)
    return (
        np.concatenate([cos, cos, cos, cos], 1).astype(np.float32),
        np.concatenate([-sin, sin, -sin, sin], 1).astype(np.float32),
    )


class RowGather:
    def __init__(self, buf, sems, h, b, straight=False):
        self.buf, self.h, self.b, self.straight = buf, h, b, straight
        self.parts = range(buf.shape[1])
        self.zs, self.ys, self.cs, self.zr, self.yr, self.cr = sems
        self.z, self.y, self.c = b // 4, (b // 2) % 2, b % 2

    def nth(self, k):
        return nearest(self.z, k)

    def at(self, z, y, c, p):
        return self.buf.at[z * 4 + y * 2 + c, p]

    def copy(self, where, send, recv, device):
        return pltpu.make_async_remote_copy(
            src_ref=where, dst_ref=where, send_sem=send, recv_sem=recv, device_id=device, device_id_type=MESH)

    def along_z(self, k, step, p):
        zz = self.nth(k)
        return self.copy(self.at(zz, self.y, self.c, p), self.zs.at[(step + 1) // 2, k, p], self.zr.at[zz, p],
                         (self.h, self.b + 4 * step))

    def to_z(self, k, p):
        return self.copy(self.at(self.z, self.y, self.c, p), self.zs.at[0, k, p], self.zr.at[self.z, p],
                         (self.h, self.nth(k) * 4 + self.b % 4))

    def over_y(self, k, p):
        zz = self.nth(k)
        return self.copy(self.at(zz, self.y, self.c, p), self.ys.at[k, p], self.yr.at[zz, p],
                         (self.h, self.b + 2 - 4 * self.y))

    def over_core(self, k, far, p):
        zz = self.nth(k)
        yy = 1 - self.y if far else self.y
        return self.copy(self.at(zz, yy, self.c, p), self.cs.at[far, k, p], self.cr.at[far, zz, p],
                         (self.h, self.b + 1 - 2 * self.c))

    def own_z(self, act):
        for p in self.parts:
            if self.straight:
                for k in range(1, 4):
                    act(self.to_z(k, p))
            else:
                for step in (1, -1):
                    @pl.when((self.z + step >= 0) & (self.z + step <= 3))
                    def _(step=step, p=p):
                        act(self.along_z(0, step, p))

    def relay(self, k, p, act):
        if self.straight:
            return
        zz = self.nth(k)

        @pl.when((zz < self.z) & (self.z < 3))
        def _():
            act(self.along_z(k, 1, p))

        @pl.when((zz > self.z) & (self.z > 0))
        def _():
            act(self.along_z(k, -1, p))

    def start(self):
        self.own_z(lambda c: c.start())
        for p in self.parts:
            self.over_y(0, p).start()
        for p in self.parts:
            self.over_core(0, 0, p).start()

    def arrived(self, where, sem):
        self.copy(where, self.zs.at[0, 0, 0], sem, (self.h, self.b)).wait_recv()

    def got_z(self, k):
        zz = self.nth(k)
        for p in self.parts:
            self.arrived(self.at(zz, self.y, self.c, p), self.zr.at[zz, p])
            self.relay(k, p, lambda c: c.start())
            self.over_y(k, p).start()
            self.over_core(k, 0, p).start()

    def got_y(self, k):
        zz = self.nth(k)
        for p in self.parts:
            self.arrived(self.at(zz, 1 - self.y, self.c, p), self.yr.at[zz, p])
            self.over_core(k, 1, p).start()

    def got_core(self, k):
        zz = self.nth(k)
        for far in range(2):
            yy = 1 - self.y if far else self.y
            for p in self.parts:
                self.arrived(self.at(zz, yy, 1 - self.c, p), self.cr.at[far, zz, p])

    def finish(self):
        self.own_z(lambda c: c.wait_send())
        for p in self.parts:
            for k in range(4):
                if k:
                    self.relay(k, p, lambda c: c.wait_send())
                self.over_y(k, p).wait_send()
                self.over_core(k, 0, p).wait_send()
                self.over_core(k, 1, p).wait_send()


def nearest(z, k):
    near = z - (z // 2) * (2 * z - 3)
    low = k + (1 - 2 * k) * near if k < 2 else k
    return low + (z // 2) * (3 - 2 * low)


def gather_sems(parts):
    DMA = pltpu.SemaphoreType.DMA
    return [DMA((2, 4, parts)), DMA((4, parts)), DMA((2, 4, parts)), DMA((4, parts)), DMA((4, parts)), DMA((2, 4, parts))]


def fold(rows):
    half = rows.shape[1] // 2
    low = jnp.concatenate([rows[16:24, :half], rows[16:24, half:]], axis=0)
    return jnp.concatenate([rows[0:16], low], axis=1).astype(bf16)


def routing_table(routes, live):
    lane = lax.broadcasted_iota(jnp.int32, (128, 128), 1)
    row = lax.broadcasted_iota(jnp.int32, (128, 128), 0)
    expert = lane.astype(f32)
    named = jnp.where((routes[:, 0:1] == expert) | (routes[:, 1:2] == expert), live, 0.0)
    before = jnp.where(lane < row, 1.0, 0.0).astype(bf16)
    rank = jnp.dot(before, named.astype(bf16), preferred_element_type=f32)
    return named, named * (rank + 1.0)


def expert_lanes(h):
    e = lax.broadcasted_iota(jnp.int32, (128, 256), 0)
    s = lax.broadcasted_iota(jnp.int32, (128, 256), 1)
    return jnp.where((s < 192) & (e == 4 * h + s // 48), 1.0, 0.0)


def slot_table(ranks, h, source_h):
    spread = jnp.dot(ranks.astype(bf16), expert_lanes(h).astype(bf16), preferred_element_type=f32)
    s = lax.broadcasted_iota(jnp.int32, (128, 256), 1)
    place_in = s % 48 - 24 * source_h
    inside = (place_in >= 0) & (place_in < 24) & (s < 192)
    return jnp.where(inside & (spread == (place_in + 1).astype(f32)), 1.0, 0.0)


def live_column(h, b, length):
    row = lax.broadcasted_iota(jnp.int32, (128, 1), 0) + ((b % 8) * 2 + h) * 128
    return jnp.where(row < length, 1.0, 0.0)


def forward_kernel(
    n_blk, all_here, lengths, tok, cot, routes, w_in, small, wo_in, cos_hbm, sin_hbm, relay_w,
    norm_hbm, q_hbm, k_hbm, v_hbm, o_hbm, att_out, smt_out, cnt_out, sm_out, wo_out, pt_out, cot_rows,
    xg, pieces, got, w_f, w_b, cos, sin, norm, q, k, v, o, sendbuf, att_in, rank_own, rank_far, cot_far, wo_all,
    ag_send, ag_recv, pc_send, pc_recv, at_send, at_recv, loc, x_send, x_recv, *gathers,
):
    h, b = lax.axis_index("head"), lax.axis_index("blk")
    me = b * 2 + h
    total = 2 * n_blk
    _, _, rank = place(0, h, b)
    cos_in = pltpu.make_async_copy(cos_hbm, cos, loc.at[9])
    sin_in = pltpu.make_async_copy(sin_hbm, sin, loc.at[10])
    cos_in.start()
    sin_in.start()
    for p in range(3):
        xg[p, rank] = tok[:, 256 * p : 256 * p + 256]
    all_here()

    def block_copy(p, m, d, slot):
        _, _, r = place(m, h, b)
        ph, pb, _ = place(d, h, b)
        return pltpu.make_async_remote_copy(
            src_ref=xg.at[p, r], dst_ref=xg.at[p, r],
            send_sem=ag_send.at[p, slot], recv_sem=ag_recv.at[p, m ^ d],
            device_id=(ph, pb), device_id_type=MESH,
        )

    def arrival(p, m):
        _, _, r = place(m, h, b)
        return pltpu.make_async_remote_copy(
            src_ref=xg.at[p, r], dst_ref=xg.at[p, r],
            send_sem=ag_send.at[p, 0], recv_sem=ag_recv.at[p, m],
            device_id=(h, b), device_id_type=MESH,
        )

    sends = []
    counts = [0, 0, 0]

    def send(p, m, d):
        copy = block_copy(p, m, d, counts[p])
        counts[p] += 1
        copy.start()
        sends.append(copy)

    dims = [X, Y, Z]
    orders = [dims[p:] + dims[:p] for p in range(3)]
    for t in range(3):
        for p in range(3):
            send(p, 0, orders[p][t])
    for p in range(3):
        send(p, 0, C)

    length = lengths[b // 8]
    named, ranks = routing_table(routes[...], live_column(h, b, length))
    rank_own[...] = ranks.astype(bf16)
    wo_all[b, 0, h] = fold(wo_in[...].astype(f32))

    w24 = w_in[...].astype(f32)
    count = pltpu.roll(jnp.sum(named, axis=0, keepdims=True), 20, 1)[:, 0:64]
    small = small[...] + jnp.where(lax.broadcasted_iota(jnp.int32, (24, 64), 0) == 0, count, 0.0)
    for j in range(12):
        cat = jnp.concatenate(
            [w24[:, 64 * j : 64 * j + 64], w24[:, 768 + 64 * j : 832 + 64 * j],
             w24[:, 1536 + 64 * j : 1600 + 64 * j], small], axis=1)
        pieces[j] = fold(cat)

    def piece_copy(kk):
        other = (me + kk) % total
        oh, ob = other % 2, other // 2
        return pltpu.make_async_remote_copy(
            src_ref=pieces.at[head_of(oh, ob)], dst_ref=got.at[me],
            send_sem=pc_send.at[kk], recv_sem=pc_recv.at[me],
            device_id=(oh, ob), device_id_type=MESH,
        )

    def send_piece(kk, carry):
        piece_copy(kk).start()
        return carry

    lax.fori_loop(1, total, send_piece, 0)
    got[me] = pieces[head_of(h, b)]

    relay_w(0)
    for p in range(3):
        d0, d1, d2 = orders[p]
        arrival(p, d0).wait_recv()
        for d in (d1, d2, C):
            send(p, d0, d)
    relay_w(1)
    for p in range(3):
        d0, d1, d2 = orders[p]
        for m in (d1, d0 ^ d1):
            arrival(p, m).wait_recv()
            for d in (d2, C):
                send(p, m, d)
    swaps = [
        pltpu.make_async_remote_copy(
            src_ref=src, dst_ref=dst, send_sem=x_send.at[n], recv_sem=x_recv.at[n],
            device_id=(1 - h, b), device_id_type=MESH)
        for n, (src, dst) in enumerate([(wo_all.at[b, 0, h], wo_all.at[b, 0, h]), (rank_own, rank_far), (cot, cot_far)])
    ]
    for c in swaps:
        c.start()
    relay_w(2)
    for p in range(3):
        d0, d1, d2 = orders[p]
        for m in (d2, d0 ^ d2, d1 ^ d2, d0 ^ d1 ^ d2):
            arrival(p, m).wait_recv()
            send(p, m, C)

    def take_piece(kk, carry):
        src = (me + kk) % total
        pltpu.make_async_remote_copy(
            src_ref=pieces.at[0], dst_ref=got.at[src],
            send_sem=pc_send.at[0], recv_sem=pc_recv.at[src],
            device_id=(h, b), device_id_type=MESH,
        ).wait_recv()
        return carry

    lax.fori_loop(1, total, take_piece, 0)

    for src in range(2 * n_blk):
        row = 24 * ((src % 2) * n_blk + src // 2)
        w_f[row : row + 16, :] = got[src, :, 0:256].astype(f32)
        low = got[src, :, 256:384].astype(f32)
        w_f[row + 16 : row + 24, 0:128] = low[0:8]
        w_f[row + 16 : row + 24, 128:256] = low[8:16]
    w_b[...] = w_f[...].astype(bf16)
    sm = pltpu.roll(w_f[:, 128:256], 64, 1)
    lane = lax.broadcasted_iota(jnp.int32, (768, 128), 1)
    cnt = jnp.sum(jnp.where((lane >= 20) & (lane < 32), sm, 0.0), axis=0, keepdims=True)
    cnt_out[...] = jnp.broadcast_to(pltpu.roll(cnt, 108, 1), (8, 128))
    sm = jnp.where(lane < 20, sm, 0.0)
    sm_out[...] = sm.astype(bf16)
    smt = jnp.transpose(sm)
    smt_out[...] = smt[0:32, :]
    gain = smt[16:17, :]

    pltpu.make_async_remote_copy(
        src_ref=wo_all.at[b, 0, h], dst_ref=wo_all.at[b, 0, 1 - h], send_sem=x_send.at[0], recv_sem=x_recv.at[0],
        device_id=(h, b), device_id_type=MESH).wait_recv()
    wo_gather = RowGather(wo_all, gathers[0:6], h, b, straight=True)
    wo_gather.start()
    swaps[1].wait_recv()
    swaps[2].wait_recv()
    pt = [slot_table(ranks, h, h).astype(bf16), slot_table(rank_far[...].astype(f32), h, 1 - h).astype(bf16)]
    pt_out[0] = pt[0]
    pt_out[1] = pt[1]
    picked = sum(
        lax.dot_general(t[:, 0:192], c[...], (((0,), (0,)), ((), ())), preferred_element_type=f32)
        for t, c in zip(pt, (cot, cot_far))).astype(bf16)
    cot_rows[b, 0] = picked[0:96]
    cot_rows[b, 1] = picked[96:192]
    cot_gather = RowGather(cot_rows, gathers[6:12], h, b, straight=True)
    cot_gather.start()

    cos_in.wait()
    sin_in.wait()

    def one_block(r, carry):
        x = [xg[p, r].astype(f32) for p in range(3)]
        mean = sum(jnp.sum(t * t, axis=1, keepdims=True) for t in x) * (1.0 / 768)
        scale = lax.rsqrt(mean + 1e-6)
        rows = pl.ds(pl.multiple_of(r * 128, 128), 128)
        acc = jnp.zeros((128, 256), f32)
        for p in range(3):
            n = (x[p] * scale * gain[:, 256 * p : 256 * p + 256]).astype(bf16)
            norm[rows, 256 * p : 256 * p + 256] = n
            acc = acc + jnp.dot(n, w_b[256 * p : 256 * p + 256, :], preferred_element_type=f32)
        qk = turned(acc[:, 0:128], cos[rows, :], sin[rows, :])
        q[rows, :] = (qk[:, 0:64] * 0.125).astype(bf16)
        k[rows, :] = qk[:, 64:128].astype(bf16)
        lane = lax.broadcasted_iota(jnp.int32, (128, 128), 1)
        v[rows, :] = jnp.where(lane < 64, acc[:, 128:256], jnp.where(lane == 64, 1.0, 0.0)).astype(bf16)
        return carry

    def of_core(core):
        return lambda i, carry: one_block((i // 4) * 8 + ((i // 2) % 2) * 4 + core * 2 + i % 2, carry)

    lax.fori_loop(0, 8, of_core(b % 2), 0)
    for p in range(3):
        for m in (C, C ^ X, C ^ Y, C ^ Z, C ^ X ^ Y, C ^ X ^ Z, C ^ Y ^ Z, C ^ X ^ Y ^ Z):
            arrival(p, m).wait_recv()
    lax.fori_loop(0, 8, of_core(1 - b % 2), 0)
    stores = [
        pltpu.make_async_copy(norm, norm_hbm, loc.at[4]),
        pltpu.make_async_copy(q, q_hbm, loc.at[5]),
        pltpu.make_async_copy(k, k_hbm, loc.at[6]),
        pltpu.make_async_copy(v, v_hbm, loc.at[7]),
    ]
    for s in stores:
        s.start()

    head = head_of(h, b)
    working = (b % 4) != 3
    base = (b // 8) * 8

    w, c = wo_gather, cot_gather
    between = {
        0: [lambda: w.got_z(1), lambda: w.got_y(0)],
        1: [lambda: w.got_z(2), lambda: w.got_z(3)],
        2: [lambda: w.got_y(1)],
        3: [lambda: w.got_y(2), lambda: c.got_z(1)],
        4: [lambda: w.got_y(3)],
        5: [lambda: w.got_core(0), lambda: w.got_core(1), lambda: c.got_y(0)],
        6: [lambda: w.got_core(2), lambda: w.got_core(3)],
        7: [],
    }

    def out_copy(r):
        return pltpu.make_async_remote_copy(
            src_ref=sendbuf.at[r], dst_ref=att_in.at[head],
            send_sem=at_send.at[r], recv_sem=at_recv.at[head],
            device_id=(r % 2, base + r // 2), device_id_type=MESH,
        )

    for i in range(8):
        width = 256 * (i + 1)
        s = lax.dot_general(q[256 * i : width, :], k[0:width, :], (((1,), (1,)), ((), ())), preferred_element_type=f32)
        key = lax.broadcasted_iota(jnp.int32, (1, width), 1)
        s = s + jnp.where(key < length, 0.0, NEG)
        rowi = lax.broadcasted_iota(jnp.int32, (256, 256), 0)
        coli = lax.broadcasted_iota(jnp.int32, (256, 256), 1)
        last = jnp.where(coli <= rowi, s[:, width - 256 :], NEG)
        s = last if i == 0 else jnp.concatenate([s[:, : width - 256], last], axis=1)
        m = jnp.max(s, axis=1, keepdims=True)
        e = jnp.exp(s - m).astype(bf16)
        ov = jnp.dot(e, v[0:width, :], preferred_element_type=f32)
        l = ov[:, 64:65]
        lane = lax.broadcasted_iota(jnp.int32, (256, 128), 1)
        ov = jnp.where(lane < 64, ov / l, m + jnp.log(l))
        o[256 * i : width, :] = ov
        oh = ov[:, 0:64]
        for half in range(2):
            r = 2 * i + half
            packed = jnp.concatenate([oh[128 * half : 128 * half + 64], oh[128 * half + 64 : 128 * half + 128]], axis=1)
            sendbuf[r] = packed.astype(bf16)

            @pl.when(working & (r != rank))
            def _(r=r):
                out_copy(r).start()
        for act in between[i]:
            act()

    o_store = pltpu.make_async_copy(o, o_hbm, loc.at[8])
    o_store.start()

    def unfolded(blk, hh):
        t = wo_all[blk, 0, hh].astype(f32)
        return jnp.concatenate(
            [t[:, 0:768], jnp.concatenate([t[0:8, 768:1152], t[8:16, 768:1152]], axis=1)], axis=0)

    for hh in range(2):
        for blk in range(0, 16, 2):
            row = 24 * (hh * 16 + blk)
            wo_out[row : row + 48, :] = jnp.concatenate([unfolded(blk, hh), unfolded(blk + 1, hh)], axis=0).astype(bf16)

    @pl.when(working)
    def _():
        att_in[head] = sendbuf[rank]

    for j in range(12):
        @pl.when(rank != home_of(j))
        def _(j=j):
            pltpu.make_async_remote_copy(
                src_ref=sendbuf.at[0], dst_ref=att_in.at[j],
                send_sem=at_send.at[0], recv_sem=at_recv.at[j],
                device_id=(h, b), device_id_type=MESH,
            ).wait_recv()

    for j in range(0, 12, 2):
        one, two = att_in[j].astype(f32), att_in[j + 1].astype(f32)
        att_out[0:64, 64 * j : 64 * j + 128] = jnp.concatenate([one[:, 0:64], two[:, 0:64]], axis=1).astype(bf16)
        att_out[64:128, 64 * j : 64 * j + 128] = jnp.concatenate([one[:, 64:128], two[:, 64:128]], axis=1).astype(bf16)

    def finish():
        for copy in sends:
            copy.wait_send()
        for c in swaps:
            c.wait_send()
        wo_gather.finish()
        cot_gather.finish()

        def sent_piece(kk, carry):
            piece_copy(kk).wait_send()
            return carry

        lax.fori_loop(1, total, sent_piece, 0)
        for r in range(16):
            @pl.when(working & (r != rank))
            def _(r=r):
                out_copy(r).wait_send()
        for s in stores:
            s.wait()
        o_store.wait()

    return cot_gather, finish


def split(x):
    high = x.astype(bf16)
    return high, (x - high.astype(f32)).astype(bf16)


def exact_dot(x, y, dims):
    high, low = split(x)
    return lax.dot_general(high, y, (dims, ((), ())), preferred_element_type=f32) + lax.dot_general(
        low, y, (dims, ((), ())), preferred_element_type=f32)


def softmax_back(p, d):
    return p * (d - jnp.sum(p * d, axis=1, keepdims=True))


def lane_of(column, n):
    lane = lax.broadcasted_iota(jnp.int32, (128, 128), 1)
    return jnp.where(lane == n, column, 0.0)


class RowScatter:
    def __init__(self, part, from_core, from_y, from_z, sems, h, b):
        self.part, self.from_core, self.from_y, self.from_z = part, from_core, from_y, from_z
        self.h, self.b = h, b
        self.cs, self.cr, self.ys, self.yr, self.zs, self.zr = sems
        self.parts = range(part.shape[1])
        self.order = [(k, p) for k in (3, 2, 1, 0) for p in self.parts]
        self.z, self.y, self.c = b // 4, (b // 2) % 2, b % 2

    def nth(self, k):
        return nearest(self.z, k)

    def blk(self, k, far_y, far_c):
        y = 1 - self.y if far_y else self.y
        c = 1 - self.c if far_c else self.c
        return self.nth(k) * 4 + y * 2 + c

    def remote(self, src, dst, send, recv, device):
        return pltpu.make_async_remote_copy(
            src_ref=src, dst_ref=dst, send_sem=send, recv_sem=recv, device_id=device, device_id_type=MESH)

    def core(self, k, far, p):
        return self.remote(self.part.at[self.blk(k, far, 1), p], self.from_core.at[k, far, p], self.cs.at[k, far, p],
                           self.cr.at[k, far, p], (self.h, self.b + 1 - 2 * self.c))

    def over_y(self, k, p):
        return self.remote(self.part.at[self.blk(k, 1, 0), p], self.from_y.at[k, p], self.ys.at[k, p], self.yr.at[k, p],
                           (self.h, self.b + 2 - 4 * self.y))

    def to_z(self, k, p):
        return self.remote(self.part.at[self.blk(k, 0, 0), p], self.from_z.at[self.z, p], self.zs.at[k, p],
                           self.zr.at[self.z, p], (self.h, self.nth(k) * 4 + self.b % 4))

    def join_y(self, k, p):
        self.core(k, 0, p).wait_recv()
        self.over_y(k, p).wait_recv()
        self.add(self.blk(k, 0, 0), p, self.from_core.at[k, 0, p], self.from_y.at[k, p])

    def add(self, blk, p, *others):
        total = self.part[blk, p].astype(f32)
        for other in others:
            total = total + other[...].astype(f32)
        self.part[blk, p] = total.astype(bf16)

    def send_core(self, k, p):
        self.core(k, 1, p).start()
        self.core(k, 0, p).start()

    def send_y(self, k, p):
        self.core(k, 1, p).wait_recv()
        self.add(self.blk(k, 1, 0), p, self.from_core.at[k, 1, p])
        self.over_y(k, p).start()

    def send_z(self, k, p):
        self.join_y(k, p)
        if k:
            self.to_z(k, p).start()

    def total(self, p):
        total = self.part[self.b, p].astype(f32)
        for k in range(1, 4):
            here = self.from_z.at[self.nth(k), p]
            self.remote(here, here, self.zs.at[0, 0], self.zr.at[self.nth(k), p], (self.h, self.b)).wait_recv()
            total = total + here[...].astype(f32)
        return total

    def finish(self, near=range(4), far=range(1, 4)):
        for p in self.parts:
            for k in near:
                self.core(k, 0, p).wait_send()
                self.core(k, 1, p).wait_send()
                self.over_y(k, p).wait_send()
            for k in far:
                self.to_z(k, p).wait_send()


def scatter_scratch(parts, rows, cols):
    DMA = pltpu.SemaphoreType.DMA
    V = pltpu.VMEM
    return [
        V((4, 2, parts, rows, cols), bf16), V((4, parts, rows, cols), bf16), V((4, parts, rows, cols), bf16),
        DMA((4, 2, parts)), DMA((4, 2, parts)), DMA((4, parts)), DMA((4, parts)), DMA((4, parts)), DMA((4, parts)),
    ]


def expert_kernel(
    n_blk, cg, lengths, att, tok, cot, prev, mix, routes, wout, sm, smt, cnt, pt, w, cot_all,
    part_hbm, g_hbm, local_out, res_out, ag_out, gs_out, misc_out, pg_out,
    x_all, cc, dgu, hid, inp, outp, gbuf, gates_in, vs_out, vs_in, n_own, n_far, g_own, g_far,
    d_out, d_in, dv_out, dv_in, ga_send, ga_recv, vs_send, vs_recv, x_send, x_recv, loc, *rest,
):
    gsems, (from_core, from_y, from_z), ssems, (out_core, out_y), osems = rest[0:6], rest[6:9], rest[9:15], rest[15:17], rest[17:21]
    h, b = lax.axis_index("head"), lax.axis_index("blk")
    length = lengths[b // 8]
    live_total = (lengths[0] + lengths[1]).astype(f32)
    live = live_column(h, b, length)
    lane = lax.broadcasted_iota(jnp.int32, (128, 128), 1)

    res = tok[...].astype(f32) + jnp.dot(att[...], wout[...], preferred_element_type=f32)
    scale = lax.rsqrt(jnp.sum(res * res, axis=1, keepdims=True) * (1.0 / 768) + 1e-6)
    xh = res * scale
    n2 = (xh * smt[17:18, :]).astype(bf16)
    small = sm[...]
    logits = jnp.dot(n2, small, preferred_element_type=f32)
    router = logits + jnp.dot(prev[...], mix[...], preferred_element_type=f32, precision=lax.Precision.HIGHEST)
    router = jnp.where(lane < 12, router, NEG)
    prob = jnp.exp(router - jnp.max(router, axis=1, keepdims=True))
    prob = prob / jnp.sum(prob, axis=1, keepdims=True)
    expert = lane.astype(f32)
    named = jnp.where((routes[:, 0:1] == expert) | (routes[:, 1:2] == expert), 1.0, 0.0)
    gates = prob * named
    n_own[...] = n2
    g_own[...] = gates
    swaps = [
        pltpu.make_async_remote_copy(
            src_ref=src, dst_ref=dst, send_sem=x_send.at[n], recv_sem=x_recv.at[n],
            device_id=(1 - h, b), device_id_type=MESH)
        for n, (src, dst) in enumerate([(n_own, n_far), (g_own, g_far), (d_out, d_in), (dv_out, dv_in)])
    ]
    swaps[0].start()
    swaps[1].start()
    cg.got_z(2)
    cg.got_y(1)
    p_own, p_far = pt[0, :, 0:192], pt[1, :, 0:192]
    rows = ((0,), (0,))
    mine = lax.dot_general(p_own, n2, (rows, ((), ())), preferred_element_type=f32)
    spread = expert_lanes(h).astype(bf16)
    pg_own = pt[0].astype(f32) * exact_dot(gates, spread, ((1,), (0,)))
    pg_out[0] = pg_own
    swaps[0].wait_recv()
    picked = (mine + lax.dot_general(p_far, n_far[...], (rows, ((), ())), preferred_element_type=f32)).astype(bf16)
    x_all[b, 0] = picked[0:96]
    x_all[b, 1] = picked[96:192]
    g = RowGather(x_all, gsems, h, b)
    g.start()
    cg.got_z(3)
    cg.got_y(2)
    cg.got_y(3)
    swaps[1].wait_recv()
    pg_far = pt[1].astype(f32) * exact_dot(g_far[...], spread, ((1,), (0,)))
    pg_out[1] = pg_far
    gates_in[b] = jnp.broadcast_to(jnp.sum(pg_own + pg_far, axis=0, keepdims=True), (8, 256))

    def gate_copy(k):
        return pltpu.make_async_remote_copy(
            src_ref=gates_in.at[b], dst_ref=gates_in.at[b], send_sem=ga_send.at[k], recv_sem=ga_recv.at[b],
            device_id=(h, (b + k) % n_blk), device_id_type=MESH)

    def vs_copy(k):
        to = (b + k) % n_blk
        return pltpu.make_async_remote_copy(
            src_ref=vs_out.at[to], dst_ref=vs_in.at[b], send_sem=vs_send.at[k], recv_sem=vs_recv.at[b],
            device_id=(h, to), device_id_type=MESH)

    def each(act):
        def body(k, carry):
            act(k)
            return carry

        lax.fori_loop(1, n_blk, body, 0)

    each(lambda k: gate_copy(k).start())

    def group(ref, k, p, ee):
        return ref[pl.ds(4 * g.nth(k), 4), p, 48 * ee : 48 * ee + 48, :]

    def put(ref, k, p, ee, value):
        ref[pl.ds(4 * g.nth(k), 4), p, 48 * ee : 48 * ee + 48, :] = value.reshape(4, 48, value.shape[1]).astype(ref.dtype)

    cols = ((1,), (1,))

    def cot_task(k):
        for e in range(4):
            rows_c = group(cot_all, k, e // 2, e % 2).reshape(192, 768)
            put(cc, k, e // 2, e % 2, lax.dot_general(rows_c, w[3 * e + 2], (cols, ((), ())), preferred_element_type=f32))

    def up_task(k):
        for e in range(4):
            p, ee = e // 2, e % 2
            x = group(x_all, k, p, ee).reshape(192, 768)
            both = lax.dot_general(x, w[3 * e : 3 * e + 2].reshape(256, 768), (cols, ((), ())), preferred_element_type=f32)
            gate, up = both[:, 0:128], both[:, 128:256]
            sig = 1.0 / (1.0 + jnp.exp(-gate))
            silu = gate * sig
            hidden = silu * up
            c = group(cc, k, p, ee).reshape(192, 128)
            put(hid, k, p, ee, hidden)
            put(cc, k, p, ee, hidden * c)
            dg = c * up * (sig * (1.0 + gate * (1.0 - sig)))
            put(dgu, k, p, ee, jnp.concatenate([dg, c * silu], axis=1))

    two = jnp.where(lane % 2 == 0, pltpu.roll(logits, 127, 1), pltpu.roll(logits, 1, 1))
    top = jnp.maximum(logits, two)
    c_mix = jnp.exp(logits - top) / (jnp.exp(logits - top) + jnp.exp(two - top))
    share = gates * live
    n2f = n2.astype(f32)
    alpha = share[:, 9:10] + share[:, 10:11] * c_mix[:, 12:13] + share[:, 11:12] * c_mix[:, 14:15]
    beta = [share[:, 10:11] * c_mix[:, 13:14], share[:, 11:12] * c_mix[:, 15:16]]
    local_out[...] = live * (res + alpha * n2f + beta[0] * smt[18:19, :] + beta[1] * smt[19:20, :])
    og = live * cot[...].astype(f32)
    og_low = og.astype(bf16)

    g.got_z(1)
    cg.got_core(0)
    cot_task(0)
    g.got_z(2)
    g.got_y(0)
    cg.got_core(1)
    cot_task(1)
    g.got_z(3)
    g.got_y(1)
    cg.got_core(2)
    cot_task(2)
    cg.got_core(3)
    cot_task(3)
    g.got_core(0)
    up_task(0)
    g.got_y(2)
    g.got_core(1)
    up_task(1)
    g.got_y(3)
    g.got_core(2)
    up_task(2)
    g.got_core(3)
    up_task(3)

    s = RowScatter(inp, from_core, from_y, from_z, ssems, h, b)
    order = s.order
    for n, (k, p) in enumerate(order):
        for ee in range(2):
            e = 2 * p + ee
            d = group(dgu, k, p, ee).reshape(192, 256)
            put(inp, k, p, ee, jnp.dot(d, w[3 * e : 3 * e + 2].reshape(256, 768), preferred_element_type=f32))
        s.send_core(k, p)
        if n:
            s.send_y(*order[n - 1])
    s.send_y(*order[7])

    ones = jnp.ones((8, 128), f32)

    def one_blk(j, carry):
        for p in range(2):
            vs_out[j, :, 128 * p : 128 * p + 96] = lax.dot_general(
                ones, cc[j, p], (cols, ((), ())), preferred_element_type=f32, precision=lax.Precision.HIGHEST)
        return carry

    lax.fori_loop(0, n_blk, one_blk, 0)
    each(lambda k: vs_copy(k).start())
    vs_in[b] = vs_out[b]
    each(lambda k: pltpu.make_async_remote_copy(
        src_ref=gates_in.at[b], dst_ref=gates_in.at[(b + k) % n_blk], send_sem=ga_send.at[0],
        recv_sem=ga_recv.at[(b + k) % n_blk], device_id=(h, b), device_id_type=MESH).wait_recv())
    gate_cols = jnp.transpose(gates_in[:, 0, :])

    def scaled(ref, p, ee):
        e = 2 * p + ee
        t = ref[:, p, 48 * ee : 48 * ee + 48, :].astype(f32)
        col = jnp.concatenate([gate_cols[48 * e : 48 * e + 48, j : j + 1] for j in range(n_blk)], axis=0)
        return (t.reshape(48 * n_blk, t.shape[2]) * col).astype(bf16)

    def store_g(e, act):
        for kind in range(3):
            act(pltpu.make_async_copy(gbuf.at[kind], g_hbm.at[:, kind, e, :], loc.at[kind]))

    def weight_task(e):
        p, ee = e // 2, e % 2
        x = x_all[:, p, 48 * ee : 48 * ee + 48, :].reshape(48 * n_blk, 768)
        c = cot_all[:, p, 48 * ee : 48 * ee + 48, :].reshape(48 * n_blk, 768)
        if e:
            store_g(e - 1, lambda c: c.wait())
        gbuf[0:2] = lax.dot_general(
            scaled(dgu, p, ee), x, (rows, ((), ())), preferred_element_type=f32).reshape(2, 128, 768)
        gbuf[2] = lax.dot_general(scaled(hid, p, ee), c, (rows, ((), ())), preferred_element_type=f32)
        store_g(e, lambda c: c.start())

    def out_task(k):
        for e in range(4):
            d = group(hid, k, e // 2, e % 2).reshape(192, 128)
            put(outp, k, e // 2, e % 2, jnp.dot(d, w[3 * e + 2], preferred_element_type=f32))

    outs = RowScatter(outp, out_core, out_y, None, (*osems, None, None), h, b)
    early = [(k, p) for k in EARLY for p in range(2)]

    def send_early():
        for n in early:
            outs.send_core(*n)
        for n in early:
            outs.send_y(*n)

    tasks = [[lambda: out_task(3), lambda: out_task(2)], [lambda: out_task(1), lambda: out_task(0)], [send_early],
             [lambda: weight_task(0)], [lambda: weight_task(1)], [lambda: weight_task(2)], [lambda: weight_task(3)], []]
    def sum_step(n):
        for act in tasks[n]:
            act()
        s.send_z(*order[n])

    def part_store(k, whole):
        zz = g.nth(k)
        at = pl.ds(4 * zz, 4) if whole else pl.ds(outs.blk(k, 0, 0), 1)
        return pltpu.make_async_copy(outp.at[at], part_hbm.at[at], loc.at[3 + k])

    for n in range(6):
        sum_step(n)
    for k in range(4):
        if k not in EARLY:
            part_store(k, True).start()

    each(lambda k: pltpu.make_async_remote_copy(
        src_ref=vs_in.at[b], dst_ref=vs_in.at[(b + k) % n_blk], send_sem=vs_send.at[0],
        recv_sem=vs_recv.at[(b + k) % n_blk], device_id=(h, b), device_id_type=MESH).wait_recv())
    vsum = jnp.sum(vs_in[:, 0, :], axis=0, keepdims=True)
    vrow = jnp.concatenate([vsum[:, 0:96], vsum[:, 128:224]], axis=1)
    spread = spread[:, 0:192]
    dv_out[...] = exact_dot(p_far.astype(f32) * vrow, spread, cols)
    swaps[3].start()
    dv_own = exact_dot(p_own.astype(f32) * vrow, spread, cols)
    u = jnp.sum(og * n2f, axis=1, keepdims=True)
    wj = jnp.dot(og_low, small, preferred_element_type=f32)
    w0, w1 = wj[:, 18:19], wj[:, 19:20]
    c = [c_mix[:, n : n + 1] for n in (12, 13, 14, 15)]
    dgate = lane_of(u, 9) + lane_of(c[0] * u + c[1] * w0, 10) + lane_of(c[2] * u + c[3] * w1, 11)
    dmix = lane_of(u, 12) + lane_of(w0, 13) + lane_of(u, 14) + lane_of(w1, 15)
    dmix = dmix * jnp.where(lane < 14, gates[:, 10:11], gates[:, 11:12])
    both = c_mix * dmix
    dmix = c_mix * (dmix - both - jnp.where(lane % 2 == 0, pltpu.roll(both, 127, 1), pltpu.roll(both, 1, 1)))
    dmix = jnp.where((lane >= 12) & (lane < 16), dmix, 0.0)
    aux = (0.01 * 12.0 / live_total) * (cnt[0:1, :] / (2.0 * live_total)) * live
    sum_step(6)
    swaps[3].wait_recv()
    dprob = named * (dgate + dv_own + dv_in[...]) + aux
    dlog = softmax_back(prob, dprob) + dmix
    dn_near = og * alpha + exact_dot(dlog, jnp.where(
        lax.broadcasted_iota(jnp.int32, (768, 128), 1) < 16, small, 0).astype(bf16), cols)
    dl_high, dl_low = split(dlog)
    gs = lax.dot_general(n2, dl_high, (rows, ((), ())), preferred_element_type=f32)
    gs = gs + lax.dot_general(n2, dl_low, (rows, ((), ())), preferred_element_type=f32)
    b_high, b_low = split(lane_of(beta[0], 18) + lane_of(beta[1], 19))
    gs = gs + lax.dot_general(og_low, b_high, (rows, ((), ())), preferred_element_type=f32)
    gs_out[...] = gs + lax.dot_general(og_low, b_low, (rows, ((), ())), preferred_element_type=f32)
    mixed = lax.dot_general(prev[...], jnp.where(lane < 12, dlog, 0.0), (rows, ((), ())), preferred_element_type=f32,
                            precision=lax.Precision.HIGHEST)
    misc_out[0:16, :] = mixed[0:16]
    misc_out[16:24, :] = jnp.broadcast_to(jnp.sum(prob * live, axis=0, keepdims=True), (8, 128))
    sum_step(7)

    din = jnp.concatenate([s.total(0), s.total(1)], axis=0).astype(bf16)
    into = ((1,), (0,))
    d_out[...] = exact_dot(pg_far[:, 0:192], din, into).astype(bf16)
    swaps[2].start()
    dn_near = dn_near + exact_dot(pg_own[:, 0:192], din, into)
    swaps[2].wait_recv()
    dn = dn_near + d_in[...].astype(f32)
    t = dn * smt[17:18, :]
    rg = og + scale * (t - xh * (jnp.sum(t * xh, axis=1, keepdims=True) * (1.0 / 768)))
    res_out[...] = rg
    ag_out[...] = lax.dot_general(rg.astype(bf16), wout[...], (cols, ((), ())), preferred_element_type=f32).astype(bf16)
    gain = jnp.broadcast_to(jnp.sum(dn * xh, axis=0, keepdims=True), (128, 768))
    gs_out[...] += jnp.where(lax.broadcasted_iota(jnp.int32, (768, 128), 1) == 17, jnp.transpose(gain), 0.0)

    for n in early:
        outs.join_y(*n)
    for k in EARLY:
        part_store(k, False).start()
    g.finish()
    s.finish()
    outs.finish(EARLY, ())
    each(lambda k: gate_copy(k).wait_send())
    each(lambda k: vs_copy(k).wait_send())
    for c in swaps:
        c.wait_send()
    for k in range(4):
        part_store(k, k not in EARLY).wait()
    store_g(3, lambda c: c.wait())


def front_kernel(n_blk, *refs):
    (lengths, tok, cot, routes_t, w_in, router_t, const_t, gains_t, vec_t, wo_in, prev_t, mix_in, cos_hbm, sin_hbm, w_hbm,
     norm_hbm, q_hbm, k_hbm, v_hbm, o_hbm, part_hbm, g_hbm, att, smt, cnt, local_out, res_out, ag_out, gs_out, misc_out, pg_out,
     gain_out, sm, wout, pt, cot_rows, turn, w, w_part, wsem, *scratch) = refs
    all_here = greet_all(lax.axis_index("head"), lax.axis_index("blk"), n_blk)
    w_loads = [pltpu.make_async_copy(w_hbm.at[:, kind], w_part.at[kind], wsem.at[kind]) for kind in range(3)]
    for c in w_loads:
        c.start()
    turn[...] = jnp.zeros_like(turn)
    turn[0, 0:12, 0:24] = router_t[...].astype(f32)
    turn[0, 12:16, 0:24] = const_t[...].astype(f32)
    turn[0, 16:18, 0:24] = gains_t[...].astype(f32)
    turn[0, 18:20, 0:24] = vec_t[...].astype(f32)
    turn[1, 0:2, :] = routes_t[...].astype(f32)
    turn[2, 0:12, :] = prev_t[...]
    turn[3, 0:12, 0:12] = mix_in[...]
    small = jnp.transpose(turn[0])[0:24, 0:64]
    gain_out[...] = small
    routes = jnp.transpose(turn[1])
    prev = jnp.transpose(turn[2])

    def relay_w(kind):
        w_loads[kind].wait()
        t = w_part[kind].astype(f32)
        for e in range(4):
            w[3 * e + kind] = t[:, e, :].astype(bf16)

    cot_gather, finish = forward_kernel(
        n_blk, all_here, lengths, tok, cot, routes, w_in, small, wo_in, cos_hbm, sin_hbm, relay_w, norm_hbm, q_hbm, k_hbm, v_hbm, o_hbm,
        att, smt, cnt, sm, wout, pt, cot_rows, *scratch[: len(forward_scratch(n_blk))])
    expert_kernel(
        n_blk, cot_gather, lengths, att, tok, cot, prev, turn.at[3], routes, wout, sm, smt, cnt, pt, w, cot_rows,
        part_hbm, g_hbm, local_out, res_out, ag_out, gs_out, misc_out, pg_out, *scratch[len(forward_scratch(n_blk)) :])
    finish()


def forward_scratch(n_blk):
    V, DMA = pltpu.VMEM, pltpu.SemaphoreType.DMA
    return [
        V((3, 16, 128, 256), bf16), V((12, 16, 384), bf16), V((2 * n_blk, 16, 384), bf16), V((768, 256), f32),
        V((768, 256), bf16), V((2048, 128), f32), V((2048, 128), f32), V((2048, 768), bf16), V((2048, 64), bf16),
        V((2048, 64), bf16), V((2048, 128), bf16), V((2048, 128), f32), V((16, 64, 128), bf16), V((12, 64, 128), bf16),
        V((128, 128), bf16), V((128, 128), bf16), V((128, 768), bf16), V((n_blk, 1, 2, 16, 1152), bf16),
        DMA((3, 16)), DMA((3, 16)), DMA((2 * n_blk,)), DMA((2 * n_blk,)), DMA((16,)), DMA((12,)), DMA((11,)), DMA((3,)), DMA((3,)),
        *gather_sems(1), *gather_sems(2),
    ]


def expert_scratch(n_blk):
    V, DMA = pltpu.VMEM, pltpu.SemaphoreType.DMA
    return [
        V((n_blk, 2, 96, 768), bf16),
        V((n_blk, 2, 96, 128), f32), V((n_blk, 2, 96, 256), bf16), V((n_blk, 2, 96, 128), bf16),
        V((n_blk, 2, 96, 768), bf16), V((n_blk, 2, 96, 768), bf16), V((3, 128, 768), f32),
        V((n_blk, 8, 256), f32), V((n_blk, 8, 256), f32), V((n_blk, 8, 256), f32),
        V((128, 768), bf16), V((128, 768), bf16), V((128, 128), f32), V((128, 128), f32),
        V((128, 768), bf16), V((128, 768), bf16), V((128, 128), f32), V((128, 128), f32),
        DMA((n_blk,)), DMA((n_blk,)), DMA((n_blk,)), DMA((n_blk,)), DMA((4,)), DMA((4,)), DMA((7,)),
        *gather_sems(2), *scatter_scratch(2, 96, 768),
        V((4, 2, 2, 96, 768), bf16), V((4, 2, 96, 768), bf16), DMA((4, 2, 2)), DMA((4, 2, 2)), DMA((4, 2)), DMA((4, 2)),
    ]


def front(lengths, tokens, cotangent, routes, w_qkv, w_router, w_const, gains, vec, w_out, prev, mix, w, n_blk):
    cos, sin = rotary_tables(2048)
    vm = pl.BlockSpec(memory_space=pltpu.VMEM)
    hbm = pl.BlockSpec(memory_space=pl.ANY)
    sds = jax.ShapeDtypeStruct
    V = pltpu.VMEM
    return pl.pallas_call(
        functools.partial(front_kernel, n_blk),
        out_shape=(
            sds((2048, 768), bf16), sds((2048, 64), bf16), sds((2048, 64), bf16), sds((2048, 128), bf16),
            sds((2048, 128), f32), sds((n_blk, 2, 96, 768), bf16), sds((128, 3, 4, 768), f32),
            sds((128, 768), bf16), sds((32, 768), f32), sds((8, 128), f32), sds((128, 768), f32), sds((128, 768), f32),
            sds((128, 768), bf16), sds((768, 128), f32), sds((24, 128), f32), sds((2, 128, 256), f32),
            sds((24, 64), f32),
        ),
        in_specs=[pl.BlockSpec(memory_space=pltpu.SMEM)] + [vm] * 11 + [hbm] * 3,
        out_specs=(hbm,) * 7 + (vm,) * 10,
        scratch_shapes=[
            V((768, 128), bf16), V((768, 768), bf16), V((2, 128, 256), bf16), V((n_blk, 2, 96, 768), bf16),
            V((4, 128, 128), f32), V((12, 128, 768), bf16), V((3, 128, 4, 768), bf16), pltpu.SemaphoreType.DMA((3,)),
            *forward_scratch(n_blk), *expert_scratch(n_blk),
        ],
        compiler_params=pltpu.CompilerParams(collective_id=0, has_side_effects=True, vmem_limit_bytes=63 * 2**20),
        cost_estimate=pl.CostEstimate(flops=8 * 10**9, bytes_accessed=3 * 10**7, transcendentals=0),
        name="front",
    )(lengths, tokens, cotangent, routes.T, w_qkv, w_router.T, w_const.T, gains.T, vec.T, w_out, prev.T, mix,
      jnp.asarray(cos), jnp.asarray(sin), w)


def backward_kernel(
    n_blk, lengths, ag, tok, res_grad, smt, att, local_out, pg, g_small, misc, w_own, small, cnt,
    norm_hbm, q_hbm, k_hbm, v_hbm, o_hbm, cos_hbm, sin_hbm, w_hbm, part_hbm,
    out, dtok_out, gq_out, go_out, router_out, const_out, vec_out, gains_out, mix_out, aux_out,
    norm, q, k, v, o, cos, sin, w_all, agbuf, do_in, do, dk, dv, dqkv, obuf, got, dproj, turn, g_f, gbuf, g_in,
    part, gpart, gfar, gsum, far_out, far_in, misc_sum, misc_in,
    a_send, a_recv, b_send, b_recv, g_send, g_recv, loc, x_send, x_recv, m_send, m_recv, *rest,
):
    h, b = lax.axis_index("head"), lax.axis_index("blk")
    me = b * 2 + h
    total = 2 * n_blk
    _, _, rank = place(0, h, b)
    base = (b // 8) * 8
    head = head_of(h, b)
    working = (b % 4) != 3
    all_here = greet_all(h, b, n_blk)
    loads = [
        pltpu.make_async_copy(src, dst, loc.at[i])
        for i, (src, dst) in enumerate([
            (q_hbm, q), (k_hbm, k), (v_hbm, v), (o_hbm, o), (cos_hbm, cos), (sin_hbm, sin), (norm_hbm, norm),
            (w_hbm, w_all), (part_hbm, part)])
    ]
    for c in loads[8:] + loads[:8]:
        c.start()
    a = ag[...].astype(f32)
    for j in range(12):
        agbuf[j] = jnp.concatenate([a[0:64, 64 * j : 64 * j + 64], a[64:128, 64 * j : 64 * j + 64]], axis=1).astype(bf16)
    all_here()

    def to_head(j):
        r = home_of(j)
        return pltpu.make_async_remote_copy(
            src_ref=agbuf.at[j], dst_ref=do_in.at[rank], send_sem=a_send.at[j], recv_sem=a_recv.at[rank],
            device_id=(r % 2, base + r // 2), device_id_type=MESH,
        )

    for j in range(12):
        @pl.when(rank != home_of(j))
        def _(j=j):
            to_head(j).start()

    def to_tokens(r):
        return pltpu.make_async_remote_copy(
            src_ref=obuf.at[r], dst_ref=got.at[head], send_sem=b_send.at[r], recv_sem=b_recv.at[head],
            device_id=(r % 2, base + r // 2), device_id_type=MESH,
        )

    def to_owner(kk):
        other = (me + kk) % total
        oh, ob = other % 2, other // 2
        return pltpu.make_async_remote_copy(
            src_ref=gbuf.at[oh * n_blk + ob], dst_ref=g_in.at[me], send_sem=g_send.at[kk], recv_sem=g_recv.at[me],
            device_id=(oh, ob), device_id_type=MESH,
        )

    length = lengths[b // 8]

    rs = RowScatter(part, *rest[0:3], rest[3:9], h, b)
    gs = RowScatter(gsum, *rest[9:12], rest[12:18], h, b)
    g_f2 = lax.dot_general(att[...], res_grad[...].astype(bf16), (((0,), (0,)), ((), ())), preferred_element_type=f32)
    for w in range(total):
        cat = jnp.concatenate([g_f2[24 * w : 24 * w + 24], g_small[24 * w : 24 * w + 24, :]], axis=1)
        gpart[w // n_blk, w % n_blk, 0] = fold(cat)
    swaps = [
        pltpu.make_async_remote_copy(
            src_ref=src, dst_ref=dst, send_sem=x_send.at[n], recv_sem=x_recv.at[n],
            device_id=(1 - h, b), device_id_type=MESH)
        for n, (src, dst) in enumerate([(gpart.at[1 - h], gfar), (far_out, far_in)])
    ]
    swaps[0].start()

    def join_planes():
        swaps[0].wait_recv()
        gsum[...] = (gpart[h].astype(f32) + gfar[...].astype(f32)).astype(bf16)
        for n in gs.order:
            gs.send_core(*n)

    loads[8].wait()
    late = [(k, p) for k in (3, 2, 1, 0) if k not in EARLY for p in range(2)]
    def z_early(ks):
        for kk in ks:
            if kk in EARLY and kk:
                for p in range(2):
                    rs.to_z(kk, p).start()

    z_early(Z_FIRST)
    for n in late:
        rs.send_core(*n)

    misc_sum[0] = misc[...]
    z = b // 4
    partners = [(1 - h, b), (h, b + 1 - 2 * (b % 2)), (h, b + 2 - 4 * ((b // 2) % 2)),
                (h, b + 4 - 8 * (z % 2)), (h, b + 8 - 16 * (z // 2))]

    def pairwise(t):
        return pltpu.make_async_remote_copy(
            src_ref=misc_sum.at[t], dst_ref=misc_in.at[t], send_sem=m_send.at[t], recv_sem=m_recv.at[t],
            device_id=partners[t], device_id_type=MESH)

    def pairwise_done(t):
        pairwise(t).wait_recv()
        misc_sum[t + 1] = misc_sum[t] + misc_in[t]
        if t < 4:
            pairwise(t + 1).start()

    pairwise(0).start()
    def step(scatter, stage, n):
        k, p = scatter.order[n]
        return lambda: getattr(scatter, stage)(k, p)

    def ry(n):
        return lambda: rs.send_y(*late[n]) if n < len(late) else None

    def rz(n):
        return lambda: rs.send_z(*late[n]) if n < len(late) else None

    def gy(n):
        return step(gs, "send_y", n)

    def gz(n):
        return step(gs, "send_z", n)

    def pd(t):
        return lambda: pairwise_done(t)

    between = {
        8: [ry(0), pd(0)], 7: [], 6: [], 5: [], 4: [ry(1), pd(1)], 3: [], 2: [], 1: [],
        0: [join_planes, ry(2), pd(2)],
    }

    @pl.when(jnp.logical_not(working))
    def _():
        do_in[...] = jnp.zeros_like(do_in)

    @pl.when(working)
    def _():
        do_in[rank] = agbuf[head]

    for c in loads[:6]:
        c.wait()
    if True:
        def unpack(r, carry):
            @pl.when((r != rank) & working)
            def _():
                pltpu.make_async_remote_copy(
                    src_ref=agbuf.at[0], dst_ref=do_in.at[r], send_sem=a_send.at[0], recv_sem=a_recv.at[r],
                    device_id=(h, b), device_id_type=MESH,
                ).wait_recv()

            t = do_in[r].astype(f32)
            rows = pl.multiple_of(r * 128, 128)
            do[pl.ds(rows, 64), :] = t[:, 0:64].astype(bf16)
            do[pl.ds(rows + 64, 64), :] = t[:, 64:128].astype(bf16)
            return carry

        lax.fori_loop(0, 16, unpack, 0)
        for act in between[8]:
            act()
        for i in range(7, -1, -1):
            width = 256 * (i + 1)
            lo = 256 * i
            qi, doi = q[lo:width, :], do[lo:width, :]
            s = lax.dot_general(qi, k[0:width, :], (((1,), (1,)), ((), ())), preferred_element_type=f32)
            key = lax.broadcasted_iota(jnp.int32, (1, width), 1)
            ov = o[lo:width, :]
            lse = ov[:, 64:65]
            s = (s - lse) + jnp.where(key < length, 0.0, NEG)
            rowi = lax.broadcasted_iota(jnp.int32, (256, 256), 0)
            coli = lax.broadcasted_iota(jnp.int32, (256, 256), 1)
            last = jnp.where(coli <= rowi, s[:, lo:], NEG)
            s = last if i == 0 else jnp.concatenate([s[:, :lo], last], axis=1)
            p = jnp.exp(s)
            dp = lax.dot_general(doi, v[0:width, 0:64], (((1,), (1,)), ((), ())), preferred_element_type=f32)
            inner = jnp.sum(doi.astype(f32) * ov[:, 0:64], axis=1, keepdims=True)
            ds = (p * (dp - inner)).astype(bf16)
            p = p.astype(bf16)
            dq = jnp.dot(ds, k[0:width, :], preferred_element_type=f32) * 0.125
            dki = lax.dot_general(ds, qi, (((0,), (0,)), ((), ())), preferred_element_type=f32)
            dvi = lax.dot_general(p, doi, (((0,), (0,)), ((), ())), preferred_element_type=f32)
            if i == 7:
                dk[...] = dki
                dv[...] = dvi
            else:
                dk[0:width, :] += dki
                dv[0:width, :] += dvi
            both = jnp.concatenate([dq, dk[lo:width, :]], axis=1)
            both = turned(both, cos[lo:width, :], -sin[lo:width, :]).astype(bf16)
            dvl = dv[lo:width, :]
            dqkv[lo:width, 0:128] = both
            dqkv[lo:width, 128:256] = jnp.concatenate([dvl, jnp.zeros_like(dvl)], axis=1).astype(bf16)
            for half in range(2):
                r = 2 * i + half
                obuf[r, 0:128, :] = both[128 * half : 128 * half + 128]
                obuf[r, 128:192, :] = jnp.concatenate(
                    [dvl[128 * half : 128 * half + 64], dvl[128 * half + 64 : 128 * half + 128]], axis=1).astype(bf16)

                @pl.when((r != rank) & working)
                def _(r=r):
                    to_tokens(r).start()
            for act in between[i]:
                act()

        @pl.when(working)
        def _():
            got[head] = obuf[rank]

        loads[6].wait()
        for c in range(3):
            g_f[256 * c : 256 * c + 256, :] = lax.dot_general(
                norm[:, 256 * c : 256 * c + 256], dqkv[...], (((0,), (0,)), ((), ())), preferred_element_type=f32)
        for w in range(total):
            gbuf[w] = fold(g_f[24 * w : 24 * w + 24, :])

        def send_g(kk, carry):
            to_owner(kk).start()
            return carry

        @pl.when(working)
        def _():
            lax.fori_loop(1, total, send_g, 0)
            g_in[me] = gbuf[h * n_blk + b]

    z_early([kk for kk in (3, 2, 1) if kk not in Z_FIRST])
    for act in (*(ry(n) for n in range(3, len(late))), gy(0), gy(1), gy(2), gy(3), rz(0)):
        act()
    rz(1)()
    pairwise_done(3)

    for j in range(12):
        @pl.when(rank != home_of(j))
        def _(j=j):
            pltpu.make_async_remote_copy(
                src_ref=obuf.at[0], dst_ref=got.at[j], send_sem=b_send.at[0], recv_sem=b_recv.at[j],
                device_id=(h, b), device_id_type=MESH,
            ).wait_recv()
    for j in range(0, 12, 2):
        one, two = got[j].astype(f32), got[j + 1].astype(f32)
        lo = 64 * j
        for part_i, at in enumerate((0, 64)):
            dproj[:, 768 * part_i + lo : 768 * part_i + lo + 128] = jnp.concatenate(
                [one[0:128, at : at + 64], two[0:128, at : at + 64]], axis=1).astype(bf16)
        dproj[0:64, 1536 + lo : 1664 + lo] = jnp.concatenate([one[128:192, 0:64], two[128:192, 0:64]], axis=1).astype(bf16)
        dproj[64:128, 1536 + lo : 1664 + lo] = jnp.concatenate([one[128:192, 64:128], two[128:192, 64:128]], axis=1).astype(bf16)
    loads[7].wait()
    dn = lax.dot_general(dproj[...], w_all[...], (((1,), (1,)), ((), ())), preferred_element_type=f32)
    pairwise_done(4)
    x = tok[...].astype(f32)
    scale = lax.rsqrt(jnp.sum(x * x, axis=1, keepdims=True) * (1.0 / 768) + 1e-6)
    xh = x * scale
    t = dn * smt[16:17, :]
    dx = scale * (t - xh * (jnp.sum(t * xh, axis=1, keepdims=True) * (1.0 / 768)))
    dtok_out[...] = (res_grad[...] + dx).astype(bf16)

    for n in range(2, len(late)):
        rz(n)()
    rows = jnp.concatenate([rs.total(0), rs.total(1)], axis=0).astype(bf16)
    far_out[...] = exact_dot(pg[1, :, 0:192], rows, ((1,), (0,))).astype(bf16)
    swaps[1].start()
    for n in range(4):
        gz(n)()
    own = exact_dot(pg[0, :, 0:192], rows, ((1,), (0,))) + local_out[...]

    for src in range(total):
        if (src // 2) % 4 == 3:
            continue

        @pl.when(me != src)
        def _(src=src):
            pltpu.make_async_remote_copy(
                src_ref=gbuf.at[0], dst_ref=g_in.at[src], send_sem=g_send.at[0], recv_sem=g_recv.at[src],
                device_id=(h, b), device_id_type=MESH,
            ).wait_recv()
    for j in range(0, 12, 2):
        pair = []
        for jj in (j, j + 1):
            t = sum(g_in[16 * s + home_of(jj)].astype(f32) for s in range(total // 16))
            pair.append(jnp.concatenate(
                [t[:, 0:256], jnp.concatenate([t[0:8, 256:384], t[8:16, 256:384]], axis=1)], axis=0))
        one, two = pair
        for part in range(3):
            gq_out[:, 768 * part + 64 * j : 768 * part + 64 * j + 128] = jnp.concatenate(
                [one[:, 64 * part : 64 * part + 64], two[:, 64 * part : 64 * part + 64]], axis=1)

    lane = lax.broadcasted_iota(jnp.int32, (24, 128), 1)
    gain_grad = jnp.sum(gq_out[...] * w_own[...].astype(f32), axis=1, keepdims=True) / small[:, 16:17]
    t = gs.total(0)
    t = jnp.concatenate([t[:, 0:896], jnp.concatenate([t[0:8, 896:1344], t[8:16, 896:1344]], axis=1)], axis=0)
    go_out[...] = t[:, 0:768]
    turn[...] = jnp.zeros_like(turn)
    turn[0:24, :] = jnp.where(lane == 16, gain_grad, t[:, 768:896])
    t = jnp.transpose(turn[...])
    router_out[...] = t[0:12, 0:24]
    const_out[...] = t[12:16, 0:24]
    gains_out[...] = t[16:18, 0:24]
    vec_out[...] = t[18:20, 0:24]
    t = misc_sum[5]
    mix_out[...] = t[0:12, 0:12]
    live_total = (lengths[0] + lengths[1]).astype(f32)
    aux = cnt[0:1, :] / (2.0 * live_total) * (t[16:17, :] / live_total)
    aux_out[...] = 12.0 * jnp.sum(aux, axis=1, keepdims=True)
    swaps[1].wait_recv()
    out[...] = (own + far_in[...].astype(f32)).astype(bf16)

    rs.finish([k for k in range(4) if k not in EARLY])
    gs.finish()
    for t in range(5):
        pairwise(t).wait_send()
    for c in swaps:
        c.wait_send()
    for j in range(12):
        @pl.when(rank != home_of(j))
        def _(j=j):
            to_head(j).wait_send()

    @pl.when(working)
    def _():
        for r in range(16):
            @pl.when(r != rank)
            def _(r=r):
                to_tokens(r).wait_send()

        def sent(kk, carry):
            to_owner(kk).wait_send()
            return carry

        lax.fori_loop(1, total, sent, 0)


def attend_back(
    lengths, ag, tok, res_grad, smt, att, local_out, pg, g_small, misc, w_own, small, cnt, norm, q, k, v, o, w_all, parts,
    n_blk,
):
    cos, sin = rotary_tables(2048)
    vm = pl.BlockSpec(memory_space=pltpu.VMEM)
    hbm = pl.BlockSpec(memory_space=pl.ANY)
    sds = jax.ShapeDtypeStruct
    DMA = pltpu.SemaphoreType.DMA
    V = pltpu.VMEM
    total = 2 * n_blk
    return pl.pallas_call(
        functools.partial(backward_kernel, n_blk),
        out_shape=(
            sds((128, 768), bf16), sds((128, 768), bf16), sds((24, 2304), f32), sds((24, 768), f32), sds((12, 24), f32),
            sds((4, 24), f32), sds((2, 24), f32), sds((2, 24), f32), sds((12, 12), f32), sds((1, 1), f32),
        ),
        in_specs=[pl.BlockSpec(memory_space=pltpu.SMEM)] + [vm] * 12 + [hbm] * 9,
        out_specs=(vm,) * 10,
        scratch_shapes=[
            V((2048, 768), bf16), V((2048, 64), bf16), V((2048, 64), bf16), V((2048, 128), bf16), V((2048, 128), f32),
            V((2048, 128), f32), V((2048, 128), f32), V((768, 2304), bf16),
            V((12, 64, 128), bf16), V((16, 64, 128), bf16), V((2048, 64), bf16), V((2048, 64), f32), V((2048, 64), f32),
            V((2048, 256), bf16), V((16, 192, 128), bf16), V((12, 192, 128), bf16), V((128, 2304), bf16), V((128, 128), f32),
            V((768, 256), f32), V((total, 16, 384), bf16), V((total, 16, 384), bf16),
            V((n_blk, 2, 96, 768), bf16), V((2, n_blk, 1, 16, 1344), bf16), V((n_blk, 1, 16, 1344), bf16), V((n_blk, 1, 16, 1344), bf16),
            V((128, 768), bf16), V((128, 768), bf16),
            V((6, 24, 128), f32), V((5, 24, 128), f32),
            DMA((12,)), DMA((16,)), DMA((16,)), DMA((12,)), DMA((total,)), DMA((total,)), DMA((9,)), DMA((2,)), DMA((2,)),
            DMA((5,)), DMA((5,)), *scatter_scratch(2, 96, 768), *scatter_scratch(1, 16, 1344),
        ],
        compiler_params=pltpu.CompilerParams(collective_id=1, has_side_effects=True, vmem_limit_bytes=60 * 2**20),
        cost_estimate=pl.CostEstimate(flops=2 * 10**9, bytes_accessed=2 * 10**7, transcendentals=0),
        name="attend_back",
    )(lengths, ag, tok, res_grad, smt, att, local_out, pg, g_small, misc, w_own, small, cnt, norm, q, k, v, o,
      jnp.asarray(cos), jnp.asarray(sin), w_all, parts)


CAP = 24


eps = 1e-06
aux_weight = 0.01
highest = lax.Precision.HIGHEST
masked_score = -1e30


def shifted(block, axis, distance):
    devices = range(lax.axis_size(axis))
    route = [(i - distance, i) for i in devices if i - distance in devices]
    return lax.ppermute(block, axis, route)


def for_sending(x):
    return jax.tree.map(lambda a: a.astype(jnp.bfloat16) if a.dtype == jnp.float32 else a, x)


def rms_norm(values, gain_vector):
    return values * lax.rsqrt(jnp.mean(values * values, axis=-1, keepdims=True) + eps) * gain_vector


def rotary(values, positions, turn_sign):
    half_width = values.shape[-1] // 2
    frequency = jnp.exp(
        jnp.arange(half_width, dtype=jnp.float32) * (-2.0 * math.log(10000.0) / values.shape[-1])
    )
    angles = positions.astype(jnp.float32)[:, None] * frequency[None, :]
    cosine = jnp.cos(angles)[:, None, :]
    sine_part = turn_sign * jnp.sin(angles)[:, None, :]
    first_half = values[..., :half_width]
    second_half = values[..., half_width:]
    return jnp.concatenate(
        [
            first_half * cosine - second_half * sine_part,
            second_half * cosine + first_half * sine_part,
        ],
        axis=-1,
    )


def slot_lengths(slot_ids, lengths):
    slot_table = jnp.arange(lengths.shape[0], dtype=jnp.int32)
    return jnp.sum(jnp.where(slot_ids[:, None] == slot_table[None, :], lengths[None, :], 0), axis=1)


def allowed_mask(query_ids, key_ids, slot_size, lengths):
    query_slot = query_ids // slot_size
    key_slot = key_ids // slot_size
    query_pos = query_ids - query_slot * slot_size
    key_pos = key_ids - key_slot * slot_size
    key_live = (key_pos < slot_lengths(key_slot, lengths)) & (key_ids >= 0)
    return (
        (query_slot[:, None] == key_slot[None, :])
        & (key_pos[None, :] <= query_pos[:, None])
        & key_live[None, :]
    )


def masked_scores(query_block, key_head, query_ids, key_ids, slot_size, lengths):
    scores = lax.dot_general(
        query_block, key_head, (((1,), (1,)), ((), ())), preferred_element_type=jnp.float32
    ) * HD ** (-0.5)
    return jnp.where(allowed_mask(query_ids, key_ids, slot_size, lengths), scores, masked_score)


def attend_forward(queries, key_all, value_all, query_ids, key_ids, slot_size, lengths):
    head_total = queries.shape[1] // HD

    def one_head(head_index):
        query_head = lax.dynamic_slice_in_dim(queries, head_index * HD, HD, 1)
        key_head = lax.dynamic_slice_in_dim(key_all, head_index * HD, HD, 1)
        value_head = lax.dynamic_slice_in_dim(value_all, head_index * HD, HD, 1)
        scores = masked_scores(query_head, key_head, query_ids, key_ids, slot_size, lengths)
        row_max = jnp.max(scores, axis=1, keepdims=True)
        weights = jnp.exp(scores - row_max)
        row_total = jnp.sum(weights, axis=1, keepdims=True)
        probs_low = (weights / row_total).astype(jnp.bfloat16)
        head_outputs = [jnp.dot(probs_low, value_head, preferred_element_type=jnp.float32)]
        log_parts = [row_max[:, 0] + jnp.log(row_total[:, 0])]
        return (jnp.concatenate(head_outputs, axis=0), jnp.concatenate(log_parts, axis=0))

    head_outputs, log_sums = lax.map(one_head, jnp.arange(head_total, dtype=jnp.int32))
    return (head_outputs.transpose(1, 0, 2).reshape(queries.shape[0], queries.shape[1]), log_sums)


def attend_backward(
    queries, key_all, value_all, out_grads, log_sums, query_ids, key_ids, slot_size, lengths
):
    head_total = queries.shape[1] // HD
    block_rows = min(512, queries.shape[0])

    def one_head(head_index):
        query_head = lax.dynamic_slice_in_dim(queries, head_index * HD, HD, 1)
        key_head = lax.dynamic_slice_in_dim(key_all, head_index * HD, HD, 1)
        value_head = lax.dynamic_slice_in_dim(value_all, head_index * HD, HD, 1)
        grad_head = lax.dynamic_slice_in_dim(out_grads, head_index * HD, HD, 1)
        log_head = lax.dynamic_index_in_dim(log_sums, head_index, 0, keepdims=False)
        key_grad = jnp.zeros(key_head.shape, jnp.float32)
        value_grad = jnp.zeros(value_head.shape, jnp.float32)
        grad_block = grad_head[0:block_rows]
        scores = masked_scores(query_head, key_head, query_ids, key_ids, slot_size, lengths)
        probs = jnp.exp(scores - log_head[0:block_rows][:, None])
        probs_low = probs.astype(jnp.bfloat16)
        prob_grads = lax.dot_general(
            grad_block, value_head, (((1,), (1,)), ((), ())), preferred_element_type=jnp.float32
        )
        row_inner = jnp.sum(probs * prob_grads, axis=1, keepdims=True)
        score_grads = (probs * (prob_grads - row_inner)).astype(jnp.bfloat16)
        query_parts = [
            jnp.dot(score_grads, key_head, preferred_element_type=jnp.float32) * HD ** (-0.5)
        ]
        key_grad = key_grad + lax.dot_general(
            score_grads, query_head, (((0,), (0,)), ((), ())), preferred_element_type=jnp.float32
        ) * HD ** (-0.5)
        value_grad = value_grad + lax.dot_general(
            probs_low, grad_block, (((0,), (0,)), ((), ())), preferred_element_type=jnp.float32
        )
        return (jnp.concatenate(query_parts, axis=0), key_grad, value_grad)

    query_grad, key_grad, value_grad = lax.map(one_head, jnp.arange(head_total, dtype=jnp.int32))
    return (
        query_grad.transpose(1, 0, 2).reshape(queries.shape[0], queries.shape[1]),
        key_grad.transpose(1, 0, 2).reshape(key_all.shape[0], key_all.shape[1]),
        value_grad.transpose(1, 0, 2).reshape(value_all.shape[0], value_all.shape[1]),
    )


def fetch_prev(key_heads, value_heads, span_count):
    key_parts = [key_heads]
    value_parts = [value_heads]
    for offset in range(1, span_count):
        arrived = shifted((key_heads, value_heads), "blk", offset)
        key_parts.append(arrived[0])
        value_parts.append(arrived[1])
    return (jnp.concatenate(key_parts, axis=0), jnp.concatenate(value_parts, axis=0))


def router_probs(normed, router_w, mixing, prev_scores):
    logits = jnp.dot(normed, router_w, precision=highest) + jnp.dot(
        prev_scores, mixing, precision=highest
    )
    return jax.nn.softmax(logits, axis=-1)


def branch_sum(router_prob, normed, const_w, vector_w, outputs_pair, choose, live_rows, real_count):
    gate_values = jnp.sum(choose * router_prob[:, None, :], axis=-1)
    expert_share = jnp.sum(choose * gate_values[:, :, None], axis=1) * live_rows[:, None]
    routed = jnp.sum(gate_values[:, :, None] * outputs_pair, axis=1)
    routed = routed + expert_share[:, real_count + 1 : real_count + 2] * normed
    const_count = vector_w.shape[1]
    const_mix = jax.nn.softmax(
        jnp.dot(normed, const_w, precision=highest).reshape(normed.shape[0], const_count, 2),
        axis=-1,
    )
    for const_index in range(const_count):
        const_out = (
            const_mix[:, const_index, 0:1] * normed
            + const_mix[:, const_index, 1:2] * vector_w[:, const_index][None, :]
        )
        routed = (
            routed
            + expert_share[:, real_count + 2 + const_index : real_count + 3 + const_index]
            * const_out
        )
    return routed


def on_device(
    tokens,
    cotangent,
    prev_logits,
    routes,
    lengths,
    w_qkv,
    w_out,
    w_router,
    w_const,
    const_vec,
    norm_gains,
    gate_mix,
    expert_weights,
):
    tok_dev = tokens.shape[0]
    model_width = tokens.shape[1]
    head_count = lax.axis_size("head")
    blk_count = lax.axis_size("blk")
    span_count = max(8, min(blk_count // 4, 8192 // (head_count * tok_dev)) * min(1, tok_dev // 64))
    head_index = lax.axis_index("head")
    blk_index = lax.axis_index("blk")
    slot_size = span_count * head_count * tok_dev
    tok_blk = head_count * tok_dev
    qkv_w, out_w, router_w, const_w, vector_w, gain_pair = (
        lax.all_gather(w_qkv, ("head", "blk"), axis=0, tiled=True),
        lax.all_gather(w_out, ("head", "blk"), axis=0, tiled=True),
        lax.all_gather(w_router, ("head", "blk"), axis=0, tiled=True),
        lax.all_gather(w_const, ("head", "blk"), axis=0, tiled=True),
        lax.all_gather(const_vec, ("head", "blk"), axis=0, tiled=True),
        lax.all_gather(norm_gains, ("head", "blk"), axis=0, tiled=True),
    )
    gain_pair = gain_pair.astype(jnp.float32)
    row_ids = (blk_index * head_count + head_index) * tok_dev + jnp.arange(tok_dev, dtype=jnp.int32)
    slot_ids = row_ids // slot_size
    positions = row_ids - slot_ids * slot_size
    live_rows = (positions < slot_lengths(slot_ids, lengths)).astype(jnp.float32)
    inputs = tokens.astype(jnp.float32)
    normed_one, norm_one_back = jax.vjp(rms_norm, inputs, gain_pair[:, 0])
    normed_one_low = normed_one.astype(jnp.bfloat16)
    projected = jnp.dot(normed_one_low, qkv_w, preferred_element_type=jnp.float32).reshape(
        tok_dev, 3, HEADS, HD
    )
    query_send = (
        rotary(projected[:, 0], positions, 1.0).astype(jnp.bfloat16).reshape(tok_dev, model_width)
    )
    key_send = (
        rotary(projected[:, 1], positions, 1.0).astype(jnp.bfloat16).reshape(tok_dev, model_width)
    )
    value_send = projected[:, 2].astype(jnp.bfloat16).reshape(tok_dev, model_width)
    query_heads, key_heads, value_heads = (
        lax.all_to_all(query_send, "head", split_axis=1, concat_axis=0, tiled=True),
        lax.all_to_all(key_send, "head", split_axis=1, concat_axis=0, tiled=True),
        lax.all_to_all(value_send, "head", split_axis=1, concat_axis=0, tiled=True),
    )
    blk_rows = blk_index * tok_blk + jnp.arange(tok_blk, dtype=jnp.int32)
    blk_pos = blk_rows - blk_rows // slot_size * slot_size
    key_ids = jnp.concatenate([blk_rows - offset * tok_blk for offset in range(span_count)], axis=0)
    key_all, value_all = fetch_prev(key_heads, value_heads, span_count)
    attended, log_sums = attend_forward(
        query_heads, key_all, value_all, blk_rows, key_ids, slot_size, lengths
    )
    attended_tok = lax.all_to_all(
        attended.astype(jnp.bfloat16), "head", split_axis=0, concat_axis=1, tiled=True
    )
    residual = inputs + jnp.dot(attended_tok, out_w, preferred_element_type=jnp.float32)
    normed_two, norm_two_back = jax.vjp(rms_norm, residual, gain_pair[:, 1])
    normed_two_low = normed_two.astype(jnp.bfloat16)
    normed_two_f = normed_two_low.astype(jnp.float32)
    router_prob, router_back = jax.vjp(
        partial(router_probs, prev_scores=prev_logits),
        normed_two_f,
        router_w.astype(jnp.float32),
        gate_mix,
    )
    expert_count = router_w.shape[1]
    real_count = expert_weights.shape[1] * head_count
    choose = (
        routes[:, :, None] == jnp.arange(expert_count, dtype=jnp.int32)[None, None, :]
    ).astype(jnp.float32)
    count_local = jnp.sum(jnp.sum(choose, axis=1) * live_rows[:, None], axis=0)
    prob_local = jnp.sum(router_prob * live_rows[:, None], axis=0)
    count_all, prob_all = lax.psum((count_local, prob_local), ("head", "blk"))
    live_total = jnp.sum(lengths).astype(jnp.float32)
    fraction = count_all / (2.0 * live_total)
    aux_loss = expert_count * jnp.sum(fraction * (prob_all / live_total))
    gate_values = jnp.sum(choose * router_prob[:, None, :], axis=-1)
    out_grad = live_rows[:, None] * cotangent.astype(jnp.float32)
    assigned = routes.reshape(-1)
    live_pairs = jnp.repeat(live_rows, 2)
    is_real = (assigned < real_count) & (live_pairs > 0)
    onehot = (
        (assigned[:, None] == jnp.arange(real_count, dtype=jnp.int32)[None, :]) & is_real[:, None]
    ).astype(jnp.int32)
    slot_rank = jnp.sum((jnp.cumsum(onehot, axis=0) - onehot) * onehot, axis=1)
    target = jnp.where(is_real, assigned * CAP + slot_rank, real_count * CAP)
    source = (
        jnp.full((real_count * CAP + 1,), 2 * tok_dev, jnp.int32)
        .at[target]
        .set(jnp.arange(2 * tok_dev, dtype=jnp.int32))[: real_count * CAP]
    )
    zero_row = jnp.zeros((1, model_width), jnp.bfloat16)
    send_rows = jnp.concatenate([normed_two_low, zero_row], axis=0)[source // 2].reshape(
        real_count, CAP, model_width
    )
    pair_grads = (gate_values.reshape(-1, 1) * jnp.repeat(out_grad, 2, axis=0)).astype(jnp.bfloat16)
    send_grads = jnp.concatenate([pair_grads, zero_row], axis=0)[source].reshape(
        real_count, CAP, model_width
    )
    expert_in, expert_cot = (
        lax.all_to_all(send_rows, "head", split_axis=0, concat_axis=1, tiled=True),
        lax.all_to_all(send_grads, "head", split_axis=0, concat_axis=1, tiled=True),
    )
    weight_piece = lax.all_gather(expert_weights, "blk", axis=0, tiled=True)
    gate_w = weight_piece[:, :, 0, :]
    up_w = weight_piece[:, :, 1, :]
    down_w = weight_piece[:, :, 2, :]
    gate_part = jnp.einsum("esd,ned->esn", expert_in, gate_w, preferred_element_type=jnp.float32)
    up_part = jnp.einsum("esd,ned->esn", expert_in, up_w, preferred_element_type=jnp.float32)
    sigmoid_part = jax.nn.sigmoid(gate_part)
    silu_part = gate_part * sigmoid_part
    hidden = (silu_part * up_part).astype(jnp.bfloat16)
    out_sum = jnp.einsum("esn,ned->esd", hidden, down_w, preferred_element_type=jnp.float32)
    hidden_grad = jnp.einsum("esd,ned->esn", expert_cot, down_w, preferred_element_type=jnp.float32)
    gate_grad = (
        hidden_grad * up_part * (sigmoid_part * (1.0 + gate_part * (1.0 - sigmoid_part)))
    ).astype(jnp.bfloat16)
    up_grad = (hidden_grad * silu_part).astype(jnp.bfloat16)
    in_grad = jnp.einsum("esn,ned->esd", gate_grad, gate_w, preferred_element_type=jnp.float32)
    in_grad = in_grad + jnp.einsum(
        "esn,ned->esd", up_grad, up_w, preferred_element_type=jnp.float32
    )
    hidden_all = hidden
    gate_all = gate_grad
    up_all = up_grad
    out_sum, in_grad, hidden_all, gate_all, up_all = (
        out_sum,
        in_grad,
        hidden_all,
        gate_all,
        up_all,
    )
    hidden_own, gate_own, up_own = (
        lax.all_to_all(hidden_all, "blk", split_axis=2, concat_axis=1, tiled=True),
        lax.all_to_all(gate_all, "blk", split_axis=2, concat_axis=1, tiled=True),
        lax.all_to_all(up_all, "blk", split_axis=2, concat_axis=1, tiled=True),
    )
    rows_in = lax.all_gather(expert_in, "blk", axis=1, tiled=True)
    rows_cot = lax.all_gather(expert_cot, "blk", axis=1, tiled=True)
    gate_w_grad = jnp.einsum("esn,esd->ned", gate_own, rows_in, preferred_element_type=jnp.float32)
    up_w_grad = jnp.einsum("esn,esd->ned", up_own, rows_in, preferred_element_type=jnp.float32)
    down_w_grad = jnp.einsum(
        "esn,esd->ned", hidden_own, rows_cot, preferred_element_type=jnp.float32
    )
    expert_grads = jnp.stack([gate_w_grad, up_w_grad, down_w_grad], axis=2)
    returned, returned_grad = (
        lax.all_to_all(
            out_sum.astype(jnp.bfloat16), "head", split_axis=1, concat_axis=0, tiled=True
        ),
        lax.all_to_all(
            in_grad.astype(jnp.bfloat16), "head", split_axis=1, concat_axis=0, tiled=True
        ),
    )
    outputs_pair = (
        jnp.concatenate([returned.reshape(-1, model_width), zero_row], axis=0)[target]
        .astype(jnp.float32)
        .reshape(tok_dev, 2, model_width)
    )
    input_pair = (
        jnp.concatenate([returned_grad.reshape(-1, model_width), zero_row], axis=0)[target]
        .astype(jnp.float32)
        .reshape(tok_dev, 2, model_width)
    )
    expert_input_grad = input_pair[:, 0] + input_pair[:, 1]
    branch, branch_back = jax.vjp(
        partial(branch_sum, choose=choose, live_rows=live_rows, real_count=real_count),
        router_prob,
        normed_two_f,
        const_w.astype(jnp.float32),
        vector_w.astype(jnp.float32),
        outputs_pair,
    )
    output = ((residual + branch) * live_rows[:, None]).astype(jnp.bfloat16)
    prob_grad, normed_grad_branch, const_grad, vector_grad, unused_grad = branch_back(out_grad)
    aux_grad = aux_weight * expert_count / live_total * fraction[None, :] * live_rows[:, None]
    normed_grad_router, router_grad, mixing_grad = router_back(prob_grad + aux_grad)
    normed_grad = normed_grad_router + normed_grad_branch + expert_input_grad
    residual_grad_norm, gain_two_grad = norm_two_back(normed_grad)
    residual_grad = out_grad + residual_grad_norm
    out_w_grad = jnp.dot(attended_tok.astype(jnp.float32).T, residual_grad, precision=highest)
    attended_grad = jnp.dot(residual_grad, out_w.astype(jnp.float32).T, precision=highest).astype(
        jnp.bfloat16
    )
    attended_grad_heads = lax.all_to_all(
        attended_grad, "head", split_axis=1, concat_axis=0, tiled=True
    )
    key_again, value_again = fetch_prev(key_heads, value_heads, span_count)
    query_grad, key_grad, value_grad = attend_backward(
        query_heads,
        key_again,
        value_again,
        attended_grad_heads,
        log_sums,
        blk_rows,
        key_ids,
        slot_size,
        lengths,
    )
    own_key = key_grad[:tok_blk]
    own_value = value_grad[:tok_blk]
    for offset in range(1, span_count):
        back_key, back_value = shifted(
            (
                for_sending(key_grad[offset * tok_blk : (offset + 1) * tok_blk]),
                for_sending(value_grad[offset * tok_blk : (offset + 1) * tok_blk]),
            ),
            "blk",
            -offset,
        )
        own_key = own_key + back_key
        own_value = own_value + back_value
    local_heads = query_heads.shape[1] // HD
    query_back = (
        rotary(query_grad.reshape(tok_blk, local_heads, HD), blk_pos, -1.0)
        .astype(jnp.bfloat16)
        .reshape(tok_blk, local_heads * HD)
    )
    key_back = (
        rotary(own_key.reshape(tok_blk, local_heads, HD), blk_pos, -1.0)
        .astype(jnp.bfloat16)
        .reshape(tok_blk, local_heads * HD)
    )
    value_back = own_value.astype(jnp.bfloat16)
    query_tok, key_tok, value_tok = (
        lax.all_to_all(query_back, "head", split_axis=0, concat_axis=1, tiled=True),
        lax.all_to_all(key_back, "head", split_axis=0, concat_axis=1, tiled=True),
        lax.all_to_all(value_back, "head", split_axis=0, concat_axis=1, tiled=True),
    )
    projected_grad = jnp.concatenate([query_tok, key_tok, value_tok], axis=1)
    qkv_grad = jnp.dot(normed_one_low.T, projected_grad, preferred_element_type=jnp.float32)
    normed_one_grad = jnp.dot(projected_grad, qkv_w.T, preferred_element_type=jnp.float32)
    inputs_grad_norm, gain_one_grad = norm_one_back(normed_one_grad)
    token_grad = (residual_grad + inputs_grad_norm).astype(jnp.bfloat16)
    weight_grads = (
        lax.psum_scatter(qkv_grad, ("head", "blk"), scatter_dimension=0, tiled=True),
        lax.psum_scatter(out_w_grad, ("head", "blk"), scatter_dimension=0, tiled=True),
        lax.psum_scatter(router_grad, ("head", "blk"), scatter_dimension=0, tiled=True),
        lax.psum_scatter(const_grad, ("head", "blk"), scatter_dimension=0, tiled=True),
        lax.psum_scatter(vector_grad, ("head", "blk"), scatter_dimension=0, tiled=True),
        lax.psum_scatter(
            jnp.stack([gain_one_grad, gain_two_grad], axis=1),
            ("head", "blk"),
            scatter_dimension=0,
            tiled=True,
        ),
    )
    mixing_total = lax.psum(mixing_grad, ("head", "blk"))
    return (
        output,
        aux_loss,
        token_grad,
        weight_grads[0],
        weight_grads[1],
        weight_grads[2],
        weight_grads[3],
        weight_grads[4],
        weight_grads[5],
        mixing_total,
        expert_grads,
    )


def settle_kernel(n, *refs):
    sources, results, (sems, *rooms) = refs[:n], refs[n : 2 * n], refs[2 * n :]
    ins, outs = [], []
    for i in range(n):
        parts = [(sources[i], rooms[i], results[i])]
        if i == n - 1:
            parts = [tuple(r.at[pl.ds(32 * c, 32)] for r in parts[0]) for c in range(4)]
        for src, room, dst in parts:
            ins.append(pltpu.make_async_copy(src, room, sems.at[0, len(ins)]))
            outs.append(pltpu.make_async_copy(room, dst, sems.at[1, len(outs)]))
    for c in ins[::-1]:
        c.start()
    for c, d in zip(ins[::-1], outs[::-1]):
        c.wait()
        d.start()
    for d in outs:
        d.wait()


def settle(*arrays):
    hbm = pl.BlockSpec(memory_space=pl.ANY)
    n = len(arrays)
    return pl.pallas_call(
        functools.partial(settle_kernel, n),
        out_shape=tuple(jax.ShapeDtypeStruct(a.shape, a.dtype) for a in arrays),
        in_specs=[hbm] * n,
        out_specs=(hbm,) * n,
        scratch_shapes=[pltpu.SemaphoreType.DMA((2, n + 3))] + [pltpu.VMEM(a.shape, a.dtype) for a in arrays],
        compiler_params=pltpu.CompilerParams(vmem_limit_bytes=63 * 2**20),
        name="settle",
    )(*arrays)


def on_device_small(
    tokens, cotangent, prev_logits, routes, lengths, w_qkv, w_out, w_router, w_const, const_vec, norm_gains, gate_mix,
    expert_weights,
):
    n_blk = lax.axis_size("blk")
    w_all = lax.all_gather(w_qkv, ("head", "blk"), axis=0, tiled=True)
    norm, q, k, v, o, parts, g_exp, att, smt, cnt, local_out, res_grad, att_grad, g_small, misc, pg, small = front(
        lengths, tokens, cotangent, routes, w_qkv, w_router, w_const, norm_gains, const_vec, w_out, prev_logits, gate_mix,
        expert_weights.transpose(0, 2, 1, 3), n_blk)
    output, token_grad, qkv_grad, g_out, g_router, g_const, g_vec, g_gains, g_mix, aux = attend_back(
        lengths, att_grad, tokens, res_grad, smt, att, local_out, pg, g_small, misc, w_qkv, small, cnt, norm, q, k, v, o, w_all,
        parts, n_blk)
    results = settle(output, token_grad, qkv_grad, g_out, g_router, g_const, g_vec, g_gains, g_mix, aux, g_exp)
    output, token_grad, qkv_grad, g_out, g_router, g_const, g_vec, g_gains, g_mix, aux, g_exp = results
    return (
        output, aux.reshape(()), token_grad, qkv_grad, g_out, g_router.T, g_const.T, g_vec.T, g_gains.T, g_mix,
        g_exp.transpose(0, 2, 1, 3),
    )


def solution(mesh):
    small = mesh.shape["blk"] == 16 and mesh.shape["head"] == 2
    return jax.shard_map(
        on_device_small if small else on_device,
        mesh=mesh,
        in_specs=(
            P(("blk", "head"), None),
            P(("blk", "head"), None),
            P(("blk", "head"), None),
            P(("blk", "head"), None),
            P(),
            P(("head", "blk"), None),
            P(("head", "blk"), None),
            P(("head", "blk"), None),
            P(("head", "blk"), None),
            P(("head", "blk"), None),
            P(("head", "blk"), None),
            P(),
            P("blk", "head", None, None),
        ),
        out_specs=(
            P(("blk", "head"), None),
            P(),
            P(("blk", "head"), None),
            P(("head", "blk"), None),
            P(("head", "blk"), None),
            P(("head", "blk"), None),
            P(("head", "blk"), None),
            P(("head", "blk"), None),
            P(("head", "blk"), None),
            P(),
            P("blk", "head", None, None),
        ),
        check_vma=False,
    )
```
